32 devices in a mesh: cfg: 2 (over x), wide: 4 (over z), narrow: 4 (over y, core).
Axes of the slice: x: 2, y: 2, z: 4, core: 2. Of those that a mesh axis runs over, the one named last changes fastest.
Arguments:
- hidden: bfloat16 [2, 512, 3072], P('cfg', 'wide', 'narrow'), may hold values from -120 to 120
- split_table: int32 [4], replicated, may hold values from 1 to 128, 256 in all
- modulation: float32 [8, 3072], P(None, 'narrow'), may hold values from -4 to 4
- expand_weight: bfloat16 [3072, 12288], P('narrow', 'wide'), may hold values from -0.109375 to 0.109375
- contract_weight: bfloat16 [12288, 3072], P('wide', 'narrow'), may hold values from -0.0546875 to 0.0546875
- output_weight: bfloat16 [3072, 64], P('narrow'), may hold values from -0.109375 to 0.109375
- latent: float32 [512, 64], P('wide'), may hold values from -6 to 6
- timestep: int32 [1], replicated, may hold values from 20 to 499
Outputs:
- layer_out: bfloat16 [2, 512, 3072], P('cfg', 'wide', 'narrow')
- clean_latent: float32 [512, 64], P('wide')
The draws below stay inside these ranges and needn't reach their ends.
Inputs may be any that keep to these rules, and one draw needn't show every extreme that they name: `split_table`: the entries sum to 256, and the largest is exactly 128.
All inputs are finite; a program needn't handle non-finite values.
Results may differ from the reference program's by a relative error of at most 0.0056.
Values may be sent and summed in bfloat16 or wider, within the bound.
No kernel may reach another device: no remote copies, remote signals or barrier semaphores. Data moves between devices by JAX's collectives and lax.ppermute only.
A program may use at most 64 MiB of HBM per device.

```python
import math
import jax
import jax.numpy as jnp
import numpy as np
from jax import lax

D = 3072
FF = 12288
PATCH = 64
TEXT = 226
CAP = 128
SLOTS = 512
TOKENS = 256
N_WIDE = 4


def draw_hidden(key, part):
    keys = jax.random.split(key, 4)
    column = jnp.arange(D, dtype=jnp.float32) / (D - 1)
    jitter = jax.random.uniform(keys[1], (D,), jnp.float32, 0.7, 1.3)
    row_draw = jax.random.uniform(keys[2], (2, SLOTS, 1), jnp.float32, 0.0, 1.0)
    centre = jnp.clip(jax.random.normal(keys[3], (2, SLOTS, 1), jnp.float32), -3.0, 3.0)
    base = jnp.clip(jax.random.normal(keys[0], (2, SLOTS, D), jnp.float32), -4.0, 4.0)
    column_scale = 3.0 ** column * jitter
    row_scale = 10.0 ** row_draw
    return (0.3 * row_scale * (base * column_scale + centre)).astype(jnp.bfloat16)


def steps_of(rng, dims, pieces, least, top_value):
    factor_of = 1.0
    for dim, parts in pieces:
        heights = jax.random.uniform(jax.random.fold_in(jax.random.fold_in(rng, 6), dim), (parts,), jnp.float32, least / len(pieces), top_value / len(pieces))
        factor_of = factor_of * jnp.repeat(jnp.exp(heights), dims[dim] // parts).reshape((-1,) + (1,) * (len(dims) - 1 - dim))
    return factor_of


def split_up(number_of, total, bound, lean):
    loads = [(1 << 20) // math.isqrt(grade ** lean) + 1 for grade in range(2, number_of + 1)]
    rest, counts = total - bound - (number_of - 1), [1] * (number_of - 1)
    while rest > 0:
        movable = [i for i in range(number_of - 1) if counts[i] < bound]
        whole, remaining = sum([loads[i] for i in movable]), rest
        for i in movable:
            more = min(bound - counts[i], max(1, remaining * loads[i] // whole), rest)
            counts[i] = counts[i] + more
            rest = rest - more
    return np.array([bound] + counts)


def uneven_parts(rng, count, total, reach, skew):
    if count == 2:
        one = jax.random.randint(rng, (), max(1, total - reach), min(reach, total - 1) + 1)
        return jnp.stack([one, total - one])
    sizes = jnp.asarray(split_up(count, total, reach, skew), jnp.int32)
    couples = (count - 1) // 2
    source_of, taker = sizes[1:1 + 2 * couples:2], sizes[2:2 + 2 * couples:2]
    room = jnp.minimum(source_of - 1, reach - taker)
    shifted = jax.random.randint(jax.random.fold_in(rng, 1), (couples,), 0, 1 << 20) % (room + 1)
    sizes = sizes.at[1:1 + 2 * couples:2].set(source_of - shifted).at[2:2 + 2 * couples:2].set(taker + shifted)
    return sizes[jax.random.permutation(jax.random.fold_in(rng, 2), count)]


def normal_values(stream_key, shape, spread, most, pieces=(), held_as=jnp.bfloat16):
    values = spread * jax.random.normal(stream_key, shape, jnp.float32)
    if pieces:
        values = values * steps_of(stream_key, shape, pieces, -0.22, 0.18)
    return jnp.clip(values, -most, most).astype(held_as)


def setup_inputs(seed: int = 0) -> dict:
    key_of = jax.random.split(jax.random.key(seed), 9)
    return {
        "hidden": draw_hidden(jax.random.fold_in(key_of[8], 71), 0),
        "split_table": uneven_parts(key_of[1], N_WIDE, TOKENS, CAP, 1).astype(jnp.int32),
        "modulation": normal_values(key_of[2], (8, D), 1.0, 4.0, ((1, 4),), jnp.float32),
        "expand_weight": normal_values(key_of[3], (D, FF), D ** -0.5, 0.109375, ((0, 4), (1, 4))),
        "contract_weight": normal_values(key_of[4], (FF, D), FF ** -0.5, 0.0546875, ((0, 4), (1, 4))),
        "output_weight": normal_values(key_of[5], (D, PATCH), D ** -0.5, 0.109375, ((0, 4),)),
        "latent": normal_values(key_of[6], (SLOTS, PATCH), 1.0, 6.0, ((0, 4),), jnp.float32),
        "timestep": jax.random.randint(key_of[7], (1,), 20, 500).astype(jnp.int32),
    }


norm_eps = 1e-05
guidance = 6.0

def alpha_table():
    steps_index = jnp.arange(1000, dtype=jnp.int32)
    start_root = 0.00085 ** 0.5
    end_root = 0.012 ** 0.5
    roots = start_root + (end_root - start_root) * steps_index.astype(jnp.float32) / 999.0
    return (steps_index, jnp.cumprod(1.0 - roots * roots))

def layer_norm(values, shifts, scaling):
    average = lax.optimization_barrier(jnp.sum(values, -1, keepdims=True)) / D
    squares = lax.optimization_barrier(jnp.sum(values * values, -1, keepdims=True)) / D
    variance = squares - average * average
    return (values - average) * lax.rsqrt(variance + norm_eps) * (1.0 + scaling) + shifts

def reference(hidden, split_table, modulation, expand_weight, contract_weight, output_weight, latent, timestep):
    slot_total = N_WIDE * CAP
    slot_index = jnp.arange(slot_total, dtype=jnp.int32)
    block_index = slot_index // CAP
    inner_index = slot_index % CAP
    offsets = jnp.cumsum(split_table) - split_table
    position = offsets[block_index] + inner_index
    slot_live = inner_index < split_table[block_index]
    is_text = slot_live & (position < TEXT)
    is_video = slot_live & (position >= TEXT)
    text_column = is_text[:, None]
    shifts = jnp.where(text_column, modulation[3], modulation[0])
    scaling = jnp.where(text_column, modulation[4], modulation[1])
    gating = jnp.where(text_column, modulation[5], modulation[2])
    values = hidden.astype(jnp.float32)
    normed = layer_norm(values, shifts, scaling).astype(jnp.bfloat16)

    def feed_forward(row_block):
        hidden_pre = jnp.dot(row_block, expand_weight, preferred_element_type=jnp.float32)
        activated = jax.nn.gelu(hidden_pre, approximate=True).astype(jnp.bfloat16)
        return jnp.dot(activated, contract_weight, preferred_element_type=jnp.float32)
    ff_result = lax.map(feed_forward, normed.reshape(2 * N_WIDE, CAP, D)).reshape(2, slot_total, D)
    layer_out = jnp.where(slot_live[:, None], values + gating * ff_result, 0.0).astype(jnp.bfloat16)
    final_in = layer_out.astype(jnp.float32)
    final_normed = layer_norm(final_in, modulation[6], modulation[7]).astype(jnp.bfloat16)
    velocity_cond = jnp.dot(final_normed[0], output_weight, preferred_element_type=jnp.float32)
    velocity_uncond = jnp.dot(final_normed[1], output_weight, preferred_element_type=jnp.float32)
    guided = guidance * velocity_cond + (1.0 - guidance) * velocity_uncond
    steps_index, alpha_bar = alpha_table()
    alpha_now = jnp.sum(jnp.where(steps_index == timestep[0], alpha_bar, 0.0))
    clean_latent = jnp.where(is_video[:, None], jnp.sqrt(alpha_now) * latent - jnp.sqrt(1.0 - alpha_now) * guided, 0.0)
    return (layer_out, clean_latent)
```

```python
import jax
import jax.numpy as jnp
from jax import lax
from jax.sharding import PartitionSpec as P

D = 3072
TEXT = 226


norm_eps = 1e-05
guidance = 6.0


def alpha_table():
    steps_index = jnp.arange(1000, dtype=jnp.int32)
    start_root = 0.00085**0.5
    end_root = 0.012**0.5
    roots = start_root + (end_root - start_root) * steps_index.astype(jnp.float32) / 999.0
    return (steps_index, jnp.cumprod(1.0 - roots * roots))


def feature_norm(values, shifts, scaling):
    totals, squares = lax.psum(
        (jnp.sum(values, -1, keepdims=True), jnp.sum(values * values, -1, keepdims=True)), "narrow"
    )
    average = totals / D
    variance = squares / D - average * average
    return (values - average) * lax.rsqrt(variance + norm_eps) * (1.0 + scaling) + shifts


def any_slice(
    hidden, split_table, modulation, expand_weight, contract_weight, output_weight, latent, timestep
):
    capacity = hidden.shape[1]
    wide_index = lax.axis_index("wide")
    table_index = jnp.arange(split_table.shape[0], dtype=jnp.int32)
    offset = jnp.sum(jnp.where(table_index < wide_index, split_table, 0))
    own_count = jnp.sum(jnp.where(table_index == wide_index, split_table, 0))
    slot_index = jnp.arange(capacity, dtype=jnp.int32)
    position = offset + slot_index
    slot_live = slot_index < own_count
    is_text = slot_live & (position < TEXT)
    is_video = slot_live & (position >= TEXT)
    text_column = is_text[:, None]
    shifts = jnp.where(text_column, modulation[3], modulation[0])
    scaling = jnp.where(text_column, modulation[4], modulation[1])
    gating = jnp.where(text_column, modulation[5], modulation[2])
    values = hidden[0].astype(jnp.float32)
    normed = feature_norm(values, shifts, scaling).astype(jnp.bfloat16)
    hidden_part = jnp.dot(
        lax.all_gather(normed, "wide", axis=0, tiled=True),
        expand_weight,
        preferred_element_type=jnp.float32,
    )
    hidden_pre = lax.psum(hidden_part, "narrow")
    activated = jax.nn.gelu(hidden_pre, approximate=True).astype(jnp.bfloat16)
    ff_result = lax.psum_scatter(
        jnp.dot(activated, contract_weight, preferred_element_type=jnp.float32),
        "wide",
        scatter_dimension=0,
        tiled=True,
    )
    layer_out = jnp.where(slot_live[:, None], values + gating * ff_result, 0.0).astype(jnp.bfloat16)
    final_in = layer_out.astype(jnp.float32)
    final_normed = feature_norm(final_in, modulation[6], modulation[7]).astype(jnp.bfloat16)
    velocity_part = jnp.dot(final_normed, output_weight, preferred_element_type=jnp.float32)
    copy_weight = jnp.where(lax.axis_index("cfg") == 0, guidance, 1.0 - guidance)
    guided = lax.psum(velocity_part * copy_weight, ("cfg", "narrow"))
    steps_index, alpha_bar = alpha_table()
    alpha_now = jnp.sum(jnp.where(steps_index == timestep[0], alpha_bar, 0.0))
    clean_latent = jnp.where(
        is_video[:, None], jnp.sqrt(alpha_now) * latent - jnp.sqrt(1.0 - alpha_now) * guided, 0.0
    )
    return (layer_out[None], clean_latent)


def swap(array, axis, distance, size):
    return lax.ppermute(array, axis, [(i, i ^ distance) for i in range(size)])


def core_swap(array):
    return swap(array, "narrow", 1, 4)


def y_swap(array):
    return swap(array, "narrow", 2, 4)


def pick(table, index):
    return jnp.sum(jnp.where(jnp.arange(4, dtype=jnp.int32) == index, table, 0))


def four_blocks(
    hidden, split_table, modulation, expand_weight, contract_weight, output_weight, latent, timestep
):
    capacity = hidden.shape[1]
    half = capacity // 2
    block = lax.axis_index("wide")
    first_core = lax.axis_index("narrow") % 2 == 0
    units = expand_weight.shape[1] // 2

    counts = split_table
    order = jnp.arange(4, dtype=jnp.int32)
    earlier = order[None, :] < order[:, None]
    largest = jnp.min(jnp.where(counts == capacity, order, 4))
    other_counts = jnp.where(order == largest, 0, counts)
    other_before = jnp.sum(jnp.where(earlier, other_counts[None, :], 0), 1)
    first_counts = jnp.where(
        order == largest, half, jnp.clip(half - other_before, 0, counts)
    )
    offsets = jnp.sum(jnp.where(earlier, counts[None, :], 0), 1)
    own_first = pick(first_counts, block)
    own_count = pick(counts, block)
    offset = pick(offsets, block)

    slot_index = jnp.arange(capacity, dtype=jnp.int32)
    position = offset + slot_index
    slot_live = slot_index < own_count
    is_text = slot_live & (position < TEXT)
    is_video = slot_live & (position >= TEXT)
    text_column = is_text[:, None]
    shifts = jnp.where(text_column, modulation[3], modulation[0])
    scaling = jnp.where(text_column, modulation[4], modulation[1])
    gating = jnp.where(text_column, modulation[5], modulation[2])

    piece_row = jnp.arange(half, dtype=jnp.int32)
    rows_a, rows_b = [], []
    base_a, base_b = 0, 0
    for s in range(4):
        of_first, of_count = pick(first_counts, block ^ s), pick(counts, block ^ s)
        rows_a.append(jnp.where(piece_row < of_first, base_a + piece_row, -1))
        slot = jnp.where(piece_row >= of_first, piece_row, piece_row + half)
        rows_b.append(jnp.where(slot < of_count, base_b + slot - of_first, -1))
        base_a, base_b = base_a + of_first, base_b + of_count - of_first
    chunk_row = jnp.arange(capacity, dtype=jnp.int32)
    place_a = (chunk_row[:, None] == jnp.concatenate(rows_a)[None, :]).astype(jnp.bfloat16)
    place_b = (chunk_row[:, None] == jnp.concatenate(rows_b)[None, :]).astype(jnp.bfloat16)

    values = hidden[0].astype(jnp.float32)
    sums = jnp.concatenate(
        [jnp.sum(values, -1)[None], jnp.sum(values * values, -1)[None]], 0
    )
    sums = sums + core_swap(sums)
    sums = sums + y_swap(sums)
    average = (sums[0] / D)[:, None]
    variance = (sums[1] / D)[:, None] - average * average
    normed = (values - average) * lax.rsqrt(variance + norm_eps) * (1.0 + scaling) + shifts
    normed = jnp.where(slot_live[:, None], normed, 0.0).astype(jnp.bfloat16)
    piece_a = normed[:half]
    piece_b = jnp.where((piece_row < own_first)[:, None], normed[half:], normed[:half])

    def feed_forward(piece, place):
        pieces = [piece] + [swap(piece, "wide", s, 4) for s in (1, 2, 3)]
        tokens = jnp.dot(
            place, jnp.concatenate(pieces, 0), preferred_element_type=jnp.float32
        ).astype(jnp.bfloat16)
        part = jnp.dot(tokens, expand_weight, preferred_element_type=jnp.float32)
        kept = jnp.where(first_core, part[:, :units], part[:, units:])
        sent = jnp.where(first_core, part[:, units:], part[:, :units]).astype(jnp.bfloat16)
        kept = kept + core_swap(sent).astype(jnp.float32)
        hidden_pre = kept + y_swap(kept.astype(jnp.bfloat16)).astype(jnp.float32)
        activated = jax.nn.gelu(hidden_pre, approximate=True).astype(jnp.bfloat16)
        other = core_swap(activated)
        whole = jnp.concatenate(
            [jnp.where(first_core, activated, other), jnp.where(first_core, other, activated)], 1
        )
        part_out = jnp.dot(whole, contract_weight, preferred_element_type=jnp.float32).astype(
            jnp.bfloat16
        )
        spread = lax.dot_general(
            place, part_out, (((0,), (0,)), ((), ())), preferred_element_type=jnp.float32
        ).astype(jnp.bfloat16)
        total = spread[:half].astype(jnp.float32)
        for s in (1, 2, 3):
            total = total + swap(spread[s * half : (s + 1) * half], "wide", s, 4).astype(jnp.float32)
        return total

    out_a = feed_forward(piece_a, place_a)
    out_b = feed_forward(piece_b, place_b)
    ff_result = jnp.concatenate(
        [jnp.where((piece_row < own_first)[:, None], out_a, out_b), out_b], 0
    )
    layer_out = jnp.where(slot_live[:, None], values + gating * ff_result, 0.0).astype(jnp.bfloat16)

    final_in = layer_out.astype(jnp.float32)
    features = final_in.shape[1]
    total = jnp.sum(final_in, -1, keepdims=True)
    square = jnp.sum(final_in * final_in, -1, keepdims=True)
    centre = total / features
    scale = 1.0 + modulation[7]
    weight = output_weight.astype(jnp.float32)
    column_scale = jnp.sum(scale[:, None] * weight, 0, keepdims=True)
    column_shift = jnp.sum(modulation[6][:, None] * weight, 0, keepdims=True)
    product = jnp.dot(
        ((final_in - centre) * scale).astype(jnp.bfloat16),
        output_weight,
        preferred_element_type=jnp.float32,
    )
    product = product + centre * column_scale
    width = product.shape[1]
    lanes = jnp.arange(width, dtype=jnp.int32)[None, :]
    side = jnp.where(lanes == 0, total, jnp.where(lanes == 1, square, 0.0))
    ends = jnp.concatenate([column_scale, column_shift], 1)
    bundle = jnp.concatenate(
        [jnp.concatenate([product, side], 1), jnp.broadcast_to(ends, (8, 2 * width))], 0
    )
    bundle = bundle + core_swap(bundle)
    bundle = bundle + y_swap(bundle)
    average = bundle[:capacity, width : width + 1] / D
    variance = bundle[:capacity, width + 1 : width + 2] / D - average * average
    velocity = (bundle[:capacity, :width] - average * bundle[capacity : capacity + 1, :width]) * lax.rsqrt(
        variance + norm_eps
    ) + bundle[capacity : capacity + 1, width:]
    copy_weight = jnp.where(lax.axis_index("cfg") == 0, guidance, 1.0 - guidance)
    velocity = velocity * copy_weight
    guided = velocity + swap(velocity, "cfg", 1, 2)

    steps_index, alpha_bar = alpha_table()
    alpha_now = jnp.sum(jnp.where(steps_index == timestep[0], alpha_bar, 0.0))
    clean_latent = jnp.where(
        is_video[:, None], jnp.sqrt(alpha_now) * latent - jnp.sqrt(1.0 - alpha_now) * guided, 0.0
    )
    return (layer_out[None], clean_latent)


def solution(mesh):
    by_swaps = (mesh.shape["wide"], mesh.shape["narrow"], mesh.shape["cfg"]) == (4, 4, 2)
    return jax.shard_map(
        four_blocks if by_swaps else any_slice,
        mesh=mesh,
        in_specs=(
            P("cfg", "wide", "narrow"),
            P(),
            P(None, "narrow"),
            P("narrow", "wide"),
            P("wide", "narrow"),
            P("narrow", None),
            P("wide", None),
            P(),
        ),
        out_specs=(P("cfg", "wide", "narrow"), P("wide", None)),
        check_vma=False,
    )
```

```python
import functools

import jax
import jax.numpy as jnp
import numpy as np
from jax import lax
from jax.experimental import pallas as pl
from jax.experimental.pallas import tpu as pltpu
from jax.sharding import PartitionSpec as P

D = 3072
TEXT = 226


norm_eps = 1e-05
guidance = 6.0


def alpha_table():
    steps_index = jnp.arange(1000, dtype=jnp.int32)
    start_root = 0.00085**0.5
    end_root = 0.012**0.5
    roots = start_root + (end_root - start_root) * steps_index.astype(jnp.float32) / 999.0
    return (steps_index, jnp.cumprod(1.0 - roots * roots))


def feature_norm(values, shifts, scaling):
    totals, squares = lax.psum(
        (jnp.sum(values, -1, keepdims=True), jnp.sum(values * values, -1, keepdims=True)), "narrow"
    )
    average = totals / D
    variance = squares / D - average * average
    return (values - average) * lax.rsqrt(variance + norm_eps) * (1.0 + scaling) + shifts


def any_slice(
    hidden, split_table, modulation, expand_weight, contract_weight, output_weight, latent, timestep
):
    capacity = hidden.shape[1]
    wide_index = lax.axis_index("wide")
    table_index = jnp.arange(split_table.shape[0], dtype=jnp.int32)
    offset = jnp.sum(jnp.where(table_index < wide_index, split_table, 0))
    own_count = jnp.sum(jnp.where(table_index == wide_index, split_table, 0))
    slot_index = jnp.arange(capacity, dtype=jnp.int32)
    position = offset + slot_index
    slot_live = slot_index < own_count
    is_text = slot_live & (position < TEXT)
    is_video = slot_live & (position >= TEXT)
    text_column = is_text[:, None]
    shifts = jnp.where(text_column, modulation[3], modulation[0])
    scaling = jnp.where(text_column, modulation[4], modulation[1])
    gating = jnp.where(text_column, modulation[5], modulation[2])
    values = hidden[0].astype(jnp.float32)
    normed = feature_norm(values, shifts, scaling).astype(jnp.bfloat16)
    hidden_part = jnp.dot(
        lax.all_gather(normed, "wide", axis=0, tiled=True),
        expand_weight,
        preferred_element_type=jnp.float32,
    )
    hidden_pre = lax.psum(hidden_part, "narrow")
    activated = jax.nn.gelu(hidden_pre, approximate=True).astype(jnp.bfloat16)
    ff_result = lax.psum_scatter(
        jnp.dot(activated, contract_weight, preferred_element_type=jnp.float32),
        "wide",
        scatter_dimension=0,
        tiled=True,
    )
    layer_out = jnp.where(slot_live[:, None], values + gating * ff_result, 0.0).astype(jnp.bfloat16)
    final_in = layer_out.astype(jnp.float32)
    final_normed = feature_norm(final_in, modulation[6], modulation[7]).astype(jnp.bfloat16)
    velocity_part = jnp.dot(final_normed, output_weight, preferred_element_type=jnp.float32)
    copy_weight = jnp.where(lax.axis_index("cfg") == 0, guidance, 1.0 - guidance)
    guided = lax.psum(velocity_part * copy_weight, ("cfg", "narrow"))
    steps_index, alpha_bar = alpha_table()
    alpha_now = jnp.sum(jnp.where(steps_index == timestep[0], alpha_bar, 0.0))
    clean_latent = jnp.where(
        is_video[:, None], jnp.sqrt(alpha_now) * latent - jnp.sqrt(1.0 - alpha_now) * guided, 0.0
    )
    return (layer_out[None], clean_latent)


QUOTAS = (0, 64, 128)
CAP = 128
CHUNKS = len(QUOTAS) - 1
F32, BF16 = jnp.float32, jnp.bfloat16


def size_of(k):
    return QUOTAS[k + 1] - QUOTAS[k]


def swap(array, axis, distance, size):
    return lax.ppermute(array, axis, [(i, i ^ distance) for i in range(size)])


def z_swaps(array):
    return [swap(array, "wide", s, 4) for s in (1, 2, 3)]


def choose(values, index):
    out = values[0]
    for i in range(1, 4):
        out = jnp.where(index == i, values[i], out)
    return out


def layout(table):
    counts = [table[b] for b in range(4)]
    largest = jnp.int32(3)
    for b in (2, 1, 0):
        largest = jnp.where(counts[b] == CAP, b, largest)
    starts, others, ranks, offsets = [], [], [], []
    rank, offset = jnp.int32(0), jnp.int32(0)
    for b in range(4):
        other = jnp.where(largest == b, 0, 1)
        ranks.append(rank * other)
        others.append(other)
        offsets.append(offset)
        rank = rank + other * counts[b]
        offset = offset + counts[b]
    block = lax.axis_index("wide")
    of = lambda values: [choose(values, jnp.bitwise_xor(block, s)) for s in range(4)]
    return of(ranks), of(counts), of(others), of(offsets)[0], choose(offsets, largest)


def text_rows(k, largest_offset):
    size = size_of(k)
    row = lax.broadcasted_iota(jnp.int32, (2 * size, 1), 0)
    rank = jnp.where(row < size, row, row - size) + QUOTAS[k]
    position = jnp.where(
        row < size, rank + largest_offset, jnp.where(rank < largest_offset, rank, rank + CAP)
    )
    return position < TEXT


def sums_kernel(mod, out_weight, w, own_out, other_out, ends_out, buffer, sems):
    core = lax.axis_index("narrow") % 2
    units = buffer.shape[1] // 2
    copies = []
    for t in range(2):
        copies.append(
            pltpu.make_async_copy(
                w.at[:, pl.ds(t * units, units)], buffer.at[:, pl.ds(t * units, units)], sems.at[t]
            )
        )
        copies[-1].start()
    row = lax.broadcasted_iota(jnp.int32, (8, 1), 0)
    rows = jnp.where(row == 0, 1.0 + mod[1:2, :], jnp.zeros((8, 1), F32))
    rows = jnp.where(row == 1, 1.0 + mod[4:5, :], rows)
    rows = jnp.where(row == 2, mod[0:1, :], rows)
    rows = jnp.where(row == 3, mod[3:4, :], rows)
    high = rows.astype(BF16)
    low = (rows - high.astype(F32)).astype(BF16)
    both = jnp.concatenate([high, low], 0)
    ends = jnp.where(row == 0, 1.0 + mod[7:8, :], mod[6:7, :])
    high = ends.astype(BF16)
    low = (ends - high.astype(F32)).astype(BF16)
    ends = jnp.dot(jnp.concatenate([high, low], 0), out_weight[...], preferred_element_type=F32)
    ends = ends[:8] + ends[8:]
    ends_out[...] = jnp.concatenate(
        [jnp.broadcast_to(ends[0:1], ends.shape), jnp.broadcast_to(ends[1:2], ends.shape)], 1
    )
    for t in range(2):
        copies[t].wait()
        part = jnp.dot(both, buffer[:, t * units : (t + 1) * units], preferred_element_type=F32)
        part = part[:8] + part[8:]

        @pl.when(core == t)
        def _():
            own_out[...] = part

        @pl.when(core != t)
        def _():
            other_out[...] = part


def fetch(w, start, buffer, sems, tiles, axis):
    width = buffer.shape[axis] // tiles
    copies = []
    for t in range(tiles):
        source = pl.ds(pl.multiple_of(start + t * width, 128), width)
        place = pl.ds(t * width, width)
        if axis == 1:
            copy = pltpu.make_async_copy(w.at[:, source], buffer.at[:, place], sems.at[t])
        else:
            copy = pltpu.make_async_copy(w.at[source, :], buffer.at[place, :], sems.at[t])
        copy.start()
        copies.append(copy)
    return copies, width


def expand_sent_kernel(k, table, mod, *refs):
    pieces = refs[: 4 * (k + 1)]
    w, z_out, sent_out, side_out, buffer, sems = refs[4 * (k + 1) :]
    core = lax.axis_index("narrow") % 2
    units = buffer.shape[1]
    tiles = sems.shape[0]
    copies, width = fetch(w, (1 - core) * units, buffer, sems, tiles, 1)

    size = size_of(k)
    ranks, counts, others, _, largest_offset = layout(table)
    places = []
    for p in range(k + 1):
        piece = size_of(p)
        lane = lax.broadcasted_iota(jnp.int32, (1, 4 * piece), 1)
        which, slot = lane // piece, lane % piece + QUOTAS[p]
        rank = slot + choose(ranks, which) - QUOTAS[k]
        live = (rank >= 0) & (rank < size) & (slot < choose(counts, which))
        row = jnp.where(live, rank + choose(others, which) * size, -1)
        at = lax.broadcasted_iota(jnp.int32, (2 * size, 4 * piece), 0)
        places.append(jnp.where(at == row, 1.0, 0.0).astype(BF16))
    place = jnp.concatenate(places, 1)
    tokens = jnp.concatenate([piece[...] for piece in pieces], 0)
    x = jnp.dot(place, tokens, preferred_element_type=F32)

    centre = (jnp.sum(x, -1, keepdims=True) / x.shape[1]).astype(BF16).astype(F32)
    x = x - centre
    total = jnp.sum(x, -1, keepdims=True)
    square = jnp.sum(x * x, -1, keepdims=True)
    text = text_rows(k, largest_offset)
    z = (x * (1.0 + jnp.where(text, mod[4:5, :], mod[1:2, :]))).astype(BF16)
    z_out[...] = z
    total_high = total.astype(BF16).astype(F32)
    square_high = square.astype(BF16).astype(F32)
    lane = lax.broadcasted_iota(jnp.int32, (2 * size, 128), 1) - 8 * core
    side = jnp.where((lane == 0) | (lane == 1), centre, 0.0)
    side = jnp.where(lane == 4, total_high, side)
    side = jnp.where(lane == 5, total - total_high, side)
    side = jnp.where(lane == 6, square_high, side)
    side = jnp.where(lane == 7, square - square_high, side).astype(BF16)
    side_out[...] = side
    sent_out[:, units:] = side
    for t in range(tiles):
        copies[t].wait()
        sent_out[:, t * width : (t + 1) * width] = jnp.dot(
            z, buffer[:, t * width : (t + 1) * width], preferred_element_type=F32
        ).astype(BF16)


def expand_kept_kernel(z, w, kept_out, buffer, sems):
    core = lax.axis_index("narrow") % 2
    units = buffer.shape[1]
    tiles = sems.shape[0]
    copies, width = fetch(w, core * units, buffer, sems, tiles, 1)
    for t in range(tiles):
        copies[t].wait()
        kept_out[:, t * width : (t + 1) * width] = jnp.dot(
            z[...], buffer[:, t * width : (t + 1) * width], preferred_element_type=F32
        )


def merge_kernel(kept, side, came, total_out, sent_out):
    units = kept.shape[1]
    total = kept[...] + came[:, :units].astype(F32)
    total_out[...] = total
    sent_out[:, :units] = total.astype(BF16)
    sent_out[:, units:] = (side[...].astype(F32) + came[:, units:].astype(F32)).astype(BF16)


def activate_kernel(k, features, table, total, sent, came, sums_own, sums_other, act_out):
    units = total.shape[1]
    size = size_of(k)
    text = text_rows(k, layout(table)[4])
    sides = [sent[:, units:].astype(F32), came[:, units:].astype(F32)]
    lane = lax.broadcasted_iota(jnp.int32, (2 * size, 128), 1)
    field = lane % 8
    used = lane < 16
    summed = sides[0] + sides[1]
    add = lambda values, mask: jnp.sum(jnp.where(mask, values, 0.0), -1, keepdims=True)
    centres = add(summed, used & (field == 0))
    totals = add(summed, used & ((field == 4) | (field == 5)))
    average = (centres * features + totals) / D
    spread = add(summed, used & ((field == 6) | (field == 7)))
    factors = []
    for side in sides:
        apart = side - average
        for core in range(2):
            own = (lane // 8) == core
            off = add(apart, own & (field == 0))
            spread = spread + off * (
                2.0 * add(side, own & ((field == 4) | (field == 5))) + features * off
            )
        factors.append(apart)
    variance = spread / D
    scale = lax.rsqrt(variance + norm_eps)
    of_text = jnp.where(text, 1, 0)
    mine = used & ((field % 2) == of_text)
    pre = total[...] + came[:, :units].astype(F32)
    extra = jnp.zeros_like(pre)
    for factor, sums in zip(factors, (sums_own, sums_other)):
        factor = jnp.where(
            mine & (field < 2), factor * scale, jnp.where(mine & (field < 4), 1.0, 0.0)
        )
        extra = extra + jnp.dot(
            factor[:, :16], sums[...], precision=lax.Precision.HIGHEST, preferred_element_type=F32
        )
    act_out[...] = jax.nn.gelu(pre * scale + extra, approximate=True).astype(BF16)


def contract_own_kernel(act, w, out, buffer, sems):
    core = lax.axis_index("narrow") % 2
    tiles = sems.shape[0]
    copies, width = fetch(w, core * buffer.shape[0], buffer, sems, tiles, 0)
    total = None
    for t in range(tiles):
        copies[t].wait()
        part = jnp.dot(
            act[:, t * width : (t + 1) * width],
            buffer[t * width : (t + 1) * width, :],
            preferred_element_type=F32,
        )
        total = part if total is None else total + part
    out[...] = total


def contract_other_kernel(k, table, act, so_far, w, *refs):
    outs, buffer, sems = refs[:4], refs[4], refs[5]
    core = lax.axis_index("narrow") % 2
    tiles = sems.shape[0]
    copies, width = fetch(w, (1 - core) * buffer.shape[0], buffer, sems, tiles, 0)
    size = size_of(k)
    ranks, counts, others, _, _ = layout(table)
    places = []
    for s in range(4):
        first = jnp.maximum(QUOTAS[k] - ranks[s], 0)
        last = jnp.minimum(counts[s], QUOTAS[k + 1] - ranks[s])
        index = lax.broadcasted_iota(jnp.int32, (size, 1), 0)
        slot = first + jnp.bitwise_and(index - first, size - 1)
        row = jnp.where(slot < last, slot + ranks[s] - QUOTAS[k] + others[s] * size, -1)
        at = lax.broadcasted_iota(jnp.int32, (size, 2 * size), 1)
        places.append(jnp.where(at == row, 1.0, 0.0).astype(BF16))
    total = so_far[...]
    for t in range(tiles):
        copies[t].wait()
        total = total + jnp.dot(
            act[:, t * width : (t + 1) * width],
            buffer[t * width : (t + 1) * width, :],
            preferred_element_type=F32,
        )
    spread = jnp.dot(
        jnp.concatenate(places, 0), total.astype(BF16), preferred_element_type=F32
    ).astype(BF16)
    for s in range(4):
        outs[s][...] = spread[s * size : (s + 1) * size]


def finish_kernel(table, hidden, mod, out_weight, ends, *refs):
    pieces, (layer_out, bundle_out) = refs[: 4 * CHUNKS], refs[4 * CHUNKS :]
    ranks, counts, _, offset, _ = layout(table)
    slot = lax.broadcasted_iota(jnp.int32, (CAP, 1), 0)
    live = slot < counts[0]
    text = slot + offset < TEXT
    rank = slot + ranks[0]
    result = jnp.zeros(hidden.shape, F32)
    for k in range(CHUNKS):
        total = pieces[4 * k][...].astype(F32)
        for s in (1, 2, 3):
            total = total + pieces[4 * k + s][...].astype(F32)
        total = jnp.concatenate([total] * (CAP // size_of(k)), 0)
        result = jnp.where((rank >= QUOTAS[k]) & (rank < QUOTAS[k + 1]), total, result)
    gate = jnp.where(text, mod[5:6, :], mod[2:3, :])
    layer = jnp.where(live, hidden[...].astype(F32) + gate * result, 0.0).astype(BF16)
    layer_out[...] = layer
    x = layer.astype(F32)
    total = jnp.sum(x, -1, keepdims=True)
    square = jnp.sum(x * x, -1, keepdims=True)
    centre = total / x.shape[1]
    product = jnp.dot(
        ((x - centre) * (1.0 + mod[7:8, :])).astype(BF16),
        out_weight[...],
        preferred_element_type=F32,
    )
    width = product.shape[1]
    bundle_out[:CAP, :width] = product + centre * ends[0:1, :width]
    lane = lax.broadcasted_iota(jnp.int32, (CAP, width), 1)
    bundle_out[:CAP, width:] = jnp.where(lane == 0, total, jnp.where(lane == 1, square, 0.0))
    bundle_out[CAP:, :] = ends[...]


def velocity_kernel(first, second, third, fourth, out):
    bundle = (first[...] + second[...]) + (third[...] + fourth[...])
    width = bundle.shape[1] // 2
    average = bundle[:CAP, width : width + 1] / D
    variance = bundle[:CAP, width + 1 : width + 2] / D - average * average
    velocity = (bundle[:CAP, :width] - average * bundle[CAP : CAP + 1, :width]) * lax.rsqrt(
        variance + norm_eps
    ) + bundle[CAP : CAP + 1, width:]
    out[...] = velocity * jnp.where(lax.axis_index("cfg") == 0, guidance, 1.0 - guidance)


def latent_kernel(table, timestep, alphas, latent, mine, other, out):
    _, counts, _, offset, _ = layout(table)
    slot = lax.broadcasted_iota(jnp.int32, (CAP, 1), 0)
    video = (slot < counts[0]) & (slot + offset >= TEXT)
    index = lax.broadcasted_iota(jnp.int32, (8, 128), 0) * 128 + lax.broadcasted_iota(
        jnp.int32, (8, 128), 1
    )
    alpha = jnp.sum(
        jnp.sum(jnp.where(index == timestep[0], alphas[...], 0.0), 0, keepdims=True),
        1,
        keepdims=True,
    )
    clean = jnp.sqrt(alpha) * latent[...] - jnp.sqrt(1.0 - alpha) * (mine[...] + other[...])
    out[...] = jnp.where(video, clean, 0.0)


def alpha_constant():
    ends = np.sqrt(np.float64(0.00085)), np.sqrt(np.float64(0.012))
    betas = np.linspace(ends[0], ends[1], 1000, dtype=np.float64) ** 2
    return np.pad(np.cumprod(1.0 - betas), (0, 24)).astype(np.float32).reshape(8, 128)


def call(kernel, outs, args, spaces, scratch=(), flops=0, moved=0):
    kinds = {"v": pltpu.VMEM, "s": pltpu.SMEM, "a": pl.ANY}
    return pl.pallas_call(
        kernel,
        out_shape=[jax.ShapeDtypeStruct(shape, dtype) for shape, dtype in outs],
        in_specs=[pl.BlockSpec(memory_space=kinds[letter]) for letter in spaces],
        out_specs=[pl.BlockSpec(memory_space=pltpu.VMEM) for _ in outs],
        scratch_shapes=list(scratch),
        compiler_params=pltpu.CompilerParams(vmem_limit_bytes=24 * 2**20),
        cost_estimate=pl.CostEstimate(flops=flops, bytes_accessed=moved, transcendentals=0),
    )(*args)


def four_blocks(
    hidden, split_table, modulation, expand_weight, contract_weight, output_weight, latent, timestep
):
    hidden = hidden[0]
    features = hidden.shape[1]
    units = expand_weight.shape[1] // 2
    width = output_weight.shape[1]
    first_core = lax.axis_index("narrow") % 2 == 0

    arrived = []
    for k in range(CHUNKS):
        piece = hidden[QUOTAS[k] : QUOTAS[k + 1]]
        arrived.append([piece] + z_swaps(piece))

    sums_mine, sums_sent, ends = call(
        sums_kernel,
        [((8, units), F32), ((8, units), F32), ((8, 2 * width), F32)],
        [modulation, output_weight, expand_weight],
        "vva",
        [pltpu.VMEM(expand_weight.shape, BF16), pltpu.SemaphoreType.DMA((2,))],
        2 * 16 * features * 2 * units,
        2 * features * 2 * units,
    )
    sums_came = swap(sums_sent, "narrow", 1, 4)
    sums_chip = jnp.where(
        first_core,
        jnp.concatenate([sums_mine, sums_came], 0),
        jnp.concatenate([sums_came, sums_mine], 0),
    )
    sums_other = swap(sums_chip, "narrow", 2, 4)

    tiles = 3
    half_flops = lambda k: 2 * 2 * size_of(k) * features * units
    half_bytes = 2 * features * units
    expand_scratch = [pltpu.VMEM((features, units), BF16), pltpu.SemaphoreType.DMA((tiles,))]
    contract_scratch = [pltpu.VMEM((units, features), BF16), pltpu.SemaphoreType.DMA((tiles,))]
    returned = []
    for k in range(CHUNKS):
        rows = 2 * size_of(k)
        pieces = [piece for phase in arrived[: k + 1] for piece in phase]
        z, sent, side = call(
            functools.partial(expand_sent_kernel, k),
            [((rows, features), BF16), ((rows, units + 128), BF16), ((rows, 128), BF16)],
            [split_table, modulation, *pieces, expand_weight],
            "sv" + "v" * len(pieces) + "a",
            expand_scratch,
            half_flops(k),
            half_bytes,
        )
        came = swap(sent, "narrow", 1, 4)
        (kept,) = call(
            expand_kept_kernel,
            [((rows, units), F32)],
            [z, expand_weight],
            "va",
            expand_scratch,
            half_flops(k),
            half_bytes,
        )
        total, sent = call(
            merge_kernel,
            [((rows, units), F32), ((rows, units + 128), BF16)],
            [kept, side, came],
            "vvv",
        )
        came = swap(sent, "narrow", 2, 4)
        (act,) = call(
            functools.partial(activate_kernel, k, features),
            [((rows, units), BF16)],
            [split_table, total, sent, came, sums_chip, sums_other],
            "svvvvv",
        )
        act_came = swap(act, "narrow", 1, 4)
        (out,) = call(
            contract_own_kernel,
            [((rows, features), F32)],
            [act, contract_weight],
            "va",
            contract_scratch,
            half_flops(k),
            half_bytes,
        )
        pieces = call(
            functools.partial(contract_other_kernel, k),
            [((size_of(k), features), BF16)] * 4,
            [split_table, act_came, out, contract_weight],
            "svva",
            contract_scratch,
            half_flops(k),
            half_bytes,
        )
        returned.append(pieces[0])
        returned.extend(swap(pieces[s], "wide", s, 4) for s in (1, 2, 3))

    layer_out, bundle = call(
        finish_kernel,
        [((CAP, features), BF16), ((CAP + 8, 2 * width), F32)],
        [split_table, hidden, modulation, output_weight, ends, *returned],
        "svvvv" + "v" * len(returned),
    )
    (velocity,) = call(
        velocity_kernel,
        [((CAP, width), F32)],
        [bundle] + [swap(bundle, "narrow", n, 4) for n in (1, 2, 3)],
        "vvvv",
    )
    (clean_latent,) = call(
        latent_kernel,
        [((CAP, width), F32)],
        [split_table, timestep, alpha_constant(), latent, velocity, swap(velocity, "cfg", 1, 2)],
        "ssvvvv",
    )
    return (layer_out[None], clean_latent)


def solution(mesh):
    by_swaps = (mesh.shape["wide"], mesh.shape["narrow"], mesh.shape["cfg"]) == (4, 4, 2)
    return jax.shard_map(
        four_blocks if by_swaps else any_slice,
        mesh=mesh,
        in_specs=(
            P("cfg", "wide", "narrow"),
            P(),
            P(None, "narrow"),
            P("narrow", "wide"),
            P("wide", "narrow"),
            P("narrow", None),
            P("wide", None),
            P(),
        ),
        out_specs=(P("cfg", "wide", "narrow"), P("wide", None)),
        check_vma=False,
    )
```

```python
import functools

import jax
import jax.numpy as jnp
import numpy as np
from jax import lax
from jax.experimental import pallas as pl
from jax.experimental.pallas import tpu as pltpu
from jax.sharding import PartitionSpec as P

D = 3072
TEXT = 226


norm_eps = 1e-05
guidance = 6.0


def alpha_table():
    steps_index = jnp.arange(1000, dtype=jnp.int32)
    start_root = 0.00085**0.5
    end_root = 0.012**0.5
    roots = start_root + (end_root - start_root) * steps_index.astype(jnp.float32) / 999.0
    return (steps_index, jnp.cumprod(1.0 - roots * roots))


def feature_norm(values, shifts, scaling):
    totals, squares = lax.psum(
        (jnp.sum(values, -1, keepdims=True), jnp.sum(values * values, -1, keepdims=True)), "narrow"
    )
    average = totals / D
    variance = squares / D - average * average
    return (values - average) * lax.rsqrt(variance + norm_eps) * (1.0 + scaling) + shifts


def any_slice(
    hidden, split_table, modulation, expand_weight, contract_weight, output_weight, latent, timestep
):
    capacity = hidden.shape[1]
    wide_index = lax.axis_index("wide")
    table_index = jnp.arange(split_table.shape[0], dtype=jnp.int32)
    offset = jnp.sum(jnp.where(table_index < wide_index, split_table, 0))
    own_count = jnp.sum(jnp.where(table_index == wide_index, split_table, 0))
    slot_index = jnp.arange(capacity, dtype=jnp.int32)
    position = offset + slot_index
    slot_live = slot_index < own_count
    is_text = slot_live & (position < TEXT)
    is_video = slot_live & (position >= TEXT)
    text_column = is_text[:, None]
    shifts = jnp.where(text_column, modulation[3], modulation[0])
    scaling = jnp.where(text_column, modulation[4], modulation[1])
    gating = jnp.where(text_column, modulation[5], modulation[2])
    values = hidden[0].astype(jnp.float32)
    normed = feature_norm(values, shifts, scaling).astype(jnp.bfloat16)
    hidden_part = jnp.dot(
        lax.all_gather(normed, "wide", axis=0, tiled=True),
        expand_weight,
        preferred_element_type=jnp.float32,
    )
    hidden_pre = lax.psum(hidden_part, "narrow")
    activated = jax.nn.gelu(hidden_pre, approximate=True).astype(jnp.bfloat16)
    ff_result = lax.psum_scatter(
        jnp.dot(activated, contract_weight, preferred_element_type=jnp.float32),
        "wide",
        scatter_dimension=0,
        tiled=True,
    )
    layer_out = jnp.where(slot_live[:, None], values + gating * ff_result, 0.0).astype(jnp.bfloat16)
    final_in = layer_out.astype(jnp.float32)
    final_normed = feature_norm(final_in, modulation[6], modulation[7]).astype(jnp.bfloat16)
    velocity_part = jnp.dot(final_normed, output_weight, preferred_element_type=jnp.float32)
    copy_weight = jnp.where(lax.axis_index("cfg") == 0, guidance, 1.0 - guidance)
    guided = lax.psum(velocity_part * copy_weight, ("cfg", "narrow"))
    steps_index, alpha_bar = alpha_table()
    alpha_now = jnp.sum(jnp.where(steps_index == timestep[0], alpha_bar, 0.0))
    clean_latent = jnp.where(
        is_video[:, None], jnp.sqrt(alpha_now) * latent - jnp.sqrt(1.0 - alpha_now) * guided, 0.0
    )
    return (layer_out[None], clean_latent)


QUOTAS = (0, 64, 128)
CAP = 128
CHUNKS = len(QUOTAS) - 1
F32, BF16 = jnp.float32, jnp.bfloat16
TILE = 512
WEIGHTS = {
    "prepare": 1,
    "expand_sent": 10**10,
    "expand_kept": 10**10,
    "merge": 1,
    "activate": 1,
    "contract_own": 10**10,
    "contract_other": 1,
}


def size_of(k):
    return QUOTAS[k + 1] - QUOTAS[k]


def swap(array, axis, distance, size):
    return lax.ppermute(array, axis, [(i, i ^ distance) for i in range(size)])


def z_swaps(array):
    return [swap(array, "wide", s, 4) for s in (1, 2, 3)]


def choose(values, index):
    out = values[0]
    for i in range(1, 4):
        out = jnp.where(index == i, values[i], out)
    return out


def layout(table):
    counts = [table[b] for b in range(4)]
    largest = jnp.int32(3)
    for b in (2, 1, 0):
        largest = jnp.where(counts[b] == CAP, b, largest)
    starts, others, ranks, offsets = [], [], [], []
    rank, offset = jnp.int32(0), jnp.int32(0)
    for b in range(4):
        other = jnp.where(largest == b, 0, 1)
        ranks.append(rank * other)
        others.append(other)
        offsets.append(offset)
        rank = rank + other * counts[b]
        offset = offset + counts[b]
    block = lax.axis_index("wide")
    of = lambda values: [choose(values, jnp.bitwise_xor(block, s)) for s in range(4)]
    return of(ranks), of(counts), of(others), of(offsets)[0], choose(offsets, largest)


def text_rows(k, largest_offset):
    size = size_of(k)
    row = lax.broadcasted_iota(jnp.int32, (2 * size, 1), 0)
    rank = jnp.where(row < size, row, row - size) + QUOTAS[k]
    position = jnp.where(
        row < size, rank + largest_offset, jnp.where(rank < largest_offset, rank, rank + CAP)
    )
    return position < TEXT


def high_low(values):
    high = values.astype(BF16)
    return high, (values - high.astype(F32)).astype(BF16)


def load(source, place, sems):
    parts = sems.shape[0]
    height = source.shape[0] // parts
    copies = []
    for t in range(parts):
        rows = pl.ds(t * height, height)
        copies.append(pltpu.make_async_copy(source.at[rows, :], place.at[rows, :], sems.at[t]))
        copies[-1].start()
    return copies


def hold_kernel(source, place, sems):
    for copy in load(source, place, sems):
        copy.wait()


def prepare_kernel(hidden, mod, out_weight, w, *refs):
    later, (held, own_out, other_out, sems) = refs[: CHUNKS - 1], refs[CHUNKS - 1 :]
    core = lax.axis_index("narrow") % 2
    units = own_out.shape[1]
    copies = load(w, held, sems)
    for k in range(1, CHUNKS):
        later[k - 1][...] = hidden[QUOTAS[k] : QUOTAS[k + 1], :]
    row = lax.broadcasted_iota(jnp.int32, (8, 1), 0)
    rows = jnp.where(row == 0, 1.0 + mod[1:2, :], jnp.zeros((8, 1), F32))
    rows = jnp.where(row == 1, 1.0 + mod[4:5, :], rows)
    rows = jnp.where(row == 2, mod[0:1, :], rows)
    rows = jnp.where(row == 3, mod[3:4, :], rows)
    both = jnp.concatenate(high_low(rows), 0)
    rows = jnp.where(row == 4, 1.0 + mod[7:8, :], jnp.zeros((8, 1), F32))
    rows = jnp.where(row == 5, mod[6:7, :], rows)
    ends = lax.dot_general(
        jnp.concatenate(high_low(rows), 0),
        out_weight[...],
        (((1,), (1,)), ((), ())),
        preferred_element_type=F32,
    )
    ends = ends[:8] + ends[8:]
    ends = jnp.concatenate([ends, jnp.zeros((8, 128 - ends.shape[1]), F32)], 1)
    for copy in copies:
        copy.wait()
    for t in range(2):
        part = jnp.dot(both, held[:, t * units : (t + 1) * units], preferred_element_type=F32)
        part = part[:8] + part[8:]

        @pl.when(core == t)
        def _():
            own_out[...] = part
            own_out[:, :128] = part[:, :128] + ends

        @pl.when(core != t)
        def _():
            other_out[...] = part
            other_out[:, :128] = part[:, :128] + ends


def chip_kernel(mine, came, out):
    first = lax.axis_index("narrow") % 2 == 0
    out[:8, :] = jnp.where(first, mine[...], came[...])
    out[8:, :] = jnp.where(first, came[...], mine[...])


def factors_kernel(mine, chip, other, out, ends_out):
    rows = []
    for sums in (chip, other):
        high, low = high_low(sums[...])
        rows += [high, low, high]
    out[...] = jnp.concatenate(rows + [jnp.zeros((32, chip.shape[1]), BF16)], 0)
    total = (chip[:8, :128] + chip[8:, :128]) + (other[:8, :128] + other[8:, :128])
    ends_out[...] = jnp.concatenate([total, mine[:, :128], jnp.zeros((112, 128), F32)], 0).T


def expand_sent_kernel(k, table, mod, *refs):
    pieces = refs[: 4 * (k + 1)]
    w = refs[4 * (k + 1)]
    z_out, sent_out, side_out = refs[-3:]
    core = lax.axis_index("narrow") % 2
    units = w.shape[1] // 2

    size = size_of(k)
    ranks, counts, others, _, largest_offset = layout(table)
    places = []
    for p in range(k + 1):
        piece = size_of(p)
        lane = lax.broadcasted_iota(jnp.int32, (1, 4 * piece), 1)
        which, slot = lane // piece, lane % piece + QUOTAS[p]
        rank = slot + choose(ranks, which) - QUOTAS[k]
        live = (rank >= 0) & (rank < size) & (slot < choose(counts, which))
        row = jnp.where(live, rank + choose(others, which) * size, -1)
        at = lax.broadcasted_iota(jnp.int32, (2 * size, 4 * piece), 0)
        places.append(jnp.where(at == row, 1.0, 0.0).astype(BF16))
    place = jnp.concatenate(places, 1)
    tokens = jnp.concatenate([piece[...] for piece in pieces], 0)
    x = jnp.dot(place, tokens, preferred_element_type=F32)

    centre = (jnp.sum(x, -1, keepdims=True) / x.shape[1]).astype(BF16).astype(F32)
    x = x - centre
    total = jnp.sum(x, -1, keepdims=True)
    square = jnp.sum(x * x, -1, keepdims=True)
    text = text_rows(k, largest_offset)
    z = (x * (1.0 + jnp.where(text, mod[4:5, :], mod[1:2, :]))).astype(BF16)
    z_out[...] = z
    total_high = total.astype(BF16).astype(F32)
    square_high = square.astype(BF16).astype(F32)
    lane = lax.broadcasted_iota(jnp.int32, (2 * size, 128), 1) - 8 * core
    side = jnp.where((lane == 0) | (lane == 1), centre, 0.0)
    side = jnp.where(lane == 4, total_high, side)
    side = jnp.where(lane == 5, total - total_high, side)
    side = jnp.where(lane == 6, square_high, side)
    side = jnp.where(lane == 7, square - square_high, side).astype(BF16)
    side_out[...] = side
    sent_out[:, units:] = side
    for t in range(0, units, TILE):
        columns = pl.ds(pl.multiple_of((1 - core) * units + t, 128), TILE)
        sent_out[:, t : t + TILE] = jnp.dot(z, w[:, columns], preferred_element_type=F32).astype(BF16)


def expand_kept_kernel(z, w, kept_out):
    core = lax.axis_index("narrow") % 2
    units = w.shape[1] // 2
    for t in range(0, units, TILE):
        columns = pl.ds(pl.multiple_of(core * units + t, 128), TILE)
        kept_out[:, t : t + TILE] = jnp.dot(z[...], w[:, columns], preferred_element_type=F32)


def merge_kernel(kept, side, came, *refs):
    total_out, sent_out = refs[-2:]
    units = kept.shape[1]
    total = kept[...] + came[:, :units].astype(F32)
    total_out[...] = total
    sent_out[:, :units] = total.astype(BF16)
    sent_out[:, units:] = (side[...].astype(F32) + came[:, units:].astype(F32)).astype(BF16)


def activate_kernel(k, features, table, total, sent, came, factors, *refs):
    act_out = refs[-1]
    units = total.shape[1]
    size = size_of(k)
    text = text_rows(k, layout(table)[4])
    sides = [sent[:, units:].astype(F32), came[:, units:].astype(F32)]
    lane = lax.broadcasted_iota(jnp.int32, (2 * size, 128), 1)
    field = lane % 8
    used = lane < 16
    summed = sides[0] + sides[1]
    add = lambda values, mask: jnp.sum(jnp.where(mask, values, 0.0), -1, keepdims=True)
    centres = add(summed, used & (field == 0))
    totals = add(summed, used & ((field == 4) | (field == 5)))
    average = (centres * features + totals) / D
    spread = add(summed, used & ((field == 6) | (field == 7)))
    aparts = []
    for side in sides:
        apart = side - average
        for core in range(2):
            own = (lane // 8) == core
            off = add(apart, own & (field == 0))
            spread = spread + off * (
                2.0 * add(side, own & ((field == 4) | (field == 5))) + features * off
            )
        aparts.append(apart)
    variance = spread / D
    scale = lax.rsqrt(variance + norm_eps)
    of_text = jnp.where(text, 1, 0)
    mine = used & ((field % 2) == of_text)
    packed, shift = None, 0
    for apart in aparts:
        factor = jnp.where(
            mine & (field < 2), apart * scale, jnp.where(mine & (field < 4), 1.0, 0.0)
        )
        high = factor.astype(BF16).astype(F32)
        for part in (high, high, factor - high):
            part = pltpu.roll(part, shift, 1) if shift else part
            packed = part if packed is None else packed + part
            shift += 16
    packed = packed.astype(BF16)
    for t in range(0, units, TILE):
        columns = slice(t, t + TILE)
        pre = total[:, columns] + came[:, columns].astype(F32)
        extra = jnp.dot(packed, factors[:, columns], preferred_element_type=F32)
        act_out[:, columns] = jax.nn.gelu(pre * scale + extra, approximate=True).astype(BF16)


def contract_own_kernel(act, w, out):
    core = lax.axis_index("narrow") % 2
    units = w.shape[0] // 2
    rows = pl.ds(pl.multiple_of(core * units, 128), units)
    out[...] = jnp.dot(act[...], w[rows, :], preferred_element_type=F32)


def contract_other_kernel(k, table, act, so_far, w, *outs):
    core = lax.axis_index("narrow") % 2
    units = w.shape[0] // 2
    rows = pl.ds(pl.multiple_of((1 - core) * units, 128), units)
    size = size_of(k)
    ranks, counts, others, _, _ = layout(table)
    places = []
    for s in range(4):
        first = jnp.maximum(QUOTAS[k] - ranks[s], 0)
        last = jnp.minimum(counts[s], QUOTAS[k + 1] - ranks[s])
        index = lax.broadcasted_iota(jnp.int32, (size, 1), 0)
        slot = first + jnp.bitwise_and(index - first, size - 1)
        row = jnp.where(slot < last, slot + ranks[s] - QUOTAS[k] + others[s] * size, -1)
        at = lax.broadcasted_iota(jnp.int32, (size, 2 * size), 1)
        places.append(jnp.where(at == row, 1.0, 0.0).astype(BF16))
    total = so_far[...] + jnp.dot(act[...], w[rows, :], preferred_element_type=F32)
    spread = jnp.dot(
        jnp.concatenate(places, 0), total.astype(BF16), preferred_element_type=F32
    ).astype(BF16)
    for s in range(4):
        outs[s][...] = spread[s * size : (s + 1) * size]


def finish_kernel(table, hidden, mod, out_weight, ends, *refs):
    pieces, (layer_out, bundle_out) = refs[: 4 * CHUNKS], refs[4 * CHUNKS :]
    ranks, counts, _, offset, _ = layout(table)
    slot = lax.broadcasted_iota(jnp.int32, (CAP, 1), 0)
    live = slot < counts[0]
    text = slot + offset < TEXT
    rank = slot + ranks[0]
    result = jnp.zeros(hidden.shape, F32)
    for k in range(CHUNKS):
        total = pieces[4 * k][...].astype(F32)
        for s in (1, 2, 3):
            total = total + pieces[4 * k + s][...].astype(F32)
        total = jnp.concatenate([total] * (CAP // size_of(k)), 0)
        result = jnp.where((rank >= QUOTAS[k]) & (rank < QUOTAS[k + 1]), total, result)
    gate = jnp.where(text, mod[5:6, :], mod[2:3, :])
    layer = jnp.where(live, hidden[...].astype(F32) + gate * result, 0.0).astype(BF16)
    layer_out[...] = layer
    x = layer.astype(F32)
    centre = jnp.sum(x, -1, keepdims=True) / x.shape[1]
    ones = jnp.ones((8, x.shape[1]), BF16)
    across = lambda left, right: lax.dot_general(
        left, right, (((1,), (1,)), ((), ())), preferred_element_type=F32
    )
    high, low = high_low(x * x)
    total, square = across(ones, layer), across(ones, high) + across(ones, low)
    width = out_weight.shape[0]
    product = across(out_weight[...], ((x - centre) * (1.0 + mod[7:8, :])).astype(BF16))
    bundle_out[:width, :] = product + total[0:1] / x.shape[1] * ends[:width, 12:13]
    row = lax.broadcasted_iota(jnp.int32, (8, CAP), 0)
    bundle_out[width:, :] = jnp.where(row == 0, total, square)


def velocity_kernel(ends, first, second, third, fourth, out):
    total = (first[...] + second[...]) + (third[...] + fourth[...])
    width = out.shape[0]
    average = total[width : width + 1] / D
    variance = total[width + 1 : width + 2] / D - average * average
    velocity = (total[:width] - average * ends[:width, 4:5]) * lax.rsqrt(
        variance + norm_eps
    ) + ends[:width, 5:6]
    out[...] = velocity * jnp.where(lax.axis_index("cfg") == 0, guidance, 1.0 - guidance)


def latent_kernel(table, timestep, alphas, latent, mine, other, out):
    _, counts, _, offset, _ = layout(table)
    slot = lax.broadcasted_iota(jnp.int32, (1, CAP), 1)
    video = (slot < counts[0]) & (slot + offset >= TEXT)
    index = lax.broadcasted_iota(jnp.int32, (8, 128), 0) * 128 + lax.broadcasted_iota(
        jnp.int32, (8, 128), 1
    )
    alpha = jnp.sum(
        jnp.sum(jnp.where(index == timestep[0], alphas[...], 0.0), 0, keepdims=True),
        1,
        keepdims=True,
    )
    clean = jnp.sqrt(alpha) * latent[...] - jnp.sqrt(1.0 - alpha) * (mine[...] + other[...])
    out[...] = jnp.where(video, clean, 0.0)


def alpha_constant():
    ends = np.sqrt(np.float64(0.00085)), np.sqrt(np.float64(0.012))
    betas = np.linspace(ends[0], ends[1], 1000, dtype=np.float64) ** 2
    return np.pad(np.cumprod(1.0 - betas), (0, 24)).astype(np.float32).reshape(8, 128)


def call(kernel, outs, args, spaces, scratch=(), weight=0):
    kinds = {"v": pltpu.VMEM, "s": pltpu.SMEM, "a": pl.ANY}
    return pl.pallas_call(
        kernel,
        out_shape=[jax.ShapeDtypeStruct(shape, dtype) for shape, dtype in outs],
        in_specs=[pl.BlockSpec(memory_space=kinds[letter]) for letter in spaces],
        out_specs=[pl.BlockSpec(memory_space=pltpu.VMEM) for _ in outs],
        scratch_shapes=list(scratch),
        compiler_params=pltpu.CompilerParams(vmem_limit_bytes=24 * 2**20),
        cost_estimate=pl.CostEstimate(flops=weight, bytes_accessed=1, transcendentals=0),
    )(*args)


def four_blocks(
    hidden, split_table, modulation, expand_weight, contract_weight, output_weight, latent, timestep
):
    hidden = hidden[0]
    features = hidden.shape[1]
    units = expand_weight.shape[1] // 2
    width = output_weight.shape[1]
    out_weight = output_weight.T

    piece = hidden[: QUOTAS[1]]
    arrived = [[piece] + z_swaps(piece)]

    in_place = lambda weight: pltpu.with_memory_space_constraint(weight, pltpu.HBM)
    *later, held_in, sums_mine, sums_sent = call(
        prepare_kernel,
        [((size_of(k), features), BF16) for k in range(1, CHUNKS)]
        + [(expand_weight.shape, BF16)]
        + [((8, units), F32)] * 2,
        [hidden, modulation, out_weight, in_place(expand_weight)],
        "vvva",
        [pltpu.SemaphoreType.DMA((4,))],
        WEIGHTS["prepare"],
    )
    (held_out,) = call(
        hold_kernel,
        [(contract_weight.shape, BF16)],
        [in_place(contract_weight)],
        "a",
        [pltpu.SemaphoreType.DMA((4,))],
        WEIGHTS["prepare"],
    )
    for piece in later:
        arrived.append([piece] + z_swaps(piece))
    (sums_chip,) = call(
        chip_kernel, [((16, units), F32)], [sums_mine, swap(sums_sent, "narrow", 1, 4)], "vv"
    )
    factors, ends = call(
        factors_kernel,
        [((128, units), BF16), ((128, 128), F32)],
        [sums_mine, sums_chip, swap(sums_chip, "narrow", 2, 4)],
        "vvv",
    )

    returned, merged = [], []
    before, merge_before = [], [factors]
    for k in range(CHUNKS):
        rows = 2 * size_of(k)
        pieces = [piece for phase in arrived[: k + 1] for piece in phase]
        z, sent, side = call(
            functools.partial(expand_sent_kernel, k),
            [((rows, features), BF16), ((rows, units + 128), BF16), ((rows, 128), BF16)],
            [split_table, modulation, *pieces, held_in, *before],
            "sv" + "v" * len(pieces) + "v" + "a" * len(before),
            (),
            WEIGHTS["expand_sent"],
        )
        came = swap(sent, "narrow", 1, 4)
        (kept,) = call(
            expand_kept_kernel,
            [((rows, units), F32)],
            [z, held_in],
            "vv",
            (),
            WEIGHTS["expand_kept"],
        )
        total, sent = call(
            merge_kernel,
            [((rows, units), F32), ((rows, units + 128), BF16)],
            [kept, side, came, *merge_before],
            "vvv" + "a" * len(merge_before),
            (),
            WEIGHTS["merge"],
        )
        before, merge_before = [sent, held_out], []
        merged.append((total, sent, swap(sent, "narrow", 2, 4)))
    before = []
    for k in range(CHUNKS):
        rows = 2 * size_of(k)
        total, sent, came = merged[k]
        if k + 1 < CHUNKS:
            before = before + [merged[k + 1][1]]
        (act,) = call(
            functools.partial(activate_kernel, k, features),
            [((rows, units), BF16)],
            [split_table, total, sent, came, factors, *before],
            "svvvv" + "a" * len(before),
            (),
            WEIGHTS["activate"],
        )
        act_came = swap(act, "narrow", 1, 4)
        (out,) = call(
            contract_own_kernel,
            [((rows, features), F32)],
            [act, held_out],
            "vv",
            (),
            WEIGHTS["contract_own"],
        )
        pieces = call(
            functools.partial(contract_other_kernel, k),
            [((size_of(k), features), BF16)] * 4,
            [split_table, act_came, out, held_out],
            "svvv",
            (),
            WEIGHTS["contract_other"],
        )
        before = [pieces[0]]
        returned.append(pieces[0])
        returned.extend(swap(pieces[s], "wide", s, 4) for s in (1, 2, 3))

    layer_out, bundle = call(
        finish_kernel,
        [((CAP, features), BF16), ((width + 8, CAP), F32)],
        [split_table, hidden, modulation, out_weight, ends, *returned],
        "svvvv" + "v" * len(returned),
    )
    (velocity,) = call(
        velocity_kernel,
        [((width, CAP), F32)],
        [ends, bundle] + [swap(bundle, "narrow", n, 4) for n in (1, 2, 3)],
        "vvvvv",
    )
    (clean_latent,) = call(
        latent_kernel,
        [((width, CAP), F32)],
        [split_table, timestep, alpha_constant(), latent.T, velocity, swap(velocity, "cfg", 1, 2)],
        "ssvvvv",
    )
    return (layer_out[None], clean_latent.T)


def solution(mesh):
    by_swaps = (mesh.shape["wide"], mesh.shape["narrow"], mesh.shape["cfg"]) == (4, 4, 2)
    return jax.shard_map(
        four_blocks if by_swaps else any_slice,
        mesh=mesh,
        in_specs=(
            P("cfg", "wide", "narrow"),
            P(),
            P(None, "narrow"),
            P("narrow", "wide"),
            P("wide", "narrow"),
            P("narrow", None),
            P("wide", None),
            P(),
        ),
        out_specs=(P("cfg", "wide", "narrow"), P("wide", None)),
        check_vma=False,
    )
```

```python
import functools

import jax
import jax.numpy as jnp
import numpy as np
from jax import lax
from jax.experimental import pallas as pl
from jax.experimental.pallas import tpu as pltpu
from jax.sharding import PartitionSpec as P

D = 3072
TEXT = 226


norm_eps = 1e-05
guidance = 6.0


def alpha_table():
    steps_index = jnp.arange(1000, dtype=jnp.int32)
    start_root = 0.00085**0.5
    end_root = 0.012**0.5
    roots = start_root + (end_root - start_root) * steps_index.astype(jnp.float32) / 999.0
    return (steps_index, jnp.cumprod(1.0 - roots * roots))


def feature_norm(values, shifts, scaling):
    totals, squares = lax.psum(
        (jnp.sum(values, -1, keepdims=True), jnp.sum(values * values, -1, keepdims=True)), "narrow"
    )
    average = totals / D
    variance = squares / D - average * average
    return (values - average) * lax.rsqrt(variance + norm_eps) * (1.0 + scaling) + shifts


def any_slice(
    hidden, split_table, modulation, expand_weight, contract_weight, output_weight, latent, timestep
):
    capacity = hidden.shape[1]
    wide_index = lax.axis_index("wide")
    table_index = jnp.arange(split_table.shape[0], dtype=jnp.int32)
    offset = jnp.sum(jnp.where(table_index < wide_index, split_table, 0))
    own_count = jnp.sum(jnp.where(table_index == wide_index, split_table, 0))
    slot_index = jnp.arange(capacity, dtype=jnp.int32)
    position = offset + slot_index
    slot_live = slot_index < own_count
    is_text = slot_live & (position < TEXT)
    is_video = slot_live & (position >= TEXT)
    text_column = is_text[:, None]
    shifts = jnp.where(text_column, modulation[3], modulation[0])
    scaling = jnp.where(text_column, modulation[4], modulation[1])
    gating = jnp.where(text_column, modulation[5], modulation[2])
    values = hidden[0].astype(jnp.float32)
    normed = feature_norm(values, shifts, scaling).astype(jnp.bfloat16)
    hidden_part = jnp.dot(
        lax.all_gather(normed, "wide", axis=0, tiled=True),
        expand_weight,
        preferred_element_type=jnp.float32,
    )
    hidden_pre = lax.psum(hidden_part, "narrow")
    activated = jax.nn.gelu(hidden_pre, approximate=True).astype(jnp.bfloat16)
    ff_result = lax.psum_scatter(
        jnp.dot(activated, contract_weight, preferred_element_type=jnp.float32),
        "wide",
        scatter_dimension=0,
        tiled=True,
    )
    layer_out = jnp.where(slot_live[:, None], values + gating * ff_result, 0.0).astype(jnp.bfloat16)
    final_in = layer_out.astype(jnp.float32)
    final_normed = feature_norm(final_in, modulation[6], modulation[7]).astype(jnp.bfloat16)
    velocity_part = jnp.dot(final_normed, output_weight, preferred_element_type=jnp.float32)
    copy_weight = jnp.where(lax.axis_index("cfg") == 0, guidance, 1.0 - guidance)
    guided = lax.psum(velocity_part * copy_weight, ("cfg", "narrow"))
    steps_index, alpha_bar = alpha_table()
    alpha_now = jnp.sum(jnp.where(steps_index == timestep[0], alpha_bar, 0.0))
    clean_latent = jnp.where(
        is_video[:, None], jnp.sqrt(alpha_now) * latent - jnp.sqrt(1.0 - alpha_now) * guided, 0.0
    )
    return (layer_out[None], clean_latent)


QUOTAS = (0, 64, 128)
CAP = 128
CHUNKS = len(QUOTAS) - 1
F32, BF16 = jnp.float32, jnp.bfloat16
TILE = 512
LONG = 10**10


def size_of(k):
    return QUOTAS[k + 1] - QUOTAS[k]


def swap(array, axis, distance, size):
    return lax.ppermute(array, axis, [(i, i ^ distance) for i in range(size)])


def z_swaps(array):
    return [swap(array, "wide", s, 4) for s in (1, 2, 3)]


def choose(values, index):
    out = values[0]
    for i in range(1, 4):
        out = jnp.where(index == i, values[i], out)
    return out


def layout(table):
    counts = [table[b] for b in range(4)]
    largest = jnp.int32(3)
    for b in (2, 1, 0):
        largest = jnp.where(counts[b] == CAP, b, largest)
    starts, others, ranks, offsets = [], [], [], []
    rank, offset = jnp.int32(0), jnp.int32(0)
    for b in range(4):
        other = jnp.where(largest == b, 0, 1)
        ranks.append(rank * other)
        others.append(other)
        offsets.append(offset)
        rank = rank + other * counts[b]
        offset = offset + counts[b]
    block = lax.axis_index("wide")
    of = lambda values: [choose(values, jnp.bitwise_xor(block, s)) for s in range(4)]
    return of(ranks), of(counts), of(others), of(offsets)[0], choose(offsets, largest)


def high_low(values):
    high = values.astype(BF16)
    return high, (values - high.astype(F32)).astype(BF16)


def load(source, place, sems):
    parts = sems.shape[0]
    height = source.shape[0] // parts
    copies = []
    for t in range(parts):
        rows = pl.ds(t * height, height)
        copies.append(pltpu.make_async_copy(source.at[rows, :], place.at[rows, :], sems.at[t]))
        copies[-1].start()
    return copies


def hold_kernel(source, _, place, sems):
    for copy in load(source, place, sems):
        copy.wait()


def text_rows(k, largest_offset):
    size = size_of(k)
    row = lax.broadcasted_iota(jnp.int32, (2 * size, 1), 0)
    rank = jnp.where(row < size, row, row - size) + QUOTAS[k]
    position = jnp.where(
        row < size, rank + largest_offset, jnp.where(rank < largest_offset, rank, rank + CAP)
    )
    return position < TEXT


def gather_matrix(k, ranks, counts, others):
    size = size_of(k)
    places = []
    for p in range(k + 1):
        piece = size_of(p)
        lane = lax.broadcasted_iota(jnp.int32, (1, 4 * piece), 1)
        which, slot = lane // piece, lane % piece + QUOTAS[p]
        rank = slot + choose(ranks, which) - QUOTAS[k]
        live = (rank >= 0) & (rank < size) & (slot < choose(counts, which))
        row = jnp.where(live, rank + choose(others, which) * size, -1)
        at = lax.broadcasted_iota(jnp.int32, (2 * size, 4 * piece), 0)
        places.append(jnp.where(at == row, 1.0, 0.0).astype(BF16))
    return jnp.concatenate(places, 1)


def spread_matrix(k, ranks, counts, others):
    size = size_of(k)
    places = []
    for s in range(4):
        first = jnp.maximum(QUOTAS[k] - ranks[s], 0)
        last = jnp.minimum(counts[s], QUOTAS[k + 1] - ranks[s])
        index = lax.broadcasted_iota(jnp.int32, (size, 1), 0)
        slot = first + jnp.bitwise_and(index - first, size - 1)
        row = jnp.where(slot < last, slot + ranks[s] - QUOTAS[k] + others[s] * size, -1)
        at = lax.broadcasted_iota(jnp.int32, (size, 2 * size), 1)
        places.append(jnp.where(at == row, 1.0, 0.0).astype(BF16))
    return jnp.concatenate(places, 0)


def prepare_kernel(table, hidden, mod_in, out_weight, w, *refs):
    later, refs = refs[: CHUNKS - 1], refs[CHUNKS - 1 :]
    gathers, refs = refs[:CHUNKS], refs[CHUNKS:]
    spreads, refs = refs[:CHUNKS], refs[CHUNKS:]
    texts, refs = refs[:CHUNKS], refs[CHUNKS:]
    held, tokens, mod, weight, mine_out, sent_out, slots_out, video_out, sems, small = refs
    core = lax.axis_index("narrow") % 2
    units = w.shape[1] // 2
    copies = [
        pltpu.make_async_copy(source, place, small.at[i])
        for i, (source, place) in enumerate(((mod_in, mod), (out_weight, weight), (hidden, tokens)))
    ]
    for copy in copies:
        copy.start()
    big = load(w, held, sems)

    ranks, counts, others, offset, largest_offset = layout(table)
    for k in range(CHUNKS):
        gathers[k][...] = gather_matrix(k, ranks, counts, others)
        spreads[k][...] = spread_matrix(k, ranks, counts, others)
        text = jnp.where(text_rows(k, largest_offset), 1.0, 0.0)
        texts[k][...] = jnp.broadcast_to(text, texts[k].shape)
    slot = lax.broadcasted_iota(jnp.int32, (CAP, 128), 0)
    lane = lax.broadcasted_iota(jnp.int32, (CAP, 128), 1)
    rank = slot + ranks[0]
    flag = lambda condition: jnp.where(condition, 1.0, 0.0)
    kind = jnp.where(lane == 0, flag(slot < counts[0]), flag(slot + offset < TEXT))
    for k in range(CHUNKS):
        kind = jnp.where(
            lane == 2 + k, flag((rank >= QUOTAS[k]) & (rank < QUOTAS[k + 1])), kind
        )
    slots_out[...] = kind
    slot = lax.broadcasted_iota(jnp.int32, (8, CAP), 1)
    video_out[...] = jnp.where((slot < counts[0]) & (slot + offset >= TEXT), 1.0, 0.0)

    for copy in copies:
        copy.wait()
    for k in range(1, CHUNKS):
        later[k - 1][...] = tokens[QUOTAS[k] : QUOTAS[k + 1], :]
    row = lax.broadcasted_iota(jnp.int32, (8, 1), 0)
    rows = jnp.where(row == 0, 1.0 + mod[1:2, :], jnp.zeros((8, 1), F32))
    rows = jnp.where(row == 1, 1.0 + mod[4:5, :], rows)
    rows = jnp.where(row == 2, mod[0:1, :], rows)
    rows = jnp.where(row == 3, mod[3:4, :], rows)
    both = jnp.concatenate(high_low(rows), 0)
    rows = jnp.where(row == 0, 1.0 + mod[7:8, :], jnp.zeros((8, 1), F32))
    rows = jnp.where(row == 1, mod[6:7, :], rows)
    ends = lax.dot_general(
        jnp.concatenate(high_low(rows), 0),
        weight[...],
        (((1,), (1,)), ((), ())),
        preferred_element_type=F32,
    )
    ends = ends[:8] + ends[8:]
    ends = jnp.concatenate([ends, jnp.zeros((8, 128 - ends.shape[1]), F32)], 1)

    def rows_of(part):
        part = jnp.where(core == 0, part, pltpu.roll(part, 4, 0))
        high, low = high_low(part)
        return jnp.concatenate([high.astype(F32), low.astype(F32)], 0).astype(BF16)

    ends = rows_of(ends)
    mine_out[:, units:] = ends
    sent_out[:, units:] = ends
    for copy in big:
        copy.wait()
    for t in range(2):
        part = jnp.dot(both, held[:, t * units : (t + 1) * units], preferred_element_type=F32)
        part = rows_of(part[:8] + part[8:])

        @pl.when(core == t)
        def _():
            mine_out[:, :units] = part

        @pl.when(core != t)
        def _():
            sent_out[:, :units] = part


def expand_sent_kernel(k, text, mod, place, *refs):
    pieces, (w, sums) = refs[: 4 * (k + 1)], refs[4 * (k + 1) : 4 * (k + 1) + 2]
    z_out, sent_out, side_out = refs[-3:]
    core = lax.axis_index("narrow") % 2
    units = w.shape[1] // 2
    rows = z_out.shape[0]
    tokens = jnp.concatenate([piece[...] for piece in pieces], 0)
    x = jnp.dot(place[...], tokens, preferred_element_type=F32)
    centre = (jnp.sum(x, -1, keepdims=True) / x.shape[1]).astype(BF16).astype(F32)
    x = x - centre
    z = (x * (1.0 + jnp.where(text[:, :1] > 0.5, mod[4:5, :], mod[1:2, :]))).astype(BF16)
    z_out[...] = z
    for t in range(0, units, TILE):
        columns = pl.ds(pl.multiple_of((1 - core) * units + t, 128), TILE)
        sent_out[:rows, t : t + TILE] = jnp.dot(
            z, w[:, columns], preferred_element_type=F32
        ).astype(BF16)
    total = jnp.sum(x, -1, keepdims=True)
    square = jnp.sum(x * x, -1, keepdims=True)
    total_high = total.astype(BF16).astype(F32)
    square_high = square.astype(BF16).astype(F32)
    lane = lax.broadcasted_iota(jnp.int32, (rows, 128), 1) - 4 * core
    side = jnp.where((lane == 0) | (lane == 1), centre, 0.0)
    side = jnp.where(lane == 16, total_high, side)
    side = jnp.where(lane == 17, total - total_high, side)
    side = jnp.where(lane == 18, square_high, side)
    side = jnp.where(lane == 19, square - square_high, side).astype(BF16)
    side_out[...] = side
    sent_out[:rows, units:] = side
    if k == 0:
        sent_out[rows:, :] = sums[...]


def expand_kept_kernel(z, w, kept_out):
    core = lax.axis_index("narrow") % 2
    units = w.shape[1] // 2
    for t in range(0, units, TILE):
        columns = pl.ds(pl.multiple_of(core * units + t, 128), TILE)
        kept_out[:, t : t + TILE] = jnp.dot(z[...], w[:, columns], preferred_element_type=F32)


def merge_kernel(k, kept, side, came, sums, total_out, sent_out):
    rows, units = kept.shape
    total = kept[...] + came[:rows, :units].astype(F32)
    total_out[...] = total
    sent_out[:rows, :units] = total.astype(BF16)
    sent_out[:rows, units:] = (side[...].astype(F32) + came[:rows, units:].astype(F32)).astype(BF16)
    if k == 0:
        sent_out[rows:, :] = (sums[...].astype(F32) + came[rows:, :].astype(F32)).astype(BF16)


def activate_kernel(features, text, total, sent, came, first_sent, first_came, *refs):
    act_out = refs[-1]
    rows, units = total.shape
    sides = [sent[:rows, units:].astype(F32), came[:rows, units:].astype(F32)]
    lane = lax.broadcasted_iota(jnp.int32, (rows, 128), 1)
    field = lane % 4
    summed = sides[0] + sides[1]
    add = lambda values, mask: jnp.sum(jnp.where(mask, values, 0.0), -1, keepdims=True)
    centres, measures = lane < 8, (lane >= 16) & (lane < 24)
    average = (
        add(summed, centres & (field == 0)) * features + add(summed, measures & (field < 2))
    ) / D
    spread = add(summed, measures & (field >= 2))
    aparts = []
    for side in sides:
        apart = jnp.where(centres, side - average, 0.0)
        for core in range(2):
            off = add(apart, lane == 4 * core)
            own = lane // 4 == 4 + core
            spread = spread + off * (2.0 * add(side, own & (field < 2)) + features * off)
        aparts.append(apart)
    scale = lax.rsqrt(spread / D + norm_eps)
    of_text = jnp.where(text[...] > 0.5, 1, 0)
    mine = centres & (lane % 2 == of_text)
    packed, shift = None, 0
    for apart in aparts:
        factor = jnp.where(mine, jnp.where(field < 2, apart * scale, 1.0), 0.0)
        high = factor.astype(BF16).astype(F32)
        for part in (high, high, factor - high, factor - high):
            part = pltpu.roll(part, shift, 1) if shift else part
            packed = part if packed is None else packed + part
            shift += 8
    packed = packed[:, :64].astype(BF16)
    own, other = first_sent[-16:, :units], first_came[-16:, :units]
    factors = jnp.concatenate([own, own, other, other], 0)
    for t in range(0, units, TILE):
        columns = slice(t, t + TILE)
        pre = total[:, columns] + came[:rows, columns].astype(F32)
        extra = jnp.dot(packed, factors[:, columns], preferred_element_type=F32)
        act_out[:, columns] = jax.nn.gelu(pre * scale + extra, approximate=True).astype(BF16)


def contract_own_kernel(k, act, w, mine, first_sent, first_came, out, *ends_out):
    core = lax.axis_index("narrow") % 2
    units = w.shape[0] // 2
    rows = pl.ds(pl.multiple_of(core * units, 128), units)
    out[...] = jnp.dot(act[...], w[rows, :], preferred_element_type=F32)
    if k == 0:
        total = first_sent[-16:, units:].astype(F32) + first_came[-16:, units:].astype(F32)
        total = total[:8] + total[8:]
        total = total + pltpu.roll(total, 4, 0)
        own = mine[:, units:].astype(F32)
        own = own[:8] + own[8:]
        own = own + pltpu.roll(own, 4, 0)
        ends_out[0][...] = jnp.concatenate([total, own, jnp.zeros((112, 128), F32)], 0).T


def contract_other_kernel(k, place, act, so_far, w, *outs):
    core = lax.axis_index("narrow") % 2
    units = w.shape[0] // 2
    rows = pl.ds(pl.multiple_of((1 - core) * units, 128), units)
    total = so_far[...] + jnp.dot(act[...], w[rows, :], preferred_element_type=F32)
    spread = jnp.dot(place[...], total.astype(BF16), preferred_element_type=F32).astype(BF16)
    size = size_of(k)
    for s in range(4):
        outs[s][...] = spread[s * size : (s + 1) * size]


def finish_kernel(slots, hidden, mod, out_weight, ends, *refs):
    pieces, (layer_out, bundle_out) = refs[: 4 * CHUNKS], refs[4 * CHUNKS :]
    result = jnp.zeros(hidden.shape, F32)
    for k in range(CHUNKS):
        total = pieces[4 * k][...].astype(F32)
        for s in (1, 2, 3):
            total = total + pieces[4 * k + s][...].astype(F32)
        total = jnp.concatenate([total] * (CAP // size_of(k)), 0)
        result = jnp.where(slots[:, 2 + k : 3 + k] > 0.5, total, result)
    gate = jnp.where(slots[:, 1:2] > 0.5, mod[5:6, :], mod[2:3, :])
    layer = hidden[...].astype(F32) + gate * result
    layer = jnp.where(slots[:, 0:1] > 0.5, layer, 0.0).astype(BF16)
    layer_out[...] = layer
    x = layer.astype(F32)
    centre = jnp.sum(x, -1, keepdims=True) / x.shape[1]
    ones = jnp.ones((8, x.shape[1]), BF16)
    across = lambda left, right: lax.dot_general(
        left, right, (((1,), (1,)), ((), ())), preferred_element_type=F32
    )
    high, low = high_low(x * x)
    total, square = across(ones, layer), across(ones, high) + across(ones, low)
    width = out_weight.shape[0]
    product = across(out_weight[...], ((x - centre) * (1.0 + mod[7:8, :])).astype(BF16))
    bundle_out[:width, :] = product + total[0:1] / x.shape[1] * ends[:width, 8:9]
    row = lax.broadcasted_iota(jnp.int32, (8, CAP), 0)
    bundle_out[width:, :] = jnp.where(row == 0, total, square)


def write_kernel(layer, out):
    out[...] = layer[...]


def velocity_kernel(ends, first, second, third, fourth, out):
    total = (first[...] + second[...]) + (third[...] + fourth[...])
    width = out.shape[0]
    average = total[width : width + 1] / D
    variance = total[width + 1 : width + 2] / D - average * average
    velocity = (total[:width] - average * ends[:width, 0:1]) * lax.rsqrt(
        variance + norm_eps
    ) + ends[:width, 1:2]
    out[...] = velocity * jnp.where(lax.axis_index("cfg") == 0, guidance, 1.0 - guidance)


def noise_kernel(timestep, alphas, video, latent, base_out, factor_out):
    index = lax.broadcasted_iota(jnp.int32, (8, 128), 0) * 128 + lax.broadcasted_iota(
        jnp.int32, (8, 128), 1
    )
    alpha = jnp.sum(
        jnp.sum(jnp.where(index == timestep[0], alphas[...], 0.0), 0, keepdims=True),
        1,
        keepdims=True,
    )
    base_out[...] = jnp.where(video[0:1] > 0.5, jnp.sqrt(alpha) * latent[...], 0.0)
    factor_out[...] = jnp.where(video[...] > 0.5, jnp.sqrt(1.0 - alpha), 0.0)


def latent_kernel(base, factor, mine, other, out):
    guided = jnp.where(factor[0:1] > 0.0, mine[...] + other[...], 0.0)
    out[...] = base[...] - factor[0:1] * guided


def alpha_constant():
    ends = np.sqrt(np.float64(0.00085)), np.sqrt(np.float64(0.012))
    betas = np.linspace(ends[0], ends[1], 1000, dtype=np.float64) ** 2
    return np.pad(np.cumprod(1.0 - betas), (0, 24)).astype(np.float32).reshape(8, 128)


def call(kernel, outs, args, spaces, scratch=(), weight=1):
    kinds = {"v": pltpu.VMEM, "s": pltpu.SMEM, "a": pl.ANY}
    return pl.pallas_call(
        kernel,
        out_shape=[jax.ShapeDtypeStruct(shape, dtype) for shape, dtype in outs],
        in_specs=[pl.BlockSpec(memory_space=kinds[letter]) for letter in spaces],
        out_specs=[pl.BlockSpec(memory_space=pltpu.VMEM) for _ in outs],
        scratch_shapes=list(scratch),
        compiler_params=pltpu.CompilerParams(vmem_limit_bytes=24 * 2**20),
        cost_estimate=pl.CostEstimate(flops=weight, bytes_accessed=1, transcendentals=0),
    )(*args)


def four_blocks(
    hidden, split_table, modulation, expand_weight, contract_weight, output_weight, latent, timestep
):
    hidden = hidden[0]
    features = hidden.shape[1]
    units = expand_weight.shape[1] // 2
    width = output_weight.shape[1]
    payload = units + 128

    piece = hidden[: QUOTAS[1]]
    arrived = [[piece] + z_swaps(piece)]

    in_place = lambda array: pltpu.with_memory_space_constraint(array, pltpu.HBM)
    chunks = range(CHUNKS)
    made = call(
        prepare_kernel,
        [((size_of(k), features), BF16) for k in chunks[1:]]
        + [((2 * size_of(k), 4 * QUOTAS[k + 1]), BF16) for k in chunks]
        + [((4 * size_of(k), 2 * size_of(k)), BF16) for k in chunks]
        + [((2 * size_of(k), 128), F32) for k in chunks]
        + [
            (expand_weight.shape, BF16),
            (hidden.shape, BF16),
            (modulation.shape, F32),
            ((width, features), BF16),
            ((16, payload), BF16),
            ((16, payload), BF16),
            ((CAP, 128), F32),
            ((8, CAP), F32),
        ],
        [
            split_table,
            in_place(hidden),
            in_place(modulation),
            in_place(output_weight.T),
            in_place(expand_weight),
        ],
        "saaaa",
        [pltpu.SemaphoreType.DMA((4,)), pltpu.SemaphoreType.DMA((3,))],
    )
    later, made = made[: CHUNKS - 1], made[CHUNKS - 1 :]
    gathers, made = made[:CHUNKS], made[CHUNKS:]
    spreads, made = made[:CHUNKS], made[CHUNKS:]
    texts, made = made[:CHUNKS], made[CHUNKS:]
    held_in, tokens, mod, out_weight, sums_mine, sums_sent, slots, video = made
    for piece in later:
        arrived.append([piece] + z_swaps(piece))

    merged = []
    before = []
    for k in chunks:
        rows = 2 * size_of(k)
        sent_rows = rows + (16 if k == 0 else 0)
        pieces = [piece for phase in arrived[: k + 1] for piece in phase]
        z, sent, side = call(
            functools.partial(expand_sent_kernel, k),
            [((rows, features), BF16), ((sent_rows, payload), BF16), ((rows, 128), BF16)],
            [texts[k], mod, gathers[k], *pieces, held_in, sums_sent, *before],
            "vvv" + "v" * len(pieces) + "vv" + "a" * len(before),
            weight=LONG,
        )
        came = swap(sent, "narrow", 1, 4)
        (kept,) = call(
            expand_kept_kernel, [((rows, units), F32)], [z, held_in], "vv", weight=LONG
        )
        total, sent = call(
            functools.partial(merge_kernel, k),
            [((rows, units), F32), ((sent_rows, payload), BF16)],
            [kept, side, came, sums_mine],
            "vvvv",
        )
        before = [sent]
        merged.append((total, sent, swap(sent, "narrow", 2, 4)))

    (held_out,) = call(
        hold_kernel,
        [(contract_weight.shape, BF16)],
        [in_place(contract_weight), merged[-1][1]],
        "aa",
        [pltpu.SemaphoreType.DMA((4,))],
    )
    returned = []
    before = [held_out]
    first = merged[0][1:]
    for k in chunks:
        rows = 2 * size_of(k)
        total, sent, came = merged[k]
        if k + 1 < CHUNKS:
            before = before + [merged[k + 1][1]]
        (act,) = call(
            functools.partial(activate_kernel, features),
            [((rows, units), BF16)],
            [texts[k], total, sent, came, *first, *before],
            "vvvvvv" + "a" * len(before),
        )
        act_came = swap(act, "narrow", 1, 4)
        out, *ends_made = call(
            functools.partial(contract_own_kernel, k),
            [((rows, features), F32)] + ([((128, 128), F32)] if k == 0 else []),
            [act, held_out, sums_mine, *first],
            "vvvvv",
            weight=LONG,
        )
        ends = ends_made[0] if k == 0 else ends
        pieces = call(
            functools.partial(contract_other_kernel, k),
            [((size_of(k), features), BF16)] * 4,
            [spreads[k], act_came, out, held_out],
            "vvvv",
        )
        before = [pieces[0]]
        returned.append(pieces[0])
        returned.extend(swap(pieces[s], "wide", s, 4) for s in (1, 2, 3))

    layer, bundle = call(
        finish_kernel,
        [((CAP, features), BF16), ((width + 8, CAP), F32)],
        [slots, tokens, mod, out_weight, ends, *returned],
        "v" * (5 + len(returned)),
    )
    (layer_out,) = call(write_kernel, [((CAP, features), BF16)], [layer], "v", weight=LONG)
    (velocity,) = call(
        velocity_kernel,
        [((width, CAP), F32)],
        [ends, bundle] + [swap(bundle, "narrow", n, 4) for n in (1, 2, 3)],
        "vvvvv",
    )
    base, factor = call(
        noise_kernel,
        [((width, CAP), F32), ((8, CAP), F32)],
        [timestep, alpha_constant(), video, latent.T],
        "svvv",
        weight=LONG,
    )
    (clean_latent,) = call(
        latent_kernel,
        [((width, CAP), F32)],
        [base, factor, velocity, swap(velocity, "cfg", 1, 2)],
        "vvvv",
    )
    return (layer_out[None], clean_latent.T)


def solution(mesh):
    by_swaps = (mesh.shape["wide"], mesh.shape["narrow"], mesh.shape["cfg"]) == (4, 4, 2)
    return jax.shard_map(
        four_blocks if by_swaps else any_slice,
        mesh=mesh,
        in_specs=(
            P("cfg", "wide", "narrow"),
            P(),
            P(None, "narrow"),
            P("narrow", "wide"),
            P("wide", "narrow"),
            P("narrow", None),
            P("wide", None),
            P(),
        ),
        out_specs=(P("cfg", "wide", "narrow"), P("wide", None)),
        check_vma=False,
    )
```

```python
import functools

import jax
import jax.numpy as jnp
import numpy as np
from jax import lax
from jax.experimental import pallas as pl
from jax.experimental.pallas import tpu as pltpu
from jax.sharding import PartitionSpec as P

D = 3072
TEXT = 226


norm_eps = 1e-05
guidance = 6.0


def alpha_table():
    steps_index = jnp.arange(1000, dtype=jnp.int32)
    start_root = 0.00085**0.5
    end_root = 0.012**0.5
    roots = start_root + (end_root - start_root) * steps_index.astype(jnp.float32) / 999.0
    return (steps_index, jnp.cumprod(1.0 - roots * roots))


def feature_norm(values, shifts, scaling):
    totals, squares = lax.psum(
        (jnp.sum(values, -1, keepdims=True), jnp.sum(values * values, -1, keepdims=True)), "narrow"
    )
    average = totals / D
    variance = squares / D - average * average
    return (values - average) * lax.rsqrt(variance + norm_eps) * (1.0 + scaling) + shifts


def any_slice(
    hidden, split_table, modulation, expand_weight, contract_weight, output_weight, latent, timestep
):
    capacity = hidden.shape[1]
    wide_index = lax.axis_index("wide")
    table_index = jnp.arange(split_table.shape[0], dtype=jnp.int32)
    offset = jnp.sum(jnp.where(table_index < wide_index, split_table, 0))
    own_count = jnp.sum(jnp.where(table_index == wide_index, split_table, 0))
    slot_index = jnp.arange(capacity, dtype=jnp.int32)
    position = offset + slot_index
    slot_live = slot_index < own_count
    is_text = slot_live & (position < TEXT)
    is_video = slot_live & (position >= TEXT)
    text_column = is_text[:, None]
    shifts = jnp.where(text_column, modulation[3], modulation[0])
    scaling = jnp.where(text_column, modulation[4], modulation[1])
    gating = jnp.where(text_column, modulation[5], modulation[2])
    values = hidden[0].astype(jnp.float32)
    normed = feature_norm(values, shifts, scaling).astype(jnp.bfloat16)
    hidden_part = jnp.dot(
        lax.all_gather(normed, "wide", axis=0, tiled=True),
        expand_weight,
        preferred_element_type=jnp.float32,
    )
    hidden_pre = lax.psum(hidden_part, "narrow")
    activated = jax.nn.gelu(hidden_pre, approximate=True).astype(jnp.bfloat16)
    ff_result = lax.psum_scatter(
        jnp.dot(activated, contract_weight, preferred_element_type=jnp.float32),
        "wide",
        scatter_dimension=0,
        tiled=True,
    )
    layer_out = jnp.where(slot_live[:, None], values + gating * ff_result, 0.0).astype(jnp.bfloat16)
    final_in = layer_out.astype(jnp.float32)
    final_normed = feature_norm(final_in, modulation[6], modulation[7]).astype(jnp.bfloat16)
    velocity_part = jnp.dot(final_normed, output_weight, preferred_element_type=jnp.float32)
    copy_weight = jnp.where(lax.axis_index("cfg") == 0, guidance, 1.0 - guidance)
    guided = lax.psum(velocity_part * copy_weight, ("cfg", "narrow"))
    steps_index, alpha_bar = alpha_table()
    alpha_now = jnp.sum(jnp.where(steps_index == timestep[0], alpha_bar, 0.0))
    clean_latent = jnp.where(
        is_video[:, None], jnp.sqrt(alpha_now) * latent - jnp.sqrt(1.0 - alpha_now) * guided, 0.0
    )
    return (layer_out[None], clean_latent)


QUOTAS = (0, 64, 128)
CAP = 128
CHUNKS = len(QUOTAS) - 1
F32, BF16 = jnp.float32, jnp.bfloat16
TILE = 512
LONG = 10**10


def size_of(k):
    return QUOTAS[k + 1] - QUOTAS[k]


def swap(array, axis, distance, size):
    return lax.ppermute(array, axis, [(i, i ^ distance) for i in range(size)])


def z_swaps(array):
    return [swap(array, "wide", s, 4) for s in (1, 2, 3)]


def choose(values, index):
    out = values[0]
    for i in range(1, 4):
        out = jnp.where(index == i, values[i], out)
    return out


def layout(table):
    counts = [table[b] for b in range(4)]
    largest = jnp.int32(3)
    for b in (2, 1, 0):
        largest = jnp.where(counts[b] == CAP, b, largest)
    starts, others, ranks, offsets = [], [], [], []
    rank, offset = jnp.int32(0), jnp.int32(0)
    for b in range(4):
        other = jnp.where(largest == b, 0, 1)
        ranks.append(rank * other)
        others.append(other)
        offsets.append(offset)
        rank = rank + other * counts[b]
        offset = offset + counts[b]
    block = lax.axis_index("wide")
    of = lambda values: [choose(values, jnp.bitwise_xor(block, s)) for s in range(4)]
    return of(ranks), of(counts), of(others), of(offsets)[0], choose(offsets, largest)


def high_low(values):
    high = values.astype(BF16)
    return high, (values - high.astype(F32)).astype(BF16)


def load(source, place, sems):
    parts = sems.shape[0]
    height = source.shape[0] // parts
    copies = []
    for t in range(parts):
        rows = pl.ds(t * height, height)
        copies.append(pltpu.make_async_copy(source.at[rows, :], place.at[rows, :], sems.at[t]))
        copies[-1].start()
    return copies


def load_half(source, half, place, sems):
    width = place.shape[1]
    copies = []
    for t in range(0, width, TILE):
        columns = pl.ds(pl.multiple_of(half * width + t, 128), TILE)
        copies.append(
            pltpu.make_async_copy(
                source.at[:, columns], place.at[:, pl.ds(t, TILE)], sems.at[len(copies)]
            )
        )
        copies[-1].start()
    return copies


def rows_of(parts, core):
    total = parts[:8] + parts[8:]
    total = jnp.where(core == 0, total, pltpu.roll(total, 4, 0))
    high, low = high_low(total)
    return jnp.concatenate([high.astype(F32), low.astype(F32)], 0).astype(BF16)


def hold_kernel(source, _, place, sems):
    for copy in load(source, place, sems):
        copy.wait()


def text_rows(k, largest_offset):
    size = size_of(k)
    row = lax.broadcasted_iota(jnp.int32, (2 * size, 1), 0)
    rank = jnp.where(row < size, row, row - size) + QUOTAS[k]
    position = jnp.where(
        row < size, rank + largest_offset, jnp.where(rank < largest_offset, rank, rank + CAP)
    )
    return position < TEXT


def gather_matrix(k, ranks, counts, others):
    size = size_of(k)
    places = []
    for p in range(k + 1):
        piece = size_of(p)
        lane = lax.broadcasted_iota(jnp.int32, (1, 4 * piece), 1)
        which, slot = lane // piece, lane % piece + QUOTAS[p]
        rank = slot + choose(ranks, which) - QUOTAS[k]
        live = (rank >= 0) & (rank < size) & (slot < choose(counts, which))
        row = jnp.where(live, rank + choose(others, which) * size, -1)
        at = lax.broadcasted_iota(jnp.int32, (2 * size, 4 * piece), 0)
        places.append(jnp.where(at == row, 1.0, 0.0).astype(BF16))
    return jnp.concatenate(places, 1)


def spread_matrix(k, ranks, counts, others):
    size = size_of(k)
    places = []
    for s in range(4):
        first = jnp.maximum(QUOTAS[k] - ranks[s], 0)
        last = jnp.minimum(counts[s], QUOTAS[k + 1] - ranks[s])
        index = lax.broadcasted_iota(jnp.int32, (size, 1), 0)
        slot = first + jnp.bitwise_and(index - first, size - 1)
        row = jnp.where(slot < last, slot + ranks[s] - QUOTAS[k] + others[s] * size, -1)
        at = lax.broadcasted_iota(jnp.int32, (size, 2 * size), 1)
        places.append(jnp.where(at == row, 1.0, 0.0).astype(BF16))
    return jnp.concatenate(places, 0)


def take_kernel(source, out, sem):
    copy = pltpu.make_async_copy(source.at[pl.ds(0, out.shape[0]), :], out, sem)
    copy.start()
    copy.wait()


def prepare_kernel(table_in, hidden, mod_in, out_weight, w, *refs):
    later, refs = refs[: CHUNKS - 1], refs[CHUNKS - 1 :]
    gathers, refs = refs[:CHUNKS], refs[CHUNKS:]
    spreads, refs = refs[:CHUNKS], refs[CHUNKS:]
    texts, refs = refs[:CHUNKS], refs[CHUNKS:]
    held, tokens, mod, weight, rows_out, ends_out, slots_out, video_out, table, sems, small = refs
    core = lax.axis_index("narrow") % 2
    sources = (table_in, mod_in, out_weight, hidden)
    copies = [
        pltpu.make_async_copy(source, place, small.at[i])
        for i, (source, place) in enumerate(zip(sources, (table, mod, weight, tokens)))
    ]
    for copy in copies:
        copy.start()
    big = load_half(w, 1 - core, held, sems)

    copies[0].wait()
    ranks, counts, others, offset, largest_offset = layout(table)
    for k in range(CHUNKS):
        gathers[k][...] = gather_matrix(k, ranks, counts, others)
        spreads[k][...] = spread_matrix(k, ranks, counts, others)
        text = jnp.where(text_rows(k, largest_offset), 1.0, 0.0)
        texts[k][...] = jnp.broadcast_to(text, texts[k].shape)
    slot = lax.broadcasted_iota(jnp.int32, (CAP, 128), 0)
    lane = lax.broadcasted_iota(jnp.int32, (CAP, 128), 1)
    rank = slot + ranks[0]
    flag = lambda condition: jnp.where(condition, 1.0, 0.0)
    kind = jnp.where(lane == 0, flag(slot < counts[0]), flag(slot + offset < TEXT))
    for k in range(CHUNKS):
        kind = jnp.where(
            lane == 2 + k, flag((rank >= QUOTAS[k]) & (rank < QUOTAS[k + 1])), kind
        )
    slots_out[...] = kind
    slot = lax.broadcasted_iota(jnp.int32, (8, CAP), 1)
    video_out[...] = jnp.where((slot < counts[0]) & (slot + offset >= TEXT), 1.0, 0.0)

    copies[1].wait()
    row = lax.broadcasted_iota(jnp.int32, (8, 1), 0)
    rows = jnp.where(row == 0, 1.0 + mod[1:2, :], jnp.zeros((8, 1), F32))
    rows = jnp.where(row == 1, 1.0 + mod[4:5, :], rows)
    rows = jnp.where(row == 2, mod[0:1, :], rows)
    rows = jnp.where(row == 3, mod[3:4, :], rows)
    rows_out[...] = jnp.concatenate(high_low(rows), 0)
    rows = jnp.where(row == 0, 1.0 + mod[7:8, :], jnp.zeros((8, 1), F32))
    rows = jnp.where(row == 1, mod[6:7, :], rows)
    copies[2].wait()
    ends = lax.dot_general(
        jnp.concatenate(high_low(rows), 0),
        weight[...],
        (((1,), (1,)), ((), ())),
        preferred_element_type=F32,
    )
    ends = rows_of(ends, core)
    ends_out[...] = jnp.concatenate([ends, jnp.zeros((16, 128 - ends.shape[1]), BF16)], 1)
    copies[3].wait()
    for k in range(1, CHUNKS):
        later[k - 1][...] = tokens[QUOTAS[k] : QUOTAS[k + 1], :]
    for copy in big:
        copy.wait()


def expand_sent_kernel(k, text, mod, place, *refs):
    pieces, (w, sums, ends) = refs[: 4 * (k + 1)], refs[4 * (k + 1) : 4 * (k + 1) + 3]
    z_out, sent_out, side_out = refs[-3:]
    core = lax.axis_index("narrow") % 2
    units = w.shape[1]
    rows = side_out.shape[0]
    tokens = jnp.concatenate([piece[...] for piece in pieces], 0)
    x = jnp.dot(place[...], tokens, preferred_element_type=F32)
    centre = (jnp.sum(x, -1, keepdims=True) / x.shape[1]).astype(BF16).astype(F32)
    x = x - centre
    z = (x * (1.0 + jnp.where(text[:, :1] > 0.5, mod[4:5, :], mod[1:2, :]))).astype(BF16)
    if k == 0:
        z = jnp.concatenate([z, sums[...]], 0)
    z_out[...] = z
    for t in range(0, units, TILE):
        product = jnp.dot(z, w[:, t : t + TILE], preferred_element_type=F32)
        sent_out[:rows, t : t + TILE] = product[:rows].astype(BF16)
        if k == 0:
            sent_out[rows:, t : t + TILE] = rows_of(product[rows:], core)
    total = jnp.sum(x, -1, keepdims=True)
    square = jnp.sum(x * x, -1, keepdims=True)
    total_high = total.astype(BF16).astype(F32)
    square_high = square.astype(BF16).astype(F32)
    lane = lax.broadcasted_iota(jnp.int32, (rows, 128), 1) - 4 * core
    side = jnp.where((lane == 0) | (lane == 1), centre, 0.0)
    side = jnp.where(lane == 16, total_high, side)
    side = jnp.where(lane == 17, total - total_high, side)
    side = jnp.where(lane == 18, square_high, side)
    side = jnp.where(lane == 19, square - square_high, side).astype(BF16)
    side_out[...] = side
    sent_out[:rows, units:] = side
    if k == 0:
        sent_out[rows:, units:] = ends[...]


def first_kept_kernel(z, w, kept_out, sums_out, held, sems):
    core = lax.axis_index("narrow") % 2
    rows = kept_out.shape[0]
    for t, copy in enumerate(load_half(w, core, held, sems)):
        copy.wait()
        columns = slice(t * TILE, (t + 1) * TILE)
        product = jnp.dot(z[...], held[:, columns], preferred_element_type=F32)
        kept_out[:, columns] = product[:rows]
        sums_out[:, columns] = rows_of(product[rows:], core)


def kept_kernel(z, w, kept_out):
    for t in range(0, w.shape[1], TILE):
        kept_out[:, t : t + TILE] = jnp.dot(z[...], w[:, t : t + TILE], preferred_element_type=F32)


def merge_kernel(k, kept, side, came, sums, ends, total_out, sent_out):
    rows, units = kept.shape
    add = lambda left, right: (left[...].astype(F32) + right.astype(F32)).astype(BF16)
    total = kept[...] + came[:rows, :units].astype(F32)
    total_out[...] = total
    sent_out[:rows, :units] = total.astype(BF16)
    sent_out[:rows, units:] = add(side, came[:rows, units:])
    if k == 0:
        sent_out[rows:, :units] = add(sums, came[rows:, :units])
        sent_out[rows:, units:] = add(ends, came[rows:, units:])


def activate_kernel(features, text, total, sent, came, first_sent, first_came, *refs):
    act_out = refs[-1]
    rows, units = total.shape
    sides = [sent[:rows, units:].astype(F32), came[:rows, units:].astype(F32)]
    lane = lax.broadcasted_iota(jnp.int32, (rows, 128), 1)
    field = lane % 4
    summed = sides[0] + sides[1]
    add = lambda values, mask: jnp.sum(jnp.where(mask, values, 0.0), -1, keepdims=True)
    centres, measures = lane < 8, (lane >= 16) & (lane < 24)
    average = (
        add(summed, centres & (field == 0)) * features + add(summed, measures & (field < 2))
    ) / D
    spread = add(summed, measures & (field >= 2))
    aparts = []
    for side in sides:
        apart = jnp.where(centres, side - average, 0.0)
        for core in range(2):
            off = add(apart, lane == 4 * core)
            own = lane // 4 == 4 + core
            spread = spread + off * (2.0 * add(side, own & (field < 2)) + features * off)
        aparts.append(apart)
    scale = lax.rsqrt(spread / D + norm_eps)
    of_text = jnp.where(text[...] > 0.5, 1, 0)
    mine = centres & (lane % 2 == of_text)
    packed, shift = None, 0
    for apart in aparts:
        factor = jnp.where(mine, jnp.where(field < 2, apart * scale, 1.0), 0.0)
        high = factor.astype(BF16).astype(F32)
        for part in (high, high, factor - high, factor - high):
            part = pltpu.roll(part, shift, 1) if shift else part
            packed = part if packed is None else packed + part
            shift += 8
    packed = packed[:, :64].astype(BF16)
    own, other = first_sent[-16:, :units], first_came[-16:, :units]
    factors = jnp.concatenate([own, own, other, other], 0)
    for t in range(0, units, TILE):
        columns = slice(t, t + TILE)
        pre = total[:, columns] + came[:rows, columns].astype(F32)
        extra = jnp.dot(packed, factors[:, columns], preferred_element_type=F32)
        act_out[:, columns] = jax.nn.gelu(pre * scale + extra, approximate=True).astype(BF16)


def contract_own_kernel(k, act, w, mine, first_sent, first_came, out, *ends_out):
    core = lax.axis_index("narrow") % 2
    units = w.shape[0] // 2
    rows = pl.ds(pl.multiple_of(core * units, 128), units)
    out[...] = jnp.dot(act[...], w[rows, :], preferred_element_type=F32)
    if k == 0:
        total = first_sent[-16:, units:].astype(F32) + first_came[-16:, units:].astype(F32)
        total = total[:8] + total[8:]
        total = total + pltpu.roll(total, 4, 0)
        own = mine[...].astype(F32)
        own = own[:8] + own[8:]
        own = own + pltpu.roll(own, 4, 0)
        ends_out[0][...] = jnp.concatenate([total, own, jnp.zeros((112, 128), F32)], 0).T


def contract_other_kernel(k, place, act, so_far, w, *outs):
    core = lax.axis_index("narrow") % 2
    units = w.shape[0] // 2
    rows = pl.ds(pl.multiple_of((1 - core) * units, 128), units)
    total = so_far[...] + jnp.dot(act[...], w[rows, :], preferred_element_type=F32)
    spread = jnp.dot(place[...], total.astype(BF16), preferred_element_type=F32).astype(BF16)
    size = size_of(k)
    for s in range(4):
        outs[s][...] = spread[s * size : (s + 1) * size]


def finish_kernel(slots, hidden, mod, out_weight, ends, *refs):
    pieces, (layer_out, bundle_out) = refs[: 4 * CHUNKS], refs[4 * CHUNKS :]
    result = jnp.zeros(hidden.shape, F32)
    for k in range(CHUNKS):
        total = pieces[4 * k][...].astype(F32)
        for s in (1, 2, 3):
            total = total + pieces[4 * k + s][...].astype(F32)
        total = jnp.concatenate([total] * (CAP // size_of(k)), 0)
        result = jnp.where(slots[:, 2 + k : 3 + k] > 0.5, total, result)
    gate = jnp.where(slots[:, 1:2] > 0.5, mod[5:6, :], mod[2:3, :])
    layer = hidden[...].astype(F32) + gate * result
    layer = jnp.where(slots[:, 0:1] > 0.5, layer, 0.0).astype(BF16)
    layer_out[...] = layer
    x = layer.astype(F32)
    centre = jnp.sum(x, -1, keepdims=True) / x.shape[1]
    ones = jnp.ones((8, x.shape[1]), BF16)
    across = lambda left, right: lax.dot_general(
        left, right, (((1,), (1,)), ((), ())), preferred_element_type=F32
    )
    high, low = high_low(x * x)
    total, square = across(ones, layer), across(ones, high) + across(ones, low)
    width = out_weight.shape[0]
    product = across(out_weight[...], ((x - centre) * (1.0 + mod[7:8, :])).astype(BF16))
    bundle_out[:width, :] = product + total[0:1] / x.shape[1] * ends[:width, 8:9]
    row = lax.broadcasted_iota(jnp.int32, (8, CAP), 0)
    bundle_out[width:, :] = jnp.where(row == 0, total, square)


def write_kernel(layer, out):
    out[...] = layer[...]


def add_kernel(left, right, out):
    out[...] = left[...] + right[...]


def noise_kernel(timestep, alphas, video, latent, base_out, factor_out):
    index = lax.broadcasted_iota(jnp.int32, (8, 128), 0) * 128 + lax.broadcasted_iota(
        jnp.int32, (8, 128), 1
    )
    alpha = jnp.sum(
        jnp.sum(jnp.where(index == timestep[0], alphas[...], 0.0), 0, keepdims=True),
        1,
        keepdims=True,
    )
    base_out[...] = jnp.where(video[0:1] > 0.5, jnp.sqrt(alpha) * latent[...], 0.0)
    factor_out[...] = jnp.where(video[...] > 0.5, jnp.sqrt(1.0 - alpha), 0.0)


def latent_kernel(base, factor, ends, mine, mine_y, other, other_y, out):
    width = out.shape[0]

    def velocity(total):
        average = total[width : width + 1] / D
        variance = total[width + 1 : width + 2] / D - average * average
        return (total[:width] - average * ends[:width, 0:1]) * lax.rsqrt(
            variance + norm_eps
        ) + ends[:width, 1:2]

    first = lax.axis_index("cfg") == 0
    guided = velocity(mine[...] + mine_y[...]) * jnp.where(first, guidance, 1.0 - guidance)
    guided = guided + velocity(other[...] + other_y[...]) * jnp.where(
        first, 1.0 - guidance, guidance
    )
    guided = jnp.where(factor[0:1] > 0.0, guided, 0.0)
    out[...] = base[...] - factor[0:1] * guided


def alpha_constant():
    ends = np.sqrt(np.float64(0.00085)), np.sqrt(np.float64(0.012))
    betas = np.linspace(ends[0], ends[1], 1000, dtype=np.float64) ** 2
    return np.pad(np.cumprod(1.0 - betas), (0, 24)).astype(np.float32).reshape(8, 128)


def call(kernel, outs, args, spaces, scratch=(), weight=1):
    kinds = {"v": pltpu.VMEM, "s": pltpu.SMEM, "a": pl.ANY}
    return pl.pallas_call(
        kernel,
        out_shape=[jax.ShapeDtypeStruct(shape, dtype) for shape, dtype in outs],
        in_specs=[pl.BlockSpec(memory_space=kinds[letter]) for letter in spaces],
        out_specs=[pl.BlockSpec(memory_space=pltpu.VMEM) for _ in outs],
        scratch_shapes=list(scratch),
        compiler_params=pltpu.CompilerParams(vmem_limit_bytes=24 * 2**20),
        cost_estimate=pl.CostEstimate(flops=weight, bytes_accessed=1, transcendentals=0),
    )(*args)


def four_blocks(
    hidden, split_table, modulation, expand_weight, contract_weight, output_weight, latent, timestep
):
    hidden = hidden[0]
    features = hidden.shape[1]
    units = expand_weight.shape[1] // 2
    width = output_weight.shape[1]
    payload = units + 128

    in_place = lambda array: pltpu.with_memory_space_constraint(array, pltpu.HBM)
    (piece,) = call(
        take_kernel,
        [((QUOTAS[1], features), BF16)],
        [in_place(hidden)],
        "a",
        [pltpu.SemaphoreType.DMA(())],
    )
    arrived = [[piece] + z_swaps(piece)]

    tiles = units // TILE
    chunks = range(CHUNKS)
    made = call(
        prepare_kernel,
        [((size_of(k), features), BF16) for k in chunks[1:]]
        + [((2 * size_of(k), 4 * QUOTAS[k + 1]), BF16) for k in chunks]
        + [((4 * size_of(k), 2 * size_of(k)), BF16) for k in chunks]
        + [((2 * size_of(k), 128), F32) for k in chunks]
        + [
            ((features, units), BF16),
            (hidden.shape, BF16),
            (modulation.shape, F32),
            ((width, features), BF16),
            ((16, features), BF16),
            ((16, 128), BF16),
            ((CAP, 128), F32),
            ((8, CAP), F32),
        ],
        [
            in_place(split_table),
            in_place(hidden),
            in_place(modulation),
            in_place(output_weight.T),
            in_place(expand_weight),
        ],
        "aaaaa",
        [
            pltpu.SMEM(split_table.shape, jnp.int32),
            pltpu.SemaphoreType.DMA((tiles,)),
            pltpu.SemaphoreType.DMA((4,)),
        ],
    )
    later, made = made[: CHUNKS - 1], made[CHUNKS - 1 :]
    gathers, made = made[:CHUNKS], made[CHUNKS:]
    spreads, made = made[:CHUNKS], made[CHUNKS:]
    texts, made = made[:CHUNKS], made[CHUNKS:]
    held_sent, tokens, mod, out_weight, rows_in, ends_mine, slots, video = made
    for piece in later:
        arrived.append([piece] + z_swaps(piece))

    merged = []
    before = []
    for k in chunks:
        rows = 2 * size_of(k)
        sent_rows = rows + (16 if k == 0 else 0)
        pieces = [piece for phase in arrived[: k + 1] for piece in phase]
        z, sent, side = call(
            functools.partial(expand_sent_kernel, k),
            [((sent_rows, features), BF16), ((sent_rows, payload), BF16), ((rows, 128), BF16)],
            [texts[k], mod, gathers[k], *pieces, held_sent, rows_in, ends_mine, *before],
            "vvv" + "v" * len(pieces) + "vvv" + "a" * len(before),
            weight=LONG,
        )
        came = swap(sent, "narrow", 1, 4)
        if k == 0:
            kept, sums, held_kept = call(
                first_kept_kernel,
                [((rows, units), F32), ((16, units), BF16), ((features, units), BF16)],
                [z, in_place(expand_weight)],
                "va",
                [pltpu.SemaphoreType.DMA((tiles,))],
                weight=LONG,
            )
        else:
            (kept,) = call(kept_kernel, [((rows, units), F32)], [z, held_kept], "vv", weight=LONG)
        total, sent = call(
            functools.partial(merge_kernel, k),
            [((rows, units), F32), ((sent_rows, payload), BF16)],
            [kept, side, came, sums, ends_mine],
            "vvvvv",
        )
        before = [sent]
        merged.append((total, sent, swap(sent, "narrow", 2, 4)))

    (held_out,) = call(
        hold_kernel,
        [(contract_weight.shape, BF16)],
        [in_place(contract_weight), merged[-1][1]],
        "aa",
        [pltpu.SemaphoreType.DMA((4,))],
    )
    returned = []
    before = [held_out]
    first = merged[0][1:]
    for k in chunks:
        rows = 2 * size_of(k)
        total, sent, came = merged[k]
        if k + 1 < CHUNKS:
            before = before + [merged[k + 1][1]]
        (act,) = call(
            functools.partial(activate_kernel, features),
            [((rows, units), BF16)],
            [texts[k], total, sent, came, *first, *before],
            "vvvvvv" + "a" * len(before),
        )
        act_came = swap(act, "narrow", 1, 4)
        out, *ends_made = call(
            functools.partial(contract_own_kernel, k),
            [((rows, features), F32)] + ([((128, 128), F32)] if k == 0 else []),
            [act, held_out, ends_mine, *first],
            "vvvvv",
            weight=LONG,
        )
        ends = ends_made[0] if k == 0 else ends
        pieces = call(
            functools.partial(contract_other_kernel, k),
            [((size_of(k), features), BF16)] * 4,
            [spreads[k], act_came, out, held_out],
            "vvvv",
        )
        before = pieces
        returned.append(pieces[0])
        returned.extend(swap(pieces[s], "wide", s, 4) for s in (1, 2, 3))

    layer, bundle = call(
        finish_kernel,
        [((CAP, features), BF16), ((width + 8, CAP), F32)],
        [slots, tokens, mod, out_weight, ends, *returned],
        "v" * (5 + len(returned)),
    )
    (layer_out,) = call(write_kernel, [((CAP, features), BF16)], [layer], "v", weight=LONG)
    (bundle,) = call(
        add_kernel, [((width + 8, CAP), F32)], [bundle, swap(bundle, "narrow", 1, 4)], "vv"
    )
    base, factor = call(
        noise_kernel,
        [((width, CAP), F32), ((8, CAP), F32)],
        [timestep, alpha_constant(), video, latent.T],
        "svvv",
        weight=LONG,
    )
    (clean_latent,) = call(
        latent_kernel,
        [((width, CAP), F32)],
        [base, factor, ends, bundle] + [swap(bundle, ("cfg", "narrow"), n, 8) for n in (2, 4, 6)],
        "vvvvvvv",
    )
    return (layer_out[None], clean_latent.T)


def solution(mesh):
    by_swaps = (mesh.shape["wide"], mesh.shape["narrow"], mesh.shape["cfg"]) == (4, 4, 2)
    return jax.shard_map(
        four_blocks if by_swaps else any_slice,
        mesh=mesh,
        in_specs=(
            P("cfg", "wide", "narrow"),
            P(),
            P(None, "narrow"),
            P("narrow", "wide"),
            P("wide", "narrow"),
            P("narrow", None),
            P("wide", None),
            P(),
        ),
        out_specs=(P("cfg", "wide", "narrow"), P("wide", None)),
        check_vma=False,
    )
```

```python
import functools

import jax
import jax.numpy as jnp
import numpy as np
from jax import lax
from jax.experimental import pallas as pl
from jax.experimental.pallas import tpu as pltpu
from jax.sharding import PartitionSpec as P

D = 3072
TEXT = 226


norm_eps = 1e-05
guidance = 6.0


def alpha_table():
    steps_index = jnp.arange(1000, dtype=jnp.int32)
    start_root = 0.00085**0.5
    end_root = 0.012**0.5
    roots = start_root + (end_root - start_root) * steps_index.astype(jnp.float32) / 999.0
    return (steps_index, jnp.cumprod(1.0 - roots * roots))


def feature_norm(values, shifts, scaling):
    totals, squares = lax.psum(
        (jnp.sum(values, -1, keepdims=True), jnp.sum(values * values, -1, keepdims=True)), "narrow"
    )
    average = totals / D
    variance = squares / D - average * average
    return (values - average) * lax.rsqrt(variance + norm_eps) * (1.0 + scaling) + shifts


def any_slice(
    hidden, split_table, modulation, expand_weight, contract_weight, output_weight, latent, timestep
):
    capacity = hidden.shape[1]
    wide_index = lax.axis_index("wide")
    table_index = jnp.arange(split_table.shape[0], dtype=jnp.int32)
    offset = jnp.sum(jnp.where(table_index < wide_index, split_table, 0))
    own_count = jnp.sum(jnp.where(table_index == wide_index, split_table, 0))
    slot_index = jnp.arange(capacity, dtype=jnp.int32)
    position = offset + slot_index
    slot_live = slot_index < own_count
    is_text = slot_live & (position < TEXT)
    is_video = slot_live & (position >= TEXT)
    text_column = is_text[:, None]
    shifts = jnp.where(text_column, modulation[3], modulation[0])
    scaling = jnp.where(text_column, modulation[4], modulation[1])
    gating = jnp.where(text_column, modulation[5], modulation[2])
    values = hidden[0].astype(jnp.float32)
    normed = feature_norm(values, shifts, scaling).astype(jnp.bfloat16)
    hidden_part = jnp.dot(
        lax.all_gather(normed, "wide", axis=0, tiled=True),
        expand_weight,
        preferred_element_type=jnp.float32,
    )
    hidden_pre = lax.psum(hidden_part, "narrow")
    activated = jax.nn.gelu(hidden_pre, approximate=True).astype(jnp.bfloat16)
    ff_result = lax.psum_scatter(
        jnp.dot(activated, contract_weight, preferred_element_type=jnp.float32),
        "wide",
        scatter_dimension=0,
        tiled=True,
    )
    layer_out = jnp.where(slot_live[:, None], values + gating * ff_result, 0.0).astype(jnp.bfloat16)
    final_in = layer_out.astype(jnp.float32)
    final_normed = feature_norm(final_in, modulation[6], modulation[7]).astype(jnp.bfloat16)
    velocity_part = jnp.dot(final_normed, output_weight, preferred_element_type=jnp.float32)
    copy_weight = jnp.where(lax.axis_index("cfg") == 0, guidance, 1.0 - guidance)
    guided = lax.psum(velocity_part * copy_weight, ("cfg", "narrow"))
    steps_index, alpha_bar = alpha_table()
    alpha_now = jnp.sum(jnp.where(steps_index == timestep[0], alpha_bar, 0.0))
    clean_latent = jnp.where(
        is_video[:, None], jnp.sqrt(alpha_now) * latent - jnp.sqrt(1.0 - alpha_now) * guided, 0.0
    )
    return (layer_out[None], clean_latent)


QUOTAS = (0, 64, 128)
CAP = 128
CHUNKS = len(QUOTAS) - 1
F32, BF16 = jnp.float32, jnp.bfloat16
TILE = 512
LONG = 10**10


def size_of(k):
    return QUOTAS[k + 1] - QUOTAS[k]


def swap(array, axis, distance, size):
    return lax.ppermute(array, axis, [(i, i ^ distance) for i in range(size)])


def z_swaps(array):
    return [swap(array, "wide", s, 4) for s in (1, 2, 3)]


def choose(values, index):
    out = values[0]
    for i in range(1, 4):
        out = jnp.where(index == i, values[i], out)
    return out


def layout(table):
    counts = [table[b] for b in range(4)]
    largest = jnp.int32(3)
    for b in (2, 1, 0):
        largest = jnp.where(counts[b] == CAP, b, largest)
    starts, others, ranks, offsets = [], [], [], []
    rank, offset = jnp.int32(0), jnp.int32(0)
    for b in range(4):
        other = jnp.where(largest == b, 0, 1)
        ranks.append(rank * other)
        others.append(other)
        offsets.append(offset)
        rank = rank + other * counts[b]
        offset = offset + counts[b]
    block = lax.axis_index("wide")
    of = lambda values: [choose(values, jnp.bitwise_xor(block, s)) for s in range(4)]
    return of(ranks), of(counts), of(others), of(offsets)[0], choose(offsets, largest)


def high_low(values):
    high = values.astype(BF16)
    return high, (values - high.astype(F32)).astype(BF16)


def load(source, place, sems):
    parts = sems.shape[0]
    height = source.shape[0] // parts
    copies = []
    for t in range(parts):
        rows = pl.ds(t * height, height)
        copies.append(pltpu.make_async_copy(source.at[rows, :], place.at[rows, :], sems.at[t]))
        copies[-1].start()
    return copies


def load_half(source, half, place, sems):
    width = place.shape[1]
    copies = []
    for t in range(0, width, TILE):
        columns = pl.ds(pl.multiple_of(half * width + t, 128), TILE)
        copies.append(
            pltpu.make_async_copy(
                source.at[:, columns], place.at[:, pl.ds(t, TILE)], sems.at[len(copies)]
            )
        )
        copies[-1].start()
    return copies


def rows_of(parts, core):
    total = parts[:8] + parts[8:]
    total = jnp.where(core == 0, total, pltpu.roll(total, 4, 0))
    high, low = high_low(total)
    return jnp.concatenate([high.astype(F32), low.astype(F32)], 0).astype(BF16)


def hold_kernel(source, _, place, sems):
    for copy in load(source, place, sems):
        copy.wait()


def text_rows(k, largest_offset):
    size = size_of(k)
    row = lax.broadcasted_iota(jnp.int32, (2 * size, 1), 0)
    rank = jnp.where(row < size, row, row - size) + QUOTAS[k]
    position = jnp.where(
        row < size, rank + largest_offset, jnp.where(rank < largest_offset, rank, rank + CAP)
    )
    return position < TEXT


def gather_matrix(k, ranks, counts, others):
    size = size_of(k)
    places = []
    for p in range(k + 1):
        piece = size_of(p)
        lane = lax.broadcasted_iota(jnp.int32, (1, 4 * piece), 1)
        which, slot = lane // piece, lane % piece + QUOTAS[p]
        rank = slot + choose(ranks, which) - QUOTAS[k]
        live = (rank >= 0) & (rank < size) & (slot < choose(counts, which))
        row = jnp.where(live, rank + choose(others, which) * size, -1)
        at = lax.broadcasted_iota(jnp.int32, (2 * size, 4 * piece), 0)
        places.append(jnp.where(at == row, 1.0, 0.0).astype(BF16))
    return jnp.concatenate(places, 1)


def spread_matrix(k, ranks, counts, others):
    size = size_of(k)
    places = []
    for s in range(4):
        first = jnp.maximum(QUOTAS[k] - ranks[s], 0)
        last = jnp.minimum(counts[s], QUOTAS[k + 1] - ranks[s])
        index = lax.broadcasted_iota(jnp.int32, (size, 1), 0)
        slot = first + jnp.bitwise_and(index - first, size - 1)
        row = jnp.where(slot < last, slot + ranks[s] - QUOTAS[k] + others[s] * size, -1)
        at = lax.broadcasted_iota(jnp.int32, (size, 2 * size), 1)
        places.append(jnp.where(at == row, 1.0, 0.0).astype(BF16))
    return jnp.concatenate(places, 0)


def take_kernel(source, out, sem):
    copy = pltpu.make_async_copy(source.at[pl.ds(0, out.shape[0]), :], out, sem)
    copy.start()
    copy.wait()


def prepare_kernel(table_in, hidden, mod_in, out_weight, w, *refs):
    later, refs = refs[: CHUNKS - 1], refs[CHUNKS - 1 :]
    gathers, refs = refs[:CHUNKS], refs[CHUNKS:]
    spreads, refs = refs[:CHUNKS], refs[CHUNKS:]
    texts, refs = refs[:CHUNKS], refs[CHUNKS:]
    held, kept, tokens, mod, weight, rows_out, ends_out, slots_out, video_out = refs[:9]
    table, sems, small = refs[9:]
    core = lax.axis_index("narrow") % 2
    sources = (table_in, mod_in, out_weight, hidden)
    copies = [
        pltpu.make_async_copy(source, place, small.at[i])
        for i, (source, place) in enumerate(zip(sources, (table, mod, weight, tokens)))
    ]
    for copy in copies:
        copy.start()
    big = load_half(w, 1 - core, held, sems.at[0]) + load_half(w, core, kept, sems.at[1])

    copies[0].wait()
    ranks, counts, others, offset, largest_offset = layout(table)
    for k in range(CHUNKS):
        gathers[k][...] = gather_matrix(k, ranks, counts, others)
        spreads[k][...] = spread_matrix(k, ranks, counts, others)
        text = jnp.where(text_rows(k, largest_offset), 1.0, 0.0)
        texts[k][...] = jnp.broadcast_to(text, texts[k].shape)
    slot = lax.broadcasted_iota(jnp.int32, (CAP, 128), 0)
    lane = lax.broadcasted_iota(jnp.int32, (CAP, 128), 1)
    rank = slot + ranks[0]
    flag = lambda condition: jnp.where(condition, 1.0, 0.0)
    kind = jnp.where(lane == 0, flag(slot < counts[0]), flag(slot + offset < TEXT))
    for k in range(CHUNKS):
        kind = jnp.where(
            lane == 2 + k, flag((rank >= QUOTAS[k]) & (rank < QUOTAS[k + 1])), kind
        )
    slots_out[...] = kind
    slot = lax.broadcasted_iota(jnp.int32, (8, CAP), 1)
    video_out[...] = jnp.where((slot < counts[0]) & (slot + offset >= TEXT), 1.0, 0.0)

    copies[1].wait()
    row = lax.broadcasted_iota(jnp.int32, (8, 1), 0)
    rows = jnp.where(row == 0, 1.0 + mod[1:2, :], jnp.zeros((8, 1), F32))
    rows = jnp.where(row == 1, 1.0 + mod[4:5, :], rows)
    rows = jnp.where(row == 2, mod[0:1, :], rows)
    rows = jnp.where(row == 3, mod[3:4, :], rows)
    rows_out[...] = jnp.concatenate(high_low(rows), 0)
    rows = jnp.where(row == 0, 1.0 + mod[7:8, :], jnp.zeros((8, 1), F32))
    rows = jnp.where(row == 1, mod[6:7, :], rows)
    copies[2].wait()
    ends = lax.dot_general(
        jnp.concatenate(high_low(rows), 0),
        weight[...],
        (((1,), (1,)), ((), ())),
        preferred_element_type=F32,
    )
    ends = rows_of(ends, core)
    ends_out[...] = jnp.concatenate([ends, jnp.zeros((16, 128 - ends.shape[1]), BF16)], 1)
    copies[3].wait()
    for k in range(1, CHUNKS):
        later[k - 1][...] = tokens[QUOTAS[k] : QUOTAS[k + 1], :]
    for copy in big:
        copy.wait()


def expand_sent_kernel(k, count, text, mod, place, *refs):
    pieces, (w, sums, ends) = refs[:count], refs[count : count + 3]
    z_out, sent_out, side_out = refs[-3:]
    core = lax.axis_index("narrow") % 2
    units = w.shape[1]
    rows = side_out.shape[0]
    tokens = jnp.concatenate([piece[...] for piece in pieces], 0)
    x = jnp.dot(place[...], tokens, preferred_element_type=F32)
    centre = (jnp.sum(x, -1, keepdims=True) / x.shape[1]).astype(BF16).astype(F32)
    x = x - centre
    z = (x * (1.0 + jnp.where(text[:, :1] > 0.5, mod[4:5, :], mod[1:2, :]))).astype(BF16)
    if k == 0:
        z = jnp.concatenate([z, sums[...]], 0)
    z_out[...] = z
    for t in range(0, units, TILE):
        product = jnp.dot(z, w[:, t : t + TILE], preferred_element_type=F32)
        sent_out[:rows, t : t + TILE] = product[:rows].astype(BF16)
        if k == 0:
            sent_out[rows:, t : t + TILE] = rows_of(product[rows:], core)
    total = jnp.sum(x, -1, keepdims=True)
    square = jnp.sum(x * x, -1, keepdims=True)
    total_high = total.astype(BF16).astype(F32)
    square_high = square.astype(BF16).astype(F32)
    lane = lax.broadcasted_iota(jnp.int32, (rows, 128), 1) - 4 * core
    side = jnp.where((lane == 0) | (lane == 1), centre, 0.0)
    side = jnp.where(lane == 16, total_high, side)
    side = jnp.where(lane == 17, total - total_high, side)
    side = jnp.where(lane == 18, square_high, side)
    side = jnp.where(lane == 19, square - square_high, side).astype(BF16)
    side_out[...] = side
    sent_out[:rows, units:] = side
    if k == 0:
        sent_out[rows:, units:] = ends[...]


def expand_kept_kernel(k, z, w, *refs):
    kept_out = refs[-1 if k else -2]
    core = lax.axis_index("narrow") % 2
    rows = kept_out.shape[0]
    for t in range(0, w.shape[1], TILE):
        columns = slice(t, t + TILE)
        product = jnp.dot(z[...], w[:, columns], preferred_element_type=F32)
        kept_out[:, columns] = product[:rows]
        if k == 0:
            refs[-1][:, columns] = rows_of(product[rows:], core)


def pair_kernel(first, second, _, out):
    out[...] = jnp.concatenate([first[...], second[...]], 0)


def merge_kernel(k, kept, side, came, sums, ends, total_out, sent_out):
    rows, units = kept.shape
    add = lambda left, right: (left[...].astype(F32) + right.astype(F32)).astype(BF16)
    total = kept[...] + came[:rows, :units].astype(F32)
    total_out[...] = total
    sent_out[:rows, :units] = total.astype(BF16)
    sent_out[:rows, units:] = add(side, came[:rows, units:])
    if k == 0:
        sent_out[rows:, :units] = add(sums, came[rows:, :units])
        sent_out[rows:, units:] = add(ends, came[rows:, units:])


def activate_kernel(features, text, total, sent, came, first_sent, first_came, *refs):
    act_out = refs[-1]
    rows, units = total.shape
    sides = [sent[:rows, units:].astype(F32), came[:rows, units:].astype(F32)]
    lane = lax.broadcasted_iota(jnp.int32, (rows, 128), 1)
    field = lane % 4
    summed = sides[0] + sides[1]
    add = lambda values, mask: jnp.sum(jnp.where(mask, values, 0.0), -1, keepdims=True)
    centres, measures = lane < 8, (lane >= 16) & (lane < 24)
    average = (
        add(summed, centres & (field == 0)) * features + add(summed, measures & (field < 2))
    ) / D
    spread = add(summed, measures & (field >= 2))
    aparts = []
    for side in sides:
        apart = jnp.where(centres, side - average, 0.0)
        for core in range(2):
            off = add(apart, lane == 4 * core)
            own = lane // 4 == 4 + core
            spread = spread + off * (2.0 * add(side, own & (field < 2)) + features * off)
        aparts.append(apart)
    scale = lax.rsqrt(spread / D + norm_eps)
    of_text = jnp.where(text[...] > 0.5, 1, 0)
    mine = centres & (lane % 2 == of_text)
    packed, shift = None, 0
    for apart in aparts:
        factor = jnp.where(mine, jnp.where(field < 2, apart * scale, 1.0), 0.0)
        high = factor.astype(BF16).astype(F32)
        for part in (high, high, factor - high, factor - high):
            part = pltpu.roll(part, shift, 1) if shift else part
            packed = part if packed is None else packed + part
            shift += 8
    packed = packed[:, :64].astype(BF16)
    own, other = first_sent[-16:, :units], first_came[-16:, :units]
    factors = jnp.concatenate([own, own, other, other], 0)
    for t in range(0, units, TILE):
        columns = slice(t, t + TILE)
        pre = total[:, columns] + came[:rows, columns].astype(F32)
        extra = jnp.dot(packed, factors[:, columns], preferred_element_type=F32)
        act_out[:, columns] = jax.nn.gelu(pre * scale + extra, approximate=True).astype(BF16)


def contract_own_kernel(k, act, w, mine, first_sent, first_came, out, *ends_out):
    core = lax.axis_index("narrow") % 2
    units = w.shape[0] // 2
    rows = pl.ds(pl.multiple_of(core * units, 128), units)
    out[...] = jnp.dot(act[...], w[rows, :], preferred_element_type=F32)
    if k == 0:
        total = first_sent[-16:, units:].astype(F32) + first_came[-16:, units:].astype(F32)
        total = total[:8] + total[8:]
        total = total + pltpu.roll(total, 4, 0)
        own = mine[...].astype(F32)
        own = own[:8] + own[8:]
        own = own + pltpu.roll(own, 4, 0)
        ends_out[0][...] = jnp.concatenate([total, own, jnp.zeros((112, 128), F32)], 0).T


def contract_other_kernel(k, place, act, so_far, w, *outs):
    core = lax.axis_index("narrow") % 2
    units = w.shape[0] // 2
    rows = pl.ds(pl.multiple_of((1 - core) * units, 128), units)
    total = so_far[...] + jnp.dot(act[...], w[rows, :], preferred_element_type=F32)
    spread = jnp.dot(place[...], total.astype(BF16), preferred_element_type=F32).astype(BF16)
    size = size_of(k)
    for s in range(4):
        outs[s][...] = spread[s * size : (s + 1) * size]


def finish_kernel(slots, hidden, mod, out_weight, ends, *refs):
    pieces, (layer_out, bundle_out) = refs[: 4 * CHUNKS], refs[4 * CHUNKS :]
    result = jnp.zeros(hidden.shape, F32)
    for k in range(CHUNKS):
        total = pieces[4 * k][...].astype(F32)
        for s in (1, 2, 3):
            total = total + pieces[4 * k + s][...].astype(F32)
        total = jnp.concatenate([total] * (CAP // size_of(k)), 0)
        result = jnp.where(slots[:, 2 + k : 3 + k] > 0.5, total, result)
    gate = jnp.where(slots[:, 1:2] > 0.5, mod[5:6, :], mod[2:3, :])
    layer = hidden[...].astype(F32) + gate * result
    layer = jnp.where(slots[:, 0:1] > 0.5, layer, 0.0).astype(BF16)
    layer_out[...] = layer
    x = layer.astype(F32)
    centre = jnp.sum(x, -1, keepdims=True) / x.shape[1]
    ones = jnp.ones((8, x.shape[1]), BF16)
    across = lambda left, right: lax.dot_general(
        left, right, (((1,), (1,)), ((), ())), preferred_element_type=F32
    )
    high, low = high_low(x * x)
    total, square = across(ones, layer), across(ones, high) + across(ones, low)
    width = out_weight.shape[0]
    product = across(out_weight[...], ((x - centre) * (1.0 + mod[7:8, :])).astype(BF16))
    bundle_out[:width, :] = product + total[0:1] / x.shape[1] * ends[:width, 8:9]
    row = lax.broadcasted_iota(jnp.int32, (8, CAP), 0)
    bundle_out[width:, :] = jnp.where(row == 0, total, square)


def write_kernel(layer, out):
    out[...] = layer[...]


def add_kernel(left, right, out):
    out[...] = left[...] + right[...]


def noise_kernel(timestep, alphas, video, latent, base_out, factor_out):
    index = lax.broadcasted_iota(jnp.int32, (8, 128), 0) * 128 + lax.broadcasted_iota(
        jnp.int32, (8, 128), 1
    )
    alpha = jnp.sum(
        jnp.sum(jnp.where(index == timestep[0], alphas[...], 0.0), 0, keepdims=True),
        1,
        keepdims=True,
    )
    base_out[...] = jnp.where(video[0:1] > 0.5, jnp.sqrt(alpha) * latent[...], 0.0)
    factor_out[...] = jnp.where(video[...] > 0.5, jnp.sqrt(1.0 - alpha), 0.0)


def latent_kernel(base, factor, ends, mine, mine_y, other, other_y, out):
    width = out.shape[0]

    def velocity(total):
        average = total[width : width + 1] / D
        variance = total[width + 1 : width + 2] / D - average * average
        return (total[:width] - average * ends[:width, 0:1]) * lax.rsqrt(
            variance + norm_eps
        ) + ends[:width, 1:2]

    first = lax.axis_index("cfg") == 0
    guided = velocity(mine[...] + mine_y[...]) * jnp.where(first, guidance, 1.0 - guidance)
    guided = guided + velocity(other[...] + other_y[...]) * jnp.where(
        first, 1.0 - guidance, guidance
    )
    guided = jnp.where(factor[0:1] > 0.0, guided, 0.0)
    out[...] = base[...] - factor[0:1] * guided


def alpha_constant():
    ends = np.sqrt(np.float64(0.00085)), np.sqrt(np.float64(0.012))
    betas = np.linspace(ends[0], ends[1], 1000, dtype=np.float64) ** 2
    return np.pad(np.cumprod(1.0 - betas), (0, 24)).astype(np.float32).reshape(8, 128)


def call(kernel, outs, args, spaces, scratch=(), weight=1):
    kinds = {"v": pltpu.VMEM, "s": pltpu.SMEM, "a": pl.ANY}
    return pl.pallas_call(
        kernel,
        out_shape=[jax.ShapeDtypeStruct(shape, dtype) for shape, dtype in outs],
        in_specs=[pl.BlockSpec(memory_space=kinds[letter]) for letter in spaces],
        out_specs=[pl.BlockSpec(memory_space=pltpu.VMEM) for _ in outs],
        scratch_shapes=list(scratch),
        compiler_params=pltpu.CompilerParams(vmem_limit_bytes=24 * 2**20),
        cost_estimate=pl.CostEstimate(flops=weight, bytes_accessed=1, transcendentals=0),
    )(*args)


def four_blocks(
    hidden, split_table, modulation, expand_weight, contract_weight, output_weight, latent, timestep
):
    hidden = hidden[0]
    features = hidden.shape[1]
    units = expand_weight.shape[1] // 2
    width = output_weight.shape[1]
    payload = units + 128

    in_place = lambda array: pltpu.with_memory_space_constraint(array, pltpu.HBM)
    (piece,) = call(
        take_kernel,
        [((QUOTAS[1], features), BF16)],
        [in_place(hidden)],
        "a",
        [pltpu.SemaphoreType.DMA(())],
    )
    arrived = [[piece] + z_swaps(piece)]

    tiles = units // TILE
    chunks = range(CHUNKS)
    made = call(
        prepare_kernel,
        [((size_of(k), features), BF16) for k in chunks[1:]]
        + [((2 * size_of(k), 4 * QUOTAS[k + 1]), BF16) for k in chunks]
        + [((4 * size_of(k), 2 * size_of(k)), BF16) for k in chunks]
        + [((2 * size_of(k), 128), F32) for k in chunks]
        + [
            ((features, units), BF16),
            ((features, units), BF16),
            (hidden.shape, BF16),
            (modulation.shape, F32),
            ((width, features), BF16),
            ((16, features), BF16),
            ((16, 128), BF16),
            ((CAP, 128), F32),
            ((8, CAP), F32),
        ],
        [
            in_place(split_table),
            in_place(hidden),
            in_place(modulation),
            in_place(output_weight.T),
            in_place(expand_weight),
        ],
        "aaaaa",
        [
            pltpu.SMEM(split_table.shape, jnp.int32),
            pltpu.SemaphoreType.DMA((2, tiles)),
            pltpu.SemaphoreType.DMA((4,)),
        ],
    )
    later, made = made[: CHUNKS - 1], made[CHUNKS - 1 :]
    gathers, made = made[:CHUNKS], made[CHUNKS:]
    spreads, made = made[:CHUNKS], made[CHUNKS:]
    texts, made = made[:CHUNKS], made[CHUNKS:]
    held_sent, held_kept, tokens, mod, out_weight, rows_in, ends_mine, slots, video = made
    neighbours = [(piece, swap(piece, "wide", 1, 4)) for piece in later]

    merged = []
    before = []
    for k in chunks:
        rows = 2 * size_of(k)
        sent_rows = rows + (16 if k == 0 else 0)
        pieces = [piece for phase in arrived for piece in phase]
        z, sent, side = call(
            functools.partial(expand_sent_kernel, k, len(pieces)),
            [((sent_rows, features), BF16), ((sent_rows, payload), BF16), ((rows, 128), BF16)],
            [texts[k], mod, gathers[k], *pieces, held_sent, rows_in, ends_mine, *before],
            "vvv" + "v" * len(pieces) + "vvv" + "a" * len(before),
            weight=LONG,
        )
        came = swap(sent, "narrow", 1, 4)
        pair = []
        if k + 1 < CHUNKS:
            pair = call(
                pair_kernel,
                [((2 * size_of(k + 1), features), BF16)],
                [*neighbours[k], z],
                "vva",
            )
            arrived.append([*pair, swap(*pair, "wide", 2, 4)])
        kept, *sums_made = call(
            functools.partial(expand_kept_kernel, k),
            [((rows, units), F32)] + ([((16, units), BF16)] if k == 0 else []),
            [z, held_kept, *pair],
            "vv" + "a" * len(pair),
            weight=LONG,
        )
        sums = sums_made[0] if k == 0 else sums
        total, sent = call(
            functools.partial(merge_kernel, k),
            [((rows, units), F32), ((sent_rows, payload), BF16)],
            [kept, side, came, sums, ends_mine],
            "vvvvv",
        )
        if k == 0:
            (held_out,) = call(
                hold_kernel,
                [(contract_weight.shape, BF16)],
                [in_place(contract_weight), sent],
                "aa",
                [pltpu.SemaphoreType.DMA((4,))],
            )
        before = [sent, held_out]
        merged.append((total, sent, swap(sent, "narrow", 2, 4)))

    returned = []
    before = []
    first = merged[0][1:]
    for k in chunks:
        rows = 2 * size_of(k)
        total, sent, came = merged[k]
        if k + 1 < CHUNKS:
            before = before + [merged[k + 1][1]]
        (act,) = call(
            functools.partial(activate_kernel, features),
            [((rows, units), BF16)],
            [texts[k], total, sent, came, *first, *before],
            "vvvvvv" + "a" * len(before),
        )
        act_came = swap(act, "narrow", 1, 4)
        out, *ends_made = call(
            functools.partial(contract_own_kernel, k),
            [((rows, features), F32)] + ([((128, 128), F32)] if k == 0 else []),
            [act, held_out, ends_mine, *first],
            "vvvvv",
            weight=LONG,
        )
        ends = ends_made[0] if k == 0 else ends
        pieces = call(
            functools.partial(contract_other_kernel, k),
            [((size_of(k), features), BF16)] * 4,
            [spreads[k], act_came, out, held_out],
            "vvvv",
        )
        before = pieces
        returned.append(pieces[0])
        returned.extend(swap(pieces[s], "wide", s, 4) for s in (1, 2, 3))

    layer, bundle = call(
        finish_kernel,
        [((CAP, features), BF16), ((width + 8, CAP), F32)],
        [slots, tokens, mod, out_weight, ends, *returned],
        "v" * (5 + len(returned)),
    )
    (layer_out,) = call(write_kernel, [((CAP, features), BF16)], [layer], "v", weight=LONG)
    (bundle,) = call(
        add_kernel, [((width + 8, CAP), F32)], [bundle, swap(bundle, "narrow", 1, 4)], "vv"
    )
    base, factor = call(
        noise_kernel,
        [((width, CAP), F32), ((8, CAP), F32)],
        [timestep, alpha_constant(), video, latent.T],
        "svvv",
        weight=LONG,
    )
    (clean_latent,) = call(
        latent_kernel,
        [((width, CAP), F32)],
        [base, factor, ends, bundle] + [swap(bundle, ("cfg", "narrow"), n, 8) for n in (2, 4, 6)],
        "vvvvvvv",
    )
    return (layer_out[None], clean_latent.T)


def solution(mesh):
    by_swaps = (mesh.shape["wide"], mesh.shape["narrow"], mesh.shape["cfg"]) == (4, 4, 2)
    return jax.shard_map(
        four_blocks if by_swaps else any_slice,
        mesh=mesh,
        in_specs=(
            P("cfg", "wide", "narrow"),
            P(),
            P(None, "narrow"),
            P("narrow", "wide"),
            P("wide", "narrow"),
            P("narrow", None),
            P("wide", None),
            P(),
        ),
        out_specs=(P("cfg", "wide", "narrow"), P("wide", None)),
        check_vma=False,
    )
```

```python
import functools

import jax
import jax.numpy as jnp
import numpy as np
from jax import lax
from jax.experimental import pallas as pl
from jax.experimental.pallas import tpu as pltpu
from jax.sharding import PartitionSpec as P

D = 3072
TEXT = 226


norm_eps = 1e-05
guidance = 6.0


def alpha_table():
    steps_index = jnp.arange(1000, dtype=jnp.int32)
    start_root = 0.00085**0.5
    end_root = 0.012**0.5
    roots = start_root + (end_root - start_root) * steps_index.astype(jnp.float32) / 999.0
    return (steps_index, jnp.cumprod(1.0 - roots * roots))


def feature_norm(values, shifts, scaling):
    totals, squares = lax.psum(
        (jnp.sum(values, -1, keepdims=True), jnp.sum(values * values, -1, keepdims=True)), "narrow"
    )
    average = totals / D
    variance = squares / D - average * average
    return (values - average) * lax.rsqrt(variance + norm_eps) * (1.0 + scaling) + shifts


def any_slice(
    hidden, split_table, modulation, expand_weight, contract_weight, output_weight, latent, timestep
):
    capacity = hidden.shape[1]
    wide_index = lax.axis_index("wide")
    table_index = jnp.arange(split_table.shape[0], dtype=jnp.int32)
    offset = jnp.sum(jnp.where(table_index < wide_index, split_table, 0))
    own_count = jnp.sum(jnp.where(table_index == wide_index, split_table, 0))
    slot_index = jnp.arange(capacity, dtype=jnp.int32)
    position = offset + slot_index
    slot_live = slot_index < own_count
    is_text = slot_live & (position < TEXT)
    is_video = slot_live & (position >= TEXT)
    text_column = is_text[:, None]
    shifts = jnp.where(text_column, modulation[3], modulation[0])
    scaling = jnp.where(text_column, modulation[4], modulation[1])
    gating = jnp.where(text_column, modulation[5], modulation[2])
    values = hidden[0].astype(jnp.float32)
    normed = feature_norm(values, shifts, scaling).astype(jnp.bfloat16)
    hidden_part = jnp.dot(
        lax.all_gather(normed, "wide", axis=0, tiled=True),
        expand_weight,
        preferred_element_type=jnp.float32,
    )
    hidden_pre = lax.psum(hidden_part, "narrow")
    activated = jax.nn.gelu(hidden_pre, approximate=True).astype(jnp.bfloat16)
    ff_result = lax.psum_scatter(
        jnp.dot(activated, contract_weight, preferred_element_type=jnp.float32),
        "wide",
        scatter_dimension=0,
        tiled=True,
    )
    layer_out = jnp.where(slot_live[:, None], values + gating * ff_result, 0.0).astype(jnp.bfloat16)
    final_in = layer_out.astype(jnp.float32)
    final_normed = feature_norm(final_in, modulation[6], modulation[7]).astype(jnp.bfloat16)
    velocity_part = jnp.dot(final_normed, output_weight, preferred_element_type=jnp.float32)
    copy_weight = jnp.where(lax.axis_index("cfg") == 0, guidance, 1.0 - guidance)
    guided = lax.psum(velocity_part * copy_weight, ("cfg", "narrow"))
    steps_index, alpha_bar = alpha_table()
    alpha_now = jnp.sum(jnp.where(steps_index == timestep[0], alpha_bar, 0.0))
    clean_latent = jnp.where(
        is_video[:, None], jnp.sqrt(alpha_now) * latent - jnp.sqrt(1.0 - alpha_now) * guided, 0.0
    )
    return (layer_out[None], clean_latent)


QUOTAS = (0, 64, 128)
CAP = 128
CHUNKS = len(QUOTAS) - 1
F32, BF16 = jnp.float32, jnp.bfloat16
TILE = 512
LONG = 10**10


def size_of(k):
    return QUOTAS[k + 1] - QUOTAS[k]


def swap(array, axis, distance, size):
    return lax.ppermute(array, axis, [(i, i ^ distance) for i in range(size)])


def z_swaps(array):
    return [swap(array, "wide", s, 4) for s in (1, 2, 3)]


def choose(values, index):
    out = values[0]
    for i in range(1, 4):
        out = jnp.where(index == i, values[i], out)
    return out


def layout(table):
    counts = [table[b] for b in range(4)]
    largest = jnp.int32(3)
    for b in (2, 1, 0):
        largest = jnp.where(counts[b] == CAP, b, largest)
    starts, others, ranks, offsets = [], [], [], []
    rank, offset = jnp.int32(0), jnp.int32(0)
    for b in range(4):
        other = jnp.where(largest == b, 0, 1)
        ranks.append(rank * other)
        others.append(other)
        offsets.append(offset)
        rank = rank + other * counts[b]
        offset = offset + counts[b]
    block = lax.axis_index("wide")
    of = lambda values: [choose(values, jnp.bitwise_xor(block, s)) for s in range(4)]
    return of(ranks), of(counts), of(others), of(offsets)[0], choose(offsets, largest)


def high_low(values):
    high = values.astype(BF16)
    return high, (values - high.astype(F32)).astype(BF16)


def load(source, place, sems):
    parts = sems.shape[0]
    height = source.shape[0] // parts
    copies = []
    for t in range(parts):
        rows = pl.ds(t * height, height)
        copies.append(pltpu.make_async_copy(source.at[rows, :], place.at[rows, :], sems.at[t]))
        copies[-1].start()
    return copies


def load_half(source, half, place, sems):
    width = place.shape[1]
    copies = []
    for t in range(0, width, TILE):
        columns = pl.ds(pl.multiple_of(half * width + t, 128), TILE)
        copies.append(
            pltpu.make_async_copy(
                source.at[:, columns], place.at[:, pl.ds(t, TILE)], sems.at[len(copies)]
            )
        )
        copies[-1].start()
    return copies


def rows_of(parts, core):
    total = parts[:8] + parts[8:]
    total = jnp.where(core == 0, total, pltpu.roll(total, 4, 0))
    high, low = high_low(total)
    return jnp.concatenate([high.astype(F32), low.astype(F32)], 0).astype(BF16)


def hold_kernel(source, _, place, sems):
    for copy in load(source, place, sems):
        copy.wait()


def text_rows(k, largest_offset):
    size = size_of(k)
    row = lax.broadcasted_iota(jnp.int32, (2 * size, 1), 0)
    rank = jnp.where(row < size, row, row - size) + QUOTAS[k]
    position = jnp.where(
        row < size, rank + largest_offset, jnp.where(rank < largest_offset, rank, rank + CAP)
    )
    return position < TEXT


def gather_matrix(k, ranks, counts, others):
    size = size_of(k)
    places = []
    for p in range(k + 1):
        piece = size_of(p)
        lane = lax.broadcasted_iota(jnp.int32, (1, 4 * piece), 1)
        which, slot = lane // piece, lane % piece + QUOTAS[p]
        rank = slot + choose(ranks, which) - QUOTAS[k]
        live = (rank >= 0) & (rank < size) & (slot < choose(counts, which))
        row = jnp.where(live, rank + choose(others, which) * size, -1)
        at = lax.broadcasted_iota(jnp.int32, (2 * size, 4 * piece), 0)
        places.append(jnp.where(at == row, 1.0, 0.0).astype(BF16))
    return jnp.concatenate(places, 1)


def spread_matrix(k, ranks, counts, others):
    size = size_of(k)
    places = []
    for s in range(4):
        first = jnp.maximum(QUOTAS[k] - ranks[s], 0)
        last = jnp.minimum(counts[s], QUOTAS[k + 1] - ranks[s])
        index = lax.broadcasted_iota(jnp.int32, (size, 1), 0)
        slot = first + jnp.bitwise_and(index - first, size - 1)
        row = jnp.where(slot < last, slot + ranks[s] - QUOTAS[k] + others[s] * size, -1)
        at = lax.broadcasted_iota(jnp.int32, (size, 2 * size), 1)
        places.append(jnp.where(at == row, 1.0, 0.0).astype(BF16))
    return jnp.concatenate(places, 0)


def take_kernel(source, *refs):
    pieces, sems = refs[:CHUNKS], refs[CHUNKS]
    copies = []
    for k in range(CHUNKS):
        rows = pl.ds(QUOTAS[k], size_of(k))
        copies.append(pltpu.make_async_copy(source.at[rows, :], pieces[k], sems.at[k]))
        copies[-1].start()
    for copy in copies:
        copy.wait()


def prepare_kernel(table_in, hidden, mod_in, out_weight, w, *refs):
    gathers, refs = refs[:CHUNKS], refs[CHUNKS:]
    spreads, refs = refs[:CHUNKS], refs[CHUNKS:]
    texts, refs = refs[:CHUNKS], refs[CHUNKS:]
    held, kept, tokens, mod, weight, rows_out, ends_out, slots_out, video_out = refs[:9]
    table, sems, small = refs[9:]
    core = lax.axis_index("narrow") % 2
    sources = (table_in, mod_in, out_weight, hidden)
    copies = [
        pltpu.make_async_copy(source, place, small.at[i])
        for i, (source, place) in enumerate(zip(sources, (table, mod, weight, tokens)))
    ]
    for copy in copies:
        copy.start()
    big = load_half(w, 1 - core, held, sems.at[0]) + load_half(w, core, kept, sems.at[1])

    copies[0].wait()
    ranks, counts, others, offset, largest_offset = layout(table)
    for k in range(CHUNKS):
        gathers[k][...] = gather_matrix(k, ranks, counts, others)
        spreads[k][...] = spread_matrix(k, ranks, counts, others)
        text = jnp.where(text_rows(k, largest_offset), 1.0, 0.0)
        texts[k][...] = jnp.broadcast_to(text, texts[k].shape)
    slot = lax.broadcasted_iota(jnp.int32, (CAP, 128), 0)
    lane = lax.broadcasted_iota(jnp.int32, (CAP, 128), 1)
    rank = slot + ranks[0]
    flag = lambda condition: jnp.where(condition, 1.0, 0.0)
    kind = jnp.where(lane == 0, flag(slot < counts[0]), flag(slot + offset < TEXT))
    for k in range(CHUNKS):
        kind = jnp.where(
            lane == 2 + k, flag((rank >= QUOTAS[k]) & (rank < QUOTAS[k + 1])), kind
        )
    slots_out[...] = kind
    slot = lax.broadcasted_iota(jnp.int32, (8, CAP), 1)
    video_out[...] = jnp.where((slot < counts[0]) & (slot + offset >= TEXT), 1.0, 0.0)

    copies[1].wait()
    row = lax.broadcasted_iota(jnp.int32, (8, 1), 0)
    rows = jnp.where(row == 0, 1.0 + mod[1:2, :], jnp.zeros((8, 1), F32))
    rows = jnp.where(row == 1, 1.0 + mod[4:5, :], rows)
    rows = jnp.where(row == 2, mod[0:1, :], rows)
    rows = jnp.where(row == 3, mod[3:4, :], rows)
    rows_out[...] = jnp.concatenate(high_low(rows), 0)
    rows = jnp.where(row == 0, 1.0 + mod[7:8, :], jnp.zeros((8, 1), F32))
    rows = jnp.where(row == 1, mod[6:7, :], rows)
    copies[2].wait()
    ends = lax.dot_general(
        jnp.concatenate(high_low(rows), 0),
        weight[...],
        (((1,), (1,)), ((), ())),
        preferred_element_type=F32,
    )
    ends = rows_of(ends, core)
    ends_out[...] = jnp.concatenate([ends, jnp.zeros((16, 128 - ends.shape[1]), BF16)], 1)
    copies[3].wait()
    for copy in big:
        copy.wait()


def expand_sent_kernel(k, count, text, mod, place, *refs):
    pieces, (w, sums, ends) = refs[:count], refs[count : count + 3]
    z_out, sent_out, side_out = refs[-3:]
    core = lax.axis_index("narrow") % 2
    units = w.shape[1]
    rows = side_out.shape[0]
    tokens = jnp.concatenate([piece[...] for piece in pieces], 0)
    x = jnp.dot(place[...], tokens, preferred_element_type=F32)
    centre = (jnp.sum(x, -1, keepdims=True) / x.shape[1]).astype(BF16).astype(F32)
    x = x - centre
    z = (x * (1.0 + jnp.where(text[:, :1] > 0.5, mod[4:5, :], mod[1:2, :]))).astype(BF16)
    if k == 0:
        z = jnp.concatenate([z, sums[...]], 0)
    z_out[...] = z
    for t in range(0, units, TILE):
        product = jnp.dot(z, w[:, t : t + TILE], preferred_element_type=F32)
        sent_out[:rows, t : t + TILE] = product[:rows].astype(BF16)
        if k == 0:
            sent_out[rows:, t : t + TILE] = rows_of(product[rows:], core)
    total = jnp.sum(x, -1, keepdims=True)
    square = jnp.sum(x * x, -1, keepdims=True)
    total_high = total.astype(BF16).astype(F32)
    square_high = square.astype(BF16).astype(F32)
    lane = lax.broadcasted_iota(jnp.int32, (rows, 128), 1) - 4 * core
    side = jnp.where((lane == 0) | (lane == 1), centre, 0.0)
    side = jnp.where(lane == 16, total_high, side)
    side = jnp.where(lane == 17, total - total_high, side)
    side = jnp.where(lane == 18, square_high, side)
    side = jnp.where(lane == 19, square - square_high, side).astype(BF16)
    side_out[...] = side
    sent_out[:rows, units:] = side
    if k == 0:
        sent_out[rows:, units:] = ends[...]


def expand_kept_kernel(k, z, w, *refs):
    kept_out = refs[-1 if k else -2]
    core = lax.axis_index("narrow") % 2
    rows = kept_out.shape[0]
    for t in range(0, w.shape[1], TILE):
        columns = slice(t, t + TILE)
        product = jnp.dot(z[...], w[:, columns], preferred_element_type=F32)
        kept_out[:, columns] = product[:rows]
        if k == 0:
            refs[-1][:, columns] = rows_of(product[rows:], core)


def pair_kernel(first, second, out):
    out[...] = jnp.concatenate([first[...], second[...]], 0)


def merge_kernel(k, kept, side, came, sums, ends, total_out, sent_out):
    rows, units = kept.shape
    add = lambda left, right: (left[...].astype(F32) + right.astype(F32)).astype(BF16)
    total = kept[...] + came[:rows, :units].astype(F32)
    total_out[...] = total
    sent_out[:rows, :units] = total.astype(BF16)
    sent_out[:rows, units:] = add(side, came[:rows, units:])
    if k == 0:
        sent_out[rows:, :units] = add(sums, came[rows:, :units])
        sent_out[rows:, units:] = add(ends, came[rows:, units:])


def activate_kernel(features, text, total, sent, came, first_sent, first_came, *refs):
    act_out = refs[-1]
    rows, units = total.shape
    sides = [sent[:rows, units:].astype(F32), came[:rows, units:].astype(F32)]
    lane = lax.broadcasted_iota(jnp.int32, (rows, 128), 1)
    field = lane % 4
    summed = sides[0] + sides[1]
    add = lambda values, mask: jnp.sum(jnp.where(mask, values, 0.0), -1, keepdims=True)
    centres, measures = lane < 8, (lane >= 16) & (lane < 24)
    average = (
        add(summed, centres & (field == 0)) * features + add(summed, measures & (field < 2))
    ) / D
    spread = add(summed, measures & (field >= 2))
    aparts = []
    for side in sides:
        apart = jnp.where(centres, side - average, 0.0)
        for core in range(2):
            off = add(apart, lane == 4 * core)
            own = lane // 4 == 4 + core
            spread = spread + off * (2.0 * add(side, own & (field < 2)) + features * off)
        aparts.append(apart)
    scale = lax.rsqrt(spread / D + norm_eps)
    of_text = jnp.where(text[...] > 0.5, 1, 0)
    mine = centres & (lane % 2 == of_text)
    packed, shift = None, 0
    for apart in aparts:
        factor = jnp.where(mine, jnp.where(field < 2, apart * scale, 1.0), 0.0)
        high = factor.astype(BF16).astype(F32)
        for part in (high, high, factor - high, factor - high):
            part = pltpu.roll(part, shift, 1) if shift else part
            packed = part if packed is None else packed + part
            shift += 8
    packed = packed[:, :64].astype(BF16)
    own, other = first_sent[-16:, :units], first_came[-16:, :units]
    factors = jnp.concatenate([own, own, other, other], 0)
    for t in range(0, units, TILE):
        columns = slice(t, t + TILE)
        pre = total[:, columns] + came[:rows, columns].astype(F32)
        extra = jnp.dot(packed, factors[:, columns], preferred_element_type=F32)
        act_out[:, columns] = jax.nn.gelu(pre * scale + extra, approximate=True).astype(BF16)


def contract_own_kernel(k, act, w, mine, first_sent, first_came, out, *ends_out):
    core = lax.axis_index("narrow") % 2
    units = w.shape[0] // 2
    rows = pl.ds(pl.multiple_of(core * units, 128), units)
    out[...] = jnp.dot(act[...], w[rows, :], preferred_element_type=F32)
    if k == 0:
        total = first_sent[-16:, units:].astype(F32) + first_came[-16:, units:].astype(F32)
        total = total[:8] + total[8:]
        total = total + pltpu.roll(total, 4, 0)
        own = mine[...].astype(F32)
        own = own[:8] + own[8:]
        own = own + pltpu.roll(own, 4, 0)
        ends_out[0][...] = jnp.concatenate([total, own, jnp.zeros((112, 128), F32)], 0).T


def contract_other_kernel(k, place, act, so_far, w, *outs):
    core = lax.axis_index("narrow") % 2
    units = w.shape[0] // 2
    rows = pl.ds(pl.multiple_of((1 - core) * units, 128), units)
    total = so_far[...] + jnp.dot(act[...], w[rows, :], preferred_element_type=F32)
    spread = jnp.dot(place[...], total.astype(BF16), preferred_element_type=F32).astype(BF16)
    size = size_of(k)
    for s in range(4):
        outs[s][...] = spread[s * size : (s + 1) * size]


def finish_kernel(slots, hidden, mod, out_weight, ends, *refs):
    pieces, (layer_out, bundle_out) = refs[: 4 * CHUNKS], refs[4 * CHUNKS :]
    result = jnp.zeros(hidden.shape, F32)
    for k in range(CHUNKS):
        total = pieces[4 * k][...].astype(F32)
        for s in (1, 2, 3):
            total = total + pieces[4 * k + s][...].astype(F32)
        total = jnp.concatenate([total] * (CAP // size_of(k)), 0)
        result = jnp.where(slots[:, 2 + k : 3 + k] > 0.5, total, result)
    gate = jnp.where(slots[:, 1:2] > 0.5, mod[5:6, :], mod[2:3, :])
    layer = hidden[...].astype(F32) + gate * result
    layer = jnp.where(slots[:, 0:1] > 0.5, layer, 0.0).astype(BF16)
    layer_out[...] = layer
    x = layer.astype(F32)
    centre = jnp.sum(x, -1, keepdims=True) / x.shape[1]
    ones = jnp.ones((8, x.shape[1]), BF16)
    across = lambda left, right: lax.dot_general(
        left, right, (((1,), (1,)), ((), ())), preferred_element_type=F32
    )
    high, low = high_low(x * x)
    total, square = across(ones, layer), across(ones, high) + across(ones, low)
    width = out_weight.shape[0]
    product = across(out_weight[...], ((x - centre) * (1.0 + mod[7:8, :])).astype(BF16))
    bundle_out[:width, :] = product + total[0:1] / x.shape[1] * ends[:width, 8:9]
    row = lax.broadcasted_iota(jnp.int32, (8, CAP), 0)
    bundle_out[width:, :] = jnp.where(row == 0, total, square)


def write_kernel(layer, out):
    out[...] = layer[...]


def add_kernel(left, right, out):
    out[...] = left[...] + right[...]


def noise_kernel(timestep, alphas, video, latent, base_out, factor_out):
    index = lax.broadcasted_iota(jnp.int32, (8, 128), 0) * 128 + lax.broadcasted_iota(
        jnp.int32, (8, 128), 1
    )
    alpha = jnp.sum(
        jnp.sum(jnp.where(index == timestep[0], alphas[...], 0.0), 0, keepdims=True),
        1,
        keepdims=True,
    )
    base_out[...] = jnp.where(video[0:1] > 0.5, jnp.sqrt(alpha) * latent[...], 0.0)
    factor_out[...] = jnp.where(video[...] > 0.5, jnp.sqrt(1.0 - alpha), 0.0)


def latent_kernel(base, factor, ends, mine, mine_y, other, other_y, out):
    width = out.shape[0]

    def velocity(total):
        average = total[width : width + 1] / D
        variance = total[width + 1 : width + 2] / D - average * average
        return (total[:width] - average * ends[:width, 0:1]) * lax.rsqrt(
            variance + norm_eps
        ) + ends[:width, 1:2]

    first = lax.axis_index("cfg") == 0
    guided = velocity(mine[...] + mine_y[...]) * jnp.where(first, guidance, 1.0 - guidance)
    guided = guided + velocity(other[...] + other_y[...]) * jnp.where(
        first, 1.0 - guidance, guidance
    )
    guided = jnp.where(factor[0:1] > 0.0, guided, 0.0)
    out[...] = base[...] - factor[0:1] * guided


def alpha_constant():
    ends = np.sqrt(np.float64(0.00085)), np.sqrt(np.float64(0.012))
    betas = np.linspace(ends[0], ends[1], 1000, dtype=np.float64) ** 2
    return np.pad(np.cumprod(1.0 - betas), (0, 24)).astype(np.float32).reshape(8, 128)


def call(kernel, outs, args, spaces, scratch=(), weight=1):
    kinds = {"v": pltpu.VMEM, "s": pltpu.SMEM, "a": pl.ANY}
    return pl.pallas_call(
        kernel,
        out_shape=[jax.ShapeDtypeStruct(shape, dtype) for shape, dtype in outs],
        in_specs=[pl.BlockSpec(memory_space=kinds[letter]) for letter in spaces],
        out_specs=[pl.BlockSpec(memory_space=pltpu.VMEM) for _ in outs],
        scratch_shapes=list(scratch),
        compiler_params=pltpu.CompilerParams(vmem_limit_bytes=24 * 2**20),
        cost_estimate=pl.CostEstimate(flops=weight, bytes_accessed=1, transcendentals=0),
    )(*args)


def four_blocks(
    hidden, split_table, modulation, expand_weight, contract_weight, output_weight, latent, timestep
):
    hidden = hidden[0]
    features = hidden.shape[1]
    units = expand_weight.shape[1] // 2
    width = output_weight.shape[1]
    payload = units + 128

    in_place = lambda array: pltpu.with_memory_space_constraint(array, pltpu.HBM)
    chunks = range(CHUNKS)
    piece, *later = call(
        take_kernel,
        [((size_of(k), features), BF16) for k in chunks],
        [in_place(hidden)],
        "a",
        [pltpu.SemaphoreType.DMA((CHUNKS,))],
    )
    arrived = [[piece] + z_swaps(piece)]
    pairs = [
        call(
            pair_kernel,
            [((2 * piece.shape[0], features), BF16)],
            [piece, swap(piece, "wide", 1, 4)],
            "vv",
        )[0]
        for piece in later
    ]

    tiles = units // TILE
    made = call(
        prepare_kernel,
        [((2 * size_of(k), 4 * QUOTAS[k + 1]), BF16) for k in chunks]
        + [((4 * size_of(k), 2 * size_of(k)), BF16) for k in chunks]
        + [((2 * size_of(k), 128), F32) for k in chunks]
        + [
            ((features, units), BF16),
            ((features, units), BF16),
            (hidden.shape, BF16),
            (modulation.shape, F32),
            ((width, features), BF16),
            ((16, features), BF16),
            ((16, 128), BF16),
            ((CAP, 128), F32),
            ((8, CAP), F32),
        ],
        [
            in_place(split_table),
            in_place(hidden),
            in_place(modulation),
            in_place(output_weight.T),
            in_place(expand_weight),
        ],
        "aaaaa",
        [
            pltpu.SMEM(split_table.shape, jnp.int32),
            pltpu.SemaphoreType.DMA((2, tiles)),
            pltpu.SemaphoreType.DMA((4,)),
        ],
    )
    gathers, made = made[:CHUNKS], made[CHUNKS:]
    spreads, made = made[:CHUNKS], made[CHUNKS:]
    texts, made = made[:CHUNKS], made[CHUNKS:]
    held_sent, held_kept, tokens, mod, out_weight, rows_in, ends_mine, slots, video = made
    merged = []
    before = pairs[:1]
    for k in chunks:
        rows = 2 * size_of(k)
        sent_rows = rows + (16 if k == 0 else 0)
        pieces = [piece for phase in arrived for piece in phase]
        z, sent, side = call(
            functools.partial(expand_sent_kernel, k, len(pieces)),
            [((sent_rows, features), BF16), ((sent_rows, payload), BF16), ((rows, 128), BF16)],
            [texts[k], mod, gathers[k], *pieces, held_sent, rows_in, ends_mine, *before],
            "vvv" + "v" * len(pieces) + "vvv" + "a" * len(before),
            weight=LONG,
        )
        came = swap(sent, "narrow", 1, 4)
        arrived.extend([pair, swap(pair, "wide", 2, 4)] for pair in pairs[k : k + 1])
        kept, *sums_made = call(
            functools.partial(expand_kept_kernel, k),
            [((rows, units), F32)] + ([((16, units), BF16)] if k == 0 else []),
            [z, held_kept],
            "vv",
            weight=LONG,
        )
        sums = sums_made[0] if k == 0 else sums
        total, sent = call(
            functools.partial(merge_kernel, k),
            [((rows, units), F32), ((sent_rows, payload), BF16)],
            [kept, side, came, sums, ends_mine],
            "vvvvv",
        )
        if k == 0:
            (held_out,) = call(
                hold_kernel,
                [(contract_weight.shape, BF16)],
                [in_place(contract_weight), sent],
                "aa",
                [pltpu.SemaphoreType.DMA((4,))],
            )
        before = [sent, held_out]
        merged.append((total, sent, swap(sent, "narrow", 2, 4)))

    returned = []
    before = []
    first = merged[0][1:]
    for k in chunks:
        rows = 2 * size_of(k)
        total, sent, came = merged[k]
        if k + 1 < CHUNKS:
            before = before + [merged[k + 1][1]]
        (act,) = call(
            functools.partial(activate_kernel, features),
            [((rows, units), BF16)],
            [texts[k], total, sent, came, *first, *before],
            "vvvvvv" + "a" * len(before),
        )
        act_came = swap(act, "narrow", 1, 4)
        out, *ends_made = call(
            functools.partial(contract_own_kernel, k),
            [((rows, features), F32)] + ([((128, 128), F32)] if k == 0 else []),
            [act, held_out, ends_mine, *first],
            "vvvvv",
            weight=LONG,
        )
        ends = ends_made[0] if k == 0 else ends
        pieces = call(
            functools.partial(contract_other_kernel, k),
            [((size_of(k), features), BF16)] * 4,
            [spreads[k], act_came, out, held_out],
            "vvvv",
        )
        before = pieces
        returned.append(pieces[0])
        returned.extend(swap(pieces[s], "wide", s, 4) for s in (1, 2, 3))

    layer, bundle = call(
        finish_kernel,
        [((CAP, features), BF16), ((width + 8, CAP), F32)],
        [slots, tokens, mod, out_weight, ends, *returned],
        "v" * (5 + len(returned)),
    )
    (layer_out,) = call(write_kernel, [((CAP, features), BF16)], [layer], "v", weight=LONG)
    (bundle,) = call(
        add_kernel, [((width + 8, CAP), F32)], [bundle, swap(bundle, "narrow", 1, 4)], "vv"
    )
    base, factor = call(
        noise_kernel,
        [((width, CAP), F32), ((8, CAP), F32)],
        [timestep, alpha_constant(), video, latent.T],
        "svvv",
        weight=LONG,
    )
    (clean_latent,) = call(
        latent_kernel,
        [((width, CAP), F32)],
        [base, factor, ends, bundle] + [swap(bundle, ("cfg", "narrow"), n, 8) for n in (2, 4, 6)],
        "vvvvvvv",
    )
    return (layer_out[None], clean_latent.T)


def solution(mesh):
    by_swaps = (mesh.shape["wide"], mesh.shape["narrow"], mesh.shape["cfg"]) == (4, 4, 2)
    return jax.shard_map(
        four_blocks if by_swaps else any_slice,
        mesh=mesh,
        in_specs=(
            P("cfg", "wide", "narrow"),
            P(),
            P(None, "narrow"),
            P("narrow", "wide"),
            P("wide", "narrow"),
            P("narrow", None),
            P("wide", None),
            P(),
        ),
        out_specs=(P("cfg", "wide", "narrow"), P("wide", None)),
        check_vma=False,
    )
```

```python
import functools

import jax
import jax.numpy as jnp
import numpy as np
from jax import lax
from jax.experimental import pallas as pl
from jax.experimental.pallas import tpu as pltpu
from jax.sharding import PartitionSpec as P

D = 3072
TEXT = 226


norm_eps = 1e-05
guidance = 6.0


def alpha_table():
    steps_index = jnp.arange(1000, dtype=jnp.int32)
    start_root = 0.00085**0.5
    end_root = 0.012**0.5
    roots = start_root + (end_root - start_root) * steps_index.astype(jnp.float32) / 999.0
    return (steps_index, jnp.cumprod(1.0 - roots * roots))


def feature_norm(values, shifts, scaling):
    totals, squares = lax.psum(
        (jnp.sum(values, -1, keepdims=True), jnp.sum(values * values, -1, keepdims=True)), "narrow"
    )
    average = totals / D
    variance = squares / D - average * average
    return (values - average) * lax.rsqrt(variance + norm_eps) * (1.0 + scaling) + shifts


def any_slice(
    hidden, split_table, modulation, expand_weight, contract_weight, output_weight, latent, timestep
):
    capacity = hidden.shape[1]
    wide_index = lax.axis_index("wide")
    table_index = jnp.arange(split_table.shape[0], dtype=jnp.int32)
    offset = jnp.sum(jnp.where(table_index < wide_index, split_table, 0))
    own_count = jnp.sum(jnp.where(table_index == wide_index, split_table, 0))
    slot_index = jnp.arange(capacity, dtype=jnp.int32)
    position = offset + slot_index
    slot_live = slot_index < own_count
    is_text = slot_live & (position < TEXT)
    is_video = slot_live & (position >= TEXT)
    text_column = is_text[:, None]
    shifts = jnp.where(text_column, modulation[3], modulation[0])
    scaling = jnp.where(text_column, modulation[4], modulation[1])
    gating = jnp.where(text_column, modulation[5], modulation[2])
    values = hidden[0].astype(jnp.float32)
    normed = feature_norm(values, shifts, scaling).astype(jnp.bfloat16)
    hidden_part = jnp.dot(
        lax.all_gather(normed, "wide", axis=0, tiled=True),
        expand_weight,
        preferred_element_type=jnp.float32,
    )
    hidden_pre = lax.psum(hidden_part, "narrow")
    activated = jax.nn.gelu(hidden_pre, approximate=True).astype(jnp.bfloat16)
    ff_result = lax.psum_scatter(
        jnp.dot(activated, contract_weight, preferred_element_type=jnp.float32),
        "wide",
        scatter_dimension=0,
        tiled=True,
    )
    layer_out = jnp.where(slot_live[:, None], values + gating * ff_result, 0.0).astype(jnp.bfloat16)
    final_in = layer_out.astype(jnp.float32)
    final_normed = feature_norm(final_in, modulation[6], modulation[7]).astype(jnp.bfloat16)
    velocity_part = jnp.dot(final_normed, output_weight, preferred_element_type=jnp.float32)
    copy_weight = jnp.where(lax.axis_index("cfg") == 0, guidance, 1.0 - guidance)
    guided = lax.psum(velocity_part * copy_weight, ("cfg", "narrow"))
    steps_index, alpha_bar = alpha_table()
    alpha_now = jnp.sum(jnp.where(steps_index == timestep[0], alpha_bar, 0.0))
    clean_latent = jnp.where(
        is_video[:, None], jnp.sqrt(alpha_now) * latent - jnp.sqrt(1.0 - alpha_now) * guided, 0.0
    )
    return (layer_out[None], clean_latent)


QUOTAS = (0, 64, 128)
CAP = 128
CHUNKS = len(QUOTAS) - 1
F32, BF16 = jnp.float32, jnp.bfloat16
TILE = 512
LONG = 10**10


def size_of(k):
    return QUOTAS[k + 1] - QUOTAS[k]


def swap(array, axis, distance, size):
    return lax.ppermute(array, axis, [(i, i ^ distance) for i in range(size)])


def z_swaps(array):
    return [swap(array, "wide", s, 4) for s in (1, 2, 3)]


def choose(values, index):
    out = values[0]
    for i in range(1, 4):
        out = jnp.where(index == i, values[i], out)
    return out


def layout(table):
    counts = [table[b] for b in range(4)]
    largest = jnp.int32(3)
    for b in (2, 1, 0):
        largest = jnp.where(counts[b] == CAP, b, largest)
    starts, others, ranks, offsets = [], [], [], []
    rank, offset = jnp.int32(0), jnp.int32(0)
    for b in range(4):
        other = jnp.where(largest == b, 0, 1)
        ranks.append(rank * other)
        others.append(other)
        offsets.append(offset)
        rank = rank + other * counts[b]
        offset = offset + counts[b]
    block = lax.axis_index("wide")
    of = lambda values: [choose(values, jnp.bitwise_xor(block, s)) for s in range(4)]
    return of(ranks), of(counts), of(others), of(offsets)[0], choose(offsets, largest)


def high_low(values):
    high = values.astype(BF16)
    return high, (values - high.astype(F32)).astype(BF16)


def load(source, place, sems):
    parts = sems.shape[0]
    height = source.shape[0] // parts
    copies = []
    for t in range(parts):
        rows = pl.ds(t * height, height)
        copies.append(pltpu.make_async_copy(source.at[rows, :], place.at[rows, :], sems.at[t]))
        copies[-1].start()
    return copies


def load_half(source, half, place, sems):
    width = place.shape[1]
    copies = []
    for t in range(0, width, TILE):
        columns = pl.ds(pl.multiple_of(half * width + t, 128), TILE)
        copies.append(
            pltpu.make_async_copy(
                source.at[:, columns], place.at[:, pl.ds(t, TILE)], sems.at[len(copies)]
            )
        )
        copies[-1].start()
    return copies


def rows_of(parts, core):
    total = parts[:8] + parts[8:]
    total = jnp.where(core == 0, total, pltpu.roll(total, 4, 0))
    high, low = high_low(total)
    return jnp.concatenate([high.astype(F32), low.astype(F32)], 0).astype(BF16)


def hold_kernel(source, _, place, sems):
    for copy in load(source, place, sems):
        copy.wait()


def text_rows(k, largest_offset):
    size = size_of(k)
    row = lax.broadcasted_iota(jnp.int32, (2 * size, 1), 0)
    rank = jnp.where(row < size, row, row - size) + QUOTAS[k]
    position = jnp.where(
        row < size, rank + largest_offset, jnp.where(rank < largest_offset, rank, rank + CAP)
    )
    return position < TEXT


def gather_matrix(k, ranks, counts, others):
    size = size_of(k)
    places = []
    for p in range(k + 1):
        piece = size_of(p)
        lane = lax.broadcasted_iota(jnp.int32, (1, 4 * piece), 1)
        which, slot = lane // piece, lane % piece + QUOTAS[p]
        rank = slot + choose(ranks, which) - QUOTAS[k]
        live = (rank >= 0) & (rank < size) & (slot < choose(counts, which))
        row = jnp.where(live, rank + choose(others, which) * size, -1)
        at = lax.broadcasted_iota(jnp.int32, (2 * size, 4 * piece), 0)
        places.append(jnp.where(at == row, 1.0, 0.0).astype(BF16))
    return jnp.concatenate(places, 1)


def spread_matrix(k, ranks, counts, others):
    size = size_of(k)
    places = []
    for s in range(4):
        first = jnp.maximum(QUOTAS[k] - ranks[s], 0)
        last = jnp.minimum(counts[s], QUOTAS[k + 1] - ranks[s])
        index = lax.broadcasted_iota(jnp.int32, (size, 1), 0)
        slot = first + jnp.bitwise_and(index - first, size - 1)
        row = jnp.where(slot < last, slot + ranks[s] - QUOTAS[k] + others[s] * size, -1)
        at = lax.broadcasted_iota(jnp.int32, (size, 2 * size), 1)
        places.append(jnp.where(at == row, 1.0, 0.0).astype(BF16))
    return jnp.concatenate(places, 0)


def take_kernel(source, whole, piece, sems):
    copies = [
        pltpu.make_async_copy(source.at[pl.ds(0, piece.shape[0]), :], piece, sems.at[0]),
        pltpu.make_async_copy(source, whole, sems.at[1]),
    ]
    for copy in copies:
        copy.start()
    for copy in copies:
        copy.wait()


def prepare_kernel(table_in, tokens, mod_in, out_weight, w, *refs):
    later, refs = refs[: CHUNKS - 1], refs[CHUNKS - 1 :]
    gathers, refs = refs[:CHUNKS], refs[CHUNKS:]
    spreads, refs = refs[:CHUNKS], refs[CHUNKS:]
    texts, refs = refs[:CHUNKS], refs[CHUNKS:]
    held, kept, mod, weight, rows_out, ends_out, slots_out, video_out = refs[:8]
    table, sems, small = refs[8:]
    core = lax.axis_index("narrow") % 2
    sources = (table_in, mod_in, out_weight)
    copies = [
        pltpu.make_async_copy(source, place, small.at[i])
        for i, (source, place) in enumerate(zip(sources, (table, mod, weight)))
    ]
    for copy in copies:
        copy.start()
    big = load_half(w, 1 - core, held, sems.at[0]) + load_half(w, core, kept, sems.at[1])

    copies[0].wait()
    ranks, counts, others, offset, largest_offset = layout(table)
    for k in range(CHUNKS):
        gathers[k][...] = gather_matrix(k, ranks, counts, others)
        spreads[k][...] = spread_matrix(k, ranks, counts, others)
        text = jnp.where(text_rows(k, largest_offset), 1.0, 0.0)
        texts[k][...] = jnp.broadcast_to(text, texts[k].shape)
    slot = lax.broadcasted_iota(jnp.int32, (CAP, 128), 0)
    lane = lax.broadcasted_iota(jnp.int32, (CAP, 128), 1)
    rank = slot + ranks[0]
    flag = lambda condition: jnp.where(condition, 1.0, 0.0)
    kind = jnp.where(lane == 0, flag(slot < counts[0]), flag(slot + offset < TEXT))
    for k in range(CHUNKS):
        kind = jnp.where(
            lane == 2 + k, flag((rank >= QUOTAS[k]) & (rank < QUOTAS[k + 1])), kind
        )
    slots_out[...] = kind
    slot = lax.broadcasted_iota(jnp.int32, (8, CAP), 1)
    video_out[...] = jnp.where((slot < counts[0]) & (slot + offset >= TEXT), 1.0, 0.0)

    copies[1].wait()
    row = lax.broadcasted_iota(jnp.int32, (8, 1), 0)
    rows = jnp.where(row == 0, 1.0 + mod[1:2, :], jnp.zeros((8, 1), F32))
    rows = jnp.where(row == 1, 1.0 + mod[4:5, :], rows)
    rows = jnp.where(row == 2, mod[0:1, :], rows)
    rows = jnp.where(row == 3, mod[3:4, :], rows)
    rows_out[...] = jnp.concatenate(high_low(rows), 0)
    rows = jnp.where(row == 0, 1.0 + mod[7:8, :], jnp.zeros((8, 1), F32))
    rows = jnp.where(row == 1, mod[6:7, :], rows)
    copies[2].wait()
    ends = lax.dot_general(
        jnp.concatenate(high_low(rows), 0),
        weight[...],
        (((1,), (1,)), ((), ())),
        preferred_element_type=F32,
    )
    ends = rows_of(ends, core)
    ends_out[...] = jnp.concatenate([ends, jnp.zeros((16, 128 - ends.shape[1]), BF16)], 1)
    for k in range(1, CHUNKS):
        later[k - 1][...] = tokens[QUOTAS[k] : QUOTAS[k + 1], :]
    for copy in big:
        copy.wait()


def expand_sent_kernel(k, text, mod, place, own, near, *refs):
    far, (w, sums, ends) = refs[: 2 * (k + 1)], refs[2 * (k + 1) : 2 * (k + 1) + 3]
    z_out, sent_out, side_out = refs[-3:]
    core = lax.axis_index("narrow") % 2
    units = w.shape[1]
    rows = side_out.shape[0]
    pieces = []
    for p in range(k + 1):
        of_chunk = slice(QUOTAS[p], QUOTAS[p + 1])
        pieces += [own[of_chunk, :], near[of_chunk, :], far[2 * p][...], far[2 * p + 1][...]]
    tokens = jnp.concatenate(pieces, 0)
    x = jnp.dot(place[...], tokens, preferred_element_type=F32)
    centre = (jnp.sum(x, -1, keepdims=True) / x.shape[1]).astype(BF16).astype(F32)
    x = x - centre
    z = (x * (1.0 + jnp.where(text[:, :1] > 0.5, mod[4:5, :], mod[1:2, :]))).astype(BF16)
    if k == 0:
        z = jnp.concatenate([z, sums[...]], 0)
    z_out[...] = z
    for t in range(0, units, TILE):
        product = jnp.dot(z, w[:, t : t + TILE], preferred_element_type=F32)
        sent_out[:rows, t : t + TILE] = product[:rows].astype(BF16)
        if k == 0:
            sent_out[rows:, t : t + TILE] = rows_of(product[rows:], core)
    total = jnp.sum(x, -1, keepdims=True)
    square = jnp.sum(x * x, -1, keepdims=True)
    total_high = total.astype(BF16).astype(F32)
    square_high = square.astype(BF16).astype(F32)
    lane = lax.broadcasted_iota(jnp.int32, (rows, 128), 1) - 4 * core
    side = jnp.where((lane == 0) | (lane == 1), centre, 0.0)
    side = jnp.where(lane == 16, total_high, side)
    side = jnp.where(lane == 17, total - total_high, side)
    side = jnp.where(lane == 18, square_high, side)
    side = jnp.where(lane == 19, square - square_high, side).astype(BF16)
    side_out[...] = side
    sent_out[:rows, units:] = side
    if k == 0:
        sent_out[rows:, units:] = ends[...]


def expand_kept_kernel(k, z, w, _, *refs):
    kept_out = refs[-1 if k else -2]
    core = lax.axis_index("narrow") % 2
    rows = kept_out.shape[0]
    for t in range(0, w.shape[1], TILE):
        columns = slice(t, t + TILE)
        product = jnp.dot(z[...], w[:, columns], preferred_element_type=F32)
        kept_out[:, columns] = product[:rows]
        if k == 0:
            refs[-1][:, columns] = rows_of(product[rows:], core)


def pass_kernel(piece, _, out):
    out[...] = piece[...]


def merge_kernel(k, kept, side, came, sums, ends, total_out, sent_out):
    rows, units = kept.shape
    add = lambda left, right: (left[...].astype(F32) + right.astype(F32)).astype(BF16)
    total = kept[...] + came[:rows, :units].astype(F32)
    total_out[...] = total
    sent_out[:rows, :units] = total.astype(BF16)
    sent_out[:rows, units:] = add(side, came[:rows, units:])
    if k == 0:
        sent_out[rows:, :units] = add(sums, came[rows:, :units])
        sent_out[rows:, units:] = add(ends, came[rows:, units:])


def activate_kernel(features, text, total, sent, came, first_sent, first_came, *refs):
    act_out = refs[-1]
    rows, units = total.shape
    sides = [sent[:rows, units:].astype(F32), came[:rows, units:].astype(F32)]
    lane = lax.broadcasted_iota(jnp.int32, (rows, 128), 1)
    field = lane % 4
    summed = sides[0] + sides[1]
    add = lambda values, mask: jnp.sum(jnp.where(mask, values, 0.0), -1, keepdims=True)
    centres, measures = lane < 8, (lane >= 16) & (lane < 24)
    average = (
        add(summed, centres & (field == 0)) * features + add(summed, measures & (field < 2))
    ) / D
    spread = add(summed, measures & (field >= 2))
    aparts = []
    for side in sides:
        apart = jnp.where(centres, side - average, 0.0)
        for core in range(2):
            off = add(apart, lane == 4 * core)
            own = lane // 4 == 4 + core
            spread = spread + off * (2.0 * add(side, own & (field < 2)) + features * off)
        aparts.append(apart)
    scale = lax.rsqrt(spread / D + norm_eps)
    of_text = jnp.where(text[...] > 0.5, 1, 0)
    mine = centres & (lane % 2 == of_text)
    packed, shift = None, 0
    for apart in aparts:
        factor = jnp.where(mine, jnp.where(field < 2, apart * scale, 1.0), 0.0)
        high = factor.astype(BF16).astype(F32)
        for part in (high, high, factor - high, factor - high):
            part = pltpu.roll(part, shift, 1) if shift else part
            packed = part if packed is None else packed + part
            shift += 8
    packed = packed[:, :64].astype(BF16)
    own, other = first_sent[-16:, :units], first_came[-16:, :units]
    factors = jnp.concatenate([own, own, other, other], 0)
    for t in range(0, units, TILE):
        columns = slice(t, t + TILE)
        pre = total[:, columns] + came[:rows, columns].astype(F32)
        extra = jnp.dot(packed, factors[:, columns], preferred_element_type=F32)
        act_out[:, columns] = jax.nn.gelu(pre * scale + extra, approximate=True).astype(BF16)


def contract_own_kernel(k, act, w, mine, first_sent, first_came, out, *ends_out):
    core = lax.axis_index("narrow") % 2
    units = w.shape[0] // 2
    rows = pl.ds(pl.multiple_of(core * units, 128), units)
    out[...] = jnp.dot(act[...], w[rows, :], preferred_element_type=F32)
    if k == 0:
        total = first_sent[-16:, units:].astype(F32) + first_came[-16:, units:].astype(F32)
        total = total[:8] + total[8:]
        total = total + pltpu.roll(total, 4, 0)
        own = mine[...].astype(F32)
        own = own[:8] + own[8:]
        own = own + pltpu.roll(own, 4, 0)
        ends_out[0][...] = jnp.concatenate([total, own, jnp.zeros((112, 128), F32)], 0).T


def contract_other_kernel(k, place, act, so_far, w, *outs):
    core = lax.axis_index("narrow") % 2
    units = w.shape[0] // 2
    rows = pl.ds(pl.multiple_of((1 - core) * units, 128), units)
    total = so_far[...] + jnp.dot(act[...], w[rows, :], preferred_element_type=F32)
    spread = jnp.dot(place[...], total.astype(BF16), preferred_element_type=F32).astype(BF16)
    size = size_of(k)
    for s in range(4):
        outs[s][...] = spread[s * size : (s + 1) * size]


def finish_kernel(slots, hidden, mod, out_weight, ends, *refs):
    pieces, (layer_out, bundle_out) = refs[: 4 * CHUNKS], refs[4 * CHUNKS :]
    result = jnp.zeros(hidden.shape, F32)
    for k in range(CHUNKS):
        total = pieces[4 * k][...].astype(F32)
        for s in (1, 2, 3):
            total = total + pieces[4 * k + s][...].astype(F32)
        total = jnp.concatenate([total] * (CAP // size_of(k)), 0)
        result = jnp.where(slots[:, 2 + k : 3 + k] > 0.5, total, result)
    gate = jnp.where(slots[:, 1:2] > 0.5, mod[5:6, :], mod[2:3, :])
    layer = hidden[...].astype(F32) + gate * result
    layer = jnp.where(slots[:, 0:1] > 0.5, layer, 0.0).astype(BF16)
    layer_out[...] = layer
    x = layer.astype(F32)
    centre = jnp.sum(x, -1, keepdims=True) / x.shape[1]
    ones = jnp.ones((8, x.shape[1]), BF16)
    across = lambda left, right: lax.dot_general(
        left, right, (((1,), (1,)), ((), ())), preferred_element_type=F32
    )
    high, low = high_low(x * x)
    total, square = across(ones, layer), across(ones, high) + across(ones, low)
    width = out_weight.shape[0]
    product = across(out_weight[...], ((x - centre) * (1.0 + mod[7:8, :])).astype(BF16))
    bundle_out[:width, :] = product + total[0:1] / x.shape[1] * ends[:width, 8:9]
    row = lax.broadcasted_iota(jnp.int32, (8, CAP), 0)
    bundle_out[width:, :] = jnp.where(row == 0, total, square)


def write_kernel(layer, out):
    out[...] = layer[...]


def add_kernel(left, right, out):
    out[...] = left[...] + right[...]


def noise_kernel(timestep, alphas, video, latent, base_out, factor_out):
    index = lax.broadcasted_iota(jnp.int32, (8, 128), 0) * 128 + lax.broadcasted_iota(
        jnp.int32, (8, 128), 1
    )
    alpha = jnp.sum(
        jnp.sum(jnp.where(index == timestep[0], alphas[...], 0.0), 0, keepdims=True),
        1,
        keepdims=True,
    )
    base_out[...] = jnp.where(video[0:1] > 0.5, jnp.sqrt(alpha) * latent[...], 0.0)
    factor_out[...] = jnp.where(video[...] > 0.5, jnp.sqrt(1.0 - alpha), 0.0)


def latent_kernel(base, factor, ends, mine, mine_y, other, other_y, out):
    width = out.shape[0]

    def velocity(total):
        average = total[width : width + 1] / D
        variance = total[width + 1 : width + 2] / D - average * average
        return (total[:width] - average * ends[:width, 0:1]) * lax.rsqrt(
            variance + norm_eps
        ) + ends[:width, 1:2]

    first = lax.axis_index("cfg") == 0
    guided = velocity(mine[...] + mine_y[...]) * jnp.where(first, guidance, 1.0 - guidance)
    guided = guided + velocity(other[...] + other_y[...]) * jnp.where(
        first, 1.0 - guidance, guidance
    )
    guided = jnp.where(factor[0:1] > 0.0, guided, 0.0)
    out[...] = base[...] - factor[0:1] * guided


def alpha_constant():
    ends = np.sqrt(np.float64(0.00085)), np.sqrt(np.float64(0.012))
    betas = np.linspace(ends[0], ends[1], 1000, dtype=np.float64) ** 2
    return np.pad(np.cumprod(1.0 - betas), (0, 24)).astype(np.float32).reshape(8, 128)


def call(kernel, outs, args, spaces, scratch=(), weight=1):
    kinds = {"v": pltpu.VMEM, "s": pltpu.SMEM, "a": pl.ANY}
    return pl.pallas_call(
        kernel,
        out_shape=[jax.ShapeDtypeStruct(shape, dtype) for shape, dtype in outs],
        in_specs=[pl.BlockSpec(memory_space=kinds[letter]) for letter in spaces],
        out_specs=[pl.BlockSpec(memory_space=pltpu.VMEM) for _ in outs],
        scratch_shapes=list(scratch),
        compiler_params=pltpu.CompilerParams(vmem_limit_bytes=24 * 2**20),
        cost_estimate=pl.CostEstimate(flops=weight, bytes_accessed=1, transcendentals=0),
    )(*args)


def four_blocks(
    hidden, split_table, modulation, expand_weight, contract_weight, output_weight, latent, timestep
):
    hidden = hidden[0]
    features = hidden.shape[1]
    units = expand_weight.shape[1] // 2
    width = output_weight.shape[1]
    payload = units + 128

    in_place = lambda array: pltpu.with_memory_space_constraint(array, pltpu.HBM)
    tokens, piece = call(
        take_kernel,
        [(hidden.shape, BF16), ((QUOTAS[1], features), BF16)],
        [in_place(hidden)],
        "a",
        [pltpu.SemaphoreType.DMA((2,))],
    )
    across = swap(piece, "wide", 2, 4)
    near = swap(tokens, "wide", 1, 4)

    tiles = units // TILE
    chunks = range(CHUNKS)
    made = call(
        prepare_kernel,
        [((size_of(k), features), BF16) for k in chunks[1:]]
        + [((2 * size_of(k), 4 * QUOTAS[k + 1]), BF16) for k in chunks]
        + [((4 * size_of(k), 2 * size_of(k)), BF16) for k in chunks]
        + [((2 * size_of(k), 128), F32) for k in chunks]
        + [
            ((features, units), BF16),
            ((features, units), BF16),
            (modulation.shape, F32),
            ((width, features), BF16),
            ((16, features), BF16),
            ((16, 128), BF16),
            ((CAP, 128), F32),
            ((8, CAP), F32),
        ],
        [
            in_place(split_table),
            tokens,
            in_place(modulation),
            in_place(output_weight.T),
            in_place(expand_weight),
        ],
        "avaaa",
        [
            pltpu.SMEM(split_table.shape, jnp.int32),
            pltpu.SemaphoreType.DMA((2, tiles)),
            pltpu.SemaphoreType.DMA((3,)),
        ],
    )
    later, made = made[: CHUNKS - 1], made[CHUNKS - 1 :]
    gathers, made = made[:CHUNKS], made[CHUNKS:]
    spreads, made = made[:CHUNKS], made[CHUNKS:]
    texts, made = made[:CHUNKS], made[CHUNKS:]
    held_sent, held_kept, mod, out_weight, rows_in, ends_mine, slots, video = made
    later = [swap(piece, "wide", 2, 4) for piece in later]
    (across,) = call(pass_kernel, [(across.shape, BF16)], [across, slots], "va")
    far = [across, swap(across, "wide", 1, 4)]

    merged = []
    before = []
    for k in chunks:
        rows = 2 * size_of(k)
        sent_rows = rows + (16 if k == 0 else 0)
        z, sent, side = call(
            functools.partial(expand_sent_kernel, k),
            [((sent_rows, features), BF16), ((sent_rows, payload), BF16), ((rows, 128), BF16)],
            [texts[k], mod, gathers[k], tokens, near, *far, held_sent, rows_in, ends_mine, *before],
            "vvvvv" + "v" * len(far) + "vvv" + "a" * len(before),
            weight=LONG,
        )
        came = swap(sent, "narrow", 1, 4)
        kept, *sums_made = call(
            functools.partial(expand_kept_kernel, k),
            [((rows, units), F32)] + ([((16, units), BF16)] if k == 0 else []),
            [z, held_kept, sent],
            "vva",
            weight=LONG if k == 0 else 1,
        )
        sums = sums_made[0] if k == 0 else sums
        total, sent = call(
            functools.partial(merge_kernel, k),
            [((rows, units), F32), ((sent_rows, payload), BF16)],
            [kept, side, came, sums, ends_mine],
            "vvvvv",
        )
        if k == 0:
            (held_out,) = call(
                hold_kernel,
                [(contract_weight.shape, BF16)],
                [in_place(contract_weight), sent],
                "aa",
                [pltpu.SemaphoreType.DMA((4,))],
                weight=LONG,
            )
        if k + 1 < CHUNKS:
            (across,) = call(
                pass_kernel, [(later[k].shape, BF16)], [later[k], sent], "va"
            )
            far.extend([across, swap(across, "wide", 1, 4)])
        before = [sent, held_out]
        merged.append((total, sent, swap(sent, "narrow", 2, 4)))

    returned = []
    before = []
    first = merged[0][1:]
    for k in chunks:
        rows = 2 * size_of(k)
        total, sent, came = merged[k]
        if k + 1 < CHUNKS:
            before = before + [merged[k + 1][1]]
        (act,) = call(
            functools.partial(activate_kernel, features),
            [((rows, units), BF16)],
            [texts[k], total, sent, came, *first, *before],
            "vvvvvv" + "a" * len(before),
        )
        act_came = swap(act, "narrow", 1, 4)
        out, *ends_made = call(
            functools.partial(contract_own_kernel, k),
            [((rows, features), F32)] + ([((128, 128), F32)] if k == 0 else []),
            [act, held_out, ends_mine, *first],
            "vvvvv",
            weight=LONG,
        )
        ends = ends_made[0] if k == 0 else ends
        pieces = call(
            functools.partial(contract_other_kernel, k),
            [((size_of(k), features), BF16)] * 4,
            [spreads[k], act_came, out, held_out],
            "vvvv",
        )
        before = pieces
        returned.append(pieces[0])
        returned.extend(swap(pieces[s], "wide", s, 4) for s in (1, 2, 3))

    layer, bundle = call(
        finish_kernel,
        [((CAP, features), BF16), ((width + 8, CAP), F32)],
        [slots, tokens, mod, out_weight, ends, *returned],
        "v" * (5 + len(returned)),
    )
    (layer_out,) = call(write_kernel, [((CAP, features), BF16)], [layer], "v", weight=LONG)
    (bundle,) = call(
        add_kernel, [((width + 8, CAP), F32)], [bundle, swap(bundle, "narrow", 1, 4)], "vv"
    )
    base, factor = call(
        noise_kernel,
        [((width, CAP), F32), ((8, CAP), F32)],
        [timestep, alpha_constant(), video, latent.T],
        "svvv",
        weight=LONG,
    )
    (clean_latent,) = call(
        latent_kernel,
        [((width, CAP), F32)],
        [base, factor, ends, bundle] + [swap(bundle, ("cfg", "narrow"), n, 8) for n in (2, 4, 6)],
        "vvvvvvv",
    )
    return (layer_out[None], clean_latent.T)


def solution(mesh):
    by_swaps = (mesh.shape["wide"], mesh.shape["narrow"], mesh.shape["cfg"]) == (4, 4, 2)
    return jax.shard_map(
        four_blocks if by_swaps else any_slice,
        mesh=mesh,
        in_specs=(
            P("cfg", "wide", "narrow"),
            P(),
            P(None, "narrow"),
            P("narrow", "wide"),
            P("wide", "narrow"),
            P("narrow", None),
            P("wide", None),
            P(),
        ),
        out_specs=(P("cfg", "wide", "narrow"), P("wide", None)),
        check_vma=False,
    )
```

```python
import functools

import jax
import jax.numpy as jnp
import numpy as np
from jax import lax
from jax.experimental import pallas as pl
from jax.experimental.pallas import tpu as pltpu
from jax.sharding import PartitionSpec as P

D = 3072
TEXT = 226


norm_eps = 1e-05
guidance = 6.0


def alpha_table():
    steps_index = jnp.arange(1000, dtype=jnp.int32)
    start_root = 0.00085**0.5
    end_root = 0.012**0.5
    roots = start_root + (end_root - start_root) * steps_index.astype(jnp.float32) / 999.0
    return (steps_index, jnp.cumprod(1.0 - roots * roots))


def feature_norm(values, shifts, scaling):
    totals, squares = lax.psum(
        (jnp.sum(values, -1, keepdims=True), jnp.sum(values * values, -1, keepdims=True)), "narrow"
    )
    average = totals / D
    variance = squares / D - average * average
    return (values - average) * lax.rsqrt(variance + norm_eps) * (1.0 + scaling) + shifts


def any_slice(
    hidden, split_table, modulation, expand_weight, contract_weight, output_weight, latent, timestep
):
    capacity = hidden.shape[1]
    wide_index = lax.axis_index("wide")
    table_index = jnp.arange(split_table.shape[0], dtype=jnp.int32)
    offset = jnp.sum(jnp.where(table_index < wide_index, split_table, 0))
    own_count = jnp.sum(jnp.where(table_index == wide_index, split_table, 0))
    slot_index = jnp.arange(capacity, dtype=jnp.int32)
    position = offset + slot_index
    slot_live = slot_index < own_count
    is_text = slot_live & (position < TEXT)
    is_video = slot_live & (position >= TEXT)
    text_column = is_text[:, None]
    shifts = jnp.where(text_column, modulation[3], modulation[0])
    scaling = jnp.where(text_column, modulation[4], modulation[1])
    gating = jnp.where(text_column, modulation[5], modulation[2])
    values = hidden[0].astype(jnp.float32)
    normed = feature_norm(values, shifts, scaling).astype(jnp.bfloat16)
    hidden_part = jnp.dot(
        lax.all_gather(normed, "wide", axis=0, tiled=True),
        expand_weight,
        preferred_element_type=jnp.float32,
    )
    hidden_pre = lax.psum(hidden_part, "narrow")
    activated = jax.nn.gelu(hidden_pre, approximate=True).astype(jnp.bfloat16)
    ff_result = lax.psum_scatter(
        jnp.dot(activated, contract_weight, preferred_element_type=jnp.float32),
        "wide",
        scatter_dimension=0,
        tiled=True,
    )
    layer_out = jnp.where(slot_live[:, None], values + gating * ff_result, 0.0).astype(jnp.bfloat16)
    final_in = layer_out.astype(jnp.float32)
    final_normed = feature_norm(final_in, modulation[6], modulation[7]).astype(jnp.bfloat16)
    velocity_part = jnp.dot(final_normed, output_weight, preferred_element_type=jnp.float32)
    copy_weight = jnp.where(lax.axis_index("cfg") == 0, guidance, 1.0 - guidance)
    guided = lax.psum(velocity_part * copy_weight, ("cfg", "narrow"))
    steps_index, alpha_bar = alpha_table()
    alpha_now = jnp.sum(jnp.where(steps_index == timestep[0], alpha_bar, 0.0))
    clean_latent = jnp.where(
        is_video[:, None], jnp.sqrt(alpha_now) * latent - jnp.sqrt(1.0 - alpha_now) * guided, 0.0
    )
    return (layer_out[None], clean_latent)


QUOTAS = (0, 64, 128)
CAP = 128
CHUNKS = len(QUOTAS) - 1
F32, BF16 = jnp.float32, jnp.bfloat16
TILE = 512
LONG = 10**10


def size_of(k):
    return QUOTAS[k + 1] - QUOTAS[k]


def swap(array, axis, distance, size):
    return lax.ppermute(array, axis, [(i, i ^ distance) for i in range(size)])


def z_swaps(array):
    return [swap(array, "wide", s, 4) for s in (1, 2, 3)]


def choose(values, index):
    out = values[0]
    for i in range(1, 4):
        out = jnp.where(index == i, values[i], out)
    return out


def layout(table):
    counts = [table[b] for b in range(4)]
    largest = jnp.int32(3)
    for b in (2, 1, 0):
        largest = jnp.where(counts[b] == CAP, b, largest)
    starts, others, ranks, offsets = [], [], [], []
    rank, offset = jnp.int32(0), jnp.int32(0)
    for b in range(4):
        other = jnp.where(largest == b, 0, 1)
        ranks.append(rank * other)
        others.append(other)
        offsets.append(offset)
        rank = rank + other * counts[b]
        offset = offset + counts[b]
    block = lax.axis_index("wide")
    of = lambda values: [choose(values, jnp.bitwise_xor(block, s)) for s in range(4)]
    return of(ranks), of(counts), of(others), of(offsets)[0], choose(offsets, largest)


def high_low(values):
    high = values.astype(BF16)
    return high, (values - high.astype(F32)).astype(BF16)


def load(source, place, sems):
    parts = sems.shape[0]
    height = source.shape[0] // parts
    copies = []
    for t in range(parts):
        rows = pl.ds(t * height, height)
        copies.append(pltpu.make_async_copy(source.at[rows, :], place.at[rows, :], sems.at[t]))
        copies[-1].start()
    return copies


def load_half(source, half, place, sems):
    width = place.shape[1]
    copies = []
    for t in range(0, width, TILE):
        columns = pl.ds(pl.multiple_of(half * width + t, 128), TILE)
        copies.append(
            pltpu.make_async_copy(
                source.at[:, columns], place.at[:, pl.ds(t, TILE)], sems.at[len(copies)]
            )
        )
        copies[-1].start()
    return copies


def rows_of(parts, core):
    total = parts[:8] + parts[8:]
    total = jnp.where(core == 0, total, pltpu.roll(total, 4, 0))
    high, low = high_low(total)
    return jnp.concatenate([high.astype(F32), low.astype(F32)], 0).astype(BF16)


def hold_kernel(source, _, place, sems):
    for copy in load(source, place, sems):
        copy.wait()


def text_rows(k, largest_offset):
    size = size_of(k)
    row = lax.broadcasted_iota(jnp.int32, (2 * size, 1), 0)
    rank = jnp.where(row < size, row, row - size) + QUOTAS[k]
    position = jnp.where(
        row < size, rank + largest_offset, jnp.where(rank < largest_offset, rank, rank + CAP)
    )
    return position < TEXT


def gather_matrix(k, ranks, counts, others):
    size = size_of(k)
    places = []
    for p in range(k + 1):
        piece = size_of(p)
        lane = lax.broadcasted_iota(jnp.int32, (1, 4 * piece), 1)
        which, slot = lane // piece, lane % piece + QUOTAS[p]
        rank = slot + choose(ranks, which) - QUOTAS[k]
        live = (rank >= 0) & (rank < size) & (slot < choose(counts, which))
        row = jnp.where(live, rank + choose(others, which) * size, -1)
        at = lax.broadcasted_iota(jnp.int32, (2 * size, 4 * piece), 0)
        places.append(jnp.where(at == row, 1.0, 0.0).astype(BF16))
    return jnp.concatenate(places, 1)


def spread_matrix(k, ranks, counts, others):
    size = size_of(k)
    places = []
    for s in range(4):
        first = jnp.maximum(QUOTAS[k] - ranks[s], 0)
        last = jnp.minimum(counts[s], QUOTAS[k + 1] - ranks[s])
        index = lax.broadcasted_iota(jnp.int32, (size, 1), 0)
        slot = first + jnp.bitwise_and(index - first, size - 1)
        row = jnp.where(slot < last, slot + ranks[s] - QUOTAS[k] + others[s] * size, -1)
        at = lax.broadcasted_iota(jnp.int32, (size, 2 * size), 1)
        places.append(jnp.where(at == row, 1.0, 0.0).astype(BF16))
    return jnp.concatenate(places, 0)


def take_kernel(source, whole, piece, sems):
    copies = [
        pltpu.make_async_copy(source.at[pl.ds(0, piece.shape[0]), :], piece, sems.at[0]),
        pltpu.make_async_copy(source, whole, sems.at[1]),
    ]
    for copy in copies:
        copy.start()
    for copy in copies:
        copy.wait()


def prepare_kernel(table_in, tokens, mod_in, out_weight, w, *refs):
    later, refs = refs[: CHUNKS - 1], refs[CHUNKS - 1 :]
    gathers, refs = refs[:CHUNKS], refs[CHUNKS:]
    spreads, refs = refs[:CHUNKS], refs[CHUNKS:]
    texts, refs = refs[:CHUNKS], refs[CHUNKS:]
    held, kept, mod, weight, rows_out, ends_out, slots_out, video_out = refs[:8]
    table, sems, small = refs[8:]
    core = lax.axis_index("narrow") % 2
    sources = (table_in, mod_in, out_weight)
    copies = [
        pltpu.make_async_copy(source, place, small.at[i])
        for i, (source, place) in enumerate(zip(sources, (table, mod, weight)))
    ]
    for copy in copies:
        copy.start()
    big = load_half(w, 1 - core, held, sems.at[0]) + load_half(w, core, kept, sems.at[1])

    copies[0].wait()
    ranks, counts, others, offset, largest_offset = layout(table)
    for k in range(CHUNKS):
        gathers[k][...] = gather_matrix(k, ranks, counts, others)
        spreads[k][...] = spread_matrix(k, ranks, counts, others)
        text = jnp.where(text_rows(k, largest_offset), 1.0, 0.0)
        texts[k][...] = jnp.broadcast_to(text, texts[k].shape)
    slot = lax.broadcasted_iota(jnp.int32, (CAP, 128), 0)
    lane = lax.broadcasted_iota(jnp.int32, (CAP, 128), 1)
    rank = slot + ranks[0]
    flag = lambda condition: jnp.where(condition, 1.0, 0.0)
    kind = jnp.where(lane == 0, flag(slot < counts[0]), flag(slot + offset < TEXT))
    for k in range(CHUNKS):
        kind = jnp.where(
            lane == 2 + k, flag((rank >= QUOTAS[k]) & (rank < QUOTAS[k + 1])), kind
        )
    slots_out[...] = kind
    slot = lax.broadcasted_iota(jnp.int32, (8, CAP), 1)
    video_out[...] = jnp.where((slot < counts[0]) & (slot + offset >= TEXT), 1.0, 0.0)

    copies[1].wait()
    row = lax.broadcasted_iota(jnp.int32, (8, 1), 0)
    rows = jnp.where(row == 0, 1.0 + mod[1:2, :], jnp.zeros((8, 1), F32))
    rows = jnp.where(row == 1, 1.0 + mod[4:5, :], rows)
    rows = jnp.where(row == 2, mod[0:1, :], rows)
    rows = jnp.where(row == 3, mod[3:4, :], rows)
    rows_out[...] = jnp.concatenate(high_low(rows), 0)
    rows = jnp.where(row == 0, 1.0 + mod[7:8, :], jnp.zeros((8, 1), F32))
    rows = jnp.where(row == 1, mod[6:7, :], rows)
    copies[2].wait()
    ends = lax.dot_general(
        jnp.concatenate(high_low(rows), 0),
        weight[...],
        (((1,), (1,)), ((), ())),
        preferred_element_type=F32,
    )
    ends = rows_of(ends, core)
    ends_out[...] = jnp.concatenate([ends, jnp.zeros((16, 128 - ends.shape[1]), BF16)], 1)
    for k in range(1, CHUNKS):
        later[k - 1][...] = tokens[QUOTAS[k] : QUOTAS[k + 1], :]
    for copy in big:
        copy.wait()


def expand_sent_kernel(k, text, mod, place, own, near, *refs):
    far, (w, sums, ends) = refs[: 2 * (k + 1)], refs[2 * (k + 1) : 2 * (k + 1) + 3]
    z_out, sent_out, side_out = refs[-3:]
    core = lax.axis_index("narrow") % 2
    units = w.shape[1]
    rows = side_out.shape[0]
    pieces = []
    for p in range(k + 1):
        of_chunk = slice(QUOTAS[p], QUOTAS[p + 1])
        pieces += [own[of_chunk, :], near[of_chunk, :], far[2 * p][...], far[2 * p + 1][...]]
    tokens = jnp.concatenate(pieces, 0)
    x = jnp.dot(place[...], tokens, preferred_element_type=F32)
    centre = (jnp.sum(x, -1, keepdims=True) / x.shape[1]).astype(BF16).astype(F32)
    x = x - centre
    z = (x * (1.0 + jnp.where(text[:, :1] > 0.5, mod[4:5, :], mod[1:2, :]))).astype(BF16)
    if k == 0:
        z = jnp.concatenate([z, sums[...]], 0)
    z_out[...] = z
    for t in range(0, units, TILE):
        product = jnp.dot(z, w[:, t : t + TILE], preferred_element_type=F32)
        sent_out[:rows, t : t + TILE] = product[:rows].astype(BF16)
        if k == 0:
            sent_out[rows:, t : t + TILE] = rows_of(product[rows:], core)
    total = jnp.sum(x, -1, keepdims=True)
    square = jnp.sum(x * x, -1, keepdims=True)
    total_high = total.astype(BF16).astype(F32)
    square_high = square.astype(BF16).astype(F32)
    lane = lax.broadcasted_iota(jnp.int32, (rows, 128), 1) - 4 * core
    side = jnp.where((lane == 0) | (lane == 1), centre, 0.0)
    side = jnp.where(lane == 16, total_high, side)
    side = jnp.where(lane == 17, total - total_high, side)
    side = jnp.where(lane == 18, square_high, side)
    side = jnp.where(lane == 19, square - square_high, side).astype(BF16)
    side_out[...] = side
    sent_out[:rows, units:] = side
    if k == 0:
        sent_out[rows:, units:] = ends[...]


def expand_kept_kernel(k, z, w, _, *refs):
    kept_out = refs[-1 if k else -2]
    core = lax.axis_index("narrow") % 2
    rows = kept_out.shape[0]
    for t in range(0, w.shape[1], TILE):
        columns = slice(t, t + TILE)
        product = jnp.dot(z[...], w[:, columns], preferred_element_type=F32)
        kept_out[:, columns] = product[:rows]
        if k == 0:
            refs[-1][:, columns] = rows_of(product[rows:], core)


def pass_kernel(piece, _, out):
    out[...] = piece[...]


def merge_kernel(k, kept, side, came, sums, ends, *refs):
    total_out, sent_out = refs[-2:]
    rows, units = kept.shape
    add = lambda left, right: (left[...].astype(F32) + right.astype(F32)).astype(BF16)
    total = kept[...] + came[:rows, :units].astype(F32)
    total_out[...] = total
    sent_out[:rows, :units] = total.astype(BF16)
    sent_out[:rows, units:] = add(side, came[:rows, units:])
    if k == 0:
        sent_out[rows:, :units] = add(sums, came[rows:, :units])
        sent_out[rows:, units:] = add(ends, came[rows:, units:])


def activate_kernel(features, text, total, sent, came, first_sent, first_came, *refs):
    act_out = refs[-1]
    rows, units = total.shape
    sides = [sent[:rows, units:].astype(F32), came[:rows, units:].astype(F32)]
    lane = lax.broadcasted_iota(jnp.int32, (rows, 128), 1)
    field = lane % 4
    summed = sides[0] + sides[1]
    add = lambda values, mask: jnp.sum(jnp.where(mask, values, 0.0), -1, keepdims=True)
    centres, measures = lane < 8, (lane >= 16) & (lane < 24)
    average = (
        add(summed, centres & (field == 0)) * features + add(summed, measures & (field < 2))
    ) / D
    spread = add(summed, measures & (field >= 2))
    aparts = []
    for side in sides:
        apart = jnp.where(centres, side - average, 0.0)
        for core in range(2):
            off = add(apart, lane == 4 * core)
            own = lane // 4 == 4 + core
            spread = spread + off * (2.0 * add(side, own & (field < 2)) + features * off)
        aparts.append(apart)
    scale = lax.rsqrt(spread / D + norm_eps)
    of_text = jnp.where(text[...] > 0.5, 1, 0)
    mine = centres & (lane % 2 == of_text)
    packed, shift = None, 0
    for apart in aparts:
        factor = jnp.where(mine, jnp.where(field < 2, apart * scale, 1.0), 0.0)
        high = factor.astype(BF16).astype(F32)
        for part in (high, high, factor - high, factor - high):
            part = pltpu.roll(part, shift, 1) if shift else part
            packed = part if packed is None else packed + part
            shift += 8
    packed = packed[:, :64].astype(BF16)
    own, other = first_sent[-16:, :units], first_came[-16:, :units]
    factors = jnp.concatenate([own, own, other, other], 0)
    for t in range(0, units, TILE):
        columns = slice(t, t + TILE)
        pre = total[:, columns] + came[:rows, columns].astype(F32)
        extra = jnp.dot(packed, factors[:, columns], preferred_element_type=F32)
        act_out[:, columns] = jax.nn.gelu(pre * scale + extra, approximate=True).astype(BF16)


def contract_own_kernel(k, act, w, mine, first_sent, first_came, out, *ends_out):
    core = lax.axis_index("narrow") % 2
    units = w.shape[0] // 2
    rows = pl.ds(pl.multiple_of(core * units, 128), units)
    out[...] = jnp.dot(act[...], w[rows, :], preferred_element_type=F32)
    if k == 0:
        total = first_sent[-16:, units:].astype(F32) + first_came[-16:, units:].astype(F32)
        total = total[:8] + total[8:]
        total = total + pltpu.roll(total, 4, 0)
        own = mine[...].astype(F32)
        own = own[:8] + own[8:]
        own = own + pltpu.roll(own, 4, 0)
        ends_out[0][...] = jnp.concatenate([total, own, jnp.zeros((112, 128), F32)], 0).T


def contract_other_kernel(k, place, act, so_far, w, *outs):
    core = lax.axis_index("narrow") % 2
    units = w.shape[0] // 2
    rows = pl.ds(pl.multiple_of((1 - core) * units, 128), units)
    total = so_far[...] + jnp.dot(act[...], w[rows, :], preferred_element_type=F32)
    spread = jnp.dot(place[...], total.astype(BF16), preferred_element_type=F32).astype(BF16)
    size = size_of(k)
    for s in range(4):
        outs[s][...] = spread[s * size : (s + 1) * size]


def finish_kernel(slots, hidden, mod, out_weight, ends, *refs):
    pieces, (layer_out, bundle_out) = refs[: 4 * CHUNKS], refs[4 * CHUNKS :]
    result = jnp.zeros(hidden.shape, F32)
    for k in range(CHUNKS):
        total = pieces[4 * k][...].astype(F32)
        for s in (1, 2, 3):
            total = total + pieces[4 * k + s][...].astype(F32)
        total = jnp.concatenate([total] * (CAP // size_of(k)), 0)
        result = jnp.where(slots[:, 2 + k : 3 + k] > 0.5, total, result)
    gate = jnp.where(slots[:, 1:2] > 0.5, mod[5:6, :], mod[2:3, :])
    layer = hidden[...].astype(F32) + gate * result
    layer = jnp.where(slots[:, 0:1] > 0.5, layer, 0.0).astype(BF16)
    layer_out[...] = layer
    x = layer.astype(F32)
    centre = jnp.sum(x, -1, keepdims=True) / x.shape[1]
    ones = jnp.ones((8, x.shape[1]), BF16)
    across = lambda left, right: lax.dot_general(
        left, right, (((1,), (1,)), ((), ())), preferred_element_type=F32
    )
    high, low = high_low(x * x)
    total, square = across(ones, layer), across(ones, high) + across(ones, low)
    width = out_weight.shape[0]
    product = across(out_weight[...], ((x - centre) * (1.0 + mod[7:8, :])).astype(BF16))
    bundle_out[:width, :] = product + total[0:1] / x.shape[1] * ends[:width, 8:9]
    row = lax.broadcasted_iota(jnp.int32, (8, CAP), 0)
    bundle_out[width:, :] = jnp.where(row == 0, total, square)


def write_kernel(layer, out):
    out[...] = layer[...]


def add_kernel(left, right, out):
    out[...] = left[...] + right[...]


def noise_kernel(timestep, alphas, video, latent, _, out):
    index = lax.broadcasted_iota(jnp.int32, (8, 128), 0) * 128 + lax.broadcasted_iota(
        jnp.int32, (8, 128), 1
    )
    alpha = jnp.sum(
        jnp.sum(jnp.where(index == timestep[0], alphas[...], 0.0), 0, keepdims=True),
        1,
        keepdims=True,
    )
    width = latent.shape[0]
    out[:width, :] = jnp.where(video[0:1] > 0.5, jnp.sqrt(alpha) * latent[...], 0.0)
    out[width:, :] = jnp.where(video[...] > 0.5, jnp.sqrt(1.0 - alpha), 0.0)


def latent_kernel(noise, ends, mine, mine_y, other, other_y, out):
    width = out.shape[0]
    factor = noise[width : width + 1]

    def velocity(total):
        average = total[width : width + 1] / D
        variance = total[width + 1 : width + 2] / D - average * average
        return (total[:width] - average * ends[:width, 0:1]) * lax.rsqrt(
            variance + norm_eps
        ) + ends[:width, 1:2]

    first = lax.axis_index("cfg") == 0
    guided = velocity(mine[...] + mine_y[...]) * jnp.where(first, guidance, 1.0 - guidance)
    guided = guided + velocity(other[...] + other_y[...]) * jnp.where(
        first, 1.0 - guidance, guidance
    )
    guided = jnp.where(factor > 0.0, guided, 0.0)
    out[...] = noise[:width] - factor * guided


def alpha_constant():
    ends = np.sqrt(np.float64(0.00085)), np.sqrt(np.float64(0.012))
    betas = np.linspace(ends[0], ends[1], 1000, dtype=np.float64) ** 2
    return np.pad(np.cumprod(1.0 - betas), (0, 24)).astype(np.float32).reshape(8, 128)


def call(kernel, outs, args, spaces, scratch=(), weight=1):
    kinds = {"v": pltpu.VMEM, "s": pltpu.SMEM, "a": pl.ANY}
    return pl.pallas_call(
        kernel,
        out_shape=[jax.ShapeDtypeStruct(shape, dtype) for shape, dtype in outs],
        in_specs=[pl.BlockSpec(memory_space=kinds[letter]) for letter in spaces],
        out_specs=[pl.BlockSpec(memory_space=pltpu.VMEM) for _ in outs],
        scratch_shapes=list(scratch),
        compiler_params=pltpu.CompilerParams(vmem_limit_bytes=24 * 2**20),
        cost_estimate=pl.CostEstimate(flops=weight, bytes_accessed=1, transcendentals=0),
    )(*args)


def four_blocks(
    hidden, split_table, modulation, expand_weight, contract_weight, output_weight, latent, timestep
):
    hidden = hidden[0]
    features = hidden.shape[1]
    units = expand_weight.shape[1] // 2
    width = output_weight.shape[1]
    payload = units + 128

    in_place = lambda array: pltpu.with_memory_space_constraint(array, pltpu.HBM)
    tokens, piece = call(
        take_kernel,
        [(hidden.shape, BF16), ((QUOTAS[1], features), BF16)],
        [in_place(hidden)],
        "a",
        [pltpu.SemaphoreType.DMA((2,))],
    )
    across = swap(piece, "wide", 2, 4)
    near = swap(tokens, "wide", 1, 4)

    tiles = units // TILE
    chunks = range(CHUNKS)
    made = call(
        prepare_kernel,
        [((size_of(k), features), BF16) for k in chunks[1:]]
        + [((2 * size_of(k), 4 * QUOTAS[k + 1]), BF16) for k in chunks]
        + [((4 * size_of(k), 2 * size_of(k)), BF16) for k in chunks]
        + [((2 * size_of(k), 128), F32) for k in chunks]
        + [
            ((features, units), BF16),
            ((features, units), BF16),
            (modulation.shape, F32),
            ((width, features), BF16),
            ((16, features), BF16),
            ((16, 128), BF16),
            ((CAP, 128), F32),
            ((8, CAP), F32),
        ],
        [
            in_place(split_table),
            tokens,
            in_place(modulation),
            in_place(output_weight.T),
            in_place(expand_weight),
        ],
        "avaaa",
        [
            pltpu.SMEM(split_table.shape, jnp.int32),
            pltpu.SemaphoreType.DMA((2, tiles)),
            pltpu.SemaphoreType.DMA((3,)),
        ],
    )
    later, made = made[: CHUNKS - 1], made[CHUNKS - 1 :]
    gathers, made = made[:CHUNKS], made[CHUNKS:]
    spreads, made = made[:CHUNKS], made[CHUNKS:]
    texts, made = made[:CHUNKS], made[CHUNKS:]
    held_sent, held_kept, mod, out_weight, rows_in, ends_mine, slots, video = made
    later = [swap(piece, "wide", 2, 4) for piece in later]
    (across,) = call(pass_kernel, [(across.shape, BF16)], [across, slots], "va")
    far = [across, swap(across, "wide", 1, 4)]

    merged = []
    before = []
    for k in chunks:
        rows = 2 * size_of(k)
        sent_rows = rows + (16 if k == 0 else 0)
        z, sent, side = call(
            functools.partial(expand_sent_kernel, k),
            [((sent_rows, features), BF16), ((sent_rows, payload), BF16), ((rows, 128), BF16)],
            [texts[k], mod, gathers[k], tokens, near, *far, held_sent, rows_in, ends_mine, *before],
            "vvvvv" + "v" * len(far) + "vvv" + "a" * len(before),
            weight=LONG,
        )
        came = swap(sent, "narrow", 1, 4)
        kept, *sums_made = call(
            functools.partial(expand_kept_kernel, k),
            [((rows, units), F32)] + ([((16, units), BF16)] if k == 0 else []),
            [z, held_kept, sent],
            "vva",
            weight=LONG if k == 0 else 1,
        )
        sums = sums_made[0] if k == 0 else sums
        if k == CHUNKS - 1:
            (held_out,) = call(
                hold_kernel,
                [(contract_weight.shape, BF16)],
                [in_place(contract_weight), z],
                "aa",
                [pltpu.SemaphoreType.DMA((4,))],
                weight=LONG,
            )
        total, sent = call(
            functools.partial(merge_kernel, k),
            [((rows, units), F32), ((sent_rows, payload), BF16)],
            [kept, side, came, sums, ends_mine, *([held_out] if k == CHUNKS - 1 else [])],
            "vvvvv" + ("a" if k == CHUNKS - 1 else ""),
        )
        if k + 1 < CHUNKS:
            (across,) = call(
                pass_kernel, [(later[k].shape, BF16)], [later[k], sent], "va"
            )
            far.extend([across, swap(across, "wide", 1, 4)])
        if k == 0:
            (noise,) = call(
                noise_kernel,
                [((width + 8, CAP), F32)],
                [timestep, alpha_constant(), video, latent.T, sent],
                "svvva",
                weight=LONG,
            )
        before = [sent, noise]
        merged.append((total, sent, swap(sent, "narrow", 2, 4)))

    returned = []
    before = []
    first = merged[0][1:]
    for k in chunks:
        rows = 2 * size_of(k)
        total, sent, came = merged[k]
        if k + 1 < CHUNKS:
            before = before + [merged[k + 1][1]]
        (act,) = call(
            functools.partial(activate_kernel, features),
            [((rows, units), BF16)],
            [texts[k], total, sent, came, *first, *before],
            "vvvvvv" + "a" * len(before),
        )
        act_came = swap(act, "narrow", 1, 4)
        out, *ends_made = call(
            functools.partial(contract_own_kernel, k),
            [((rows, features), F32)] + ([((128, 128), F32)] if k == 0 else []),
            [act, held_out, ends_mine, *first],
            "vvvvv",
            weight=LONG,
        )
        ends = ends_made[0] if k == 0 else ends
        pieces = call(
            functools.partial(contract_other_kernel, k),
            [((size_of(k), features), BF16)] * 4,
            [spreads[k], act_came, out, held_out],
            "vvvv",
        )
        before = pieces
        returned.append(pieces[0])
        returned.extend(swap(pieces[s], "wide", s, 4) for s in (1, 2, 3))

    layer, bundle = call(
        finish_kernel,
        [((CAP, features), BF16), ((width + 8, CAP), F32)],
        [slots, tokens, mod, out_weight, ends, *returned],
        "v" * (5 + len(returned)),
    )
    (layer_out,) = call(write_kernel, [((CAP, features), BF16)], [layer], "v", weight=LONG)
    (bundle,) = call(
        add_kernel, [((width + 8, CAP), F32)], [bundle, swap(bundle, "narrow", 1, 4)], "vv"
    )
    (clean_latent,) = call(
        latent_kernel,
        [((width, CAP), F32)],
        [noise, ends, bundle] + [swap(bundle, ("cfg", "narrow"), n, 8) for n in (2, 4, 6)],
        "vvvvvv",
    )
    return (layer_out[None], clean_latent.T)


def solution(mesh):
    by_swaps = (mesh.shape["wide"], mesh.shape["narrow"], mesh.shape["cfg"]) == (4, 4, 2)
    return jax.shard_map(
        four_blocks if by_swaps else any_slice,
        mesh=mesh,
        in_specs=(
            P("cfg", "wide", "narrow"),
            P(),
            P(None, "narrow"),
            P("narrow", "wide"),
            P("wide", "narrow"),
            P("narrow", None),
            P("wide", None),
            P(),
        ),
        out_specs=(P("cfg", "wide", "narrow"), P("wide", None)),
        check_vma=False,
    )
```

```python
import functools

import jax
import jax.numpy as jnp
import numpy as np
from jax import lax
from jax.experimental import pallas as pl
from jax.experimental.pallas import tpu as pltpu
from jax.sharding import PartitionSpec as P

D = 3072
TEXT = 226


norm_eps = 1e-05
guidance = 6.0


def alpha_table():
    steps_index = jnp.arange(1000, dtype=jnp.int32)
    start_root = 0.00085**0.5
    end_root = 0.012**0.5
    roots = start_root + (end_root - start_root) * steps_index.astype(jnp.float32) / 999.0
    return (steps_index, jnp.cumprod(1.0 - roots * roots))


def feature_norm(values, shifts, scaling):
    totals, squares = lax.psum(
        (jnp.sum(values, -1, keepdims=True), jnp.sum(values * values, -1, keepdims=True)), "narrow"
    )
    average = totals / D
    variance = squares / D - average * average
    return (values - average) * lax.rsqrt(variance + norm_eps) * (1.0 + scaling) + shifts


def any_slice(
    hidden, split_table, modulation, expand_weight, contract_weight, output_weight, latent, timestep
):
    capacity = hidden.shape[1]
    wide_index = lax.axis_index("wide")
    table_index = jnp.arange(split_table.shape[0], dtype=jnp.int32)
    offset = jnp.sum(jnp.where(table_index < wide_index, split_table, 0))
    own_count = jnp.sum(jnp.where(table_index == wide_index, split_table, 0))
    slot_index = jnp.arange(capacity, dtype=jnp.int32)
    position = offset + slot_index
    slot_live = slot_index < own_count
    is_text = slot_live & (position < TEXT)
    is_video = slot_live & (position >= TEXT)
    text_column = is_text[:, None]
    shifts = jnp.where(text_column, modulation[3], modulation[0])
    scaling = jnp.where(text_column, modulation[4], modulation[1])
    gating = jnp.where(text_column, modulation[5], modulation[2])
    values = hidden[0].astype(jnp.float32)
    normed = feature_norm(values, shifts, scaling).astype(jnp.bfloat16)
    hidden_part = jnp.dot(
        lax.all_gather(normed, "wide", axis=0, tiled=True),
        expand_weight,
        preferred_element_type=jnp.float32,
    )
    hidden_pre = lax.psum(hidden_part, "narrow")
    activated = jax.nn.gelu(hidden_pre, approximate=True).astype(jnp.bfloat16)
    ff_result = lax.psum_scatter(
        jnp.dot(activated, contract_weight, preferred_element_type=jnp.float32),
        "wide",
        scatter_dimension=0,
        tiled=True,
    )
    layer_out = jnp.where(slot_live[:, None], values + gating * ff_result, 0.0).astype(jnp.bfloat16)
    final_in = layer_out.astype(jnp.float32)
    final_normed = feature_norm(final_in, modulation[6], modulation[7]).astype(jnp.bfloat16)
    velocity_part = jnp.dot(final_normed, output_weight, preferred_element_type=jnp.float32)
    copy_weight = jnp.where(lax.axis_index("cfg") == 0, guidance, 1.0 - guidance)
    guided = lax.psum(velocity_part * copy_weight, ("cfg", "narrow"))
    steps_index, alpha_bar = alpha_table()
    alpha_now = jnp.sum(jnp.where(steps_index == timestep[0], alpha_bar, 0.0))
    clean_latent = jnp.where(
        is_video[:, None], jnp.sqrt(alpha_now) * latent - jnp.sqrt(1.0 - alpha_now) * guided, 0.0
    )
    return (layer_out[None], clean_latent)


QUOTAS = (0, 64, 128)
CAP = 128
CHUNKS = len(QUOTAS) - 1
F32, BF16 = jnp.float32, jnp.bfloat16
TILE = 512
LONG = 10**10


def size_of(k):
    return QUOTAS[k + 1] - QUOTAS[k]


def swap(array, axis, distance, size):
    return lax.ppermute(array, axis, [(i, i ^ distance) for i in range(size)])


def z_swaps(array):
    return [swap(array, "wide", s, 4) for s in (1, 2, 3)]


def choose(values, index):
    out = values[0]
    for i in range(1, 4):
        out = jnp.where(index == i, values[i], out)
    return out


def layout(table):
    counts = [table[b] for b in range(4)]
    largest = jnp.int32(3)
    for b in (2, 1, 0):
        largest = jnp.where(counts[b] == CAP, b, largest)
    starts, others, ranks, offsets = [], [], [], []
    rank, offset = jnp.int32(0), jnp.int32(0)
    for b in range(4):
        other = jnp.where(largest == b, 0, 1)
        ranks.append(rank * other)
        others.append(other)
        offsets.append(offset)
        rank = rank + other * counts[b]
        offset = offset + counts[b]
    block = lax.axis_index("wide")
    of = lambda values: [choose(values, jnp.bitwise_xor(block, s)) for s in range(4)]
    return of(ranks), of(counts), of(others), of(offsets)[0], choose(offsets, largest)


def high_low(values):
    high = values.astype(BF16)
    return high, (values - high.astype(F32)).astype(BF16)


def load(source, place, sems):
    parts = sems.shape[0]
    height = source.shape[0] // parts
    copies = []
    for t in range(parts):
        rows = pl.ds(t * height, height)
        copies.append(pltpu.make_async_copy(source.at[rows, :], place.at[rows, :], sems.at[t]))
        copies[-1].start()
    return copies


def load_half(source, half, place, sems):
    width = place.shape[1]
    copies = []
    for t in range(0, width, TILE):
        columns = pl.ds(pl.multiple_of(half * width + t, 128), TILE)
        copies.append(
            pltpu.make_async_copy(
                source.at[:, columns], place.at[:, pl.ds(t, TILE)], sems.at[len(copies)]
            )
        )
        copies[-1].start()
    return copies


def rows_of(parts, core):
    total = parts[:8] + parts[8:]
    total = jnp.where(core == 0, total, pltpu.roll(total, 4, 0))
    high, low = high_low(total)
    return jnp.concatenate([high.astype(F32), low.astype(F32)], 0).astype(BF16)


def hold_kernel(source, *refs):
    place, sems = refs[-2:]
    for copy in load(source, place, sems):
        copy.wait()


def text_rows(k, largest_offset):
    size = size_of(k)
    row = lax.broadcasted_iota(jnp.int32, (2 * size, 1), 0)
    rank = jnp.where(row < size, row, row - size) + QUOTAS[k]
    position = jnp.where(
        row < size, rank + largest_offset, jnp.where(rank < largest_offset, rank, rank + CAP)
    )
    return position < TEXT


def gather_matrix(k, ranks, counts, others):
    size = size_of(k)
    places = []
    for p in range(k + 1):
        piece = size_of(p)
        lane = lax.broadcasted_iota(jnp.int32, (1, 4 * piece), 1)
        which, slot = lane // piece, lane % piece + QUOTAS[p]
        rank = slot + choose(ranks, which) - QUOTAS[k]
        live = (rank >= 0) & (rank < size) & (slot < choose(counts, which))
        row = jnp.where(live, rank + choose(others, which) * size, -1)
        at = lax.broadcasted_iota(jnp.int32, (2 * size, 4 * piece), 0)
        places.append(jnp.where(at == row, 1.0, 0.0).astype(BF16))
    return jnp.concatenate(places, 1)


def spread_matrix(k, ranks, counts, others):
    size = size_of(k)
    places = []
    for s in range(4):
        first = jnp.maximum(QUOTAS[k] - ranks[s], 0)
        last = jnp.minimum(counts[s], QUOTAS[k + 1] - ranks[s])
        index = lax.broadcasted_iota(jnp.int32, (size, 1), 0)
        slot = first + jnp.bitwise_and(index - first, size - 1)
        row = jnp.where(slot < last, slot + ranks[s] - QUOTAS[k] + others[s] * size, -1)
        at = lax.broadcasted_iota(jnp.int32, (size, 2 * size), 1)
        places.append(jnp.where(at == row, 1.0, 0.0).astype(BF16))
    return jnp.concatenate(places, 0)


def take_kernel(source, whole, piece, sems):
    copies = [
        pltpu.make_async_copy(source.at[pl.ds(0, piece.shape[0]), :], piece, sems.at[0]),
        pltpu.make_async_copy(source, whole, sems.at[1]),
    ]
    for copy in copies:
        copy.start()
    for copy in copies:
        copy.wait()


def prepare_kernel(table_in, tokens, mod_in, out_weight, w, *refs):
    later, refs = refs[: CHUNKS - 1], refs[CHUNKS - 1 :]
    gathers, refs = refs[:CHUNKS], refs[CHUNKS:]
    spreads, refs = refs[:CHUNKS], refs[CHUNKS:]
    texts, refs = refs[:CHUNKS], refs[CHUNKS:]
    held, kept, mod, weight, rows_out, ends_out, slots_out, video_out = refs[:8]
    table, sems, small = refs[8:]
    core = lax.axis_index("narrow") % 2
    sources = (table_in, mod_in, out_weight)
    copies = [
        pltpu.make_async_copy(source, place, small.at[i])
        for i, (source, place) in enumerate(zip(sources, (table, mod, weight)))
    ]
    for copy in copies:
        copy.start()
    big = load_half(w, 1 - core, held, sems.at[0]) + load_half(w, core, kept, sems.at[1])

    copies[0].wait()
    ranks, counts, others, offset, largest_offset = layout(table)
    for k in range(CHUNKS):
        gathers[k][...] = gather_matrix(k, ranks, counts, others)
        spreads[k][...] = spread_matrix(k, ranks, counts, others)
        text = jnp.where(text_rows(k, largest_offset), 1.0, 0.0)
        texts[k][...] = jnp.broadcast_to(text, texts[k].shape)
    slot = lax.broadcasted_iota(jnp.int32, (CAP, 128), 0)
    lane = lax.broadcasted_iota(jnp.int32, (CAP, 128), 1)
    rank = slot + ranks[0]
    flag = lambda condition: jnp.where(condition, 1.0, 0.0)
    kind = jnp.where(lane == 0, flag(slot < counts[0]), flag(slot + offset < TEXT))
    for k in range(CHUNKS):
        kind = jnp.where(
            lane == 2 + k, flag((rank >= QUOTAS[k]) & (rank < QUOTAS[k + 1])), kind
        )
    slots_out[...] = kind
    slot = lax.broadcasted_iota(jnp.int32, (8, CAP), 1)
    video_out[...] = jnp.where((slot < counts[0]) & (slot + offset >= TEXT), 1.0, 0.0)

    copies[1].wait()
    row = lax.broadcasted_iota(jnp.int32, (8, 1), 0)
    rows = jnp.where(row == 0, 1.0 + mod[1:2, :], jnp.zeros((8, 1), F32))
    rows = jnp.where(row == 1, 1.0 + mod[4:5, :], rows)
    rows = jnp.where(row == 2, mod[0:1, :], rows)
    rows = jnp.where(row == 3, mod[3:4, :], rows)
    rows_out[...] = jnp.concatenate(high_low(rows), 0)
    rows = jnp.where(row == 0, 1.0 + mod[7:8, :], jnp.zeros((8, 1), F32))
    rows = jnp.where(row == 1, mod[6:7, :], rows)
    copies[2].wait()
    ends = lax.dot_general(
        jnp.concatenate(high_low(rows), 0),
        weight[...],
        (((1,), (1,)), ((), ())),
        preferred_element_type=F32,
    )
    ends = rows_of(ends, core)
    ends_out[...] = jnp.concatenate([ends, jnp.zeros((16, 128 - ends.shape[1]), BF16)], 1)
    for k in range(1, CHUNKS):
        later[k - 1][...] = tokens[QUOTAS[k] : QUOTAS[k + 1], :]
    for copy in big:
        copy.wait()


def expand_sent_kernel(k, text, mod, place, own, near, *refs):
    far, (w, sums, ends) = refs[: 2 * (k + 1)], refs[2 * (k + 1) : 2 * (k + 1) + 3]
    z_out, sent_out, side_out = refs[-3:]
    core = lax.axis_index("narrow") % 2
    units = w.shape[1]
    rows = side_out.shape[0]
    pieces = []
    for p in range(k + 1):
        of_chunk = slice(QUOTAS[p], QUOTAS[p + 1])
        pieces += [own[of_chunk, :], near[of_chunk, :], far[2 * p][...], far[2 * p + 1][...]]
    tokens = jnp.concatenate(pieces, 0)
    x = jnp.dot(place[...], tokens, preferred_element_type=F32)
    centre = (jnp.sum(x, -1, keepdims=True) / x.shape[1]).astype(BF16).astype(F32)
    x = x - centre
    z = (x * (1.0 + jnp.where(text[:, :1] > 0.5, mod[4:5, :], mod[1:2, :]))).astype(BF16)
    if k == 0:
        z = jnp.concatenate([z, sums[...]], 0)
    z_out[...] = z
    for t in range(0, units, TILE):
        product = jnp.dot(z, w[:, t : t + TILE], preferred_element_type=F32)
        sent_out[:rows, t : t + TILE] = product[:rows].astype(BF16)
        if k == 0:
            sent_out[rows:, t : t + TILE] = rows_of(product[rows:], core)
    total = jnp.sum(x, -1, keepdims=True)
    square = jnp.sum(x * x, -1, keepdims=True)
    total_high = total.astype(BF16).astype(F32)
    square_high = square.astype(BF16).astype(F32)
    lane = lax.broadcasted_iota(jnp.int32, (rows, 128), 1) - 4 * core
    side = jnp.where((lane == 0) | (lane == 1), centre, 0.0)
    side = jnp.where(lane == 16, total_high, side)
    side = jnp.where(lane == 17, total - total_high, side)
    side = jnp.where(lane == 18, square_high, side)
    side = jnp.where(lane == 19, square - square_high, side).astype(BF16)
    side_out[...] = side
    sent_out[:rows, units:] = side
    if k == 0:
        sent_out[rows:, units:] = ends[...]


def expand_kept_kernel(k, z, w, _, *refs):
    kept_out = refs[-1 if k else -2]
    core = lax.axis_index("narrow") % 2
    rows = kept_out.shape[0]
    for t in range(0, w.shape[1], TILE):
        columns = slice(t, t + TILE)
        product = jnp.dot(z[...], w[:, columns], preferred_element_type=F32)
        kept_out[:, columns] = product[:rows]
        if k == 0:
            refs[-1][:, columns] = rows_of(product[rows:], core)


def pass_kernel(piece, _, out):
    out[...] = piece[...]


def across_rows(side):
    height = side.shape[0]
    if height < 128:
        side = jnp.concatenate([side, jnp.zeros((128 - height, 128), F32)], 0)
    return side.T


def merge_kernel(k, kept, side, came, sums, ends, *refs):
    total_out, sent_out, side_out, stats_out = refs[-4:]
    rows, units = kept.shape
    add = lambda left, right: left[...].astype(F32) + right.astype(F32)
    total = kept[...] + came[:rows, :units].astype(F32)
    total_out[...] = total
    sent_out[:rows, :] = total.astype(BF16)
    both = add(side, came[:rows, units:])
    side_out[...] = both
    stats_out[:32, :] = across_rows(both)[:32].astype(BF16)
    if k == 0:
        sent_out[rows:, :] = add(sums, came[rows:, :units]).astype(BF16)
        stats_out[32:, :] = add(ends, came[rows:, units:]).astype(BF16)


def activate_kernel(features, text, total, came, side, stats, first_sent, first_came, *refs):
    act_out = refs[-1]
    rows, units = total.shape
    sides = [side[...], across_rows(stats[:32, :].astype(F32))[:rows]]
    lane = lax.broadcasted_iota(jnp.int32, (rows, 128), 1)
    field = lane % 4
    summed = sides[0] + sides[1]
    add = lambda values, mask: jnp.sum(jnp.where(mask, values, 0.0), -1, keepdims=True)
    centres, measures = lane < 8, (lane >= 16) & (lane < 24)
    average = (
        add(summed, centres & (field == 0)) * features + add(summed, measures & (field < 2))
    ) / D
    spread = add(summed, measures & (field >= 2))
    aparts = []
    for side in sides:
        apart = jnp.where(centres, side - average, 0.0)
        for core in range(2):
            off = add(apart, lane == 4 * core)
            own = lane // 4 == 4 + core
            spread = spread + off * (2.0 * add(side, own & (field < 2)) + features * off)
        aparts.append(apart)
    scale = lax.rsqrt(spread / D + norm_eps)
    of_text = jnp.where(text[...] > 0.5, 1, 0)
    mine = centres & (lane % 2 == of_text)
    packed, shift = None, 0
    for apart in aparts:
        factor = jnp.where(mine, jnp.where(field < 2, apart * scale, 1.0), 0.0)
        high = factor.astype(BF16).astype(F32)
        for part in (high, high, factor - high, factor - high):
            part = pltpu.roll(part, shift, 1) if shift else part
            packed = part if packed is None else packed + part
            shift += 8
    packed = packed[:, :64].astype(BF16)
    own, other = first_sent[-16:, :units], first_came[-16:, :units]
    factors = jnp.concatenate([own, own, other, other], 0)
    for t in range(0, units, TILE):
        columns = slice(t, t + TILE)
        pre = total[:, columns] + came[:rows, columns].astype(F32)
        extra = jnp.dot(packed, factors[:, columns], preferred_element_type=F32)
        act_out[:, columns] = jax.nn.gelu(pre * scale + extra, approximate=True).astype(BF16)


def contract_own_kernel(k, act, w, mine, chip, other, out, *ends_out):
    core = lax.axis_index("narrow") % 2
    units = w.shape[0] // 2
    rows = pl.ds(pl.multiple_of(core * units, 128), units)
    out[...] = jnp.dot(act[...], w[rows, :], preferred_element_type=F32)
    if k == 0:
        total = chip[-16:, :].astype(F32) + other[-16:, :].astype(F32)
        total = total[:8] + total[8:]
        total = total + pltpu.roll(total, 4, 0)
        own = mine[...].astype(F32)
        own = own[:8] + own[8:]
        own = own + pltpu.roll(own, 4, 0)
        ends_out[0][...] = jnp.concatenate([total, own, jnp.zeros((112, 128), F32)], 0).T


def contract_other_kernel(k, place, act, so_far, w, *outs):
    core = lax.axis_index("narrow") % 2
    units = w.shape[0] // 2
    rows = pl.ds(pl.multiple_of((1 - core) * units, 128), units)
    total = so_far[...] + jnp.dot(act[...], w[rows, :], preferred_element_type=F32)
    spread = jnp.dot(place[...], total.astype(BF16), preferred_element_type=F32).astype(BF16)
    size = size_of(k)
    for s in range(4):
        outs[s][...] = spread[s * size : (s + 1) * size]


def finish_kernel(slots, hidden, mod, out_weight, ends, *refs):
    pieces, (layer_out, bundle_out) = refs[: 4 * CHUNKS], refs[4 * CHUNKS :]
    result = jnp.zeros(hidden.shape, F32)
    for k in range(CHUNKS):
        total = pieces[4 * k][...].astype(F32)
        for s in (1, 2, 3):
            total = total + pieces[4 * k + s][...].astype(F32)
        total = jnp.concatenate([total] * (CAP // size_of(k)), 0)
        result = jnp.where(slots[:, 2 + k : 3 + k] > 0.5, total, result)
    gate = jnp.where(slots[:, 1:2] > 0.5, mod[5:6, :], mod[2:3, :])
    layer = hidden[...].astype(F32) + gate * result
    layer = jnp.where(slots[:, 0:1] > 0.5, layer, 0.0).astype(BF16)
    layer_out[...] = layer
    x = layer.astype(F32)
    centre = jnp.sum(x, -1, keepdims=True) / x.shape[1]
    ones = jnp.ones((8, x.shape[1]), BF16)
    across = lambda left, right: lax.dot_general(
        left, right, (((1,), (1,)), ((), ())), preferred_element_type=F32
    )
    high, low = high_low(x * x)
    total, square = across(ones, layer), across(ones, high) + across(ones, low)
    width = out_weight.shape[0]
    product = across(out_weight[...], ((x - centre) * (1.0 + mod[7:8, :])).astype(BF16))
    bundle_out[:width, :] = product + total[0:1] / x.shape[1] * ends[:width, 8:9]
    row = lax.broadcasted_iota(jnp.int32, (8, CAP), 0)
    bundle_out[width:, :] = jnp.where(row == 0, total, square)


def write_kernel(layer, out):
    out[...] = layer[...]


def add_kernel(left, right, out):
    out[...] = left[...] + right[...]


def noise_kernel(timestep, alphas, video, latent, _, out):
    index = lax.broadcasted_iota(jnp.int32, (8, 128), 0) * 128 + lax.broadcasted_iota(
        jnp.int32, (8, 128), 1
    )
    alpha = jnp.sum(
        jnp.sum(jnp.where(index == timestep[0], alphas[...], 0.0), 0, keepdims=True),
        1,
        keepdims=True,
    )
    width = latent.shape[0]
    out[:width, :] = jnp.where(video[0:1] > 0.5, jnp.sqrt(alpha) * latent[...], 0.0)
    out[width:, :] = jnp.where(video[...] > 0.5, jnp.sqrt(1.0 - alpha), 0.0)


def latent_kernel(noise, ends, mine, other_y, other, mine_y, out):
    width = out.shape[0]
    factor = noise[width : width + 1]

    def velocity(total):
        average = total[width : width + 1] / D
        variance = total[width + 1 : width + 2] / D - average * average
        return (total[:width] - average * ends[:width, 0:1]) * lax.rsqrt(
            variance + norm_eps
        ) + ends[:width, 1:2]

    first = lax.axis_index("cfg") == 0
    guided = velocity(mine[...] + mine_y[...]) * jnp.where(first, guidance, 1.0 - guidance)
    guided = guided + velocity(other[...] + other_y[...]) * jnp.where(
        first, 1.0 - guidance, guidance
    )
    guided = jnp.where(factor > 0.0, guided, 0.0)
    out[...] = noise[:width] - factor * guided


def alpha_constant():
    ends = np.sqrt(np.float64(0.00085)), np.sqrt(np.float64(0.012))
    betas = np.linspace(ends[0], ends[1], 1000, dtype=np.float64) ** 2
    return np.pad(np.cumprod(1.0 - betas), (0, 24)).astype(np.float32).reshape(8, 128)


def call(kernel, outs, args, spaces, scratch=(), weight=1):
    kinds = {"v": pltpu.VMEM, "s": pltpu.SMEM, "a": pl.ANY}
    return pl.pallas_call(
        kernel,
        out_shape=[jax.ShapeDtypeStruct(shape, dtype) for shape, dtype in outs],
        in_specs=[pl.BlockSpec(memory_space=kinds[letter]) for letter in spaces],
        out_specs=[pl.BlockSpec(memory_space=pltpu.VMEM) for _ in outs],
        scratch_shapes=list(scratch),
        compiler_params=pltpu.CompilerParams(vmem_limit_bytes=24 * 2**20),
        cost_estimate=pl.CostEstimate(flops=weight, bytes_accessed=1, transcendentals=0),
    )(*args)


def four_blocks(
    hidden, split_table, modulation, expand_weight, contract_weight, output_weight, latent, timestep
):
    hidden = hidden[0]
    features = hidden.shape[1]
    units = expand_weight.shape[1] // 2
    width = output_weight.shape[1]
    payload = units + 128

    in_place = lambda array: pltpu.with_memory_space_constraint(array, pltpu.HBM)
    tokens, piece = call(
        take_kernel,
        [(hidden.shape, BF16), ((QUOTAS[1], features), BF16)],
        [in_place(hidden)],
        "a",
        [pltpu.SemaphoreType.DMA((2,))],
    )
    across = swap(piece, "wide", 2, 4)
    near = swap(tokens, "wide", 1, 4)

    tiles = units // TILE
    chunks = range(CHUNKS)
    made = call(
        prepare_kernel,
        [((size_of(k), features), BF16) for k in chunks[1:]]
        + [((2 * size_of(k), 4 * QUOTAS[k + 1]), BF16) for k in chunks]
        + [((4 * size_of(k), 2 * size_of(k)), BF16) for k in chunks]
        + [((2 * size_of(k), 128), F32) for k in chunks]
        + [
            ((features, units), BF16),
            ((features, units), BF16),
            (modulation.shape, F32),
            ((width, features), BF16),
            ((16, features), BF16),
            ((16, 128), BF16),
            ((CAP, 128), F32),
            ((8, CAP), F32),
        ],
        [
            in_place(split_table),
            tokens,
            in_place(modulation),
            in_place(output_weight.T),
            in_place(expand_weight),
        ],
        "avaaa",
        [
            pltpu.SMEM(split_table.shape, jnp.int32),
            pltpu.SemaphoreType.DMA((2, tiles)),
            pltpu.SemaphoreType.DMA((3,)),
        ],
    )
    later, made = made[: CHUNKS - 1], made[CHUNKS - 1 :]
    gathers, made = made[:CHUNKS], made[CHUNKS:]
    spreads, made = made[:CHUNKS], made[CHUNKS:]
    texts, made = made[:CHUNKS], made[CHUNKS:]
    held_sent, held_kept, mod, out_weight, rows_in, ends_mine, slots, video = made
    later = [swap(piece, "wide", 2, 4) for piece in later]
    (across,) = call(pass_kernel, [(across.shape, BF16)], [across, slots], "va")
    far = [across, swap(across, "wide", 1, 4)]

    merged = []
    before = []
    for k in chunks:
        rows = 2 * size_of(k)
        sent_rows = rows + (16 if k == 0 else 0)
        z, sent, side = call(
            functools.partial(expand_sent_kernel, k),
            [((sent_rows, features), BF16), ((sent_rows, payload), BF16), ((rows, 128), BF16)],
            [texts[k], mod, gathers[k], tokens, near, *far, held_sent, rows_in, ends_mine, *before],
            "vvvvv" + "v" * len(far) + "vvv" + "a" * len(before),
            weight=LONG,
        )
        came = swap(sent, "narrow", 1, 4)
        kept, *sums_made = call(
            functools.partial(expand_kept_kernel, k),
            [((rows, units), F32)] + ([((16, units), BF16)] if k == 0 else []),
            [z, held_kept, sent],
            "vva",
            weight=LONG if k == 0 else 1,
        )
        sums = sums_made[0] if k == 0 else sums
        total, sent, side, stats = call(
            functools.partial(merge_kernel, k),
            [
                ((rows, units), F32),
                ((sent_rows, units), BF16),
                ((rows, 128), F32),
                ((sent_rows - rows + 32, 128), BF16),
            ],
            [kept, side, came, sums, ends_mine],
            "vvvvv",
        )
        if k + 1 < CHUNKS:
            (across,) = call(
                pass_kernel, [(later[k].shape, BF16)], [later[k], sent], "va"
            )
            far.extend([across, swap(across, "wide", 1, 4)])
        if k == 0:
            (held_out,) = call(
                hold_kernel,
                [(contract_weight.shape, BF16)],
                [in_place(contract_weight), across, stats],
                "aaa",
                [pltpu.SemaphoreType.DMA((4,))],
                weight=LONG,
            )
        if k == 0:
            (noise,) = call(
                noise_kernel,
                [((width + 8, CAP), F32)],
                [timestep, alpha_constant(), video, latent.T, sent],
                "svvva",
                weight=LONG,
            )
        before = [sent, noise, held_out]
        came, stats_came = [swap(array, "narrow", 2, 4) for array in (sent, stats)]
        merged.append((sent, stats, [total, came, side, stats_came]))

    returned = []
    before = []
    first = [merged[0][0], merged[0][2][1]]
    first_stats = [merged[0][1], merged[0][2][3]]
    for k in chunks:
        rows = 2 * size_of(k)
        if k + 1 < CHUNKS:
            before = before + [merged[k + 1][0], merged[k + 1][1]]
        (act,) = call(
            functools.partial(activate_kernel, features),
            [((rows, units), BF16)],
            [texts[k], *merged[k][2], *first, *before],
            "vvvvvvv" + "a" * len(before),
        )
        act_came = swap(act, "narrow", 1, 4)
        out, *ends_made = call(
            functools.partial(contract_own_kernel, k),
            [((rows, features), F32)] + ([((128, 128), F32)] if k == 0 else []),
            [act, held_out, ends_mine, *first_stats],
            "vvvvv",
            weight=LONG,
        )
        ends = ends_made[0] if k == 0 else ends
        pieces = call(
            functools.partial(contract_other_kernel, k),
            [((size_of(k), features), BF16)] * 4,
            [spreads[k], act_came, out, held_out],
            "vvvv",
        )
        before = pieces
        distances = (3, 2, 1) if k + 1 < CHUNKS else (3, 2, 1)
        returned += [pieces[0], *(swap(pieces[s], "wide", s, 4) for s in distances)]

    layer, bundle = call(
        finish_kernel,
        [((CAP, features), BF16), ((width + 8, CAP), F32)],
        [slots, tokens, mod, out_weight, ends, *returned],
        "v" * (5 + len(returned)),
    )
    (layer_out,) = call(write_kernel, [((CAP, features), BF16)], [layer], "v", weight=LONG)
    (bundle,) = call(
        add_kernel, [((width + 8, CAP), F32)], [bundle, swap(bundle, "narrow", 1, 4)], "vv"
    )
    (clean_latent,) = call(
        latent_kernel,
        [((width, CAP), F32)],
        [noise, ends, bundle] + [swap(bundle, ("cfg", "narrow"), n, 8) for n in (6, 4, 2)],
        "vvvvvv",
    )
    return (layer_out[None], clean_latent.T)


def solution(mesh):
    by_swaps = (mesh.shape["wide"], mesh.shape["narrow"], mesh.shape["cfg"]) == (4, 4, 2)
    return jax.shard_map(
        four_blocks if by_swaps else any_slice,
        mesh=mesh,
        in_specs=(
            P("cfg", "wide", "narrow"),
            P(),
            P(None, "narrow"),
            P("narrow", "wide"),
            P("wide", "narrow"),
            P("narrow", None),
            P("wide", None),
            P(),
        ),
        out_specs=(P("cfg", "wide", "narrow"), P("wide", None)),
        check_vma=False,
    )
```

```python
import functools

import jax
import jax.numpy as jnp
import numpy as np
from jax import lax
from jax.experimental import pallas as pl
from jax.experimental.pallas import tpu as pltpu
from jax.sharding import PartitionSpec as P

D = 3072
TEXT = 226


norm_eps = 1e-05
guidance = 6.0


def alpha_table():
    steps_index = jnp.arange(1000, dtype=jnp.int32)
    start_root = 0.00085**0.5
    end_root = 0.012**0.5
    roots = start_root + (end_root - start_root) * steps_index.astype(jnp.float32) / 999.0
    return (steps_index, jnp.cumprod(1.0 - roots * roots))


def feature_norm(values, shifts, scaling):
    totals, squares = lax.psum(
        (jnp.sum(values, -1, keepdims=True), jnp.sum(values * values, -1, keepdims=True)), "narrow"
    )
    average = totals / D
    variance = squares / D - average * average
    return (values - average) * lax.rsqrt(variance + norm_eps) * (1.0 + scaling) + shifts


def any_slice(
    hidden, split_table, modulation, expand_weight, contract_weight, output_weight, latent, timestep
):
    capacity = hidden.shape[1]
    wide_index = lax.axis_index("wide")
    table_index = jnp.arange(split_table.shape[0], dtype=jnp.int32)
    offset = jnp.sum(jnp.where(table_index < wide_index, split_table, 0))
    own_count = jnp.sum(jnp.where(table_index == wide_index, split_table, 0))
    slot_index = jnp.arange(capacity, dtype=jnp.int32)
    position = offset + slot_index
    slot_live = slot_index < own_count
    is_text = slot_live & (position < TEXT)
    is_video = slot_live & (position >= TEXT)
    text_column = is_text[:, None]
    shifts = jnp.where(text_column, modulation[3], modulation[0])
    scaling = jnp.where(text_column, modulation[4], modulation[1])
    gating = jnp.where(text_column, modulation[5], modulation[2])
    values = hidden[0].astype(jnp.float32)
    normed = feature_norm(values, shifts, scaling).astype(jnp.bfloat16)
    hidden_part = jnp.dot(
        lax.all_gather(normed, "wide", axis=0, tiled=True),
        expand_weight,
        preferred_element_type=jnp.float32,
    )
    hidden_pre = lax.psum(hidden_part, "narrow")
    activated = jax.nn.gelu(hidden_pre, approximate=True).astype(jnp.bfloat16)
    ff_result = lax.psum_scatter(
        jnp.dot(activated, contract_weight, preferred_element_type=jnp.float32),
        "wide",
        scatter_dimension=0,
        tiled=True,
    )
    layer_out = jnp.where(slot_live[:, None], values + gating * ff_result, 0.0).astype(jnp.bfloat16)
    final_in = layer_out.astype(jnp.float32)
    final_normed = feature_norm(final_in, modulation[6], modulation[7]).astype(jnp.bfloat16)
    velocity_part = jnp.dot(final_normed, output_weight, preferred_element_type=jnp.float32)
    copy_weight = jnp.where(lax.axis_index("cfg") == 0, guidance, 1.0 - guidance)
    guided = lax.psum(velocity_part * copy_weight, ("cfg", "narrow"))
    steps_index, alpha_bar = alpha_table()
    alpha_now = jnp.sum(jnp.where(steps_index == timestep[0], alpha_bar, 0.0))
    clean_latent = jnp.where(
        is_video[:, None], jnp.sqrt(alpha_now) * latent - jnp.sqrt(1.0 - alpha_now) * guided, 0.0
    )
    return (layer_out[None], clean_latent)


QUOTAS = (0, 64, 128)
CAP = 128
CHUNKS = len(QUOTAS) - 1
F32, BF16 = jnp.float32, jnp.bfloat16
TILE = 512
LONG = 10**10


def size_of(k):
    return QUOTAS[k + 1] - QUOTAS[k]


def swap(array, axis, distance, size):
    return lax.ppermute(array, axis, [(i, i ^ distance) for i in range(size)])


def z_swaps(array):
    return [swap(array, "wide", s, 4) for s in (1, 2, 3)]


def choose(values, index):
    out = values[0]
    for i in range(1, 4):
        out = jnp.where(index == i, values[i], out)
    return out


def layout(table):
    counts = [table[b] for b in range(4)]
    largest = jnp.int32(3)
    for b in (2, 1, 0):
        largest = jnp.where(counts[b] == CAP, b, largest)
    starts, others, ranks, offsets = [], [], [], []
    rank, offset = jnp.int32(0), jnp.int32(0)
    for b in range(4):
        other = jnp.where(largest == b, 0, 1)
        ranks.append(rank * other)
        others.append(other)
        offsets.append(offset)
        rank = rank + other * counts[b]
        offset = offset + counts[b]
    block = lax.axis_index("wide")
    of = lambda values: [choose(values, jnp.bitwise_xor(block, s)) for s in range(4)]
    return of(ranks), of(counts), of(others), of(offsets)[0], choose(offsets, largest)


def high_low(values):
    high = values.astype(BF16)
    return high, (values - high.astype(F32)).astype(BF16)


def load(source, place, sems):
    parts = sems.shape[0]
    height = source.shape[0] // parts
    copies = []
    for t in range(parts):
        rows = pl.ds(t * height, height)
        copies.append(pltpu.make_async_copy(source.at[rows, :], place.at[rows, :], sems.at[t]))
        copies[-1].start()
    return copies


def load_half(source, half, place, sems):
    width = place.shape[1]
    copies = []
    for t in range(0, width, TILE):
        columns = pl.ds(pl.multiple_of(half * width + t, 128), TILE)
        copies.append(
            pltpu.make_async_copy(
                source.at[:, columns], place.at[:, pl.ds(t, TILE)], sems.at[len(copies)]
            )
        )
        copies[-1].start()
    return copies


def rows_of(parts, core):
    total = parts[:8] + parts[8:]
    total = jnp.where(core == 0, total, pltpu.roll(total, 4, 0))
    high, low = high_low(total)
    return jnp.concatenate([high.astype(F32), low.astype(F32)], 0).astype(BF16)


def hold_kernel(source, *refs):
    place, sems = refs[-2:]
    for copy in load(source, place, sems):
        copy.wait()


def text_rows(k, largest_offset):
    size = size_of(k)
    row = lax.broadcasted_iota(jnp.int32, (2 * size, 1), 0)
    rank = jnp.where(row < size, row, row - size) + QUOTAS[k]
    position = jnp.where(
        row < size, rank + largest_offset, jnp.where(rank < largest_offset, rank, rank + CAP)
    )
    return position < TEXT


def gather_matrix(k, ranks, counts, others):
    size = size_of(k)
    places = []
    for p in range(k + 1):
        piece = size_of(p)
        lane = lax.broadcasted_iota(jnp.int32, (1, 4 * piece), 1)
        which, slot = lane // piece, lane % piece + QUOTAS[p]
        rank = slot + choose(ranks, which) - QUOTAS[k]
        live = (rank >= 0) & (rank < size) & (slot < choose(counts, which))
        row = jnp.where(live, rank + choose(others, which) * size, -1)
        at = lax.broadcasted_iota(jnp.int32, (2 * size, 4 * piece), 0)
        places.append(jnp.where(at == row, 1.0, 0.0).astype(BF16))
    return jnp.concatenate(places, 1)


def spread_matrix(k, ranks, counts, others):
    size = size_of(k)
    places = []
    for s in range(4):
        first = jnp.maximum(QUOTAS[k] - ranks[s], 0)
        last = jnp.minimum(counts[s], QUOTAS[k + 1] - ranks[s])
        index = lax.broadcasted_iota(jnp.int32, (size, 1), 0)
        slot = first + jnp.bitwise_and(index - first, size - 1)
        row = jnp.where(slot < last, slot + ranks[s] - QUOTAS[k] + others[s] * size, -1)
        at = lax.broadcasted_iota(jnp.int32, (size, 2 * size), 1)
        places.append(jnp.where(at == row, 1.0, 0.0).astype(BF16))
    return jnp.concatenate(places, 0)


def take_kernel(source, whole, piece, sems):
    copies = [
        pltpu.make_async_copy(source.at[pl.ds(0, piece.shape[0]), :], piece, sems.at[0]),
        pltpu.make_async_copy(source, whole, sems.at[1]),
    ]
    for copy in copies:
        copy.start()
    for copy in copies:
        copy.wait()


def prepare_kernel(table_in, timestep, tokens, mod_in, out_weight, w, *refs):
    later, refs = refs[: CHUNKS - 1], refs[CHUNKS - 1 :]
    gathers, refs = refs[:CHUNKS], refs[CHUNKS:]
    spreads, refs = refs[:CHUNKS], refs[CHUNKS:]
    texts, refs = refs[:CHUNKS], refs[CHUNKS:]
    held, kept, mod, weight, rows_out, ends_out, slots_out, video_out, step_out = refs[:9]
    table, sems, small = refs[9:]
    step_out[...] = jnp.full(step_out.shape, timestep[0], jnp.int32)
    core = lax.axis_index("narrow") % 2
    sources = (table_in, mod_in, out_weight)
    copies = [
        pltpu.make_async_copy(source, place, small.at[i])
        for i, (source, place) in enumerate(zip(sources, (table, mod, weight)))
    ]
    for copy in copies:
        copy.start()
    big = load_half(w, 1 - core, held, sems.at[0]) + load_half(w, core, kept, sems.at[1])

    copies[0].wait()
    ranks, counts, others, offset, largest_offset = layout(table)
    for k in range(CHUNKS):
        gathers[k][...] = gather_matrix(k, ranks, counts, others)
        spreads[k][...] = spread_matrix(k, ranks, counts, others)
        text = jnp.where(text_rows(k, largest_offset), 1.0, 0.0)
        texts[k][...] = jnp.broadcast_to(text, texts[k].shape)
    slot = lax.broadcasted_iota(jnp.int32, (CAP, 128), 0)
    lane = lax.broadcasted_iota(jnp.int32, (CAP, 128), 1)
    rank = slot + ranks[0]
    flag = lambda condition: jnp.where(condition, 1.0, 0.0)
    kind = jnp.where(lane == 0, flag(slot < counts[0]), flag(slot + offset < TEXT))
    for k in range(CHUNKS):
        kind = jnp.where(
            lane == 2 + k, flag((rank >= QUOTAS[k]) & (rank < QUOTAS[k + 1])), kind
        )
    slots_out[...] = kind
    slot = lax.broadcasted_iota(jnp.int32, (8, CAP), 1)
    video_out[...] = jnp.where((slot < counts[0]) & (slot + offset >= TEXT), 1.0, 0.0)

    copies[1].wait()
    row = lax.broadcasted_iota(jnp.int32, (8, 1), 0)
    rows = jnp.where(row == 0, 1.0 + mod[1:2, :], jnp.zeros((8, 1), F32))
    rows = jnp.where(row == 1, 1.0 + mod[4:5, :], rows)
    rows = jnp.where(row == 2, mod[0:1, :], rows)
    rows = jnp.where(row == 3, mod[3:4, :], rows)
    rows_out[...] = jnp.concatenate(high_low(rows), 0)
    rows = jnp.where(row == 0, 1.0 + mod[7:8, :], jnp.zeros((8, 1), F32))
    rows = jnp.where(row == 1, mod[6:7, :], rows)
    copies[2].wait()
    ends = lax.dot_general(
        jnp.concatenate(high_low(rows), 0),
        weight[...],
        (((1,), (1,)), ((), ())),
        preferred_element_type=F32,
    )
    ends = rows_of(ends, core)
    ends_out[...] = jnp.concatenate([ends, jnp.zeros((16, 128 - ends.shape[1]), BF16)], 1)
    for k in range(1, CHUNKS):
        later[k - 1][...] = tokens[QUOTAS[k] : QUOTAS[k + 1], :]
    for copy in big:
        copy.wait()


def expand_sent_kernel(k, text, mod, place, own, near, *refs):
    far, (w, sums, ends) = refs[: 2 * (k + 1)], refs[2 * (k + 1) : 2 * (k + 1) + 3]
    z_out, sent_out, side_out = refs[-3:]
    core = lax.axis_index("narrow") % 2
    units = w.shape[1]
    rows = place.shape[0]
    pieces = []
    for p in range(k + 1):
        of_chunk = slice(QUOTAS[p], QUOTAS[p + 1])
        pieces += [own[of_chunk, :], near[of_chunk, :], far[2 * p][...], far[2 * p + 1][...]]
    tokens = jnp.concatenate(pieces, 0)
    x = jnp.dot(place[...], tokens, preferred_element_type=F32)
    centre = (jnp.sum(x, -1, keepdims=True) / x.shape[1]).astype(BF16).astype(F32)
    x = x - centre
    z = (x * (1.0 + jnp.where(text[:, :1] > 0.5, mod[4:5, :], mod[1:2, :]))).astype(BF16)
    if k == 0:
        z = jnp.concatenate([z, sums[...]], 0)
    z_out[...] = z
    if k == 0:
        lead = side_out.shape[1] - 8 * 128
        side_out[:, units:lead] = ends[...]
    for t in range(0, units, TILE):
        columns = slice(t, t + TILE)
        product = jnp.dot(z, w[:, columns], preferred_element_type=F32)
        sent_out[:, columns] = product[:rows].astype(BF16)
        if k == 0:
            side_out[:, columns] = rows_of(product[rows:], core)
    total = jnp.sum(x, -1, keepdims=True)
    square = jnp.sum(x * x, -1, keepdims=True)
    total_high = total.astype(BF16).astype(F32)
    square_high = square.astype(BF16).astype(F32)
    lane = lax.broadcasted_iota(jnp.int32, (rows, 128), 1) - 4 * core
    side = jnp.where((lane == 0) | (lane == 1), centre, 0.0)
    side = jnp.where(lane == 16, total_high, side)
    side = jnp.where(lane == 17, total - total_high, side)
    side = jnp.where(lane == 18, square_high, side)
    side = jnp.where(lane == 19, square - square_high, side).astype(BF16)
    if k == 0:
        for i in range(rows // 16):
            side_out[:, lead + 128 * i : lead + 128 * (i + 1)] = side[16 * i : 16 * (i + 1)]
    else:
        side_out[...] = side


def expand_kept_kernel(k, z, w, _, __, *refs):
    kept_out = refs[-1 if k else -2]
    core = lax.axis_index("narrow") % 2
    rows = kept_out.shape[0]
    for t in range(0, w.shape[1], TILE):
        columns = slice(t, t + TILE)
        product = jnp.dot(z[...], w[:, columns], preferred_element_type=F32)
        kept_out[:, columns] = product[:rows]
        if k == 0:
            refs[-1][:, columns] = rows_of(product[rows:], core)


def pass_kernel(piece, _, out):
    out[...] = piece[...]


def across_rows(side):
    height = side.shape[0]
    if height < 128:
        side = jnp.concatenate([side, jnp.zeros((128 - height, 128), F32)], 0)
    return side.T


def stats_kernel(k, rows, side, came, *refs):
    side_out, stats_out = refs[-2:]
    lead = stats_out.shape[1] - 256
    if k == 0:
        kept_sums = refs[0]
        units = kept_sums.shape[1]
        stats_out[:, :units] = (kept_sums[...].astype(F32) + came[:, :units].astype(F32)).astype(BF16)
        both = side[:, units:].astype(F32) + came[:, units:].astype(F32)
        stats_out[:, units:lead] = both[:, : lead - units].astype(BF16)
        both = both[:, lead - units :]
        both = jnp.concatenate([both[:, 128 * i : 128 * (i + 1)] for i in range(rows // 16)], 0)
    else:
        both = side[...].astype(F32) + came[...].astype(F32)
    side_out[...] = both
    stats = across_rows(both)[:32].astype(BF16)
    stats_out[:, lead : lead + 128] = stats[:16]
    stats_out[:, lead + 128 :] = stats[16:]


def merge_kernel(kept, came, _, sent_out):
    sent_out[...] = (kept[...] + came[...].astype(F32)).astype(BF16)


def activate_kernel(features, text, total, came, side, stats, first_sent, first_came, *refs):
    act_out = refs[-1]
    rows, units = act_out.shape
    lead = stats.shape[1] - 256
    stats = jnp.concatenate([stats[:, lead : lead + 128], stats[:, lead + 128 :]], 0)
    sides = [side[...], across_rows(stats.astype(F32))[:rows]]
    lane = lax.broadcasted_iota(jnp.int32, (rows, 128), 1)
    field = lane % 4
    summed = sides[0] + sides[1]
    add = lambda values, mask: jnp.sum(jnp.where(mask, values, 0.0), -1, keepdims=True)
    centres, measures = lane < 8, (lane >= 16) & (lane < 24)
    average = (
        add(summed, centres & (field == 0)) * features + add(summed, measures & (field < 2))
    ) / D
    spread = add(summed, measures & (field >= 2))
    aparts = []
    for side in sides:
        apart = jnp.where(centres, side - average, 0.0)
        for core in range(2):
            off = add(apart, lane == 4 * core)
            own = lane // 4 == 4 + core
            spread = spread + off * (2.0 * add(side, own & (field < 2)) + features * off)
        aparts.append(apart)
    scale = lax.rsqrt(spread / D + norm_eps)
    of_text = jnp.where(text[...] > 0.5, 1, 0)
    mine = centres & (lane % 2 == of_text)
    packed, shift = None, 0
    for apart in aparts:
        factor = jnp.where(mine, jnp.where(field < 2, apart * scale, 1.0), 0.0)
        high = factor.astype(BF16).astype(F32)
        for part in (high, high, factor - high, factor - high):
            part = pltpu.roll(part, shift, 1) if shift else part
            packed = part if packed is None else packed + part
            shift += 8
    packed = packed[:, :64].astype(BF16)
    own, other = first_sent[:, :units], first_came[:, :units]
    factors = jnp.concatenate([own, own, other, other], 0)
    for t in range(0, units, TILE):
        columns = slice(t, t + TILE)
        pre = total[:rows, columns].astype(F32) + came[:rows, columns].astype(F32)
        extra = jnp.dot(packed, factors[:, columns], preferred_element_type=F32)
        act_out[:, columns] = jax.nn.gelu(pre * scale + extra, approximate=True).astype(BF16)


def contract_own_kernel(k, act, w, mine, chip, other, out, *ends_out):
    core = lax.axis_index("narrow") % 2
    units = w.shape[0] // 2
    rows = pl.ds(pl.multiple_of(core * units, 128), units)
    out[...] = jnp.dot(act[...], w[rows, :], preferred_element_type=F32)
    if k == 0:
        units = w.shape[0] // 2
        ends = slice(units, units + 128)
        total = chip[:, ends].astype(F32) + other[:, ends].astype(F32)
        total = total[:8] + total[8:]
        total = total + pltpu.roll(total, 4, 0)
        own = mine[...].astype(F32)
        own = own[:8] + own[8:]
        own = own + pltpu.roll(own, 4, 0)
        ends_out[0][...] = jnp.concatenate([total, own, jnp.zeros((112, 128), F32)], 0).T


def contract_other_kernel(k, place, act, so_far, w, *outs):
    core = lax.axis_index("narrow") % 2
    units = w.shape[0] // 2
    rows = pl.ds(pl.multiple_of((1 - core) * units, 128), units)
    total = so_far[...] + jnp.dot(act[...], w[rows, :], preferred_element_type=F32)
    spread = jnp.dot(place[...], total.astype(BF16), preferred_element_type=F32).astype(BF16)
    size = size_of(k)
    for s in range(4):
        outs[s][...] = spread[s * size : (s + 1) * size]


def finish_kernel(slots, hidden, mod, out_weight, ends, *refs):
    pieces, (layer_out, bundle_out) = refs[: 4 * CHUNKS], refs[4 * CHUNKS :]
    result = jnp.zeros(hidden.shape, F32)
    for k in range(CHUNKS):
        total = pieces[4 * k][...].astype(F32)
        for s in (1, 2, 3):
            total = total + pieces[4 * k + s][...].astype(F32)
        total = jnp.concatenate([total] * (CAP // size_of(k)), 0)
        result = jnp.where(slots[:, 2 + k : 3 + k] > 0.5, total, result)
    gate = jnp.where(slots[:, 1:2] > 0.5, mod[5:6, :], mod[2:3, :])
    layer = hidden[...].astype(F32) + gate * result
    layer = jnp.where(slots[:, 0:1] > 0.5, layer, 0.0).astype(BF16)
    layer_out[...] = layer
    x = layer.astype(F32)
    centre = jnp.sum(x, -1, keepdims=True) / x.shape[1]
    ones = jnp.ones((8, x.shape[1]), BF16)
    across = lambda left, right: lax.dot_general(
        left, right, (((1,), (1,)), ((), ())), preferred_element_type=F32
    )
    high, low = high_low(x * x)
    total, square = across(ones, layer), across(ones, high) + across(ones, low)
    width = out_weight.shape[0]
    product = across(out_weight[...], ((x - centre) * (1.0 + mod[7:8, :])).astype(BF16))
    bundle_out[:width, :] = product + total[0:1] / x.shape[1] * ends[:width, 8:9]
    row = lax.broadcasted_iota(jnp.int32, (8, CAP), 0)
    bundle_out[width:, :] = jnp.where(row == 0, total, square)


def write_kernel(layer, out):
    out[...] = layer[...]


def add_kernel(left, right, out):
    out[...] = left[...] + right[...]


def noise_kernel(step, alphas, video, latent, _, out):
    index = lax.broadcasted_iota(jnp.int32, (8, 128), 0) * 128 + lax.broadcasted_iota(
        jnp.int32, (8, 128), 1
    )
    alpha = jnp.sum(
        jnp.sum(jnp.where(index == step[...], alphas[...], 0.0), 0, keepdims=True),
        1,
        keepdims=True,
    )
    width = latent.shape[0]
    out[:width, :] = jnp.where(video[0:1] > 0.5, jnp.sqrt(alpha) * latent[...], 0.0)
    out[width:, :] = jnp.where(video[...] > 0.5, jnp.sqrt(1.0 - alpha), 0.0)


def latent_kernel(noise, ends, mine, other_y, other, mine_y, out):
    width = out.shape[0]
    factor = noise[width : width + 1]

    def velocity(total):
        average = total[width : width + 1] / D
        variance = total[width + 1 : width + 2] / D - average * average
        return (total[:width] - average * ends[:width, 0:1]) * lax.rsqrt(
            variance + norm_eps
        ) + ends[:width, 1:2]

    first = lax.axis_index("cfg") == 0
    guided = velocity(mine[...] + mine_y[...]) * jnp.where(first, guidance, 1.0 - guidance)
    guided = guided + velocity(other[...] + other_y[...]) * jnp.where(
        first, 1.0 - guidance, guidance
    )
    guided = jnp.where(factor > 0.0, guided, 0.0)
    out[...] = noise[:width] - factor * guided


def alpha_constant():
    ends = np.sqrt(np.float64(0.00085)), np.sqrt(np.float64(0.012))
    betas = np.linspace(ends[0], ends[1], 1000, dtype=np.float64) ** 2
    return np.pad(np.cumprod(1.0 - betas), (0, 24)).astype(np.float32).reshape(8, 128)


def call(kernel, outs, args, spaces, scratch=(), weight=1):
    kinds = {"v": pltpu.VMEM, "s": pltpu.SMEM, "a": pl.ANY}
    return pl.pallas_call(
        kernel,
        out_shape=[jax.ShapeDtypeStruct(shape, dtype) for shape, dtype in outs],
        in_specs=[pl.BlockSpec(memory_space=kinds[letter]) for letter in spaces],
        out_specs=[pl.BlockSpec(memory_space=pltpu.VMEM) for _ in outs],
        scratch_shapes=list(scratch),
        compiler_params=pltpu.CompilerParams(vmem_limit_bytes=24 * 2**20),
        cost_estimate=pl.CostEstimate(flops=weight, bytes_accessed=1, transcendentals=0),
    )(*args)


def four_blocks(
    hidden, split_table, modulation, expand_weight, contract_weight, output_weight, latent, timestep
):
    hidden = hidden[0]
    features = hidden.shape[1]
    units = expand_weight.shape[1] // 2
    width = output_weight.shape[1]
    payload = units + 128

    in_place = lambda array: pltpu.with_memory_space_constraint(array, pltpu.HBM)
    tokens, piece = call(
        take_kernel,
        [(hidden.shape, BF16), ((QUOTAS[1], features), BF16)],
        [in_place(hidden)],
        "a",
        [pltpu.SemaphoreType.DMA((2,))],
    )
    across = swap(piece, "wide", 2, 4)
    near = swap(tokens, "wide", 1, 4)

    tiles = units // TILE
    chunks = range(CHUNKS)
    made = call(
        prepare_kernel,
        [((size_of(k), features), BF16) for k in chunks[1:]]
        + [((2 * size_of(k), 4 * QUOTAS[k + 1]), BF16) for k in chunks]
        + [((4 * size_of(k), 2 * size_of(k)), BF16) for k in chunks]
        + [((2 * size_of(k), 128), F32) for k in chunks]
        + [
            ((features, units), BF16),
            ((features, units), BF16),
            (modulation.shape, F32),
            ((width, features), BF16),
            ((16, features), BF16),
            ((16, 128), BF16),
            ((CAP, 128), F32),
            ((8, CAP), F32),
            ((8, 128), jnp.int32),
        ],
        [
            in_place(split_table),
            timestep,
            tokens,
            in_place(modulation),
            in_place(output_weight.T),
            in_place(expand_weight),
        ],
        "asvaaa",
        [
            pltpu.SMEM(split_table.shape, jnp.int32),
            pltpu.SemaphoreType.DMA((2, tiles)),
            pltpu.SemaphoreType.DMA((3,)),
        ],
    )
    later, made = made[: CHUNKS - 1], made[CHUNKS - 1 :]
    gathers, made = made[:CHUNKS], made[CHUNKS:]
    spreads, made = made[:CHUNKS], made[CHUNKS:]
    texts, made = made[:CHUNKS], made[CHUNKS:]
    held_sent, held_kept, mod, out_weight, rows_in, ends_mine, slots, video, step = made
    later = [swap(piece, "wide", 2, 4) for piece in later]
    (across,) = call(pass_kernel, [(across.shape, BF16)], [across, slots], "va")
    far = [across, swap(across, "wide", 1, 4)]

    merged = []
    before = []
    for k in chunks:
        rows = 2 * size_of(k)
        extra = 16 if k == 0 else 0
        z, sent, side = call(
            functools.partial(expand_sent_kernel, k),
            [
                ((rows + extra, features), BF16),
                ((rows, units), BF16),
                ((16, payload + 8 * rows) if k == 0 else (rows, 128), BF16),
            ],
            [texts[k], mod, gathers[k], tokens, near, *far, held_sent, rows_in, ends_mine, *before],
            "vvvvv" + "v" * len(far) + "vvv" + "a" * len(before),
            weight=LONG,
        )
        side_came, came = [swap(array, "narrow", 1, 4) for array in (side, sent)]
        kept, *sums_made = call(
            functools.partial(expand_kept_kernel, k),
            [((rows, units), F32)] + ([((16, units), BF16)] if k == 0 else []),
            [z, held_kept, sent, side],
            "vvaa",
            weight=LONG,
        )
        side, stats = call(
            functools.partial(stats_kernel, k, rows),
            [((rows, 128), F32), ((16, 256 + (payload if k == 0 else 0)), BF16)],
            [side, side_came, *sums_made],
            "vv" + "v" * len(sums_made),
        )
        stats_came = swap(stats, "narrow", 2, 4)
        (sent,) = call(merge_kernel, [((rows, units), BF16)], [kept, came, stats], "vva")
        if k + 1 < CHUNKS:
            (across,) = call(
                pass_kernel, [(later[k].shape, BF16)], [later[k], sent], "va"
            )
            far.extend([across, swap(across, "wide", 1, 4)])
        if k == 0:
            (held_out,) = call(
                hold_kernel,
                [(contract_weight.shape, BF16)],
                [in_place(contract_weight), across, stats],
                "aaa",
                [pltpu.SemaphoreType.DMA((4,))],
                weight=LONG,
            )
        if k == 0:
            (noise,) = call(
                noise_kernel,
                [((width + 8, CAP), F32)],
                [step, alpha_constant(), video, latent.T, sent],
                "vvvva",
                weight=LONG,
            )
        before = [sent, noise, held_out]
        came = swap(sent, "narrow", 2, 4)
        merged.append((sent, stats, [sent, came, side, stats_came]))

    returned = []
    before = []
    first = [merged[0][1], merged[0][2][3]]
    for k in chunks:
        rows = 2 * size_of(k)
        if k + 1 < CHUNKS:
            before = before + [merged[k + 1][0], merged[k + 1][1]]
        (act,) = call(
            functools.partial(activate_kernel, features),
            [((rows, units), BF16)],
            [texts[k], *merged[k][2], *first, *before],
            "vvvvvvv" + "a" * len(before),
        )
        act_came = swap(act, "narrow", 1, 4)
        out, *ends_made = call(
            functools.partial(contract_own_kernel, k),
            [((rows, features), F32)] + ([((128, 128), F32)] if k == 0 else []),
            [act, held_out, ends_mine, *first],
            "vvvvv",
            weight=LONG,
        )
        ends = ends_made[0] if k == 0 else ends
        pieces = call(
            functools.partial(contract_other_kernel, k),
            [((size_of(k), features), BF16)] * 4,
            [spreads[k], act_came, out, held_out],
            "vvvv",
        )
        before = pieces
        distances = (3, 2, 1) if k + 1 < CHUNKS else (3, 2, 1)
        returned += [pieces[0], *(swap(pieces[s], "wide", s, 4) for s in distances)]

    layer, bundle = call(
        finish_kernel,
        [((CAP, features), BF16), ((width + 8, CAP), F32)],
        [slots, tokens, mod, out_weight, ends, *returned],
        "v" * (5 + len(returned)),
    )
    (layer_out,) = call(write_kernel, [((CAP, features), BF16)], [layer], "v", weight=LONG)
    (bundle,) = call(
        add_kernel, [((width + 8, CAP), F32)], [bundle, swap(bundle, "narrow", 1, 4)], "vv"
    )
    (clean_latent,) = call(
        latent_kernel,
        [((width, CAP), F32)],
        [noise, ends, bundle] + [swap(bundle, ("cfg", "narrow"), n, 8) for n in (6, 4, 2)],
        "vvvvvv",
    )
    return (layer_out[None], clean_latent.T)


def solution(mesh):
    by_swaps = (mesh.shape["wide"], mesh.shape["narrow"], mesh.shape["cfg"]) == (4, 4, 2)
    return jax.shard_map(
        four_blocks if by_swaps else any_slice,
        mesh=mesh,
        in_specs=(
            P("cfg", "wide", "narrow"),
            P(),
            P(None, "narrow"),
            P("narrow", "wide"),
            P("wide", "narrow"),
            P("narrow", None),
            P("wide", None),
            P(),
        ),
        out_specs=(P("cfg", "wide", "narrow"), P("wide", None)),
        check_vma=False,
    )
```

```python
import functools

import jax
import jax.numpy as jnp
import numpy as np
from jax import lax
from jax.experimental import pallas as pl
from jax.experimental.pallas import tpu as pltpu
from jax.sharding import PartitionSpec as P

D = 3072
TEXT = 226


norm_eps = 1e-05
guidance = 6.0


def alpha_table():
    steps_index = jnp.arange(1000, dtype=jnp.int32)
    start_root = 0.00085**0.5
    end_root = 0.012**0.5
    roots = start_root + (end_root - start_root) * steps_index.astype(jnp.float32) / 999.0
    return (steps_index, jnp.cumprod(1.0 - roots * roots))


def feature_norm(values, shifts, scaling):
    totals, squares = lax.psum(
        (jnp.sum(values, -1, keepdims=True), jnp.sum(values * values, -1, keepdims=True)), "narrow"
    )
    average = totals / D
    variance = squares / D - average * average
    return (values - average) * lax.rsqrt(variance + norm_eps) * (1.0 + scaling) + shifts


def any_slice(
    hidden, split_table, modulation, expand_weight, contract_weight, output_weight, latent, timestep
):
    capacity = hidden.shape[1]
    wide_index = lax.axis_index("wide")
    table_index = jnp.arange(split_table.shape[0], dtype=jnp.int32)
    offset = jnp.sum(jnp.where(table_index < wide_index, split_table, 0))
    own_count = jnp.sum(jnp.where(table_index == wide_index, split_table, 0))
    slot_index = jnp.arange(capacity, dtype=jnp.int32)
    position = offset + slot_index
    slot_live = slot_index < own_count
    is_text = slot_live & (position < TEXT)
    is_video = slot_live & (position >= TEXT)
    text_column = is_text[:, None]
    shifts = jnp.where(text_column, modulation[3], modulation[0])
    scaling = jnp.where(text_column, modulation[4], modulation[1])
    gating = jnp.where(text_column, modulation[5], modulation[2])
    values = hidden[0].astype(jnp.float32)
    normed = feature_norm(values, shifts, scaling).astype(jnp.bfloat16)
    hidden_part = jnp.dot(
        lax.all_gather(normed, "wide", axis=0, tiled=True),
        expand_weight,
        preferred_element_type=jnp.float32,
    )
    hidden_pre = lax.psum(hidden_part, "narrow")
    activated = jax.nn.gelu(hidden_pre, approximate=True).astype(jnp.bfloat16)
    ff_result = lax.psum_scatter(
        jnp.dot(activated, contract_weight, preferred_element_type=jnp.float32),
        "wide",
        scatter_dimension=0,
        tiled=True,
    )
    layer_out = jnp.where(slot_live[:, None], values + gating * ff_result, 0.0).astype(jnp.bfloat16)
    final_in = layer_out.astype(jnp.float32)
    final_normed = feature_norm(final_in, modulation[6], modulation[7]).astype(jnp.bfloat16)
    velocity_part = jnp.dot(final_normed, output_weight, preferred_element_type=jnp.float32)
    copy_weight = jnp.where(lax.axis_index("cfg") == 0, guidance, 1.0 - guidance)
    guided = lax.psum(velocity_part * copy_weight, ("cfg", "narrow"))
    steps_index, alpha_bar = alpha_table()
    alpha_now = jnp.sum(jnp.where(steps_index == timestep[0], alpha_bar, 0.0))
    clean_latent = jnp.where(
        is_video[:, None], jnp.sqrt(alpha_now) * latent - jnp.sqrt(1.0 - alpha_now) * guided, 0.0
    )
    return (layer_out[None], clean_latent)


QUOTAS = (0, 64, 128)
CAP = 128
CHUNKS = len(QUOTAS) - 1
F32, BF16 = jnp.float32, jnp.bfloat16
TILE = 512
LONG = 10**10


def size_of(k):
    return QUOTAS[k + 1] - QUOTAS[k]


def swap(array, axis, distance, size):
    return lax.ppermute(array, axis, [(i, i ^ distance) for i in range(size)])


def z_swaps(array):
    return [swap(array, "wide", s, 4) for s in (1, 2, 3)]


def choose(values, index):
    out = values[0]
    for i in range(1, 4):
        out = jnp.where(index == i, values[i], out)
    return out


def layout(table):
    counts = [table[b] for b in range(4)]
    largest = jnp.int32(3)
    for b in (2, 1, 0):
        largest = jnp.where(counts[b] == CAP, b, largest)
    starts, others, ranks, offsets = [], [], [], []
    rank, offset = jnp.int32(0), jnp.int32(0)
    for b in range(4):
        other = jnp.where(largest == b, 0, 1)
        ranks.append(rank * other)
        others.append(other)
        offsets.append(offset)
        rank = rank + other * counts[b]
        offset = offset + counts[b]
    block = lax.axis_index("wide")
    of = lambda values: [choose(values, jnp.bitwise_xor(block, s)) for s in range(4)]
    return of(ranks), of(counts), of(others), of(offsets)[0], choose(offsets, largest)


def high_low(values):
    high = values.astype(BF16)
    return high, (values - high.astype(F32)).astype(BF16)


def load(source, place, sems):
    parts = sems.shape[0]
    height = source.shape[0] // parts
    copies = []
    for t in range(parts):
        rows = pl.ds(t * height, height)
        copies.append(pltpu.make_async_copy(source.at[rows, :], place.at[rows, :], sems.at[t]))
        copies[-1].start()
    return copies


def load_half(source, half, place, sems):
    width = place.shape[1]
    copies = []
    for t in range(0, width, TILE):
        columns = pl.ds(pl.multiple_of(half * width + t, 128), TILE)
        copies.append(
            pltpu.make_async_copy(
                source.at[:, columns], place.at[:, pl.ds(t, TILE)], sems.at[len(copies)]
            )
        )
        copies[-1].start()
    return copies


def rows_of(parts, core):
    total = parts[:8] + parts[8:]
    total = jnp.where(core == 0, total, pltpu.roll(total, 4, 0))
    high, low = high_low(total)
    return jnp.concatenate([high.astype(F32), low.astype(F32)], 0).astype(BF16)


def hold_kernel(source, *refs):
    place, sems = refs[-2:]
    for copy in load(source, place, sems):
        copy.wait()


def text_rows(k, largest_offset):
    size = size_of(k)
    row = lax.broadcasted_iota(jnp.int32, (2 * size, 1), 0)
    rank = jnp.where(row < size, row, row - size) + QUOTAS[k]
    position = jnp.where(
        row < size, rank + largest_offset, jnp.where(rank < largest_offset, rank, rank + CAP)
    )
    return position < TEXT


def gather_matrix(k, ranks, counts, others):
    size = size_of(k)
    places = []
    for p in range(k + 1):
        piece = size_of(p)
        lane = lax.broadcasted_iota(jnp.int32, (1, 4 * piece), 1)
        which, slot = lane // piece, lane % piece + QUOTAS[p]
        rank = slot + choose(ranks, which) - QUOTAS[k]
        live = (rank >= 0) & (rank < size) & (slot < choose(counts, which))
        row = jnp.where(live, rank + choose(others, which) * size, -1)
        at = lax.broadcasted_iota(jnp.int32, (2 * size, 4 * piece), 0)
        places.append(jnp.where(at == row, 1.0, 0.0).astype(BF16))
    return jnp.concatenate(places, 1)


def spread_matrix(k, ranks, counts, others):
    size = size_of(k)
    places = []
    for s in range(4):
        first = jnp.maximum(QUOTAS[k] - ranks[s], 0)
        last = jnp.minimum(counts[s], QUOTAS[k + 1] - ranks[s])
        index = lax.broadcasted_iota(jnp.int32, (size, 1), 0)
        slot = first + jnp.bitwise_and(index - first, size - 1)
        row = jnp.where(slot < last, slot + ranks[s] - QUOTAS[k] + others[s] * size, -1)
        at = lax.broadcasted_iota(jnp.int32, (size, 2 * size), 1)
        places.append(jnp.where(at == row, 1.0, 0.0).astype(BF16))
    return jnp.concatenate(places, 0)


def take_kernel(source, piece, sem):
    copy = pltpu.make_async_copy(source.at[pl.ds(0, piece.shape[0]), :], piece, sem)
    copy.start()
    copy.wait()


def prepare_kernel(table_in, timestep, tokens_in, mod_in, out_weight, w, *refs):
    later, refs = refs[: CHUNKS - 1], refs[CHUNKS - 1 :]
    gathers, refs = refs[:CHUNKS], refs[CHUNKS:]
    spreads, refs = refs[:CHUNKS], refs[CHUNKS:]
    texts, refs = refs[:CHUNKS], refs[CHUNKS:]
    held, kept, tokens, mod, weight, rows_out, ends_out, slots_out, video_out, step_out = refs[:10]
    table, sems, small = refs[10:]
    step_out[...] = jnp.full(step_out.shape, timestep[0], jnp.int32)
    core = lax.axis_index("narrow") % 2
    sources = (table_in, mod_in, out_weight, tokens_in)
    copies = [
        pltpu.make_async_copy(source, place, small.at[i])
        for i, (source, place) in enumerate(zip(sources, (table, mod, weight, tokens)))
    ]
    for copy in copies:
        copy.start()
    big = load_half(w, 1 - core, held, sems.at[0]) + load_half(w, core, kept, sems.at[1])

    copies[0].wait()
    ranks, counts, others, offset, largest_offset = layout(table)
    for k in range(CHUNKS):
        gathers[k][...] = gather_matrix(k, ranks, counts, others)
        spreads[k][...] = spread_matrix(k, ranks, counts, others)
        text = jnp.where(text_rows(k, largest_offset), 1.0, 0.0)
        texts[k][...] = jnp.broadcast_to(text, texts[k].shape)
    slot = lax.broadcasted_iota(jnp.int32, (CAP, 128), 0)
    lane = lax.broadcasted_iota(jnp.int32, (CAP, 128), 1)
    rank = slot + ranks[0]
    flag = lambda condition: jnp.where(condition, 1.0, 0.0)
    kind = jnp.where(lane == 0, flag(slot < counts[0]), flag(slot + offset < TEXT))
    for k in range(CHUNKS):
        kind = jnp.where(
            lane == 2 + k, flag((rank >= QUOTAS[k]) & (rank < QUOTAS[k + 1])), kind
        )
    slots_out[...] = kind
    slot = lax.broadcasted_iota(jnp.int32, (8, CAP), 1)
    video_out[...] = jnp.where((slot < counts[0]) & (slot + offset >= TEXT), 1.0, 0.0)

    copies[1].wait()
    row = lax.broadcasted_iota(jnp.int32, (8, 1), 0)
    rows = jnp.where(row == 0, 1.0 + mod[1:2, :], jnp.zeros((8, 1), F32))
    rows = jnp.where(row == 1, 1.0 + mod[4:5, :], rows)
    rows = jnp.where(row == 2, mod[0:1, :], rows)
    rows = jnp.where(row == 3, mod[3:4, :], rows)
    rows_out[...] = jnp.concatenate(high_low(rows), 0)
    rows = jnp.where(row == 0, 1.0 + mod[7:8, :], jnp.zeros((8, 1), F32))
    rows = jnp.where(row == 1, mod[6:7, :], rows)
    copies[2].wait()
    ends = lax.dot_general(
        jnp.concatenate(high_low(rows), 0),
        weight[...],
        (((1,), (1,)), ((), ())),
        preferred_element_type=F32,
    )
    ends = rows_of(ends, core)
    ends_out[...] = jnp.concatenate([ends, jnp.zeros((16, 128 - ends.shape[1]), BF16)], 1)
    copies[3].wait()
    for k in range(1, CHUNKS):
        later[k - 1][...] = tokens[QUOTAS[k] : QUOTAS[k + 1], :]
    for copy in big:
        copy.wait()


def expand_sent_kernel(k, text, mod, place, own, near, *refs):
    far, (w, sums, ends) = refs[: 2 * (k + 1)], refs[2 * (k + 1) : 2 * (k + 1) + 3]
    z_out, sent_out, side_out = refs[-3:]
    core = lax.axis_index("narrow") % 2
    units = w.shape[1]
    rows = place.shape[0]
    pieces = []
    for p in range(k + 1):
        of_chunk = slice(QUOTAS[p], QUOTAS[p + 1])
        pieces += [own[of_chunk, :], near[of_chunk, :], far[2 * p][...], far[2 * p + 1][...]]
    tokens = jnp.concatenate(pieces, 0)
    x = jnp.dot(place[...], tokens, preferred_element_type=F32)
    centre = (jnp.sum(x, -1, keepdims=True) / x.shape[1]).astype(BF16).astype(F32)
    x = x - centre
    z = (x * (1.0 + jnp.where(text[:, :1] > 0.5, mod[4:5, :], mod[1:2, :]))).astype(BF16)
    if k == 0:
        z = jnp.concatenate([z, sums[...]], 0)
    z_out[...] = z
    if k == 0:
        lead = side_out.shape[1] - 8 * 128
        side_out[:, units:lead] = ends[...]
    for t in range(0, units, TILE):
        columns = slice(t, t + TILE)
        product = jnp.dot(z, w[:, columns], preferred_element_type=F32)
        sent_out[:, columns] = product[:rows].astype(BF16)
        if k == 0:
            side_out[:, columns] = rows_of(product[rows:], core)
    total = jnp.sum(x, -1, keepdims=True)
    square = jnp.sum(x * x, -1, keepdims=True)
    total_high = total.astype(BF16).astype(F32)
    square_high = square.astype(BF16).astype(F32)
    lane = lax.broadcasted_iota(jnp.int32, (rows, 128), 1) - 4 * core
    side = jnp.where((lane == 0) | (lane == 1), centre, 0.0)
    side = jnp.where(lane == 16, total_high, side)
    side = jnp.where(lane == 17, total - total_high, side)
    side = jnp.where(lane == 18, square_high, side)
    side = jnp.where(lane == 19, square - square_high, side).astype(BF16)
    if k == 0:
        for i in range(rows // 16):
            side_out[:, lead + 128 * i : lead + 128 * (i + 1)] = side[16 * i : 16 * (i + 1)]
    else:
        side_out[...] = side


def expand_kept_kernel(k, z, w, _, __, *refs):
    kept_out = refs[-1 if k else -2]
    core = lax.axis_index("narrow") % 2
    rows = kept_out.shape[0]
    for t in range(0, w.shape[1], TILE):
        columns = slice(t, t + TILE)
        product = jnp.dot(z[...], w[:, columns], preferred_element_type=F32)
        kept_out[:, columns] = product[:rows]
        if k == 0:
            refs[-1][:, columns] = rows_of(product[rows:], core)


def pass_kernel(piece, _, out):
    out[...] = piece[...]


def across_rows(side):
    height = side.shape[0]
    if height < 128:
        side = jnp.concatenate([side, jnp.zeros((128 - height, 128), F32)], 0)
    return side.T


def stats_kernel(k, rows, side, came, *refs):
    side_out, stats_out = refs[-2:]
    lead = stats_out.shape[1] - 256
    if k == 0:
        kept_sums = refs[0]
        units = kept_sums.shape[1]
        stats_out[:, :units] = (kept_sums[...].astype(F32) + came[:, :units].astype(F32)).astype(BF16)
        both = side[:, units:].astype(F32) + came[:, units:].astype(F32)
        stats_out[:, units:lead] = both[:, : lead - units].astype(BF16)
        both = both[:, lead - units :]
        both = jnp.concatenate([both[:, 128 * i : 128 * (i + 1)] for i in range(rows // 16)], 0)
    else:
        both = side[...].astype(F32) + came[...].astype(F32)
    side_out[...] = both
    stats = across_rows(both)[:32].astype(BF16)
    stats_out[:, lead : lead + 128] = stats[:16]
    stats_out[:, lead + 128 :] = stats[16:]


def merge_kernel(kept, came, _, sent_out):
    sent_out[...] = (kept[...] + came[...].astype(F32)).astype(BF16)


def activate_kernel(features, text, total, came, side, stats, first_sent, first_came, *refs):
    act_out = refs[-1]
    rows, units = act_out.shape
    lead = stats.shape[1] - 256
    stats = jnp.concatenate([stats[:, lead : lead + 128], stats[:, lead + 128 :]], 0)
    sides = [side[...], across_rows(stats.astype(F32))[:rows]]
    lane = lax.broadcasted_iota(jnp.int32, (rows, 128), 1)
    field = lane % 4
    summed = sides[0] + sides[1]
    add = lambda values, mask: jnp.sum(jnp.where(mask, values, 0.0), -1, keepdims=True)
    centres, measures = lane < 8, (lane >= 16) & (lane < 24)
    average = (
        add(summed, centres & (field == 0)) * features + add(summed, measures & (field < 2))
    ) / D
    spread = add(summed, measures & (field >= 2))
    aparts = []
    for side in sides:
        apart = jnp.where(centres, side - average, 0.0)
        for core in range(2):
            off = add(apart, lane == 4 * core)
            own = lane // 4 == 4 + core
            spread = spread + off * (2.0 * add(side, own & (field < 2)) + features * off)
        aparts.append(apart)
    scale = lax.rsqrt(spread / D + norm_eps)
    of_text = jnp.where(text[...] > 0.5, 1, 0)
    mine = centres & (lane % 2 == of_text)
    packed, shift = None, 0
    for apart in aparts:
        factor = jnp.where(mine, jnp.where(field < 2, apart * scale, 1.0), 0.0)
        high = factor.astype(BF16).astype(F32)
        for part in (high, high, factor - high, factor - high):
            part = pltpu.roll(part, shift, 1) if shift else part
            packed = part if packed is None else packed + part
            shift += 8
    packed = packed[:, :64].astype(BF16)
    own, other = first_sent[:, :units], first_came[:, :units]
    factors = jnp.concatenate([own, own, other, other], 0)
    for t in range(0, units, TILE):
        columns = slice(t, t + TILE)
        pre = total[:rows, columns].astype(F32) + came[:rows, columns].astype(F32)
        extra = jnp.dot(packed, factors[:, columns], preferred_element_type=F32)
        act_out[:, columns] = jax.nn.gelu(pre * scale + extra, approximate=True).astype(BF16)


def contract_own_kernel(k, act, w, mine, chip, other, out, *ends_out):
    core = lax.axis_index("narrow") % 2
    units = w.shape[0] // 2
    rows = pl.ds(pl.multiple_of(core * units, 128), units)
    out[...] = jnp.dot(act[...], w[rows, :], preferred_element_type=F32)
    if k == 0:
        units = w.shape[0] // 2
        ends = slice(units, units + 128)
        total = chip[:, ends].astype(F32) + other[:, ends].astype(F32)
        total = total[:8] + total[8:]
        total = total + pltpu.roll(total, 4, 0)
        own = mine[...].astype(F32)
        own = own[:8] + own[8:]
        own = own + pltpu.roll(own, 4, 0)
        ends_out[0][...] = jnp.concatenate([total, own, jnp.zeros((112, 128), F32)], 0).T


def contract_other_kernel(k, place, act, so_far, w, *outs):
    core = lax.axis_index("narrow") % 2
    units = w.shape[0] // 2
    rows = pl.ds(pl.multiple_of((1 - core) * units, 128), units)
    total = so_far[...] + jnp.dot(act[...], w[rows, :], preferred_element_type=F32)
    spread = jnp.dot(place[...], total.astype(BF16), preferred_element_type=F32).astype(BF16)
    size = size_of(k)
    for s in range(4):
        outs[s][...] = spread[s * size : (s + 1) * size]


def finish_kernel(slots, hidden, mod, out_weight, ends, *refs):
    pieces, (layer_out, bundle_out) = refs[: 4 * CHUNKS], refs[4 * CHUNKS :]
    result = jnp.zeros(hidden.shape, F32)
    for k in range(CHUNKS):
        total = pieces[4 * k][...].astype(F32)
        for s in (1, 2, 3):
            total = total + pieces[4 * k + s][...].astype(F32)
        total = jnp.concatenate([total] * (CAP // size_of(k)), 0)
        result = jnp.where(slots[:, 2 + k : 3 + k] > 0.5, total, result)
    gate = jnp.where(slots[:, 1:2] > 0.5, mod[5:6, :], mod[2:3, :])
    layer = hidden[...].astype(F32) + gate * result
    layer = jnp.where(slots[:, 0:1] > 0.5, layer, 0.0).astype(BF16)
    layer_out[...] = layer
    x = layer.astype(F32)
    centre = jnp.sum(x, -1, keepdims=True) / x.shape[1]
    ones = jnp.ones((8, x.shape[1]), BF16)
    across = lambda left, right: lax.dot_general(
        left, right, (((1,), (1,)), ((), ())), preferred_element_type=F32
    )
    high, low = high_low(x * x)
    total, square = across(ones, layer), across(ones, high) + across(ones, low)
    width = out_weight.shape[0]
    product = across(out_weight[...], ((x - centre) * (1.0 + mod[7:8, :])).astype(BF16))
    bundle_out[:width, :] = product + total[0:1] / x.shape[1] * ends[:width, 8:9]
    row = lax.broadcasted_iota(jnp.int32, (8, CAP), 0)
    bundle_out[width:, :] = jnp.where(row == 0, total, square)


def write_kernel(layer, out):
    out[...] = layer[...]


def add_kernel(left, right, out):
    out[...] = left[...] + right[...]


def noise_kernel(step, alphas, video, latent, _, out):
    index = lax.broadcasted_iota(jnp.int32, (8, 128), 0) * 128 + lax.broadcasted_iota(
        jnp.int32, (8, 128), 1
    )
    alpha = jnp.sum(
        jnp.sum(jnp.where(index == step[...], alphas[...], 0.0), 0, keepdims=True),
        1,
        keepdims=True,
    )
    width = latent.shape[0]
    out[:width, :] = jnp.where(video[0:1] > 0.5, jnp.sqrt(alpha) * latent[...], 0.0)
    out[width:, :] = jnp.where(video[...] > 0.5, jnp.sqrt(1.0 - alpha), 0.0)


def latent_kernel(noise, ends, mine, other_y, other, mine_y, out):
    width = out.shape[0]
    factor = noise[width : width + 1]

    def velocity(total):
        average = total[width : width + 1] / D
        variance = total[width + 1 : width + 2] / D - average * average
        return (total[:width] - average * ends[:width, 0:1]) * lax.rsqrt(
            variance + norm_eps
        ) + ends[:width, 1:2]

    first = lax.axis_index("cfg") == 0
    guided = velocity(mine[...] + mine_y[...]) * jnp.where(first, guidance, 1.0 - guidance)
    guided = guided + velocity(other[...] + other_y[...]) * jnp.where(
        first, 1.0 - guidance, guidance
    )
    guided = jnp.where(factor > 0.0, guided, 0.0)
    out[...] = noise[:width] - factor * guided


def alpha_constant():
    ends = np.sqrt(np.float64(0.00085)), np.sqrt(np.float64(0.012))
    betas = np.linspace(ends[0], ends[1], 1000, dtype=np.float64) ** 2
    return np.pad(np.cumprod(1.0 - betas), (0, 24)).astype(np.float32).reshape(8, 128)


def call(kernel, outs, args, spaces, scratch=(), weight=1):
    kinds = {"v": pltpu.VMEM, "s": pltpu.SMEM, "a": pl.ANY}
    return pl.pallas_call(
        kernel,
        out_shape=[jax.ShapeDtypeStruct(shape, dtype) for shape, dtype in outs],
        in_specs=[pl.BlockSpec(memory_space=kinds[letter]) for letter in spaces],
        out_specs=[pl.BlockSpec(memory_space=pltpu.VMEM) for _ in outs],
        scratch_shapes=list(scratch),
        compiler_params=pltpu.CompilerParams(vmem_limit_bytes=24 * 2**20),
        cost_estimate=pl.CostEstimate(flops=weight, bytes_accessed=1, transcendentals=0),
    )(*args)


def four_blocks(
    hidden, split_table, modulation, expand_weight, contract_weight, output_weight, latent, timestep
):
    hidden = hidden[0]
    features = hidden.shape[1]
    units = expand_weight.shape[1] // 2
    width = output_weight.shape[1]
    payload = units + 128

    in_place = lambda array: pltpu.with_memory_space_constraint(array, pltpu.HBM)
    (piece,) = call(
        take_kernel,
        [((QUOTAS[1], features), BF16)],
        [in_place(hidden)],
        "a",
        [pltpu.SemaphoreType.DMA(())],
    )
    across = swap(piece, "wide", 2, 4)
    near = swap(hidden, "wide", 1, 4)

    tiles = units // TILE
    chunks = range(CHUNKS)
    made = call(
        prepare_kernel,
        [((size_of(k), features), BF16) for k in chunks[1:]]
        + [((2 * size_of(k), 4 * QUOTAS[k + 1]), BF16) for k in chunks]
        + [((4 * size_of(k), 2 * size_of(k)), BF16) for k in chunks]
        + [((2 * size_of(k), 128), F32) for k in chunks]
        + [
            ((features, units), BF16),
            ((features, units), BF16),
            (hidden.shape, BF16),
            (modulation.shape, F32),
            ((width, features), BF16),
            ((16, features), BF16),
            ((16, 128), BF16),
            ((CAP, 128), F32),
            ((8, CAP), F32),
            ((8, 128), jnp.int32),
        ],
        [
            in_place(split_table),
            timestep,
            in_place(hidden),
            in_place(modulation),
            in_place(output_weight.T),
            in_place(expand_weight),
        ],
        "asaaaa",
        [
            pltpu.SMEM(split_table.shape, jnp.int32),
            pltpu.SemaphoreType.DMA((2, tiles)),
            pltpu.SemaphoreType.DMA((4,)),
        ],
    )
    later, made = made[: CHUNKS - 1], made[CHUNKS - 1 :]
    gathers, made = made[:CHUNKS], made[CHUNKS:]
    spreads, made = made[:CHUNKS], made[CHUNKS:]
    texts, made = made[:CHUNKS], made[CHUNKS:]
    held_sent, held_kept, tokens, mod, out_weight, rows_in, ends_mine, slots, video, step = made
    later = [swap(piece, "wide", 2, 4) for piece in later]
    (across,) = call(pass_kernel, [(across.shape, BF16)], [across, slots], "va")
    far = [across, swap(across, "wide", 1, 4)]

    merged = []
    before = []
    for k in chunks:
        rows = 2 * size_of(k)
        extra = 16 if k == 0 else 0
        z, sent, side = call(
            functools.partial(expand_sent_kernel, k),
            [
                ((rows + extra, features), BF16),
                ((rows, units), BF16),
                ((16, payload + 8 * rows) if k == 0 else (rows, 128), BF16),
            ],
            [texts[k], mod, gathers[k], tokens, near, *far, held_sent, rows_in, ends_mine, *before],
            "vvvvv" + "v" * len(far) + "vvv" + "a" * len(before),
            weight=LONG,
        )
        side_came, came = [swap(array, "narrow", 1, 4) for array in (side, sent)]
        kept, *sums_made = call(
            functools.partial(expand_kept_kernel, k),
            [((rows, units), F32)] + ([((16, units), BF16)] if k == 0 else []),
            [z, held_kept, sent, side],
            "vvaa",
            weight=LONG,
        )
        side, stats = call(
            functools.partial(stats_kernel, k, rows),
            [((rows, 128), F32), ((16, 256 + (payload if k == 0 else 0)), BF16)],
            [side, side_came, *sums_made],
            "vv" + "v" * len(sums_made),
        )
        stats_came = swap(stats, "narrow", 2, 4)
        (sent,) = call(merge_kernel, [((rows, units), BF16)], [kept, came, stats], "vva")
        if k + 1 < CHUNKS:
            (across,) = call(
                pass_kernel, [(later[k].shape, BF16)], [later[k], sent], "va"
            )
            far.extend([across, swap(across, "wide", 1, 4)])
        if k == 0:
            (held_out,) = call(
                hold_kernel,
                [(contract_weight.shape, BF16)],
                [in_place(contract_weight), across, stats],
                "aaa",
                [pltpu.SemaphoreType.DMA((4,))],
                weight=LONG,
            )
        if k == 0:
            (noise,) = call(
                noise_kernel,
                [((width + 8, CAP), F32)],
                [step, alpha_constant(), video, latent.T, sent],
                "vvvva",
                weight=LONG,
            )
        before = [sent, noise, held_out]
        came = swap(sent, "narrow", 2, 4)
        merged.append((sent, stats, [sent, came, side, stats_came]))

    returned = []
    before = []
    first = [merged[0][1], merged[0][2][3]]
    for k in chunks:
        rows = 2 * size_of(k)
        if k + 1 < CHUNKS:
            before = before + [merged[k + 1][0], merged[k + 1][1]]
        (act,) = call(
            functools.partial(activate_kernel, features),
            [((rows, units), BF16)],
            [texts[k], *merged[k][2], *first, *before],
            "vvvvvvv" + "a" * len(before),
        )
        act_came = swap(act, "narrow", 1, 4)
        out, *ends_made = call(
            functools.partial(contract_own_kernel, k),
            [((rows, features), F32)] + ([((128, 128), F32)] if k == 0 else []),
            [act, held_out, ends_mine, *first],
            "vvvvv",
            weight=LONG,
        )
        ends = ends_made[0] if k == 0 else ends
        pieces = call(
            functools.partial(contract_other_kernel, k),
            [((size_of(k), features), BF16)] * 4,
            [spreads[k], act_came, out, held_out],
            "vvvv",
        )
        before = pieces
        distances = (3, 2, 1) if k + 1 < CHUNKS else (2, 3, 1)
        returned += [pieces[0], *(swap(pieces[s], "wide", s, 4) for s in distances)]

    layer, bundle = call(
        finish_kernel,
        [((CAP, features), BF16), ((width + 8, CAP), F32)],
        [slots, tokens, mod, out_weight, ends, *returned],
        "v" * (5 + len(returned)),
    )
    (layer_out,) = call(write_kernel, [((CAP, features), BF16)], [layer], "v", weight=LONG)
    (bundle,) = call(
        add_kernel, [((width + 8, CAP), F32)], [bundle, swap(bundle, "narrow", 1, 4)], "vv"
    )
    (clean_latent,) = call(
        latent_kernel,
        [((width, CAP), F32)],
        [noise, ends, bundle] + [swap(bundle, ("cfg", "narrow"), n, 8) for n in (6, 4, 2)],
        "vvvvvv",
    )
    return (layer_out[None], clean_latent.T)


def solution(mesh):
    by_swaps = (mesh.shape["wide"], mesh.shape["narrow"], mesh.shape["cfg"]) == (4, 4, 2)
    return jax.shard_map(
        four_blocks if by_swaps else any_slice,
        mesh=mesh,
        in_specs=(
            P("cfg", "wide", "narrow"),
            P(),
            P(None, "narrow"),
            P("narrow", "wide"),
            P("wide", "narrow"),
            P("narrow", None),
            P("wide", None),
            P(),
        ),
        out_specs=(P("cfg", "wide", "narrow"), P("wide", None)),
        check_vma=False,
    )
```

```python
import functools

import jax
import jax.numpy as jnp
import numpy as np
from jax import lax
from jax.experimental import pallas as pl
from jax.experimental.pallas import tpu as pltpu
from jax.sharding import PartitionSpec as P

D = 3072
TEXT = 226


norm_eps = 1e-05
guidance = 6.0


def alpha_table():
    steps_index = jnp.arange(1000, dtype=jnp.int32)
    start_root = 0.00085**0.5
    end_root = 0.012**0.5
    roots = start_root + (end_root - start_root) * steps_index.astype(jnp.float32) / 999.0
    return (steps_index, jnp.cumprod(1.0 - roots * roots))


def feature_norm(values, shifts, scaling):
    totals, squares = lax.psum(
        (jnp.sum(values, -1, keepdims=True), jnp.sum(values * values, -1, keepdims=True)), "narrow"
    )
    average = totals / D
    variance = squares / D - average * average
    return (values - average) * lax.rsqrt(variance + norm_eps) * (1.0 + scaling) + shifts


def any_slice(
    hidden, split_table, modulation, expand_weight, contract_weight, output_weight, latent, timestep
):
    capacity = hidden.shape[1]
    wide_index = lax.axis_index("wide")
    table_index = jnp.arange(split_table.shape[0], dtype=jnp.int32)
    offset = jnp.sum(jnp.where(table_index < wide_index, split_table, 0))
    own_count = jnp.sum(jnp.where(table_index == wide_index, split_table, 0))
    slot_index = jnp.arange(capacity, dtype=jnp.int32)
    position = offset + slot_index
    slot_live = slot_index < own_count
    is_text = slot_live & (position < TEXT)
    is_video = slot_live & (position >= TEXT)
    text_column = is_text[:, None]
    shifts = jnp.where(text_column, modulation[3], modulation[0])
    scaling = jnp.where(text_column, modulation[4], modulation[1])
    gating = jnp.where(text_column, modulation[5], modulation[2])
    values = hidden[0].astype(jnp.float32)
    normed = feature_norm(values, shifts, scaling).astype(jnp.bfloat16)
    hidden_part = jnp.dot(
        lax.all_gather(normed, "wide", axis=0, tiled=True),
        expand_weight,
        preferred_element_type=jnp.float32,
    )
    hidden_pre = lax.psum(hidden_part, "narrow")
    activated = jax.nn.gelu(hidden_pre, approximate=True).astype(jnp.bfloat16)
    ff_result = lax.psum_scatter(
        jnp.dot(activated, contract_weight, preferred_element_type=jnp.float32),
        "wide",
        scatter_dimension=0,
        tiled=True,
    )
    layer_out = jnp.where(slot_live[:, None], values + gating * ff_result, 0.0).astype(jnp.bfloat16)
    final_in = layer_out.astype(jnp.float32)
    final_normed = feature_norm(final_in, modulation[6], modulation[7]).astype(jnp.bfloat16)
    velocity_part = jnp.dot(final_normed, output_weight, preferred_element_type=jnp.float32)
    copy_weight = jnp.where(lax.axis_index("cfg") == 0, guidance, 1.0 - guidance)
    guided = lax.psum(velocity_part * copy_weight, ("cfg", "narrow"))
    steps_index, alpha_bar = alpha_table()
    alpha_now = jnp.sum(jnp.where(steps_index == timestep[0], alpha_bar, 0.0))
    clean_latent = jnp.where(
        is_video[:, None], jnp.sqrt(alpha_now) * latent - jnp.sqrt(1.0 - alpha_now) * guided, 0.0
    )
    return (layer_out[None], clean_latent)


QUOTAS = (0, 64, 128)
CAP = 128
CHUNKS = len(QUOTAS) - 1
F32, BF16 = jnp.float32, jnp.bfloat16
TILE = 768
LONG = 10**10


def size_of(k):
    return QUOTAS[k + 1] - QUOTAS[k]


def swap(array, axis, distance, size):
    return lax.ppermute(array, axis, [(i, i ^ distance) for i in range(size)])


def z_swaps(array):
    return [swap(array, "wide", s, 4) for s in (1, 2, 3)]


def choose(values, index):
    out = values[0]
    for i in range(1, 4):
        out = jnp.where(index == i, values[i], out)
    return out


def layout(table):
    counts = [table[b] for b in range(4)]
    largest = jnp.int32(3)
    for b in (2, 1, 0):
        largest = jnp.where(counts[b] == CAP, b, largest)
    starts, others, ranks, offsets = [], [], [], []
    rank, offset = jnp.int32(0), jnp.int32(0)
    for b in range(4):
        other = jnp.where(largest == b, 0, 1)
        ranks.append(rank * other)
        others.append(other)
        offsets.append(offset)
        rank = rank + other * counts[b]
        offset = offset + counts[b]
    block = lax.axis_index("wide")
    of = lambda values: [choose(values, jnp.bitwise_xor(block, s)) for s in range(4)]
    return of(ranks), of(counts), of(others), of(offsets)[0], choose(offsets, largest)


def high_low(values):
    high = values.astype(BF16)
    return high, (values - high.astype(F32)).astype(BF16)


def load(source, place, sems):
    parts = sems.shape[0]
    height = source.shape[0] // parts
    copies = []
    for t in range(parts):
        rows = pl.ds(t * height, height)
        copies.append(pltpu.make_async_copy(source.at[rows, :], place.at[rows, :], sems.at[t]))
        copies[-1].start()
    return copies


def load_half(source, half, place, sems):
    width = place.shape[1]
    copies = []
    for t in range(0, width, TILE):
        columns = pl.ds(pl.multiple_of(half * width + t, 128), TILE)
        copies.append(
            pltpu.make_async_copy(
                source.at[:, columns], place.at[:, pl.ds(t, TILE)], sems.at[len(copies)]
            )
        )
        copies[-1].start()
    return copies


def rows_of(parts, core):
    total = parts[:8] + parts[8:]
    total = jnp.where(core == 0, total, pltpu.roll(total, 4, 0))
    high, low = high_low(total)
    return jnp.concatenate([high.astype(F32), low.astype(F32)], 0).astype(BF16)


def hold_kernel(source, *refs):
    place, sems = refs[-2:]
    for copy in load(source, place, sems):
        copy.wait()


def text_rows(k, largest_offset):
    size = size_of(k)
    row = lax.broadcasted_iota(jnp.int32, (2 * size, 1), 0)
    rank = jnp.where(row < size, row, row - size) + QUOTAS[k]
    position = jnp.where(
        row < size, rank + largest_offset, jnp.where(rank < largest_offset, rank, rank + CAP)
    )
    return position < TEXT


def gather_matrix(k, ranks, counts, others):
    size = size_of(k)
    places = []
    for p in range(k + 1):
        piece = size_of(p)
        lane = lax.broadcasted_iota(jnp.int32, (1, 4 * piece), 1)
        which, slot = lane // piece, lane % piece + QUOTAS[p]
        rank = slot + choose(ranks, which) - QUOTAS[k]
        live = (rank >= 0) & (rank < size) & (slot < choose(counts, which))
        row = jnp.where(live, rank + choose(others, which) * size, -1)
        at = lax.broadcasted_iota(jnp.int32, (2 * size, 4 * piece), 0)
        places.append(jnp.where(at == row, 1.0, 0.0).astype(BF16))
    return jnp.concatenate(places, 1)


def spread_matrix(k, ranks, counts, others):
    size = size_of(k)
    places = []
    for s in range(4):
        first = jnp.maximum(QUOTAS[k] - ranks[s], 0)
        last = jnp.minimum(counts[s], QUOTAS[k + 1] - ranks[s])
        index = lax.broadcasted_iota(jnp.int32, (size, 1), 0)
        slot = first + jnp.bitwise_and(index - first, size - 1)
        row = jnp.where(slot < last, slot + ranks[s] - QUOTAS[k] + others[s] * size, -1)
        at = lax.broadcasted_iota(jnp.int32, (size, 2 * size), 1)
        places.append(jnp.where(at == row, 1.0, 0.0).astype(BF16))
    return jnp.concatenate(places, 0)


def take_kernel(source, piece, sem):
    copy = pltpu.make_async_copy(source.at[pl.ds(0, piece.shape[0]), :], piece, sem)
    copy.start()
    copy.wait()


def prepare_kernel(table_in, timestep, tokens_in, mod_in, out_weight, w, *refs):
    later, refs = refs[: CHUNKS - 1], refs[CHUNKS - 1 :]
    gathers, refs = refs[:CHUNKS], refs[CHUNKS:]
    spreads, refs = refs[:CHUNKS], refs[CHUNKS:]
    texts, refs = refs[:CHUNKS], refs[CHUNKS:]
    held, kept, tokens, mod, weight, rows_out, ends_out, slots_out, video_out, step_out = refs[:10]
    table, sems, small = refs[10:]
    step_out[...] = jnp.full(step_out.shape, timestep[0], jnp.int32)
    core = lax.axis_index("narrow") % 2
    sources = (table_in, mod_in, out_weight, tokens_in)
    copies = [
        pltpu.make_async_copy(source, place, small.at[i])
        for i, (source, place) in enumerate(zip(sources, (table, mod, weight, tokens)))
    ]
    for copy in copies:
        copy.start()
    big = load_half(w, 1 - core, held, sems.at[0]) + load_half(w, core, kept, sems.at[1])

    copies[0].wait()
    ranks, counts, others, offset, largest_offset = layout(table)
    for k in range(CHUNKS):
        gathers[k][...] = gather_matrix(k, ranks, counts, others)
        spreads[k][...] = spread_matrix(k, ranks, counts, others)
        text = jnp.where(text_rows(k, largest_offset), 1.0, 0.0)
        texts[k][...] = jnp.broadcast_to(text, texts[k].shape)
    slot = lax.broadcasted_iota(jnp.int32, (CAP, 128), 0)
    lane = lax.broadcasted_iota(jnp.int32, (CAP, 128), 1)
    rank = slot + ranks[0]
    flag = lambda condition: jnp.where(condition, 1.0, 0.0)
    kind = jnp.where(lane == 0, flag(slot < counts[0]), flag(slot + offset < TEXT))
    for k in range(CHUNKS):
        kind = jnp.where(
            lane == 2 + k, flag((rank >= QUOTAS[k]) & (rank < QUOTAS[k + 1])), kind
        )
    slots_out[...] = kind
    slot = lax.broadcasted_iota(jnp.int32, (8, CAP), 1)
    video_out[...] = jnp.where((slot < counts[0]) & (slot + offset >= TEXT), 1.0, 0.0)

    copies[1].wait()
    row = lax.broadcasted_iota(jnp.int32, (8, 1), 0)
    rows = jnp.where(row == 0, 1.0 + mod[1:2, :], jnp.zeros((8, 1), F32))
    rows = jnp.where(row == 1, 1.0 + mod[4:5, :], rows)
    rows = jnp.where(row == 2, mod[0:1, :], rows)
    rows = jnp.where(row == 3, mod[3:4, :], rows)
    rows_out[...] = jnp.concatenate(high_low(rows), 0)
    rows = jnp.where(row == 0, 1.0 + mod[7:8, :], jnp.zeros((8, 1), F32))
    rows = jnp.where(row == 1, mod[6:7, :], rows)
    copies[2].wait()
    ends = lax.dot_general(
        jnp.concatenate(high_low(rows), 0),
        weight[...],
        (((1,), (1,)), ((), ())),
        preferred_element_type=F32,
    )
    ends = rows_of(ends, core)
    ends_out[...] = jnp.concatenate([ends, jnp.zeros((16, 128 - ends.shape[1]), BF16)], 1)
    copies[3].wait()
    for k in range(1, CHUNKS):
        later[k - 1][...] = tokens[QUOTAS[k] : QUOTAS[k + 1], :]
    for copy in big:
        copy.wait()


def expand_sent_kernel(k, text, mod, place, own, near, *refs):
    far, (w, sums, ends) = refs[: 2 * (k + 1)], refs[2 * (k + 1) : 2 * (k + 1) + 3]
    z_out, sent_out, side_out = refs[-3:]
    core = lax.axis_index("narrow") % 2
    units = w.shape[1]
    rows = place.shape[0]
    pieces = []
    for p in range(k + 1):
        of_chunk = slice(QUOTAS[p], QUOTAS[p + 1])
        pieces += [own[of_chunk, :], near[of_chunk, :], far[2 * p][...], far[2 * p + 1][...]]
    tokens = jnp.concatenate(pieces, 0)
    x = jnp.dot(place[...], tokens, preferred_element_type=F32)
    centre = (jnp.sum(x, -1, keepdims=True) / x.shape[1]).astype(BF16).astype(F32)
    x = x - centre
    z = (x * (1.0 + jnp.where(text[:, :1] > 0.5, mod[4:5, :], mod[1:2, :]))).astype(BF16)
    if k == 0:
        z = jnp.concatenate([z, sums[...]], 0)
    z_out[...] = z
    if k == 0:
        lead = side_out.shape[1] - 8 * 128
        side_out[:, units:lead] = ends[...]
    for t in range(0, units, TILE):
        columns = slice(t, t + TILE)
        product = jnp.dot(z, w[:, columns], preferred_element_type=F32)
        sent_out[:, columns] = product[:rows].astype(BF16)
        if k == 0:
            side_out[:, columns] = rows_of(product[rows:], core)
    total = jnp.sum(x, -1, keepdims=True)
    square = jnp.sum(x * x, -1, keepdims=True)
    total_high = total.astype(BF16).astype(F32)
    square_high = square.astype(BF16).astype(F32)
    lane = lax.broadcasted_iota(jnp.int32, (rows, 128), 1) - 4 * core
    side = jnp.where((lane == 0) | (lane == 1), centre, 0.0)
    side = jnp.where(lane == 16, total_high, side)
    side = jnp.where(lane == 17, total - total_high, side)
    side = jnp.where(lane == 18, square_high, side)
    side = jnp.where(lane == 19, square - square_high, side).astype(BF16)
    if k == 0:
        for i in range(rows // 16):
            side_out[:, lead + 128 * i : lead + 128 * (i + 1)] = side[16 * i : 16 * (i + 1)]
    else:
        side_out[...] = side


def expand_kept_kernel(k, z, w, _, __, *refs):
    kept_out = refs[-1 if k else -2]
    core = lax.axis_index("narrow") % 2
    rows = kept_out.shape[0]
    for t in range(0, w.shape[1], TILE):
        columns = slice(t, t + TILE)
        product = jnp.dot(z[...], w[:, columns], preferred_element_type=F32)
        kept_out[:, columns] = product[:rows]
        if k == 0:
            refs[-1][:, columns] = rows_of(product[rows:], core)


def pass_kernel(piece, _, out):
    out[...] = piece[...]


def across_rows(side):
    height = side.shape[0]
    if height < 128:
        side = jnp.concatenate([side, jnp.zeros((128 - height, 128), F32)], 0)
    return side.T


def stats_kernel(k, rows, side, came, *refs):
    side_out, stats_out = refs[-2:]
    lead = stats_out.shape[1] - 256
    if k == 0:
        kept_sums = refs[0]
        units = kept_sums.shape[1]
        stats_out[:, :units] = (kept_sums[...].astype(F32) + came[:, :units].astype(F32)).astype(BF16)
        both = side[:, units:].astype(F32) + came[:, units:].astype(F32)
        stats_out[:, units:lead] = both[:, : lead - units].astype(BF16)
        both = both[:, lead - units :]
        both = jnp.concatenate([both[:, 128 * i : 128 * (i + 1)] for i in range(rows // 16)], 0)
    else:
        both = side[...].astype(F32) + came[...].astype(F32)
    side_out[...] = both
    stats = across_rows(both)[:32].astype(BF16)
    stats_out[:, lead : lead + 128] = stats[:16]
    stats_out[:, lead + 128 :] = stats[16:]


def merge_kernel(kept, came, _, sent_out):
    sent_out[...] = (kept[...] + came[...].astype(F32)).astype(BF16)


def rows_kernel(features, text, side, stats, *refs):
    out = refs[-1]
    rows = side.shape[0]
    lead = stats.shape[1] - 256
    stats = jnp.concatenate([stats[:, lead : lead + 128], stats[:, lead + 128 :]], 0)
    sides = [side[...], across_rows(stats.astype(F32))[:rows]]
    lane = lax.broadcasted_iota(jnp.int32, (rows, 128), 1)
    field = lane % 4
    summed = sides[0] + sides[1]
    add = lambda values, mask: jnp.sum(jnp.where(mask, values, 0.0), -1, keepdims=True)
    centres, measures = lane < 8, (lane >= 16) & (lane < 24)
    average = (
        add(summed, centres & (field == 0)) * features + add(summed, measures & (field < 2))
    ) / D
    spread = add(summed, measures & (field >= 2))
    aparts = []
    for side in sides:
        apart = jnp.where(centres, side - average, 0.0)
        for core in range(2):
            off = add(apart, lane == 4 * core)
            own = lane // 4 == 4 + core
            spread = spread + off * (2.0 * add(side, own & (field < 2)) + features * off)
        aparts.append(apart)
    scale = lax.rsqrt(spread / D + norm_eps)
    of_text = jnp.where(text[...] > 0.5, 1, 0)
    mine = centres & (lane % 2 == of_text)
    packed, shift = None, 0
    for apart in aparts:
        factor = jnp.where(mine, jnp.where(field < 2, apart * scale, 1.0), 0.0)
        high = factor.astype(BF16).astype(F32)
        for part in (high, high, factor - high, factor - high):
            part = pltpu.roll(part, shift, 1) if shift else part
            packed = part if packed is None else packed + part
            shift += 8
    out[...] = jnp.where(lane < 64, packed, scale)


def activate_kernel(total, came, rows_in, first_sent, first_came, *refs):
    act_out = refs[-1]
    rows, units = act_out.shape
    packed, scale = rows_in[:, :64].astype(BF16), rows_in[:, 64:65]
    own, other = first_sent[:, :units], first_came[:, :units]
    factors = jnp.concatenate([own, own, other, other], 0)
    for t in range(0, units, TILE):
        columns = slice(t, t + TILE)
        pre = total[:rows, columns].astype(F32) + came[:rows, columns].astype(F32)
        extra = jnp.dot(packed, factors[:, columns], preferred_element_type=F32)
        act_out[:, columns] = jax.nn.gelu(pre * scale + extra, approximate=True).astype(BF16)


def contract_own_kernel(k, act, w, mine, chip, other, out, *ends_out):
    core = lax.axis_index("narrow") % 2
    units = w.shape[0] // 2
    rows = pl.ds(pl.multiple_of(core * units, 128), units)
    out[...] = jnp.dot(act[...], w[rows, :], preferred_element_type=F32)
    if k == 0:
        units = w.shape[0] // 2
        ends = slice(units, units + 128)
        total = chip[:, ends].astype(F32) + other[:, ends].astype(F32)
        total = total[:8] + total[8:]
        total = total + pltpu.roll(total, 4, 0)
        own = mine[...].astype(F32)
        own = own[:8] + own[8:]
        own = own + pltpu.roll(own, 4, 0)
        ends_out[0][...] = jnp.concatenate([total, own, jnp.zeros((112, 128), F32)], 0).T


def contract_other_kernel(k, place, act, so_far, w, *refs):
    outs = refs[-4:]
    core = lax.axis_index("narrow") % 2
    units = w.shape[0] // 2
    rows = pl.ds(pl.multiple_of((1 - core) * units, 128), units)
    total = so_far[...] + jnp.dot(act[...], w[rows, :], preferred_element_type=F32)
    spread = jnp.dot(place[...], total.astype(BF16), preferred_element_type=F32).astype(BF16)
    size = size_of(k)
    for s in range(4):
        outs[s][...] = spread[s * size : (s + 1) * size]


def finish_kernel(slots, hidden, mod, out_weight, ends, *refs):
    pieces, (layer_out, bundle_out) = refs[: 4 * CHUNKS], refs[4 * CHUNKS :]
    result = jnp.zeros(hidden.shape, F32)
    for k in range(CHUNKS):
        total = pieces[4 * k][...].astype(F32)
        for s in (1, 2, 3):
            total = total + pieces[4 * k + s][...].astype(F32)
        total = jnp.concatenate([total] * (CAP // size_of(k)), 0)
        result = jnp.where(slots[:, 2 + k : 3 + k] > 0.5, total, result)
    gate = jnp.where(slots[:, 1:2] > 0.5, mod[5:6, :], mod[2:3, :])
    layer = hidden[...].astype(F32) + gate * result
    layer = jnp.where(slots[:, 0:1] > 0.5, layer, 0.0).astype(BF16)
    layer_out[...] = layer
    x = layer.astype(F32)
    centre = jnp.sum(x, -1, keepdims=True) / x.shape[1]
    ones = jnp.ones((8, x.shape[1]), BF16)
    across = lambda left, right: lax.dot_general(
        left, right, (((1,), (1,)), ((), ())), preferred_element_type=F32
    )
    high, low = high_low(x * x)
    total, square = across(ones, layer), across(ones, high) + across(ones, low)
    width = out_weight.shape[0]
    product = across(out_weight[...], ((x - centre) * (1.0 + mod[7:8, :])).astype(BF16))
    bundle_out[:width, :] = product + total[0:1] / x.shape[1] * ends[:width, 8:9]
    row = lax.broadcasted_iota(jnp.int32, (8, CAP), 0)
    bundle_out[width:, :] = jnp.where(row == 0, total, square)


def write_kernel(layer, out):
    out[...] = layer[...]


def add_kernel(left, right, out):
    out[...] = left[...] + right[...]


def noise_kernel(step, alphas, video, latent, _, out):
    index = lax.broadcasted_iota(jnp.int32, (8, 128), 0) * 128 + lax.broadcasted_iota(
        jnp.int32, (8, 128), 1
    )
    alpha = jnp.sum(
        jnp.sum(jnp.where(index == step[...], alphas[...], 0.0), 0, keepdims=True),
        1,
        keepdims=True,
    )
    width = latent.shape[0]
    out[:width, :] = jnp.where(video[0:1] > 0.5, jnp.sqrt(alpha) * latent[...], 0.0)
    out[width:, :] = jnp.where(video[...] > 0.5, jnp.sqrt(1.0 - alpha), 0.0)


def latent_kernel(noise, ends, mine, other_y, other, mine_y, out):
    width = out.shape[0]
    factor = noise[width : width + 1]

    def velocity(total):
        average = total[width : width + 1] / D
        variance = total[width + 1 : width + 2] / D - average * average
        return (total[:width] - average * ends[:width, 0:1]) * lax.rsqrt(
            variance + norm_eps
        ) + ends[:width, 1:2]

    first = lax.axis_index("cfg") == 0
    guided = velocity(mine[...] + mine_y[...]) * jnp.where(first, guidance, 1.0 - guidance)
    guided = guided + velocity(other[...] + other_y[...]) * jnp.where(
        first, 1.0 - guidance, guidance
    )
    guided = jnp.where(factor > 0.0, guided, 0.0)
    out[...] = noise[:width] - factor * guided


def alpha_constant():
    ends = np.sqrt(np.float64(0.00085)), np.sqrt(np.float64(0.012))
    betas = np.linspace(ends[0], ends[1], 1000, dtype=np.float64) ** 2
    return np.pad(np.cumprod(1.0 - betas), (0, 24)).astype(np.float32).reshape(8, 128)


def call(kernel, outs, args, spaces, scratch=(), weight=1):
    kinds = {"v": pltpu.VMEM, "s": pltpu.SMEM, "a": pl.ANY}
    return pl.pallas_call(
        kernel,
        out_shape=[jax.ShapeDtypeStruct(shape, dtype) for shape, dtype in outs],
        in_specs=[pl.BlockSpec(memory_space=kinds[letter]) for letter in spaces],
        out_specs=[pl.BlockSpec(memory_space=pltpu.VMEM) for _ in outs],
        scratch_shapes=list(scratch),
        compiler_params=pltpu.CompilerParams(vmem_limit_bytes=24 * 2**20),
        cost_estimate=pl.CostEstimate(flops=weight, bytes_accessed=1, transcendentals=0),
    )(*args)


def four_blocks(
    hidden, split_table, modulation, expand_weight, contract_weight, output_weight, latent, timestep
):
    hidden = hidden[0]
    features = hidden.shape[1]
    units = expand_weight.shape[1] // 2
    width = output_weight.shape[1]
    payload = units + 128

    in_place = lambda array: pltpu.with_memory_space_constraint(array, pltpu.HBM)
    (piece,) = call(
        take_kernel,
        [((QUOTAS[1], features), BF16)],
        [in_place(hidden)],
        "a",
        [pltpu.SemaphoreType.DMA(())],
    )
    across = swap(piece, "wide", 2, 4)
    near = swap(hidden, "wide", 1, 4)

    tiles = units // TILE
    chunks = range(CHUNKS)
    made = call(
        prepare_kernel,
        [((size_of(k), features), BF16) for k in chunks[1:]]
        + [((2 * size_of(k), 4 * QUOTAS[k + 1]), BF16) for k in chunks]
        + [((4 * size_of(k), 2 * size_of(k)), BF16) for k in chunks]
        + [((2 * size_of(k), 128), F32) for k in chunks]
        + [
            ((features, units), BF16),
            ((features, units), BF16),
            (hidden.shape, BF16),
            (modulation.shape, F32),
            ((width, features), BF16),
            ((16, features), BF16),
            ((16, 128), BF16),
            ((CAP, 128), F32),
            ((8, CAP), F32),
            ((8, 128), jnp.int32),
        ],
        [
            in_place(split_table),
            timestep,
            in_place(hidden),
            in_place(modulation),
            in_place(output_weight.T),
            in_place(expand_weight),
        ],
        "asaaaa",
        [
            pltpu.SMEM(split_table.shape, jnp.int32),
            pltpu.SemaphoreType.DMA((2, tiles)),
            pltpu.SemaphoreType.DMA((4,)),
        ],
    )
    later, made = made[: CHUNKS - 1], made[CHUNKS - 1 :]
    gathers, made = made[:CHUNKS], made[CHUNKS:]
    spreads, made = made[:CHUNKS], made[CHUNKS:]
    texts, made = made[:CHUNKS], made[CHUNKS:]
    held_sent, held_kept, tokens, mod, out_weight, rows_in, ends_mine, slots, video, step = made
    later = [swap(piece, "wide", 2, 4) for piece in later]
    (across,) = call(pass_kernel, [(across.shape, BF16)], [across, slots], "va")
    far = [across, swap(across, "wide", 1, 4)]

    merged = []
    before = []
    for k in chunks:
        rows = 2 * size_of(k)
        extra = 16 if k == 0 else 0
        z, sent, side = call(
            functools.partial(expand_sent_kernel, k),
            [
                ((rows + extra, features), BF16),
                ((rows, units), BF16),
                ((16, payload + 8 * rows) if k == 0 else (rows, 128), BF16),
            ],
            [texts[k], mod, gathers[k], tokens, near, *far, held_sent, rows_in, ends_mine, *before],
            "vvvvv" + "v" * len(far) + "vvv" + "a" * len(before),
            weight=LONG,
        )
        side_came, came = [swap(array, "narrow", 1, 4) for array in (side, sent)]
        kept, *sums_made = call(
            functools.partial(expand_kept_kernel, k),
            [((rows, units), F32)] + ([((16, units), BF16)] if k == 0 else []),
            [z, held_kept, sent, side],
            "vvaa",
            weight=LONG,
        )
        side, stats = call(
            functools.partial(stats_kernel, k, rows),
            [((rows, 128), F32), ((16, 256 + (payload if k == 0 else 0)), BF16)],
            [side, side_came, *sums_made],
            "vv" + "v" * len(sums_made),
        )
        stats_came = swap(stats, "narrow", 2, 4)
        (sent,) = call(merge_kernel, [((rows, units), BF16)], [kept, came, stats], "vva")
        if k + 1 < CHUNKS:
            (across,) = call(
                pass_kernel, [(later[k].shape, BF16)], [later[k], sent], "va"
            )
            far.extend([across, swap(across, "wide", 1, 4)])
        if k == 0:
            (held_out,) = call(
                hold_kernel,
                [(contract_weight.shape, BF16)],
                [in_place(contract_weight), across, stats],
                "aaa",
                [pltpu.SemaphoreType.DMA((4,))],
                weight=LONG,
            )
        if k == 0:
            (noise,) = call(
                noise_kernel,
                [((width + 8, CAP), F32)],
                [step, alpha_constant(), video, latent.T, sent],
                "vvvva",
                weight=LONG,
            )
        before = [sent, noise, held_out]
        came = swap(sent, "narrow", 2, 4)
        merged.append((sent, stats, [sent, came, side, stats_came]))

    returned = []
    before = []
    first = [merged[0][1], merged[0][2][3]]
    def rows_call(k, *after):
        return call(
            functools.partial(rows_kernel, features),
            [((2 * size_of(k), 128), F32)],
            [texts[k], *merged[k][2][2:], *after],
            "vvv" + "a" * len(after),
        )[0]

    of_rows = [rows_call(0, merged[-1][0])]
    for k in chunks:
        rows = 2 * size_of(k)
        if k + 1 < CHUNKS:
            before = before + [merged[k + 1][0], merged[k + 1][1]]
        (act,) = call(
            activate_kernel,
            [((rows, units), BF16)],
            [*merged[k][2][:2], of_rows[k], *first, *before],
            "vvvvv" + "a" * len(before),
        )
        act_came = swap(act, "narrow", 1, 4)
        if k + 1 < CHUNKS:
            of_rows.append(rows_call(k + 1, act))
        out, *ends_made = call(
            functools.partial(contract_own_kernel, k),
            [((rows, features), F32)] + ([((128, 128), F32)] if k == 0 else []),
            [act, held_out, ends_mine, *first],
            "vvvvv",
            weight=LONG,
        )
        ends = ends_made[0] if k == 0 else ends
        pieces = call(
            functools.partial(contract_other_kernel, k),
            [((size_of(k), features), BF16)] * 4,
            [spreads[k], act_came, out, held_out, *of_rows[k + 1 : k + 2]],
            "vvvv" + "a" * len(of_rows[k + 1 : k + 2]),
        )
        before = pieces
        distances = (3, 2, 1) if k + 1 < CHUNKS else (2, 3, 1)
        returned += [pieces[0], *(swap(pieces[s], "wide", s, 4) for s in distances)]

    layer, bundle = call(
        finish_kernel,
        [((CAP, features), BF16), ((width + 8, CAP), F32)],
        [slots, tokens, mod, out_weight, ends, *returned],
        "v" * (5 + len(returned)),
    )
    (layer_out,) = call(write_kernel, [((CAP, features), BF16)], [layer], "v", weight=LONG)
    (bundle,) = call(
        add_kernel, [((width + 8, CAP), F32)], [bundle, swap(bundle, "narrow", 1, 4)], "vv"
    )
    (clean_latent,) = call(
        latent_kernel,
        [((width, CAP), F32)],
        [noise, ends, bundle] + [swap(bundle, ("cfg", "narrow"), n, 8) for n in (6, 4, 2)],
        "vvvvvv",
    )
    return (layer_out[None], clean_latent.T)


def solution(mesh):
    by_swaps = (mesh.shape["wide"], mesh.shape["narrow"], mesh.shape["cfg"]) == (4, 4, 2)
    return jax.shard_map(
        four_blocks if by_swaps else any_slice,
        mesh=mesh,
        in_specs=(
            P("cfg", "wide", "narrow"),
            P(),
            P(None, "narrow"),
            P("narrow", "wide"),
            P("wide", "narrow"),
            P("narrow", None),
            P("wide", None),
            P(),
        ),
        out_specs=(P("cfg", "wide", "narrow"), P("wide", None)),
        check_vma=False,
    )
```

```python
import functools

import jax
import jax.numpy as jnp
import numpy as np
from jax import lax
from jax.experimental import pallas as pl
from jax.experimental.pallas import tpu as pltpu
from jax.sharding import PartitionSpec as P

D = 3072
TEXT = 226


norm_eps = 1e-05
guidance = 6.0


def alpha_table():
    steps_index = jnp.arange(1000, dtype=jnp.int32)
    start_root = 0.00085**0.5
    end_root = 0.012**0.5
    roots = start_root + (end_root - start_root) * steps_index.astype(jnp.float32) / 999.0
    return (steps_index, jnp.cumprod(1.0 - roots * roots))


def feature_norm(values, shifts, scaling):
    totals, squares = lax.psum(
        (jnp.sum(values, -1, keepdims=True), jnp.sum(values * values, -1, keepdims=True)), "narrow"
    )
    average = totals / D
    variance = squares / D - average * average
    return (values - average) * lax.rsqrt(variance + norm_eps) * (1.0 + scaling) + shifts


def any_slice(
    hidden, split_table, modulation, expand_weight, contract_weight, output_weight, latent, timestep
):
    capacity = hidden.shape[1]
    wide_index = lax.axis_index("wide")
    table_index = jnp.arange(split_table.shape[0], dtype=jnp.int32)
    offset = jnp.sum(jnp.where(table_index < wide_index, split_table, 0))
    own_count = jnp.sum(jnp.where(table_index == wide_index, split_table, 0))
    slot_index = jnp.arange(capacity, dtype=jnp.int32)
    position = offset + slot_index
    slot_live = slot_index < own_count
    is_text = slot_live & (position < TEXT)
    is_video = slot_live & (position >= TEXT)
    text_column = is_text[:, None]
    shifts = jnp.where(text_column, modulation[3], modulation[0])
    scaling = jnp.where(text_column, modulation[4], modulation[1])
    gating = jnp.where(text_column, modulation[5], modulation[2])
    values = hidden[0].astype(jnp.float32)
    normed = feature_norm(values, shifts, scaling).astype(jnp.bfloat16)
    hidden_part = jnp.dot(
        lax.all_gather(normed, "wide", axis=0, tiled=True),
        expand_weight,
        preferred_element_type=jnp.float32,
    )
    hidden_pre = lax.psum(hidden_part, "narrow")
    activated = jax.nn.gelu(hidden_pre, approximate=True).astype(jnp.bfloat16)
    ff_result = lax.psum_scatter(
        jnp.dot(activated, contract_weight, preferred_element_type=jnp.float32),
        "wide",
        scatter_dimension=0,
        tiled=True,
    )
    layer_out = jnp.where(slot_live[:, None], values + gating * ff_result, 0.0).astype(jnp.bfloat16)
    final_in = layer_out.astype(jnp.float32)
    final_normed = feature_norm(final_in, modulation[6], modulation[7]).astype(jnp.bfloat16)
    velocity_part = jnp.dot(final_normed, output_weight, preferred_element_type=jnp.float32)
    copy_weight = jnp.where(lax.axis_index("cfg") == 0, guidance, 1.0 - guidance)
    guided = lax.psum(velocity_part * copy_weight, ("cfg", "narrow"))
    steps_index, alpha_bar = alpha_table()
    alpha_now = jnp.sum(jnp.where(steps_index == timestep[0], alpha_bar, 0.0))
    clean_latent = jnp.where(
        is_video[:, None], jnp.sqrt(alpha_now) * latent - jnp.sqrt(1.0 - alpha_now) * guided, 0.0
    )
    return (layer_out[None], clean_latent)


QUOTAS = (0, 64, 128)
CAP = 128
VIDEO = 32
CHUNKS = len(QUOTAS) - 1
F32, BF16 = jnp.float32, jnp.bfloat16
TILE = 768
LONG = 10**10


def size_of(k):
    return QUOTAS[k + 1] - QUOTAS[k]


def swap(array, axis, distance, size):
    return lax.ppermute(array, axis, [(i, i ^ distance) for i in range(size)])


def z_swaps(array):
    return [swap(array, "wide", s, 4) for s in (1, 2, 3)]


def choose(values, index):
    out = values[0]
    for i in range(1, 4):
        out = jnp.where(index == i, values[i], out)
    return out


def layout(table):
    counts = [table[b] for b in range(4)]
    largest = jnp.int32(3)
    for b in (2, 1, 0):
        largest = jnp.where(counts[b] == CAP, b, largest)
    starts, others, ranks, offsets = [], [], [], []
    rank, offset = jnp.int32(0), jnp.int32(0)
    for b in range(4):
        other = jnp.where(largest == b, 0, 1)
        ranks.append(rank * other)
        others.append(other)
        offsets.append(offset)
        rank = rank + other * counts[b]
        offset = offset + counts[b]
    block = lax.axis_index("wide")
    of = lambda values: [choose(values, jnp.bitwise_xor(block, s)) for s in range(4)]
    return of(ranks), of(counts), of(others), of(offsets)[0], choose(offsets, largest)


def high_low(values):
    high = values.astype(BF16)
    return high, (values - high.astype(F32)).astype(BF16)


def load(source, place, sems):
    parts = sems.shape[0]
    height = source.shape[0] // parts
    copies = []
    for t in range(parts):
        rows = pl.ds(t * height, height)
        copies.append(pltpu.make_async_copy(source.at[rows, :], place.at[rows, :], sems.at[t]))
        copies[-1].start()
    return copies


def load_half(source, half, place, sems):
    width = place.shape[1]
    copies = []
    for t in range(0, width, TILE):
        columns = pl.ds(pl.multiple_of(half * width + t, 128), TILE)
        copies.append(
            pltpu.make_async_copy(
                source.at[:, columns], place.at[:, pl.ds(t, TILE)], sems.at[len(copies)]
            )
        )
        copies[-1].start()
    return copies


def rows_of(parts, core):
    total = parts[:8] + parts[8:]
    total = jnp.where(core == 0, total, pltpu.roll(total, 4, 0))
    high, low = high_low(total)
    return jnp.concatenate([high.astype(F32), low.astype(F32)], 0).astype(BF16)


def hold_kernel(source, *refs):
    place, sems = refs[-2:]
    for copy in load(source, place, sems):
        copy.wait()


def text_rows(k, largest_offset):
    size = size_of(k)
    row = lax.broadcasted_iota(jnp.int32, (2 * size, 1), 0)
    rank = jnp.where(row < size, row, row - size) + QUOTAS[k]
    position = jnp.where(
        row < size, rank + largest_offset, jnp.where(rank < largest_offset, rank, rank + CAP)
    )
    return position < TEXT


def gather_matrix(k, ranks, counts, others):
    size = size_of(k)
    places = []
    for p in range(k + 1):
        piece = size_of(p)
        lane = lax.broadcasted_iota(jnp.int32, (1, 4 * piece), 1)
        which, slot = lane // piece, lane % piece + QUOTAS[p]
        rank = slot + choose(ranks, which) - QUOTAS[k]
        live = (rank >= 0) & (rank < size) & (slot < choose(counts, which))
        row = jnp.where(live, rank + choose(others, which) * size, -1)
        at = lax.broadcasted_iota(jnp.int32, (2 * size, 4 * piece), 0)
        places.append(jnp.where(at == row, 1.0, 0.0).astype(BF16))
    return jnp.concatenate(places, 1)


def spread_matrix(k, ranks, counts, others):
    size = size_of(k)
    places = []
    for s in range(4):
        first = jnp.maximum(QUOTAS[k] - ranks[s], 0)
        last = jnp.minimum(counts[s], QUOTAS[k + 1] - ranks[s])
        index = lax.broadcasted_iota(jnp.int32, (size, 1), 0)
        slot = first + jnp.bitwise_and(index - first, size - 1)
        row = jnp.where(slot < last, slot + ranks[s] - QUOTAS[k] + others[s] * size, -1)
        at = lax.broadcasted_iota(jnp.int32, (size, 2 * size), 1)
        places.append(jnp.where(at == row, 1.0, 0.0).astype(BF16))
    return jnp.concatenate(places, 0)


def take_kernel(source, piece, sem):
    copy = pltpu.make_async_copy(source.at[pl.ds(0, piece.shape[0]), :], piece, sem)
    copy.start()
    copy.wait()


def prepare_kernel(table_in, timestep, tokens_in, mod_in, out_weight, w, *refs):
    later, refs = refs[: CHUNKS - 1], refs[CHUNKS - 1 :]
    gathers, refs = refs[:CHUNKS], refs[CHUNKS:]
    spreads, refs = refs[:CHUNKS], refs[CHUNKS:]
    texts, refs = refs[:CHUNKS], refs[CHUNKS:]
    held, kept, tokens, mod, weight, rows_out, ends_out, slots_out, video_out, step_out = refs[:10]
    table, sems, small = refs[10:]
    step_out[...] = jnp.full(step_out.shape, timestep[0], jnp.int32)
    core = lax.axis_index("narrow") % 2
    sources = (table_in, mod_in, out_weight, tokens_in)
    copies = [
        pltpu.make_async_copy(source, place, small.at[i])
        for i, (source, place) in enumerate(zip(sources, (table, mod, weight, tokens)))
    ]
    for copy in copies:
        copy.start()
    big = load_half(w, 1 - core, held, sems.at[0]) + load_half(w, core, kept, sems.at[1])

    copies[0].wait()
    ranks, counts, others, offset, largest_offset = layout(table)
    for k in range(CHUNKS):
        gathers[k][...] = gather_matrix(k, ranks, counts, others)
        spreads[k][...] = spread_matrix(k, ranks, counts, others)
        text = jnp.where(text_rows(k, largest_offset), 1.0, 0.0)
        texts[k][...] = jnp.broadcast_to(text, texts[k].shape)
    slot = lax.broadcasted_iota(jnp.int32, (CAP, 128), 0)
    lane = lax.broadcasted_iota(jnp.int32, (CAP, 128), 1)
    rank = slot + ranks[0]
    flag = lambda condition: jnp.where(condition, 1.0, 0.0)
    kind = jnp.where(lane == 0, flag(slot < counts[0]), flag(slot + offset < TEXT))
    for k in range(CHUNKS):
        kind = jnp.where(
            lane == 2 + k, flag((rank >= QUOTAS[k]) & (rank < QUOTAS[k + 1])), kind
        )
    slots_out[...] = kind
    slot = lax.broadcasted_iota(jnp.int32, (8, CAP), 1)
    video_out[...] = jnp.where((slot < counts[0]) & (slot + offset >= TEXT), 1.0, 0.0)

    copies[1].wait()
    row = lax.broadcasted_iota(jnp.int32, (8, 1), 0)
    rows = jnp.where(row == 0, 1.0 + mod[1:2, :], jnp.zeros((8, 1), F32))
    rows = jnp.where(row == 1, 1.0 + mod[4:5, :], rows)
    rows = jnp.where(row == 2, mod[0:1, :], rows)
    rows = jnp.where(row == 3, mod[3:4, :], rows)
    rows_out[...] = jnp.concatenate(high_low(rows), 0)
    rows = jnp.where(row == 0, 1.0 + mod[7:8, :], jnp.zeros((8, 1), F32))
    rows = jnp.where(row == 1, mod[6:7, :], rows)
    copies[2].wait()
    ends = lax.dot_general(
        jnp.concatenate(high_low(rows), 0),
        weight[...],
        (((1,), (1,)), ((), ())),
        preferred_element_type=F32,
    )
    ends = rows_of(ends, core)
    ends_out[...] = jnp.concatenate([ends, jnp.zeros((16, 128 - ends.shape[1]), BF16)], 1)
    copies[3].wait()
    for k in range(1, CHUNKS):
        later[k - 1][...] = tokens[QUOTAS[k] : QUOTAS[k + 1], :]
    for copy in big:
        copy.wait()


def expand_sent_kernel(k, text, mod, place, own, near, *refs):
    far, (w, sums, ends) = refs[: 2 * (k + 1)], refs[2 * (k + 1) : 2 * (k + 1) + 3]
    z_out, sent_out, side_out = refs[-3:]
    core = lax.axis_index("narrow") % 2
    units = w.shape[1]
    rows = place.shape[0]
    pieces = []
    for p in range(k + 1):
        of_chunk = slice(QUOTAS[p], QUOTAS[p + 1])
        pieces += [own[of_chunk, :], near[of_chunk, :], far[2 * p][...], far[2 * p + 1][...]]
    tokens = jnp.concatenate(pieces, 0)
    x = jnp.dot(place[...], tokens, preferred_element_type=F32)
    centre = (jnp.sum(x, -1, keepdims=True) / x.shape[1]).astype(BF16).astype(F32)
    x = x - centre
    z = (x * (1.0 + jnp.where(text[:, :1] > 0.5, mod[4:5, :], mod[1:2, :]))).astype(BF16)
    if k == 0:
        z = jnp.concatenate([z, sums[...]], 0)
    z_out[...] = z
    if k == 0:
        lead = side_out.shape[1] - 8 * 128
        side_out[:, units:lead] = ends[...]
    for t in range(0, units, TILE):
        columns = slice(t, t + TILE)
        product = jnp.dot(z, w[:, columns], preferred_element_type=F32)
        sent_out[:, columns] = product[:rows].astype(BF16)
        if k == 0:
            side_out[:, columns] = rows_of(product[rows:], core)
    total = jnp.sum(x, -1, keepdims=True)
    square = jnp.sum(x * x, -1, keepdims=True)
    total_high = total.astype(BF16).astype(F32)
    square_high = square.astype(BF16).astype(F32)
    lane = lax.broadcasted_iota(jnp.int32, (rows, 128), 1) - 4 * core
    side = jnp.where((lane == 0) | (lane == 1), centre, 0.0)
    side = jnp.where(lane == 16, total_high, side)
    side = jnp.where(lane == 17, total - total_high, side)
    side = jnp.where(lane == 18, square_high, side)
    side = jnp.where(lane == 19, square - square_high, side).astype(BF16)
    if k == 0:
        for i in range(rows // 16):
            side_out[:, lead + 128 * i : lead + 128 * (i + 1)] = side[16 * i : 16 * (i + 1)]
    else:
        side_out[...] = side


def expand_kept_kernel(k, z, w, _, __, *refs):
    kept_out = refs[-1 if k else -2]
    core = lax.axis_index("narrow") % 2
    rows = kept_out.shape[0]
    for t in range(0, w.shape[1], TILE):
        columns = slice(t, t + TILE)
        product = jnp.dot(z[...], w[:, columns], preferred_element_type=F32)
        kept_out[:, columns] = product[:rows]
        if k == 0:
            refs[-1][:, columns] = rows_of(product[rows:], core)


def pass_kernel(piece, _, out):
    out[...] = piece[...]


def across_rows(side):
    height = side.shape[0]
    if height < 128:
        side = jnp.concatenate([side, jnp.zeros((128 - height, 128), F32)], 0)
    return side.T


def stats_kernel(k, rows, side, came, *refs):
    side_out, stats_out = refs[-2:]
    lead = stats_out.shape[1] - 256
    if k == 0:
        kept_sums = refs[0]
        units = kept_sums.shape[1]
        stats_out[:, :units] = (kept_sums[...].astype(F32) + came[:, :units].astype(F32)).astype(BF16)
        both = side[:, units:].astype(F32) + came[:, units:].astype(F32)
        stats_out[:, units:lead] = both[:, : lead - units].astype(BF16)
        both = both[:, lead - units :]
        both = jnp.concatenate([both[:, 128 * i : 128 * (i + 1)] for i in range(rows // 16)], 0)
    else:
        both = side[...].astype(F32) + came[...].astype(F32)
    side_out[...] = both
    stats = across_rows(both)[:32].astype(BF16)
    stats_out[:, lead : lead + 128] = stats[:16]
    stats_out[:, lead + 128 :] = stats[16:]


def merge_kernel(kept, came, _, sent_out):
    sent_out[...] = (kept[...] + came[...].astype(F32)).astype(BF16)


def rows_kernel(features, text, side, stats, *refs):
    out = refs[-1]
    rows = side.shape[0]
    lead = stats.shape[1] - 256
    stats = jnp.concatenate([stats[:, lead : lead + 128], stats[:, lead + 128 :]], 0)
    sides = [side[...], across_rows(stats.astype(F32))[:rows]]
    lane = lax.broadcasted_iota(jnp.int32, (rows, 128), 1)
    field = lane % 4
    summed = sides[0] + sides[1]
    add = lambda values, mask: jnp.sum(jnp.where(mask, values, 0.0), -1, keepdims=True)
    centres, measures = lane < 8, (lane >= 16) & (lane < 24)
    average = (
        add(summed, centres & (field == 0)) * features + add(summed, measures & (field < 2))
    ) / D
    spread = add(summed, measures & (field >= 2))
    aparts = []
    for side in sides:
        apart = jnp.where(centres, side - average, 0.0)
        for core in range(2):
            off = add(apart, lane == 4 * core)
            own = lane // 4 == 4 + core
            spread = spread + off * (2.0 * add(side, own & (field < 2)) + features * off)
        aparts.append(apart)
    scale = lax.rsqrt(spread / D + norm_eps)
    of_text = jnp.where(text[...] > 0.5, 1, 0)
    mine = centres & (lane % 2 == of_text)
    packed, shift = None, 0
    for apart in aparts:
        factor = jnp.where(mine, jnp.where(field < 2, apart * scale, 1.0), 0.0)
        high = factor.astype(BF16).astype(F32)
        for part in (high, high, factor - high, factor - high):
            part = pltpu.roll(part, shift, 1) if shift else part
            packed = part if packed is None else packed + part
            shift += 8
    out[...] = jnp.where(lane < 64, packed, scale)


def activate_kernel(total, came, rows_in, first_sent, first_came, *refs):
    act_out = refs[-1]
    rows, units = act_out.shape
    packed, scale = rows_in[:, :64].astype(BF16), rows_in[:, 64:65]
    own, other = first_sent[:, :units], first_came[:, :units]
    factors = jnp.concatenate([own, own, other, other], 0)
    for t in range(0, units, TILE):
        columns = slice(t, t + TILE)
        pre = total[:rows, columns].astype(F32) + came[:rows, columns].astype(F32)
        extra = jnp.dot(packed, factors[:, columns], preferred_element_type=F32)
        act_out[:, columns] = jax.nn.gelu(pre * scale + extra, approximate=True).astype(BF16)


def contract_own_kernel(k, act, w, mine, chip, other, out, *ends_out):
    core = lax.axis_index("narrow") % 2
    units = w.shape[0] // 2
    rows = pl.ds(pl.multiple_of(core * units, 128), units)
    out[...] = jnp.dot(act[...], w[rows, :], preferred_element_type=F32)
    if k == 0:
        units = w.shape[0] // 2
        ends = slice(units, units + 128)
        total = chip[:, ends].astype(F32) + other[:, ends].astype(F32)
        total = total[:8] + total[8:]
        total = total + pltpu.roll(total, 4, 0)
        own = mine[...].astype(F32)
        own = own[:8] + own[8:]
        own = own + pltpu.roll(own, 4, 0)
        ends_out[0][...] = jnp.concatenate([total, own, jnp.zeros((112, 128), F32)], 0)


def contract_other_kernel(k, place, act, so_far, w, *refs):
    outs = refs[-4:]
    core = lax.axis_index("narrow") % 2
    units = w.shape[0] // 2
    rows = pl.ds(pl.multiple_of((1 - core) * units, 128), units)
    total = so_far[...] + jnp.dot(act[...], w[rows, :], preferred_element_type=F32)
    spread = jnp.dot(place[...], total.astype(BF16), preferred_element_type=F32).astype(BF16)
    size = size_of(k)
    for s in range(4):
        outs[s][...] = spread[s * size : (s + 1) * size]


def finish_kernel(slots, hidden, mod, out_weight, ends, *refs):
    pieces, (layer_out, bundle_out) = refs[: 4 * CHUNKS], refs[4 * CHUNKS :]
    result = jnp.zeros(hidden.shape, F32)
    for k in range(CHUNKS):
        total = pieces[4 * k][...].astype(F32)
        for s in (1, 2, 3):
            total = total + pieces[4 * k + s][...].astype(F32)
        total = jnp.concatenate([total] * (CAP // size_of(k)), 0)
        result = jnp.where(slots[:, 2 + k : 3 + k] > 0.5, total, result)
    gate = jnp.where(slots[:, 1:2] > 0.5, mod[5:6, :], mod[2:3, :])
    layer = hidden[...].astype(F32) + gate * result
    layer = jnp.where(slots[:, 0:1] > 0.5, layer, 0.0).astype(BF16)
    layer_out[...] = layer
    x = layer.astype(F32)
    total = jnp.sum(x, -1, keepdims=True)
    square = jnp.sum(x * x, -1, keepdims=True)
    centre = total / x.shape[1]
    width = out_weight.shape[0]
    product = lax.dot_general(
        ((x - centre) * (1.0 + mod[7:8, :])).astype(BF16),
        out_weight[...],
        (((1,), (1,)), ((), ())),
        preferred_element_type=F32,
    )
    product = product + centre * ends[8:9, :width]
    lane = lax.broadcasted_iota(jnp.int32, (CAP, width), 1)
    side = jnp.where(lane == 0, total, jnp.where(lane == 1, square, 0.0))
    video = (slots[:, 0:1] > 0.5) & (slots[:, 1:2] < 0.5)
    bundle = jnp.where(video, jnp.concatenate([product, side], 1), 0.0)
    kept = bundle[:VIDEO]
    for first in range(VIDEO, CAP, VIDEO):
        kept = kept + bundle[first : first + VIDEO]
    bundle_out[...] = kept


def write_kernel(layer, out):
    out[...] = layer[...]


def add_kernel(left, right, out):
    out[...] = left[...] + right[...]


def noise_kernel(step, alphas, video, latent, _, out):
    index = lax.broadcasted_iota(jnp.int32, (8, 128), 0) * 128 + lax.broadcasted_iota(
        jnp.int32, (8, 128), 1
    )
    alpha = jnp.sum(
        jnp.sum(jnp.where(index == step[...], alphas[...], 0.0), 0, keepdims=True),
        1,
        keepdims=True,
    )
    width = latent.shape[0]
    out[:width, :] = jnp.where(video[0:1] > 0.5, jnp.sqrt(alpha) * latent[...], 0.0)
    out[width:, :] = jnp.where(video[...] > 0.5, jnp.sqrt(1.0 - alpha), 0.0)


def latent_kernel(noise, ends, mine, other_y, other, mine_y, out):
    width = out.shape[0]
    factor = noise[width : width + 1]

    def velocity(total):
        average = total[:, width : width + 1] / D
        variance = total[:, width + 1 : width + 2] / D - average * average
        return (total[:, :width] - average * ends[0:1, :width]) * lax.rsqrt(
            variance + norm_eps
        ) + ends[1:2, :width]

    first = lax.axis_index("cfg") == 0
    guided = velocity(mine[...] + mine_y[...]) * jnp.where(first, guidance, 1.0 - guidance)
    guided = guided + velocity(other[...] + other_y[...]) * jnp.where(
        first, 1.0 - guidance, guidance
    )
    guided = jnp.concatenate([guided] * (CAP // VIDEO), 0)
    guided = jnp.concatenate([guided, jnp.zeros((CAP, 128 - width), F32)], 1).T[:width]
    guided = jnp.where(factor > 0.0, guided, 0.0)
    out[...] = noise[:width] - factor * guided


def alpha_constant():
    ends = np.sqrt(np.float64(0.00085)), np.sqrt(np.float64(0.012))
    betas = np.linspace(ends[0], ends[1], 1000, dtype=np.float64) ** 2
    return np.pad(np.cumprod(1.0 - betas), (0, 24)).astype(np.float32).reshape(8, 128)


def call(kernel, outs, args, spaces, scratch=(), weight=1):
    kinds = {"v": pltpu.VMEM, "s": pltpu.SMEM, "a": pl.ANY}
    return pl.pallas_call(
        kernel,
        out_shape=[jax.ShapeDtypeStruct(shape, dtype) for shape, dtype in outs],
        in_specs=[pl.BlockSpec(memory_space=kinds[letter]) for letter in spaces],
        out_specs=[pl.BlockSpec(memory_space=pltpu.VMEM) for _ in outs],
        scratch_shapes=list(scratch),
        compiler_params=pltpu.CompilerParams(vmem_limit_bytes=24 * 2**20),
        cost_estimate=pl.CostEstimate(flops=weight, bytes_accessed=1, transcendentals=0),
    )(*args)


def four_blocks(
    hidden, split_table, modulation, expand_weight, contract_weight, output_weight, latent, timestep
):
    hidden = hidden[0]
    features = hidden.shape[1]
    units = expand_weight.shape[1] // 2
    width = output_weight.shape[1]
    payload = units + 128

    in_place = lambda array: pltpu.with_memory_space_constraint(array, pltpu.HBM)
    (piece,) = call(
        take_kernel,
        [((QUOTAS[1], features), BF16)],
        [in_place(hidden)],
        "a",
        [pltpu.SemaphoreType.DMA(())],
    )
    across = swap(piece, "wide", 2, 4)
    near = swap(hidden, "wide", 1, 4)

    tiles = units // TILE
    chunks = range(CHUNKS)
    made = call(
        prepare_kernel,
        [((size_of(k), features), BF16) for k in chunks[1:]]
        + [((2 * size_of(k), 4 * QUOTAS[k + 1]), BF16) for k in chunks]
        + [((4 * size_of(k), 2 * size_of(k)), BF16) for k in chunks]
        + [((2 * size_of(k), 128), F32) for k in chunks]
        + [
            ((features, units), BF16),
            ((features, units), BF16),
            (hidden.shape, BF16),
            (modulation.shape, F32),
            ((width, features), BF16),
            ((16, features), BF16),
            ((16, 128), BF16),
            ((CAP, 128), F32),
            ((8, CAP), F32),
            ((8, 128), jnp.int32),
        ],
        [
            in_place(split_table),
            timestep,
            in_place(hidden),
            in_place(modulation),
            in_place(output_weight.T),
            in_place(expand_weight),
        ],
        "asaaaa",
        [
            pltpu.SMEM(split_table.shape, jnp.int32),
            pltpu.SemaphoreType.DMA((2, tiles)),
            pltpu.SemaphoreType.DMA((4,)),
        ],
    )
    later, made = made[: CHUNKS - 1], made[CHUNKS - 1 :]
    gathers, made = made[:CHUNKS], made[CHUNKS:]
    spreads, made = made[:CHUNKS], made[CHUNKS:]
    texts, made = made[:CHUNKS], made[CHUNKS:]
    held_sent, held_kept, tokens, mod, out_weight, rows_in, ends_mine, slots, video, step = made
    later = [swap(piece, "wide", 2, 4) for piece in later]
    (across,) = call(pass_kernel, [(across.shape, BF16)], [across, slots], "va")
    far = [across, swap(across, "wide", 1, 4)]

    merged = []
    before = []
    for k in chunks:
        rows = 2 * size_of(k)
        extra = 16 if k == 0 else 0
        z, sent, side = call(
            functools.partial(expand_sent_kernel, k),
            [
                ((rows + extra, features), BF16),
                ((rows, units), BF16),
                ((16, payload + 8 * rows) if k == 0 else (rows, 128), BF16),
            ],
            [texts[k], mod, gathers[k], tokens, near, *far, held_sent, rows_in, ends_mine, *before],
            "vvvvv" + "v" * len(far) + "vvv" + "a" * len(before),
            weight=LONG,
        )
        side_came, came = [swap(array, "narrow", 1, 4) for array in (side, sent)]
        kept, *sums_made = call(
            functools.partial(expand_kept_kernel, k),
            [((rows, units), F32)] + ([((16, units), BF16)] if k == 0 else []),
            [z, held_kept, sent, side],
            "vvaa",
            weight=LONG,
        )
        side, stats = call(
            functools.partial(stats_kernel, k, rows),
            [((rows, 128), F32), ((16, 256 + (payload if k == 0 else 0)), BF16)],
            [side, side_came, *sums_made],
            "vv" + "v" * len(sums_made),
        )
        stats_came = swap(stats, "narrow", 2, 4)
        (sent,) = call(merge_kernel, [((rows, units), BF16)], [kept, came, stats], "vva")
        if k + 1 < CHUNKS:
            (across,) = call(
                pass_kernel, [(later[k].shape, BF16)], [later[k], sent], "va"
            )
            far.extend([across, swap(across, "wide", 1, 4)])
        if k == 0:
            (held_out,) = call(
                hold_kernel,
                [(contract_weight.shape, BF16)],
                [in_place(contract_weight), across, stats],
                "aaa",
                [pltpu.SemaphoreType.DMA((4,))],
                weight=LONG,
            )
        if k == 0:
            (noise,) = call(
                noise_kernel,
                [((width + 8, CAP), F32)],
                [step, alpha_constant(), video, latent.T, sent],
                "vvvva",
                weight=LONG,
            )
        before = [sent, noise, held_out]
        came = swap(sent, "narrow", 2, 4)
        merged.append((sent, stats, [sent, came, side, stats_came]))

    returned = []
    before = []
    first = [merged[0][1], merged[0][2][3]]
    def rows_call(k, *after):
        return call(
            functools.partial(rows_kernel, features),
            [((2 * size_of(k), 128), F32)],
            [texts[k], *merged[k][2][2:], *after],
            "vvv" + "a" * len(after),
        )[0]

    of_rows = [rows_call(0, merged[-1][0])]
    for k in chunks:
        rows = 2 * size_of(k)
        if k + 1 < CHUNKS:
            before = before + [merged[k + 1][0], merged[k + 1][1]]
        (act,) = call(
            activate_kernel,
            [((rows, units), BF16)],
            [*merged[k][2][:2], of_rows[k], *first, *before],
            "vvvvv" + "a" * len(before),
        )
        act_came = swap(act, "narrow", 1, 4)
        if k + 1 < CHUNKS:
            of_rows.append(rows_call(k + 1, act))
        out, *ends_made = call(
            functools.partial(contract_own_kernel, k),
            [((rows, features), F32)] + ([((128, 128), F32)] if k == 0 else []),
            [act, held_out, ends_mine, *first],
            "vvvvv",
            weight=LONG,
        )
        ends = ends_made[0] if k == 0 else ends
        pieces = call(
            functools.partial(contract_other_kernel, k),
            [((size_of(k), features), BF16)] * 4,
            [spreads[k], act_came, out, held_out, *of_rows[k + 1 : k + 2]],
            "vvvv" + "a" * len(of_rows[k + 1 : k + 2]),
        )
        before = pieces
        distances = (3, 2, 1) if k + 1 < CHUNKS else (2, 3, 1)
        returned += [pieces[0], *(swap(pieces[s], "wide", s, 4) for s in distances)]

    layer, bundle = call(
        finish_kernel,
        [((CAP, features), BF16), ((VIDEO, 2 * width), F32)],
        [slots, tokens, mod, out_weight, ends, *returned],
        "v" * (5 + len(returned)),
    )
    (layer_out,) = call(write_kernel, [((CAP, features), BF16)], [layer], "v", weight=LONG)
    (bundle,) = call(
        add_kernel, [((VIDEO, 2 * width), F32)], [bundle, swap(bundle, "narrow", 1, 4)], "vv"
    )
    (clean_latent,) = call(
        latent_kernel,
        [((width, CAP), F32)],
        [noise, ends, bundle] + [swap(bundle, ("cfg", "narrow"), n, 8) for n in (6, 4, 2)],
        "vvvvvv",
    )
    return (layer_out[None], clean_latent.T)


def solution(mesh):
    by_swaps = (mesh.shape["wide"], mesh.shape["narrow"], mesh.shape["cfg"]) == (4, 4, 2)
    return jax.shard_map(
        four_blocks if by_swaps else any_slice,
        mesh=mesh,
        in_specs=(
            P("cfg", "wide", "narrow"),
            P(),
            P(None, "narrow"),
            P("narrow", "wide"),
            P("wide", "narrow"),
            P("narrow", None),
            P("wide", None),
            P(),
        ),
        out_specs=(P("cfg", "wide", "narrow"), P("wide", None)),
        check_vma=False,
    )
```

```python
import functools

import jax
import jax.numpy as jnp
import numpy as np
from jax import lax
from jax.experimental import pallas as pl
from jax.experimental.pallas import tpu as pltpu
from jax.sharding import PartitionSpec as P

D = 3072
TEXT = 226


norm_eps = 1e-05
guidance = 6.0


def alpha_table():
    steps_index = jnp.arange(1000, dtype=jnp.int32)
    start_root = 0.00085**0.5
    end_root = 0.012**0.5
    roots = start_root + (end_root - start_root) * steps_index.astype(jnp.float32) / 999.0
    return (steps_index, jnp.cumprod(1.0 - roots * roots))


def feature_norm(values, shifts, scaling):
    totals, squares = lax.psum(
        (jnp.sum(values, -1, keepdims=True), jnp.sum(values * values, -1, keepdims=True)), "narrow"
    )
    average = totals / D
    variance = squares / D - average * average
    return (values - average) * lax.rsqrt(variance + norm_eps) * (1.0 + scaling) + shifts


def any_slice(
    hidden, split_table, modulation, expand_weight, contract_weight, output_weight, latent, timestep
):
    capacity = hidden.shape[1]
    wide_index = lax.axis_index("wide")
    table_index = jnp.arange(split_table.shape[0], dtype=jnp.int32)
    offset = jnp.sum(jnp.where(table_index < wide_index, split_table, 0))
    own_count = jnp.sum(jnp.where(table_index == wide_index, split_table, 0))
    slot_index = jnp.arange(capacity, dtype=jnp.int32)
    position = offset + slot_index
    slot_live = slot_index < own_count
    is_text = slot_live & (position < TEXT)
    is_video = slot_live & (position >= TEXT)
    text_column = is_text[:, None]
    shifts = jnp.where(text_column, modulation[3], modulation[0])
    scaling = jnp.where(text_column, modulation[4], modulation[1])
    gating = jnp.where(text_column, modulation[5], modulation[2])
    values = hidden[0].astype(jnp.float32)
    normed = feature_norm(values, shifts, scaling).astype(jnp.bfloat16)
    hidden_part = jnp.dot(
        lax.all_gather(normed, "wide", axis=0, tiled=True),
        expand_weight,
        preferred_element_type=jnp.float32,
    )
    hidden_pre = lax.psum(hidden_part, "narrow")
    activated = jax.nn.gelu(hidden_pre, approximate=True).astype(jnp.bfloat16)
    ff_result = lax.psum_scatter(
        jnp.dot(activated, contract_weight, preferred_element_type=jnp.float32),
        "wide",
        scatter_dimension=0,
        tiled=True,
    )
    layer_out = jnp.where(slot_live[:, None], values + gating * ff_result, 0.0).astype(jnp.bfloat16)
    final_in = layer_out.astype(jnp.float32)
    final_normed = feature_norm(final_in, modulation[6], modulation[7]).astype(jnp.bfloat16)
    velocity_part = jnp.dot(final_normed, output_weight, preferred_element_type=jnp.float32)
    copy_weight = jnp.where(lax.axis_index("cfg") == 0, guidance, 1.0 - guidance)
    guided = lax.psum(velocity_part * copy_weight, ("cfg", "narrow"))
    steps_index, alpha_bar = alpha_table()
    alpha_now = jnp.sum(jnp.where(steps_index == timestep[0], alpha_bar, 0.0))
    clean_latent = jnp.where(
        is_video[:, None], jnp.sqrt(alpha_now) * latent - jnp.sqrt(1.0 - alpha_now) * guided, 0.0
    )
    return (layer_out[None], clean_latent)


QUOTAS = (0, 64, 128)
CAP = 128
VIDEO = 32
CHUNKS = len(QUOTAS) - 1
F32, BF16 = jnp.float32, jnp.bfloat16
TILE = 768
LONG = 10**10


def size_of(k):
    return QUOTAS[k + 1] - QUOTAS[k]


def swap(array, axis, distance, size):
    return lax.ppermute(array, axis, [(i, i ^ distance) for i in range(size)])


def z_swaps(array):
    return [swap(array, "wide", s, 4) for s in (1, 2, 3)]


def choose(values, index):
    out = values[0]
    for i in range(1, 4):
        out = jnp.where(index == i, values[i], out)
    return out


def layout(table):
    counts = [table[b] for b in range(4)]
    largest = jnp.int32(3)
    for b in (2, 1, 0):
        largest = jnp.where(counts[b] == CAP, b, largest)
    starts, others, ranks, offsets = [], [], [], []
    rank, offset = jnp.int32(0), jnp.int32(0)
    for b in range(4):
        other = jnp.where(largest == b, 0, 1)
        ranks.append(rank * other)
        others.append(other)
        offsets.append(offset)
        rank = rank + other * counts[b]
        offset = offset + counts[b]
    block = lax.axis_index("wide")
    of = lambda values: [choose(values, jnp.bitwise_xor(block, s)) for s in range(4)]
    return of(ranks), of(counts), of(others), of(offsets)[0], choose(offsets, largest)


def high_low(values):
    high = values.astype(BF16)
    return high, (values - high.astype(F32)).astype(BF16)


def load(source, place, sems):
    parts = sems.shape[0]
    height = source.shape[0] // parts
    copies = []
    for t in range(parts):
        rows = pl.ds(t * height, height)
        copies.append(pltpu.make_async_copy(source.at[rows, :], place.at[rows, :], sems.at[t]))
        copies[-1].start()
    return copies


def load_half(source, half, place, sems):
    width = place.shape[1]
    copies = []
    for t in range(0, width, TILE):
        columns = pl.ds(pl.multiple_of(half * width + t, 128), TILE)
        copies.append(
            pltpu.make_async_copy(
                source.at[:, columns], place.at[:, pl.ds(t, TILE)], sems.at[len(copies)]
            )
        )
        copies[-1].start()
    return copies


def rows_of(parts, core):
    total = parts[:8] + parts[8:]
    total = jnp.where(core == 0, total, pltpu.roll(total, 4, 0))
    high, low = high_low(total)
    return jnp.concatenate([high.astype(F32), low.astype(F32)], 0).astype(BF16)


def hold_kernel(source, *refs):
    place, sems = refs[-2:]
    for copy in load(source, place, sems):
        copy.wait()


def text_rows(k, largest_offset):
    size = size_of(k)
    row = lax.broadcasted_iota(jnp.int32, (2 * size, 1), 0)
    rank = jnp.where(row < size, row, row - size) + QUOTAS[k]
    position = jnp.where(
        row < size, rank + largest_offset, jnp.where(rank < largest_offset, rank, rank + CAP)
    )
    return position < TEXT


def gather_matrix(k, ranks, counts, others):
    size = size_of(k)
    places = []
    for p in range(k + 1):
        piece = size_of(p)
        lane = lax.broadcasted_iota(jnp.int32, (1, 4 * piece), 1)
        which, slot = lane // piece, lane % piece + QUOTAS[p]
        rank = slot + choose(ranks, which) - QUOTAS[k]
        live = (rank >= 0) & (rank < size) & (slot < choose(counts, which))
        row = jnp.where(live, rank + choose(others, which) * size, -1)
        at = lax.broadcasted_iota(jnp.int32, (2 * size, 4 * piece), 0)
        places.append(jnp.where(at == row, 1.0, 0.0).astype(BF16))
    return jnp.concatenate(places, 1)


def spread_matrix(k, ranks, counts, others):
    size = size_of(k)
    places = []
    for s in range(4):
        first = jnp.maximum(QUOTAS[k] - ranks[s], 0)
        last = jnp.minimum(counts[s], QUOTAS[k + 1] - ranks[s])
        index = lax.broadcasted_iota(jnp.int32, (size, 1), 0)
        slot = first + jnp.bitwise_and(index - first, size - 1)
        row = jnp.where(slot < last, slot + ranks[s] - QUOTAS[k] + others[s] * size, -1)
        at = lax.broadcasted_iota(jnp.int32, (size, 2 * size), 1)
        places.append(jnp.where(at == row, 1.0, 0.0).astype(BF16))
    return jnp.concatenate(places, 0)


def take_kernel(source, piece, sem):
    copy = pltpu.make_async_copy(source.at[pl.ds(0, piece.shape[0]), :], piece, sem)
    copy.start()
    copy.wait()


def prepare_kernel(table_in, timestep, tokens_in, mod_in, out_weight, w, *refs):
    later, refs = refs[: CHUNKS - 1], refs[CHUNKS - 1 :]
    gathers, refs = refs[:CHUNKS], refs[CHUNKS:]
    spreads, refs = refs[:CHUNKS], refs[CHUNKS:]
    texts, refs = refs[:CHUNKS], refs[CHUNKS:]
    held, kept, tokens, mod, weight, rows_out, ends_out, slots_out, video_out, step_out = refs[:10]
    table, sems, small = refs[10:]
    step_out[...] = jnp.full(step_out.shape, timestep[0], jnp.int32)
    core = lax.axis_index("narrow") % 2
    sources = (table_in, mod_in, out_weight, tokens_in)
    copies = [
        pltpu.make_async_copy(source, place, small.at[i])
        for i, (source, place) in enumerate(zip(sources, (table, mod, weight, tokens)))
    ]
    for copy in copies:
        copy.start()
    big = load_half(w, 1 - core, held, sems.at[0]) + load_half(w, core, kept, sems.at[1])

    copies[0].wait()
    ranks, counts, others, offset, largest_offset = layout(table)
    for k in range(CHUNKS):
        gathers[k][...] = gather_matrix(k, ranks, counts, others)
        spreads[k][...] = spread_matrix(k, ranks, counts, others)
        text = jnp.where(text_rows(k, largest_offset), 1.0, 0.0)
        texts[k][...] = jnp.broadcast_to(text, texts[k].shape)
    slot = lax.broadcasted_iota(jnp.int32, (CAP, 128), 0)
    lane = lax.broadcasted_iota(jnp.int32, (CAP, 128), 1)
    rank = slot + ranks[0]
    flag = lambda condition: jnp.where(condition, 1.0, 0.0)
    kind = jnp.where(lane == 0, flag(slot < counts[0]), flag(slot + offset < TEXT))
    for k in range(CHUNKS):
        kind = jnp.where(
            lane == 2 + k, flag((rank >= QUOTAS[k]) & (rank < QUOTAS[k + 1])), kind
        )
    slots_out[...] = kind
    slot = lax.broadcasted_iota(jnp.int32, (8, CAP), 1)
    video_out[...] = jnp.where((slot < counts[0]) & (slot + offset >= TEXT), 1.0, 0.0)

    copies[1].wait()
    row = lax.broadcasted_iota(jnp.int32, (8, 1), 0)
    rows = jnp.where(row == 0, 1.0 + mod[1:2, :], jnp.zeros((8, 1), F32))
    rows = jnp.where(row == 1, 1.0 + mod[4:5, :], rows)
    rows = jnp.where(row == 2, mod[0:1, :], rows)
    rows = jnp.where(row == 3, mod[3:4, :], rows)
    rows_out[...] = jnp.concatenate(high_low(rows), 0)
    rows = jnp.where(row == 0, 1.0 + mod[7:8, :], jnp.zeros((8, 1), F32))
    rows = jnp.where(row == 1, mod[6:7, :], rows)
    copies[2].wait()
    ends = lax.dot_general(
        jnp.concatenate(high_low(rows), 0),
        weight[...],
        (((1,), (1,)), ((), ())),
        preferred_element_type=F32,
    )
    ends = rows_of(ends, core)
    ends_out[...] = jnp.concatenate([ends, jnp.zeros((16, 128 - ends.shape[1]), BF16)], 1)
    copies[3].wait()
    for k in range(1, CHUNKS):
        later[k - 1][...] = tokens[QUOTAS[k] : QUOTAS[k + 1], :]
    for copy in big:
        copy.wait()


def expand_sent_kernel(k, text, mod, place, own, near, *refs):
    far, (w, sums, ends) = refs[: 2 * (k + 1)], refs[2 * (k + 1) : 2 * (k + 1) + 3]
    z_out, sent_out, side_out = refs[-3:]
    core = lax.axis_index("narrow") % 2
    units = w.shape[1]
    rows = place.shape[0]
    pieces = []
    for p in range(k + 1):
        of_chunk = slice(QUOTAS[p], QUOTAS[p + 1])
        pieces += [own[of_chunk, :], near[of_chunk, :], far[2 * p][...], far[2 * p + 1][...]]
    tokens = jnp.concatenate(pieces, 0)
    x = jnp.dot(place[...], tokens, preferred_element_type=F32)
    centre = (jnp.sum(x, -1, keepdims=True) / x.shape[1]).astype(BF16).astype(F32)
    x = x - centre
    z = (x * (1.0 + jnp.where(text[:, :1] > 0.5, mod[4:5, :], mod[1:2, :]))).astype(BF16)
    if k == 0:
        z = jnp.concatenate([z, sums[...]], 0)
    z_out[...] = z
    if k == 0:
        lead = side_out.shape[1] - 8 * 128
        side_out[:, units:lead] = ends[...]
    for t in range(0, units, TILE):
        columns = slice(t, t + TILE)
        product = jnp.dot(z, w[:, columns], preferred_element_type=F32)
        sent_out[:, columns] = product[:rows].astype(BF16)
        if k == 0:
            side_out[:, columns] = rows_of(product[rows:], core)
    total = jnp.sum(x, -1, keepdims=True)
    square = jnp.sum(x * x, -1, keepdims=True)
    total_high = total.astype(BF16).astype(F32)
    square_high = square.astype(BF16).astype(F32)
    lane = lax.broadcasted_iota(jnp.int32, (rows, 128), 1) - 4 * core
    side = jnp.where((lane == 0) | (lane == 1), centre, 0.0)
    side = jnp.where(lane == 16, total_high, side)
    side = jnp.where(lane == 17, total - total_high, side)
    side = jnp.where(lane == 18, square_high, side)
    side = jnp.where(lane == 19, square - square_high, side).astype(BF16)
    if k == 0:
        for i in range(rows // 16):
            side_out[:, lead + 128 * i : lead + 128 * (i + 1)] = side[16 * i : 16 * (i + 1)]
    else:
        side_out[...] = side


def expand_kept_kernel(k, z, w, _, __, *refs):
    kept_out = refs[-1 if k else -2]
    core = lax.axis_index("narrow") % 2
    rows = kept_out.shape[0]
    for t in range(0, w.shape[1], TILE):
        columns = slice(t, t + TILE)
        product = jnp.dot(z[...], w[:, columns], preferred_element_type=F32)
        kept_out[:, columns] = product[:rows]
        if k == 0:
            refs[-1][:, columns] = rows_of(product[rows:], core)


def pass_kernel(piece, _, out):
    out[...] = piece[...]


def across_rows(side):
    height = side.shape[0]
    if height < 128:
        side = jnp.concatenate([side, jnp.zeros((128 - height, 128), F32)], 0)
    return side.T


def stats_kernel(k, rows, side, came, *refs):
    side_out, stats_out = refs[-2:]
    lead = stats_out.shape[1] - 256
    if k == 0:
        kept_sums = refs[0]
        units = kept_sums.shape[1]
        stats_out[:, :units] = (kept_sums[...].astype(F32) + came[:, :units].astype(F32)).astype(BF16)
        both = side[:, units:].astype(F32) + came[:, units:].astype(F32)
        stats_out[:, units:lead] = both[:, : lead - units].astype(BF16)
        both = both[:, lead - units :]
        both = jnp.concatenate([both[:, 128 * i : 128 * (i + 1)] for i in range(rows // 16)], 0)
    else:
        both = side[...].astype(F32) + came[...].astype(F32)
    side_out[...] = both
    stats = across_rows(both)[:32].astype(BF16)
    stats_out[:, lead : lead + 128] = stats[:16]
    stats_out[:, lead + 128 :] = stats[16:]


def merge_kernel(kept, came, _, sent_out):
    sent_out[...] = (kept[...] + came[...].astype(F32)).astype(BF16)


def rows_kernel(features, text, side, stats, *refs):
    out = refs[-1]
    rows = side.shape[0]
    lead = stats.shape[1] - 256
    stats = jnp.concatenate([stats[:, lead : lead + 128], stats[:, lead + 128 :]], 0)
    sides = [side[...], across_rows(stats.astype(F32))[:rows]]
    lane = lax.broadcasted_iota(jnp.int32, (rows, 128), 1)
    field = lane % 4
    summed = sides[0] + sides[1]
    add = lambda values, mask: jnp.sum(jnp.where(mask, values, 0.0), -1, keepdims=True)
    centres, measures = lane < 8, (lane >= 16) & (lane < 24)
    average = (
        add(summed, centres & (field == 0)) * features + add(summed, measures & (field < 2))
    ) / D
    spread = add(summed, measures & (field >= 2))
    aparts = []
    for side in sides:
        apart = jnp.where(centres, side - average, 0.0)
        for core in range(2):
            off = add(apart, lane == 4 * core)
            own = lane // 4 == 4 + core
            spread = spread + off * (2.0 * add(side, own & (field < 2)) + features * off)
        aparts.append(apart)
    scale = lax.rsqrt(spread / D + norm_eps)
    of_text = jnp.where(text[...] > 0.5, 1, 0)
    mine = centres & (lane % 2 == of_text)
    packed, shift = None, 0
    for apart in aparts:
        factor = jnp.where(mine, jnp.where(field < 2, apart * scale, 1.0), 0.0)
        high = factor.astype(BF16).astype(F32)
        for part in (high, high, factor - high, factor - high):
            part = pltpu.roll(part, shift, 1) if shift else part
            packed = part if packed is None else packed + part
            shift += 8
    out[...] = jnp.where(lane < 64, packed, scale)


def activate_kernel(total, came, rows_in, first_sent, first_came, *refs):
    act_out = refs[-1]
    rows, units = act_out.shape
    packed, scale = rows_in[:, :64].astype(BF16), rows_in[:, 64:65]
    own, other = first_sent[:, :units], first_came[:, :units]
    factors = jnp.concatenate([own, own, other, other], 0)
    for t in range(0, units, TILE):
        columns = slice(t, t + TILE)
        pre = total[:rows, columns].astype(F32) + came[:rows, columns].astype(F32)
        extra = jnp.dot(packed, factors[:, columns], preferred_element_type=F32)
        act_out[:, columns] = jax.nn.gelu(pre * scale + extra, approximate=True).astype(BF16)


def contract_own_kernel(k, act, w, mine, chip, other, out, *ends_out):
    core = lax.axis_index("narrow") % 2
    units = w.shape[0] // 2
    rows = pl.ds(pl.multiple_of(core * units, 128), units)
    out[...] = jnp.dot(act[...], w[rows, :], preferred_element_type=F32)
    if k == 0:
        units = w.shape[0] // 2
        ends = slice(units, units + 128)
        total = chip[:, ends].astype(F32) + other[:, ends].astype(F32)
        total = total[:8] + total[8:]
        total = total + pltpu.roll(total, 4, 0)
        own = mine[...].astype(F32)
        own = own[:8] + own[8:]
        own = own + pltpu.roll(own, 4, 0)
        ends_out[0][...] = jnp.concatenate([total, own, jnp.zeros((112, 128), F32)], 0)


def contract_other_kernel(k, place, act, so_far, w, *refs):
    outs = refs[-4:]
    core = lax.axis_index("narrow") % 2
    units = w.shape[0] // 2
    rows = pl.ds(pl.multiple_of((1 - core) * units, 128), units)
    total = so_far[...] + jnp.dot(act[...], w[rows, :], preferred_element_type=F32)
    spread = jnp.dot(place[...], total.astype(BF16), preferred_element_type=F32).astype(BF16)
    size = size_of(k)
    for s in range(4):
        outs[s][...] = spread[s * size : (s + 1) * size]


def total_kernel(first, second, third, fourth, *refs):
    total = first[...].astype(F32) + second[...].astype(F32)
    refs[-1][...] = total + (third[...].astype(F32) + fourth[...].astype(F32))


def finish_kernel(slots, hidden, mod, out_weight, ends, *refs):
    totals, pieces = refs[: CHUNKS - 1], refs[CHUNKS - 1 : -2]
    layer_out, bundle_out = refs[-2:]
    total = pieces[0][...].astype(F32)
    for piece in pieces[1:]:
        total = total + piece[...].astype(F32)
    totals = [*(earlier[...] for earlier in totals), total]
    result = jnp.zeros(hidden.shape, F32)
    for k in range(CHUNKS):
        total = jnp.concatenate([totals[k]] * (CAP // size_of(k)), 0)
        result = jnp.where(slots[:, 2 + k : 3 + k] > 0.5, total, result)
    gate = jnp.where(slots[:, 1:2] > 0.5, mod[5:6, :], mod[2:3, :])
    layer = hidden[...].astype(F32) + gate * result
    layer = jnp.where(slots[:, 0:1] > 0.5, layer, 0.0).astype(BF16)
    layer_out[...] = layer
    x = layer.astype(F32)
    total = jnp.sum(x, -1, keepdims=True)
    square = jnp.sum(x * x, -1, keepdims=True)
    centre = total / x.shape[1]
    width = out_weight.shape[0]
    product = lax.dot_general(
        ((x - centre) * (1.0 + mod[7:8, :])).astype(BF16),
        out_weight[...],
        (((1,), (1,)), ((), ())),
        preferred_element_type=F32,
    )
    product = product + centre * ends[8:9, :width]
    lane = lax.broadcasted_iota(jnp.int32, (CAP, width), 1)
    side = jnp.where(lane == 0, total, jnp.where(lane == 1, square, 0.0))
    video = (slots[:, 0:1] > 0.5) & (slots[:, 1:2] < 0.5)
    bundle = jnp.where(video, jnp.concatenate([product, side], 1), 0.0)
    kept = bundle[:VIDEO]
    for first in range(VIDEO, CAP, VIDEO):
        kept = kept + bundle[first : first + VIDEO]
    bundle_out[...] = kept


def write_kernel(layer, out):
    out[...] = layer[...]


def add_kernel(left, right, out):
    out[...] = left[...] + right[...]


def noise_kernel(step, alphas, video, latent, _, out):
    index = lax.broadcasted_iota(jnp.int32, (8, 128), 0) * 128 + lax.broadcasted_iota(
        jnp.int32, (8, 128), 1
    )
    alpha = jnp.sum(
        jnp.sum(jnp.where(index == step[...], alphas[...], 0.0), 0, keepdims=True),
        1,
        keepdims=True,
    )
    width = latent.shape[0]
    out[:width, :] = jnp.where(video[0:1] > 0.5, jnp.sqrt(alpha) * latent[...], 0.0)
    out[width:, :] = jnp.where(video[...] > 0.5, jnp.sqrt(1.0 - alpha), 0.0)


def latent_kernel(noise, ends, mine, other_y, other, mine_y, out):
    width = out.shape[0]
    factor = noise[width : width + 1]

    def velocity(total):
        average = total[:, width : width + 1] / D
        variance = total[:, width + 1 : width + 2] / D - average * average
        return (total[:, :width] - average * ends[0:1, :width]) * lax.rsqrt(
            variance + norm_eps
        ) + ends[1:2, :width]

    first = lax.axis_index("cfg") == 0
    guided = velocity(mine[...] + mine_y[...]) * jnp.where(first, guidance, 1.0 - guidance)
    guided = guided + velocity(other[...] + other_y[...]) * jnp.where(
        first, 1.0 - guidance, guidance
    )
    guided = jnp.concatenate([guided] * (CAP // VIDEO), 0)
    guided = jnp.concatenate([guided, jnp.zeros((CAP, 128 - width), F32)], 1).T[:width]
    guided = jnp.where(factor > 0.0, guided, 0.0)
    out[...] = noise[:width] - factor * guided


def alpha_constant():
    ends = np.sqrt(np.float64(0.00085)), np.sqrt(np.float64(0.012))
    betas = np.linspace(ends[0], ends[1], 1000, dtype=np.float64) ** 2
    return np.pad(np.cumprod(1.0 - betas), (0, 24)).astype(np.float32).reshape(8, 128)


def call(kernel, outs, args, spaces, scratch=(), weight=1):
    kinds = {"v": pltpu.VMEM, "s": pltpu.SMEM, "a": pl.ANY}
    return pl.pallas_call(
        kernel,
        out_shape=[jax.ShapeDtypeStruct(shape, dtype) for shape, dtype in outs],
        in_specs=[pl.BlockSpec(memory_space=kinds[letter]) for letter in spaces],
        out_specs=[pl.BlockSpec(memory_space=pltpu.VMEM) for _ in outs],
        scratch_shapes=list(scratch),
        compiler_params=pltpu.CompilerParams(vmem_limit_bytes=24 * 2**20),
        cost_estimate=pl.CostEstimate(flops=weight, bytes_accessed=1, transcendentals=0),
    )(*args)


def four_blocks(
    hidden, split_table, modulation, expand_weight, contract_weight, output_weight, latent, timestep
):
    hidden = hidden[0]
    features = hidden.shape[1]
    units = expand_weight.shape[1] // 2
    width = output_weight.shape[1]
    payload = units + 128

    in_place = lambda array: pltpu.with_memory_space_constraint(array, pltpu.HBM)
    (piece,) = call(
        take_kernel,
        [((QUOTAS[1], features), BF16)],
        [in_place(hidden)],
        "a",
        [pltpu.SemaphoreType.DMA(())],
    )
    across = swap(piece, "wide", 2, 4)
    near = swap(hidden, "wide", 1, 4)

    tiles = units // TILE
    chunks = range(CHUNKS)
    made = call(
        prepare_kernel,
        [((size_of(k), features), BF16) for k in chunks[1:]]
        + [((2 * size_of(k), 4 * QUOTAS[k + 1]), BF16) for k in chunks]
        + [((4 * size_of(k), 2 * size_of(k)), BF16) for k in chunks]
        + [((2 * size_of(k), 128), F32) for k in chunks]
        + [
            ((features, units), BF16),
            ((features, units), BF16),
            (hidden.shape, BF16),
            (modulation.shape, F32),
            ((width, features), BF16),
            ((16, features), BF16),
            ((16, 128), BF16),
            ((CAP, 128), F32),
            ((8, CAP), F32),
            ((8, 128), jnp.int32),
        ],
        [
            in_place(split_table),
            timestep,
            in_place(hidden),
            in_place(modulation),
            in_place(output_weight.T),
            in_place(expand_weight),
        ],
        "asaaaa",
        [
            pltpu.SMEM(split_table.shape, jnp.int32),
            pltpu.SemaphoreType.DMA((2, tiles)),
            pltpu.SemaphoreType.DMA((4,)),
        ],
    )
    later, made = made[: CHUNKS - 1], made[CHUNKS - 1 :]
    gathers, made = made[:CHUNKS], made[CHUNKS:]
    spreads, made = made[:CHUNKS], made[CHUNKS:]
    texts, made = made[:CHUNKS], made[CHUNKS:]
    held_sent, held_kept, tokens, mod, out_weight, rows_in, ends_mine, slots, video, step = made
    later = [swap(piece, "wide", 2, 4) for piece in later]
    (across,) = call(pass_kernel, [(across.shape, BF16)], [across, slots], "va")
    far = [across, swap(across, "wide", 1, 4)]

    merged = []
    before = []
    for k in chunks:
        rows = 2 * size_of(k)
        extra = 16 if k == 0 else 0
        z, sent, side = call(
            functools.partial(expand_sent_kernel, k),
            [
                ((rows + extra, features), BF16),
                ((rows, units), BF16),
                ((16, payload + 8 * rows) if k == 0 else (rows, 128), BF16),
            ],
            [texts[k], mod, gathers[k], tokens, near, *far, held_sent, rows_in, ends_mine, *before],
            "vvvvv" + "v" * len(far) + "vvv" + "a" * len(before),
            weight=LONG,
        )
        side_came, came = [swap(array, "narrow", 1, 4) for array in (side, sent)]
        kept, *sums_made = call(
            functools.partial(expand_kept_kernel, k),
            [((rows, units), F32)] + ([((16, units), BF16)] if k == 0 else []),
            [z, held_kept, sent, side],
            "vvaa",
            weight=LONG,
        )
        side, stats = call(
            functools.partial(stats_kernel, k, rows),
            [((rows, 128), F32), ((16, 256 + (payload if k == 0 else 0)), BF16)],
            [side, side_came, *sums_made],
            "vv" + "v" * len(sums_made),
        )
        stats_came = swap(stats, "narrow", 2, 4)
        (sent,) = call(merge_kernel, [((rows, units), BF16)], [kept, came, stats], "vva")
        if k + 1 < CHUNKS:
            (across,) = call(
                pass_kernel, [(later[k].shape, BF16)], [later[k], sent], "va"
            )
            far.extend([across, swap(across, "wide", 1, 4)])
        if k == 0:
            (held_out,) = call(
                hold_kernel,
                [(contract_weight.shape, BF16)],
                [in_place(contract_weight), across, stats],
                "aaa",
                [pltpu.SemaphoreType.DMA((4,))],
                weight=LONG,
            )
        if k == 0:
            (noise,) = call(
                noise_kernel,
                [((width + 8, CAP), F32)],
                [step, alpha_constant(), video, latent.T, sent],
                "vvvva",
                weight=LONG,
            )
        before = [sent, noise, held_out]
        came = swap(sent, "narrow", 2, 4)
        merged.append((sent, stats, [sent, came, side, stats_came]))

    returned = []
    before = []
    first = [merged[0][1], merged[0][2][3]]
    def rows_call(k, *after):
        return call(
            functools.partial(rows_kernel, features),
            [((2 * size_of(k), 128), F32)],
            [texts[k], *merged[k][2][2:], *after],
            "vvv" + "a" * len(after),
        )[0]

    of_rows = [rows_call(0, merged[-1][0])]
    for k in chunks:
        rows = 2 * size_of(k)
        if k + 1 < CHUNKS:
            before = before + [merged[k + 1][0], merged[k + 1][1]]
        (act,) = call(
            activate_kernel,
            [((rows, units), BF16)],
            [*merged[k][2][:2], of_rows[k], *first, *before],
            "vvvvv" + "a" * len(before),
        )
        act_came = swap(act, "narrow", 1, 4)
        if k + 1 < CHUNKS:
            of_rows.append(rows_call(k + 1, act))
        out, *ends_made = call(
            functools.partial(contract_own_kernel, k),
            [((rows, features), F32)] + ([((128, 128), F32)] if k == 0 else []),
            [act, held_out, ends_mine, *first],
            "vvvvv",
            weight=LONG,
        )
        ends = ends_made[0] if k == 0 else ends
        pieces = call(
            functools.partial(contract_other_kernel, k),
            [((size_of(k), features), BF16)] * 4,
            [spreads[k], act_came, out, held_out, *of_rows[k + 1 : k + 2]],
            "vvvv" + "a" * len(of_rows[k + 1 : k + 2]),
        )
        before = pieces
        distances = (3, 2, 1) if k + 1 < CHUNKS else (2, 3, 1)
        arrived = [pieces[0], *(swap(pieces[s], "wide", s, 4) for s in distances)]
        if k + 1 < CHUNKS:
            arrived = call(
                total_kernel, [((size_of(k), features), F32)], arrived, "vvvv", weight=LONG
            )
        returned += arrived

    layer, bundle = call(
        finish_kernel,
        [((CAP, features), BF16), ((VIDEO, 2 * width), F32)],
        [slots, tokens, mod, out_weight, ends, *returned],
        "v" * (5 + len(returned)),
    )
    (layer_out,) = call(write_kernel, [((CAP, features), BF16)], [layer], "v", weight=LONG)
    (bundle,) = call(
        add_kernel, [((VIDEO, 2 * width), F32)], [bundle, swap(bundle, "narrow", 1, 4)], "vv"
    )
    (clean_latent,) = call(
        latent_kernel,
        [((width, CAP), F32)],
        [noise, ends, bundle] + [swap(bundle, ("cfg", "narrow"), n, 8) for n in (6, 4, 2)],
        "vvvvvv",
    )
    return (layer_out[None], clean_latent.T)


def solution(mesh):
    by_swaps = (mesh.shape["wide"], mesh.shape["narrow"], mesh.shape["cfg"]) == (4, 4, 2)
    return jax.shard_map(
        four_blocks if by_swaps else any_slice,
        mesh=mesh,
        in_specs=(
            P("cfg", "wide", "narrow"),
            P(),
            P(None, "narrow"),
            P("narrow", "wide"),
            P("wide", "narrow"),
            P("narrow", None),
            P("wide", None),
            P(),
        ),
        out_specs=(P("cfg", "wide", "narrow"), P("wide", None)),
        check_vma=False,
    )
```
